128 devices in a mesh: grid: 64 (over z, y, x), cell: 2 (over core).
Axes of the slice: x: 4, y: 4, z: 4, core: 2. Of those that a mesh axis runs over, the one named last changes fastest.
Arguments:
- spectrum: bfloat16 [1296, 512, 128], P(None, ('grid', 'cell')), may hold values from 0.049804688 to 1
- depth_factor: float32 [512, 128], P(('grid', 'cell')), may hold values from 0.5 to 1
- wet_mask: int32 [512, 128], P(('grid', 'cell')), may hold values 0 or 1
- frac_index: int32 [512, 128], P(('grid', 'cell')), may hold values from 0 to 3
- boundary_map: int32 [512, 2], P(('grid', 'cell')), may hold values from 0 to 511
- average_map: int32 [512, 128], P(('grid', 'cell')), may hold values from 0 to 511
- dia_plus: int32 [1296], replicated, may hold values from 0 to 1295
- dia_minus: int32 [1296], replicated, may hold values from 0 to 1295
- dia_coef: float32 [36], replicated, may hold values from 0.05 to 10
Outputs:
- spectrum_next: bfloat16 [1296, 512, 128], P(None, ('grid', 'cell'))
The draws below stay inside these ranges and needn't reach their ends.
Inputs may be any that keep to these rules, and one draw needn't show every extreme that they name: `boundary_map`: indices of parent cells within the strip of the same index. `average_map`: indices of parent cells within the strip of the same index; the parent grid's own entries are not read.
All inputs are finite; a program needn't handle non-finite values. No bound on the sum of `wet_mask` on one device may be relied on, other than what follows from the above.
Results may differ from the reference program's by a relative error of at most 0.0004.
Values may be sent and summed in bfloat16 or wider, within the bound.
No kernel may reach another device: no remote copies, remote signals or barrier semaphores. Data moves between devices by JAX's collectives and lax.ppermute only.
A program may use at most 64 MiB of HBM per device.

```python
import math
import jax
import jax.numpy as jnp

NF = 36
ND = 36
BINS = 1296
RX = 4
NY = 128
SUB = 2
CELLS_DEV = 512
ROWS = 512
N_GRID = 64
N_CELL = 2


def set_ends(array, stream_key, smallest, largest):
    extent = array.shape
    spot = [jax.random.randint(jax.random.fold_in(stream_key, axis), (), 0, extent[axis]) for axis in range(len(extent))]
    array = array.at[tuple(spot)].set(smallest)
    longest = extent.index(max(extent))
    spot[longest] = (spot[longest] + 1) % extent[longest]
    return array.at[tuple(spot)].set(largest)


def shard_levels(own_key, dims, shards, smallest, top_value):
    gain, own = 1.0, jax.random.fold_in(own_key, 6)
    for dim, blocks in shards:
        heights = jnp.exp(jax.random.uniform(jax.random.fold_in(own, dim), (blocks,), jnp.float32, smallest / len(shards), top_value / len(shards)))
        gain = gain * jnp.repeat(heights, dims[dim] // blocks).reshape([-1 if axis == dim else 1 for axis in range(len(dims))])
    return gain


def setup_inputs(seed: int = 0) -> dict:
    keys = jax.random.split(jax.random.key(seed), 10)
    spectrum = jnp.clip(jnp.exp(math.log(1.0) - 2.9996462 * jax.random.uniform(keys[0], (BINS, ROWS, NY), jnp.float32) ** shard_levels(keys[0], (BINS, ROWS, NY), ((1, 128),), -0.2, 0.2)), 0.049804688, 1.0).astype(jnp.bfloat16)
    depth_factor = jnp.clip(0.5 + 0.5 * jax.random.uniform(keys[1], (ROWS, NY), jnp.float32) ** shard_levels(keys[1], (ROWS, NY), ((0, 128),), -0.2, 0.2), 0.5, 1.0)
    wet_mask = set_ends((jax.random.randint(keys[2], (ROWS, NY), 0, 8) < 7).astype(jnp.int32), jax.random.fold_in(keys[2], 1), 0, 1)
    frac_index = set_ends(jax.random.randint(keys[3], (ROWS, NY), 0, 4), jax.random.fold_in(keys[3], 1), 0, 3).astype(jnp.int32)
    boundary_map = set_ends(jax.random.randint(keys[4], (ROWS, 2), 0, CELLS_DEV), jax.random.fold_in(keys[4], 1), 0, CELLS_DEV - 1).astype(jnp.int32)
    average_map = set_ends(jax.random.randint(keys[5], (ROWS, NY), 0, CELLS_DEV), jax.random.fold_in(keys[5], 1), 0, CELLS_DEV - 1).astype(jnp.int32)
    dia_plus = set_ends(jax.random.randint(keys[6], (BINS,), 0, BINS), jax.random.fold_in(keys[6], 1), 0, BINS - 1).astype(jnp.int32)
    dia_minus = set_ends(jax.random.randint(keys[7], (BINS,), 0, BINS), jax.random.fold_in(keys[7], 1), 0, BINS - 1).astype(jnp.int32)
    dia_coef = jnp.clip(jnp.exp(jax.random.uniform(keys[8], (NF,), jnp.float32, math.log(0.05), math.log(10.0))), 0.05, 10.0)
    return {"spectrum": spectrum, "depth_factor": depth_factor, "wet_mask": wet_mask, "frac_index": frac_index, "boundary_map": boundary_map, "average_map": average_map, "dia_plus": dia_plus, "dia_minus": dia_minus, "dia_coef": dia_coef}


FRACTIONS = (0.25, 0.5, 0.75, 1.0)


def speeds():
    frequency = jnp.arange(NF, dtype=jnp.float32)
    group_speed = 0.45 * jnp.exp(-math.log(1.1) * frequency)
    angles = (2.0 * math.pi / ND) * jnp.arange(ND, dtype=jnp.float32)
    along_x = (group_speed[:, None] * jnp.cos(angles)[None, :]).reshape(NF * ND)
    along_y = (group_speed[:, None] * jnp.sin(angles)[None, :]).reshape(NF * ND)
    return along_x, along_y


def fraction(frac_index):
    open_share = jnp.zeros(frac_index.shape, jnp.float32)
    for position, share in enumerate(FRACTIONS):
        open_share = open_share + jnp.where(frac_index == position, share, 0.0)
    return open_share


def substep(spectra, depth_cells, weight_cells, wet_cells, along_x, along_y):
    face_x = 0.5 * (depth_cells[:-1] + depth_cells[1:]) * weight_cells[:-1] * weight_cells[1:]
    speed_x = along_x[:, None, None] * face_x[None]
    flux_x = jnp.maximum(speed_x, 0.0) * spectra[:, :-1] + jnp.minimum(speed_x, 0.0) * spectra[:, 1:]
    interior = spectra[:, 1:-1]
    depth_inner = depth_cells[1:-1]
    weight_inner = weight_cells[1:-1]
    face_y = 0.5 * (depth_inner[:, :-1] + depth_inner[:, 1:]) * weight_inner[:, :-1] * weight_inner[:, 1:]
    speed_y = along_y[:, None, None] * face_y[None]
    flux_y = jnp.maximum(speed_y, 0.0) * interior[:, :, :-1] + jnp.minimum(speed_y, 0.0) * interior[:, :, 1:]
    zero_flux = jnp.zeros(interior.shape[:2] + (1,), jnp.float32)
    flux_y = jnp.concatenate([zero_flux, flux_y, zero_flux], axis=2)
    change = flux_x[:, 1:] - flux_x[:, :-1] + flux_y[:, :, 1:] - flux_y[:, :, :-1]
    return (interior - change) * wet_cells[1:-1][None]


def interact(spectra, dia_plus, dia_minus, dia_coef):
    plus_bins = jnp.take(spectra, dia_plus, axis=0)
    minus_bins = jnp.take(spectra, dia_minus, axis=0)
    coefficient = jnp.repeat(dia_coef, ND)[:, None]
    source = coefficient * (spectra * spectra * (plus_bins + minus_bins) - 2.0 * spectra * plus_bins * minus_bins)
    return jnp.maximum(spectra + 0.2 * source, 0.0)


def pad_rows(values):
    widths = [(0, 0)] * values.ndim
    widths[-2] = (1, 1)
    return jnp.pad(values, widths)


def reference(spectrum, depth_factor, wet_mask, frac_index, boundary_map, average_map, dia_plus, dia_minus, dia_coef):
    along_x, along_y = speeds()
    group_rows = N_CELL * RX
    cell_count = RX * NY
    fields = spectrum.astype(jnp.float32).reshape(BINS, N_GRID, group_rows, NY)
    parent_start = fields[:, N_GRID - 1].reshape(BINS, N_CELL, cell_count)
    owners = (jnp.arange(group_rows, dtype=jnp.int32) // RX).astype(jnp.int32)
    child_outputs = []
    child_sums = jnp.zeros((BINS, N_CELL * cell_count), jnp.float32)
    counts = jnp.zeros((N_CELL * cell_count,), jnp.float32)
    parent_evolved = None
    for group_index in range(N_GRID):
        first = group_index * group_rows
        spectra = fields[:, group_index]
        wet_cells = wet_mask[first:first + group_rows].astype(jnp.float32)
        weight_cells = wet_cells * fraction(frac_index[first:first + group_rows])
        depth_cells = depth_factor[first:first + group_rows]
        if group_index < N_GRID - 1:
            edge_map = boundary_map[first:first + group_rows]
            edge_values = parent_start[:, owners[:, None], edge_map]
            spectra = spectra.at[:, :, 0].set(edge_values[:, :, 0])
            spectra = spectra.at[:, :, NY - 1].set(edge_values[:, :, 1])
        for repeat in range(SUB):
            spectra = substep(pad_rows(spectra), pad_rows(depth_cells), pad_rows(weight_cells), pad_rows(wet_cells), along_x, along_y)
        evolved = interact(spectra.reshape(BINS, group_rows * NY), dia_plus, dia_minus, dia_coef)
        if group_index < N_GRID - 1:
            child_outputs.append(evolved.reshape(BINS, group_rows, NY).astype(jnp.bfloat16))
            segment = (owners[:, None] * cell_count + average_map[first:first + group_rows]).reshape(-1).astype(jnp.int32)
            child_sums = child_sums + jax.ops.segment_sum(evolved.T, segment, num_segments=N_CELL * cell_count).T
            counts = counts + jax.ops.segment_sum(jnp.ones(segment.shape, jnp.float32), segment, num_segments=N_CELL * cell_count)
        else:
            parent_evolved = evolved
    parent = (parent_evolved + child_sums) / (1.0 + counts)[None, :]
    child_outputs.append(parent.reshape(BINS, group_rows, NY).astype(jnp.bfloat16))
    return jnp.concatenate(child_outputs, axis=1)
```

```python
import math

import jax
import jax.numpy as jnp
from jax import lax
from jax.sharding import PartitionSpec as P

NF = 36
ND = 36
SUB = 2
SIDE = 4
BIN_GROUPS = 16

FRACTIONS = (0.25, 0.5, 0.75, 1.0)


def speeds():
    frequency = jnp.arange(NF, dtype=jnp.float32)
    group_speed = 0.45 * jnp.exp(-math.log(1.1) * frequency)
    angles = 2.0 * math.pi / ND * jnp.arange(ND, dtype=jnp.float32)
    along_x = (group_speed[:, None] * jnp.cos(angles)[None, :]).reshape(NF * ND)
    along_y = (group_speed[:, None] * jnp.sin(angles)[None, :]).reshape(NF * ND)
    return (along_x, along_y)


def fraction(frac_index):
    open_share = jnp.zeros(frac_index.shape, jnp.float32)
    for position, share in enumerate(FRACTIONS):
        open_share = open_share + jnp.where(frac_index == position, share, 0.0)
    return open_share


def substep(spectra, depth_cells, weight_cells, wet_cells, along_x, along_y):
    face_x = 0.5 * (depth_cells[:-1] + depth_cells[1:]) * weight_cells[:-1] * weight_cells[1:]
    speed_x = along_x[:, None, None] * face_x[None]
    flux_x = (
        jnp.maximum(speed_x, 0.0) * spectra[:, :-1] + jnp.minimum(speed_x, 0.0) * spectra[:, 1:]
    )
    interior = spectra[:, 1:-1]
    depth_inner = depth_cells[1:-1]
    weight_inner = weight_cells[1:-1]
    face_y = (
        0.5
        * (depth_inner[:, :-1] + depth_inner[:, 1:])
        * weight_inner[:, :-1]
        * weight_inner[:, 1:]
    )
    speed_y = along_y[:, None, None] * face_y[None]
    flux_y = (
        jnp.maximum(speed_y, 0.0) * interior[:, :, :-1]
        + jnp.minimum(speed_y, 0.0) * interior[:, :, 1:]
    )
    zero_flux = jnp.zeros(interior.shape[:2] + (1,), jnp.float32)
    flux_y = jnp.concatenate([zero_flux, flux_y, zero_flux], axis=2)
    change = flux_x[:, 1:] - flux_x[:, :-1] + flux_y[:, :, 1:] - flux_y[:, :, :-1]
    return (interior - change) * wet_cells[1:-1][None]


def interact(spectra, dia_plus, dia_minus, dia_coef):
    plus_bins = jnp.take(spectra, dia_plus, axis=0)
    minus_bins = jnp.take(spectra, dia_minus, axis=0)
    coefficient = jnp.repeat(dia_coef, ND)[:, None]
    source = coefficient * (
        spectra * spectra * (plus_bins + minus_bins) - 2.0 * spectra * plus_bins * minus_bins
    )
    return jnp.maximum(spectra + 0.2 * source, 0.0)


def place(z, y, x):
    return (z % SIDE * SIDE + y % SIDE) * SIDE + x % SIDE


def layout():
    last = SIDE - 1
    hubs = [
        place(last, last, last),
        place(last, last, last - 1),
        place(last, last - 1, last),
        place(last - 1, last, last),
    ]
    classes = [[] for _ in range(SIDE)]
    for z in range(SIDE):
        for y in range(SIDE):
            for x in range(SIDE):
                classes[(x + 2 * y + 3 * z) % SIDE].append(place(z, y, x))
    owned = [next(c for c in classes if hub in c) for hub in hubs]
    return (hubs, owned)


def cell_halo(x, width):
    rows = x.shape[1]
    first = lax.axis_index("cell") == 0
    mine = jnp.where(first, x[:, rows - width :], x[:, :width])
    other = lax.ppermute(mine, "cell", [(0, 1), (1, 0)])
    none = jnp.zeros_like(other)
    return jnp.concatenate(
        [jnp.where(first, none, other), x, jnp.where(first, other, none)], axis=1
    )


def on_device(
    spectrum,
    depth_factor,
    wet_mask,
    frac_index,
    boundary_map,
    average_map,
    dia_plus,
    dia_minus,
    dia_coef,
):
    bin_count, row_count, col_count = spectrum.shape
    cell_count = row_count * col_count
    along_x, along_y = speeds()
    groups = lax.axis_size("grid")
    parent = groups - 1
    is_parent = lax.axis_index("grid") == parent
    hubs, owned = layout()
    edges = 2 * row_count
    quarter = bin_count // len(hubs)
    group_bins = bin_count // BIN_GROUPS

    wet_cells = wet_mask.astype(jnp.float32)
    weight_cells = wet_cells * fraction(frac_index)
    statics = jnp.stack([depth_factor, weight_cells, wet_cells])
    static_ext = cell_halo(statics, SUB)

    flat = spectrum.reshape(bin_count, cell_count)
    held = jnp.where(is_parent, flat[:quarter], 0)
    for k in range(1, len(hubs)):
        part = flat[k * quarter : (k + 1) * quarter]
        held = held + lax.ppermute(part, "grid", [(parent, hubs[k])])
    maps = jnp.broadcast_to(boundary_map.reshape(1, edges), (groups, edges))
    maps = lax.all_to_all(maps, "grid", 0, 0)
    pick = (
        jnp.arange(cell_count, dtype=jnp.int32)[:, None] == maps.reshape(1, groups * edges)
    ).astype(jnp.bfloat16)
    picked = jnp.dot(held, pick, preferred_element_type=jnp.float32).astype(jnp.bfloat16)
    picked = picked.reshape(quarter, groups, edges).transpose(1, 2, 0)
    picked = lax.all_to_all(picked, "grid", 0, 0)
    picked = jnp.concatenate([picked[hub] for hub in hubs], axis=1)
    edge_values = picked.T.reshape(bin_count, row_count, 2)

    column = lax.broadcasted_iota(jnp.int32, (1, 1, col_count), 2)
    child_flag = jnp.logical_not(is_parent)
    start = jnp.where(child_flag & (column == 0), edge_values[:, :, 0:1], spectrum)
    start = jnp.where(child_flag & (column == col_count - 1), edge_values[:, :, 1:2], start)
    spectra = cell_halo(start, SUB).astype(jnp.float32)
    for repeat in range(SUB):
        rows = slice(repeat, 2 * SUB + row_count - repeat)
        spectra = substep(
            spectra, static_ext[0, rows], static_ext[1, rows], static_ext[2, rows], along_x, along_y
        )
    evolved = interact(spectra.reshape(bin_count, cell_count), dia_plus, dia_minus, dia_coef)

    cells = jnp.arange(cell_count, dtype=jnp.int32)
    target = jnp.where(is_parent, cells, average_map.reshape(-1))
    onehot = (target[:, None] == cells[None, :]).astype(jnp.float32)
    term = jnp.dot(
        evolved, onehot, precision=lax.Precision.HIGHEST, preferred_element_type=jnp.float32
    )
    count = jnp.sum(onehot, axis=0)
    term = term.reshape(BIN_GROUPS, group_bins, row_count, col_count).transpose(0, 2, 1, 3)
    count = jnp.broadcast_to(
        count.reshape(1, row_count, 1, col_count), (BIN_GROUPS, row_count, 1, col_count)
    )
    pieces = jnp.concatenate([term, count], axis=2)
    pieces = pieces.reshape(groups, group_bins + 1, col_count)
    total = jnp.sum(lax.all_to_all(pieces, "grid", 0, 0), axis=0)
    average = (total[:group_bins] / total[group_bins:]).astype(jnp.bfloat16)

    members = len(owned[0])
    copies = jnp.broadcast_to(average[None], (members,) + average.shape)
    gathered = lax.all_to_all(copies, "grid", 0, 0, axis_index_groups=owned)
    parts = [gathered]
    for k in range(1, len(hubs)):
        parts.append(lax.ppermute(gathered, "grid", [(hubs[k], parent)]))
    where_is = {}
    for k, devices in enumerate(owned):
        for position, device in enumerate(devices):
            where_is[device] = k * members + position
    blended = jnp.concatenate(parts, axis=0)
    blended = jnp.stack([blended[where_is[d]] for d in range(groups)])
    blended = blended.reshape(BIN_GROUPS, row_count, group_bins, col_count).transpose(0, 2, 1, 3)
    blended = blended.reshape(bin_count, row_count, col_count)
    evolved = evolved.reshape(bin_count, row_count, col_count).astype(jnp.bfloat16)
    return jnp.where(is_parent, blended, evolved)


def solution(mesh):
    placed = (
        P(None, ("grid", "cell"), None),
        P(("grid", "cell"), None),
        P(("grid", "cell"), None),
        P(("grid", "cell"), None),
        P(("grid", "cell"), None),
        P(("grid", "cell"), None),
        P(),
        P(),
        P(),
    )
    return jax.shard_map(
        on_device,
        mesh=mesh,
        in_specs=placed,
        out_specs=P(None, ("grid", "cell"), None),
        check_vma=False,
    )
```

```python
import functools
import math

import jax
import jax.numpy as jnp
from jax import lax
from jax.experimental import pallas as pl
from jax.experimental.pallas import tpu as pltpu
from jax.sharding import PartitionSpec as P

NF = 36
ND = 36
SIDE = 4
ROWS = 4
COLS = 128
CELLS = ROWS * COLS
BINS = NF * ND
FLAT = BINS * ROWS
PAD = 8
PIECES = SIDE**3
PIECE = FLAT // PIECES
TALL = 88
COPY = 96
BLOCK = 72
CHUNK = 432
VMEM_BYTES = 56 * 1024 * 1024

FRACTIONS = (0.25, 0.5, 0.75, 1.0)


def fraction(frac_index):
    open_share = jnp.zeros(frac_index.shape, jnp.float32)
    for position, share in enumerate(FRACTIONS):
        open_share = open_share + jnp.where(frac_index == position, share, 0.0)
    return open_share


def place(z, y, x):
    return (z % SIDE * SIDE + y % SIDE) * SIDE + x % SIDE


def layout():
    last = SIDE - 1
    hubs = [
        place(last, last, last),
        place(last, last, last - 1),
        place(last, last - 1, last),
        place(last - 1, last, last),
    ]
    classes = [[] for _ in range(SIDE)]
    for z in range(SIDE):
        for y in range(SIDE):
            for x in range(SIDE):
                classes[(x + 2 * y + 3 * z) % SIDE].append(place(z, y, x))
    owned = [next(c for c in classes if hub in c) for hub in hubs]
    return (hubs, owned)


def bin_block(ref, index):
    return ref[8 * index : 8 * index + 8, :]


def step_kernel(
    plus_ref,
    minus_ref,
    speed_ref,
    coef_ref,
    flag_ref,
    spec_ref,
    near_ref,
    edge_ref,
    spot_ref,
    stat_ref,
    cos_ref,
    sin_ref,
    cosb_ref,
    sinb_ref,
    target_ref,
    out_ref,
    pieces_ref,
    dens,
    flat,
    halo,
    evol,
    near,
    hot,
    count,
):
    first = flag_ref[0] == 1
    child = flag_ref[1]
    adjacent = 3 * flag_ref[0]
    sign = jnp.where(first, 1.0, -1.0)
    lane = lax.broadcasted_iota(jnp.int32, (16, COLS), 1)
    ends = jnp.where((lane == 0) | (lane == COLS - 1), child, 0) > 0

    many = CHUNK
    lane_many = lax.broadcasted_iota(jnp.int32, (many, COLS), 1)
    ends_many = jnp.where((lane_many == 0) | (lane_many == COLS - 1), child, 0) > 0

    def lay_edges(c, carry):
        base = pl.multiple_of(c * many, 16)
        laid = jnp.dot(
            edge_ref[pl.ds(base, many), :], spot_ref[...], preferred_element_type=jnp.float32
        )
        for r in range(ROWS):
            flat[pl.ds(base * ROWS + r, many, stride=ROWS), :] = laid[:, r * COLS : (r + 1) * COLS]
        for n in range(2):
            raw = near_ref[n, pl.ds(base, many), :].astype(jnp.float32)
            at = (ROWS + n) * COLS
            near[n, pl.ds(base, many), :] = jnp.where(ends_many, laid[:, at : at + COLS], raw)
        return carry

    lax.fori_loop(0, BINS // many, lay_edges, 0)

    def begin(i, carry):
        for u in range(4):
            at = pl.multiple_of(i * 64 + u * 16, 16)
            raw = spec_ref[pl.ds(at, 16), :].astype(jnp.float32)
            dens[pl.ds(PAD + at, 16), :] = jnp.where(ends, flat[pl.ds(at, 16), :], raw)
            halo[pl.ds(at, 16), :] = jnp.zeros((16, COLS), jnp.float32)
        return carry

    lax.fori_loop(0, FLAT // 64, begin, 0)

    face_x, face_y, wet, face_an, face_nb, face_n, wet_n = (bin_block(stat_ref, i) for i in range(7))
    low = lax.broadcasted_iota(jnp.int32, (8, COLS), 0) < ROWS

    def block(k, carry):
        bins = pl.multiple_of(k * BLOCK, 8)
        rows = pl.multiple_of(k * (BLOCK * ROWS), 16)
        g0, g1 = speed_ref[2 * k], speed_ref[2 * k + 1]

        def halo_flux(j):
            n1 = near[0, pl.ds(bins + 8 * j, 8), :]
            own = dens[pl.ds(PAD + rows + 32 * j + adjacent, 8, stride=ROWS), :]
            cosv = bin_block(cosb_ref, j)
            cp, cm = jnp.maximum(cosv, 0.0), jnp.minimum(cosv, 0.0)
            top, bottom = jnp.where(first, own, n1), jnp.where(first, n1, own)
            flux = face_an * (cp * top + cm * bottom)
            halo[pl.ds(rows + 32 * j + adjacent, 8, stride=ROWS), :] = sign * flux
            return n1, cp, cm, flux

        def advance(p):
            at = rows + 8 * p
            rho = dens[pl.ds(PAD + at, 8), :]
            cosv, sinv = bin_block(cos_ref, p % 18), bin_block(sin_ref, p % 18)
            after = pltpu.roll(rho, 7, 0)
            right = pltpu.roll(rho, COLS - 1, 1)
            fx = face_x * (jnp.maximum(cosv, 0.0) * rho + jnp.minimum(cosv, 0.0) * after)
            fy = face_y * (jnp.maximum(sinv, 0.0) * rho + jnp.minimum(sinv, 0.0) * right)
            change = (fx - pltpu.roll(fx, 1, 0)) + (fy - pltpu.roll(fy, 1, 1))
            change = change + halo[pl.ds(at, 8), :]
            dens[pl.ds(PAD + at, 8), :] = (rho - (g0 if p < 18 else g1) * change) * wet

        for j in range(BLOCK // 8):
            n1, cp, cm, flux = halo_flux(j)
            n2 = near[1, pl.ds(bins + 8 * j, 8), :]
            sinv = bin_block(sinb_ref, j)
            top, bottom = jnp.where(first, n1, n2), jnp.where(first, n2, n1)
            beyond = face_nb * (cp * top + cm * bottom)
            fy = face_n * (
                jnp.maximum(sinv, 0.0) * n1
                + jnp.minimum(sinv, 0.0) * pltpu.roll(n1, COLS - 1, 1)
            )
            change = sign * (beyond - flux) + (fy - pltpu.roll(fy, 1, 1))
            speed = g0 if j < 4 else (jnp.where(low, g0, g1) if j == 4 else g1)
            near[0, pl.ds(bins + 8 * j, 8), :] = (n1 - speed * change) * wet_n
        for p in range(BLOCK // 2):
            advance(p)
        for j in range(BLOCK // 8):
            halo_flux(j)
        for p in range(BLOCK // 2):
            advance(p)
        return carry

    lax.fori_loop(0, BINS // BLOCK, block, 0)

    def interact(f, carry):
        rows = pl.multiple_of(f * (ND * ROWS), 16)
        scale = 0.2 * coef_ref[f]

        def partner(ref, b):
            lower = dens[pl.ds(ref[f * ND + b], 8), :]
            upper = dens[pl.ds(ref[f * ND + b + 1] - ROWS, 8), :]
            return jnp.where(low, lower, upper)

        for g in range(ND // 4):
            done = []
            for h in range(2):
                b = 4 * g + 2 * h
                mine = dens[pl.ds(PAD + rows + 4 * b, 8), :]
                plus, minus = partner(plus_ref, b), partner(minus_ref, b)
                source = mine * (mine * (plus + minus) - 2.0 * (plus * minus))
                value = jnp.maximum(mine + scale * source, 0.0)
                evol[pl.ds(rows + 4 * b, 8), :] = value
                done.append(value)
            out_ref[pl.ds(rows + 16 * g, 16), :] = jnp.concatenate(done, axis=0).astype(jnp.bfloat16)
        return carry

    lax.fori_loop(0, NF, interact, 0)

    row = lax.broadcasted_iota(jnp.int32, (CELLS, COLS), 0)
    for r in range(ROWS):
        same = row == target_ref[r : r + 1, :]
        hot[:, r * COLS : (r + 1) * COLS] = jnp.where(same, 1.0, 0.0).astype(jnp.bfloat16)
    inner = (((1,), (1,)), ((), ()))
    number = lax.dot_general(
        jnp.ones((16, CELLS), jnp.bfloat16), hot[...], inner, preferred_element_type=jnp.float32
    )
    count[...] = jnp.zeros_like(count)
    for r in range(ROWS):
        count[PIECE + r : PIECE + r + 1, :] = number[0:1, r * COLS : (r + 1) * COLS]

    def sums(c, carry):
        base = c * (many * ROWS)
        parts = [evol[pl.ds(base + r, many, stride=ROWS), :] for r in range(ROWS)]
        value = jnp.concatenate(parts, axis=1)
        head = value.astype(jnp.bfloat16)
        tail = (value - head.astype(jnp.float32)).astype(jnp.bfloat16)
        total = lax.dot_general(head, hot[...], inner, preferred_element_type=jnp.float32)
        total += lax.dot_general(tail, hot[...], inner, preferred_element_type=jnp.float32)
        for r in range(ROWS):
            flat[pl.ds(base + r, many, stride=ROWS), :] = total[:, r * COLS : (r + 1) * COLS]
        return carry

    lax.fori_loop(0, BINS // many, sums, 0)
    inside = lax.broadcasted_iota(jnp.int32, (TALL, COLS), 0) < PIECE

    def cut(j, carry):
        pieces_ref[j] = jnp.where(inside, flat[pl.ds(j * PIECE, TALL), :], count[...])
        return carry

    lax.fori_loop(0, PIECES, cut, 0)


def evolve(*operands, interpret=False):
    smem = pl.BlockSpec(memory_space=pltpu.SMEM)
    vmem = pl.BlockSpec(memory_space=pltpu.VMEM)
    return pl.pallas_call(
        step_kernel,
        out_shape=(
            jax.ShapeDtypeStruct((FLAT, COLS), jnp.bfloat16),
            jax.ShapeDtypeStruct((PIECES, TALL, COLS), jnp.float32),
        ),
        in_specs=[smem] * 5 + [vmem] * 10,
        out_specs=(vmem, vmem),
        scratch_shapes=[
            pltpu.VMEM((FLAT + 2 * PAD, COLS), jnp.float32),
            pltpu.VMEM((FLAT + 2 * PAD, COLS), jnp.float32),
            pltpu.VMEM((FLAT, COLS), jnp.float32),
            pltpu.VMEM((FLAT, COLS), jnp.float32),
            pltpu.VMEM((2, BINS, COLS), jnp.float32),
            pltpu.VMEM((CELLS, CELLS), jnp.bfloat16),
            pltpu.VMEM((TALL, COLS), jnp.float32),
        ],
        compiler_params=pltpu.CompilerParams(vmem_limit_bytes=VMEM_BYTES),
        cost_estimate=pl.CostEstimate(
            flops=1_400_000_000, bytes_accessed=10_000_000, transcendentals=0
        ),
        interpret=interpret,
    )(*operands)


def lay_kernel(where_is, flag_ref, a_ref, b_ref, c_ref, d_ref, _, out_ref, wide, narrow, sem):
    parts = (a_ref, b_ref, c_ref, d_ref)

    @pl.when(flag_ref[1] == 0)
    def _():
        for j, (k, position) in enumerate(where_is):
            piece = parts[k][position].astype(jnp.float32)
            wide[j * PIECE : j * PIECE + COPY, :] = piece

        def narrower(i, carry):
            for u in range(4):
                at = pl.multiple_of(i * 64 + u * 16, 16)
                narrow[pl.ds(at, 16), :] = wide[pl.ds(at, 16), :].astype(jnp.bfloat16)
            return carry

        lax.fori_loop(0, FLAT // 64, narrower, 0)
        copy = pltpu.make_async_copy(narrow, out_ref, sem)
        copy.start()
        copy.wait()


def lay(where_is, flags, parts, evolved):
    vmem = pl.BlockSpec(memory_space=pltpu.VMEM)
    anywhere = pl.BlockSpec(memory_space=pl.ANY)
    return pl.pallas_call(
        functools.partial(lay_kernel, where_is),
        out_shape=jax.ShapeDtypeStruct((FLAT, COLS), jnp.bfloat16),
        in_specs=[pl.BlockSpec(memory_space=pltpu.SMEM)] + [vmem] * 4 + [anywhere],
        out_specs=anywhere,
        scratch_shapes=[
            pltpu.VMEM((FLAT + 2 * PAD, COLS), jnp.float32),
            pltpu.VMEM((FLAT, COLS), jnp.bfloat16),
            pltpu.SemaphoreType.DMA,
        ],
        input_output_aliases={5: 0},
        compiler_params=pltpu.CompilerParams(vmem_limit_bytes=VMEM_BYTES),
    )(flags, *parts, evolved)


def tables():
    frequency = jnp.arange(NF, dtype=jnp.float32)
    group_speed = 0.45 * jnp.exp(-math.log(1.1) * frequency)
    angles = 2.0 * math.pi / ND * jnp.arange(ND, dtype=jnp.float32)

    def wide(values, times):
        return jnp.broadcast_to(jnp.repeat(values, times)[:, None], (ND * times, COLS))

    cosine, sine = jnp.cos(angles), jnp.sin(angles)
    per_row = (wide(cosine, ROWS), wide(sine, ROWS))
    twice = BLOCK // ND
    per_bin = (jnp.tile(wide(cosine, 1), (twice, 1)), jnp.tile(wide(sine, 1), (twice, 1)))
    return (group_speed,) + per_row + per_bin


def spots():
    source = jnp.arange(COLS)[:, None]
    lane = jnp.arange((ROWS + 2) * COLS)[None, :]
    block, column = lane // COLS, lane % COLS
    chosen = ((column == 0) & (source == 2 * block)) | (
        (column == COLS - 1) & (source == 2 * block + 1)
    )
    return chosen.astype(jnp.bfloat16)


def faces(depth, weight, wet, near_statics):
    def between(d0, d1, w0, w1):
        return 0.5 * (d0 + d1) * w0 * w1

    def along(d, w):
        return jnp.pad(between(d[:, :-1], d[:, 1:], w[:, :-1], w[:, 1:]), ((0, 0), (0, 1)))

    first = lax.axis_index("cell") == 0
    face_x = jnp.pad(between(depth[:-1], depth[1:], weight[:-1], weight[1:]), ((0, 1), (0, 0)))
    face_y = along(depth, weight)
    d_own = jnp.where(first, depth[-1:], depth[:1])
    w_own = jnp.where(first, weight[-1:], weight[:1])
    d_near, w_near, wet_near = near_statics
    face_an = between(d_own, d_near[:1], w_own, w_near[:1])
    face_nb = between(d_near[:1], d_near[1:], w_near[:1], w_near[1:])
    face_n = along(d_near[:1], w_near[:1])
    blocks = [jnp.tile(v, (2, 1)) for v in (face_x, face_y, wet)]
    blocks += [jnp.tile(v, (8, 1)) for v in (face_an, face_nb, face_n, wet_near[:1])]
    return jnp.concatenate(blocks, axis=0)


def facing(x, axis):
    first = lax.axis_index("cell") == 0
    near = [lax.index_in_dim(x, i, axis, keepdims=False) for i in range(ROWS)]
    return jnp.stack(
        [jnp.where(first, near[3], near[0]), jnp.where(first, near[2], near[1])], axis=0
    )


def swap(x):
    return lax.ppermute(x, "cell", [(0, 1), (1, 0)])


def on_device(
    spectrum,
    depth_factor,
    wet_mask,
    frac_index,
    boundary_map,
    average_map,
    dia_plus,
    dia_minus,
    dia_coef,
):
    groups = lax.axis_size("grid")
    parent = groups - 1
    mine = lax.axis_index("grid")
    is_parent = mine == parent
    hubs, owned = layout()
    edges = 2 * ROWS
    quarter = BINS // len(hubs)
    spec = spectrum.reshape(FLAT, COLS)

    held = jnp.where(is_parent, spec[: quarter * ROWS], 0)
    for k in range(1, len(hubs)):
        part = spec[k * quarter * ROWS : (k + 1) * quarter * ROWS]
        held = held + lax.ppermute(part, "grid", [(parent, hubs[k])])
    maps = jnp.broadcast_to(boundary_map.reshape(1, edges), (groups, edges))
    maps = lax.all_to_all(maps, "grid", 0, 0)

    near = swap(facing(spectrum, 1))
    wet = wet_mask.astype(jnp.float32)
    weight = wet * fraction(frac_index)
    near_statics = swap(facing(jnp.stack([depth_factor, weight, wet], axis=1), 0))
    stat = faces(depth_factor, weight, wet, near_statics.transpose(1, 0, 2))

    pick = (
        jnp.arange(CELLS, dtype=jnp.int32)[:, None] == maps.reshape(1, groups * edges)
    ).astype(jnp.bfloat16)
    picked = jnp.dot(held.reshape(quarter, CELLS), pick, preferred_element_type=jnp.float32)
    picked = picked.astype(jnp.bfloat16).reshape(quarter, groups, edges).transpose(1, 2, 0)
    picked = lax.all_to_all(picked, "grid", 0, 0)
    picked = jnp.concatenate([picked[hub] for hub in hubs], axis=1)
    far = swap(facing(picked.reshape(ROWS, 2, BINS), 0)).reshape(4, BINS)
    edge = jnp.concatenate(
        [picked, far, jnp.zeros((COLS - edges - 4, BINS), jnp.bfloat16)], axis=0
    ).T

    first = (lax.axis_index("cell") == 0).astype(jnp.int32)
    flags = jnp.stack([first, jnp.where(is_parent, 0, 1)]).astype(jnp.int32)
    cells = jnp.arange(CELLS, dtype=jnp.int32).reshape(ROWS, COLS)
    target = jnp.where(is_parent, cells, average_map)
    group_speed, cosine, sine, cosine_bin, sine_bin = tables()
    evolved, pieces = evolve(
        dia_plus * ROWS + PAD,
        dia_minus * ROWS + PAD,
        group_speed,
        dia_coef,
        flags,
        spec,
        near,
        edge,
        spots(),
        stat,
        cosine,
        sine,
        cosine_bin,
        sine_bin,
        target,
    )

    total = jnp.sum(lax.all_to_all(pieces, "grid", 0, 0), axis=0)
    number = total[PIECE : PIECE + ROWS]
    number = lax.dynamic_slice_in_dim(
        jnp.concatenate([number, number], axis=0), mine % ROWS, ROWS, axis=0
    )
    number = jnp.tile(number, (TALL // ROWS, 1))
    average = (total / jnp.maximum(number, 1.0)).astype(jnp.bfloat16)
    average = jnp.pad(average, ((0, COPY - TALL), (0, 0)))

    members = len(owned[0])
    copies = jnp.broadcast_to(average[None], (members,) + average.shape)
    gathered = lax.all_to_all(copies, "grid", 0, 0, axis_index_groups=owned)
    parts = [gathered]
    for k in range(1, len(hubs)):
        parts.append(lax.ppermute(gathered, "grid", [(hubs[k], parent)]))
    where_is = [None] * groups
    for k, devices in enumerate(owned):
        for position, device in enumerate(devices):
            where_is[device] = (k, position)
    return lay(tuple(where_is), flags, parts, evolved).reshape(BINS, ROWS, COLS)


def solution(mesh):
    placed = (
        P(None, ("grid", "cell"), None),
        P(("grid", "cell"), None),
        P(("grid", "cell"), None),
        P(("grid", "cell"), None),
        P(("grid", "cell"), None),
        P(("grid", "cell"), None),
        P(),
        P(),
        P(),
    )
    return jax.shard_map(
        on_device,
        mesh=mesh,
        in_specs=placed,
        out_specs=P(None, ("grid", "cell"), None),
        check_vma=False,
    )
```

```python
import functools
import math

import jax
import jax.numpy as jnp
import numpy as np
from jax import lax
from jax.experimental import pallas as pl
from jax.experimental.pallas import tpu as pltpu
from jax.sharding import PartitionSpec as P

NF = 36
ND = 36
SIDE = 4
ROWS = 4
COLS = 128
CELLS = ROWS * COLS
BINS = NF * ND
FLAT = BINS * ROWS
PAD = 8
PIECES = SIDE**3
PIECE = FLAT // PIECES
TALL = 88
BLOCK = 72
CHUNK = 432
UNIT = 512.0
STEPS = 65534.0
OFFSET = 32767
VMEM_BYTES = 56 * 1024 * 1024

FRACTIONS = (0.25, 0.5, 0.75, 1.0)


def fraction(frac_index):
    open_share = jnp.zeros(frac_index.shape, jnp.float32)
    for position, share in enumerate(FRACTIONS):
        open_share = open_share + jnp.where(frac_index == position, share, 0.0)
    return open_share


def place(z, y, x):
    return (z % SIDE * SIDE + y % SIDE) * SIDE + x % SIDE


def hub_places():
    last = SIDE - 1
    return [
        place(last, last, last),
        place(last, last, last - 1),
        place(last, last - 1, last),
        place(last - 1, last, last),
    ]


def bin_block(ref, index):
    return ref[8 * index : 8 * index + 8, :]


def prepare_kernel(
    flag_ref,
    map_ref,
    spec_ref,
    depth_ref,
    wet_ref,
    frac_ref,
    near_ref,
    stat_ref,
    maps_ref,
    part1_ref,
    part2_ref,
    part3_ref,
    dens,
):
    first = flag_ref[0] == 1
    lane = lax.broadcasted_iota(jnp.int32, (PIECES, COLS), 1)
    maps = jnp.zeros((PIECES, COLS), jnp.int32)
    for r in range(ROWS):
        for side in range(2):
            maps = jnp.where(lane == 2 * r + side, map_ref[side, r], maps)
    maps_ref[...] = maps

    wet = wet_ref[...].astype(jnp.float32)
    values = (depth_ref[...], wet * fraction(frac_ref[...]), wet)
    for i, value in enumerate(values):
        stat_ref[2 * i : 2 * i + 1, :] = jnp.where(first, value[3:4], value[0:1])
        stat_ref[2 * i + 1 : 2 * i + 2, :] = jnp.where(first, value[2:3], value[1:2])
    stat_ref[6:8, :] = jnp.zeros((2, COLS), jnp.float32)

    part = FLAT // SIDE
    for k, ref in enumerate((part1_ref, part2_ref, part3_ref)):
        ref[...] = spec_ref[(k + 1) * part : (k + 2) * part, :]

    def widen(i, carry):
        for u in range(4):
            at = pl.multiple_of(i * 64 + u * 16, 16)
            dens[pl.ds(at, 16), :] = spec_ref[pl.ds(at, 16), :].astype(jnp.float32)
        return carry

    lax.fori_loop(0, FLAT // 64, widen, 0)
    nearer = 3 * flag_ref[0]
    farther = 1 + flag_ref[0]

    def pull(i, carry):
        for u in range(3):
            at = pl.multiple_of(i * 48 + u * 16, 16)
            for n, row in enumerate((nearer, farther)):
                rows = dens[pl.ds(at * ROWS + row, 16, stride=ROWS), :]
                near_ref[n, pl.ds(at, 16), :] = rows.astype(jnp.bfloat16)
        return carry

    lax.fori_loop(0, BINS // 48, pull, 0)


def prepare(*operands, interpret=False):
    smem = pl.BlockSpec(memory_space=pltpu.SMEM)
    vmem = pl.BlockSpec(memory_space=pltpu.VMEM)
    part = jax.ShapeDtypeStruct((FLAT // SIDE, COLS), jnp.bfloat16)
    return pl.pallas_call(
        prepare_kernel,
        out_shape=(
            jax.ShapeDtypeStruct((2, BINS, COLS), jnp.bfloat16),
            jax.ShapeDtypeStruct((8, COLS), jnp.float32),
            jax.ShapeDtypeStruct((PIECES, COLS), jnp.int32),
            part,
            part,
            part,
        ),
        in_specs=[smem] * 2 + [vmem] * 4,
        out_specs=(vmem,) * 6,
        scratch_shapes=[pltpu.VMEM((FLAT, COLS), jnp.float32)],
        compiler_params=pltpu.CompilerParams(vmem_limit_bytes=VMEM_BYTES),
        interpret=interpret,
    )(*operands)


def step_kernel(
    plus_ref,
    minus_ref,
    speed_ref,
    coef_ref,
    flag_ref,
    spec_ref,
    near_ref,
    edge_ref,
    spot_ref,
    depth_ref,
    wet_ref,
    frac_ref,
    stat_ref,
    cos_ref,
    sin_ref,
    cosb_ref,
    sinb_ref,
    target_ref,
    out_ref,
    pieces_ref,
    dens,
    flat,
    halo,
    evol,
    near,
    hot,
    count,
):
    first = flag_ref[0] == 1
    child = flag_ref[1]
    adjacent = 3 * flag_ref[0]
    sign = jnp.where(first, 1.0, -1.0)
    lane = lax.broadcasted_iota(jnp.int32, (16, COLS), 1)
    ends = jnp.where((lane == 0) | (lane == COLS - 1), child, 0) > 0

    many = CHUNK
    lane_many = lax.broadcasted_iota(jnp.int32, (many, COLS), 1)
    ends_many = jnp.where((lane_many == 0) | (lane_many == COLS - 1), child, 0) > 0

    def lay_edges(c, carry):
        base = pl.multiple_of(c * many, 16)
        laid = jnp.dot(
            edge_ref[pl.ds(base, many), :], spot_ref[...], preferred_element_type=jnp.float32
        )
        for r in range(ROWS):
            flat[pl.ds(base * ROWS + r, many, stride=ROWS), :] = laid[:, r * COLS : (r + 1) * COLS]
        for n in range(2):
            raw = near_ref[n, pl.ds(base, many), :].astype(jnp.float32)
            at = (ROWS + n) * COLS
            near[n, pl.ds(base, many), :] = jnp.where(ends_many, laid[:, at : at + COLS], raw)
        return carry

    lax.fori_loop(0, BINS // many, lay_edges, 0)

    def begin(i, carry):
        for u in range(4):
            at = pl.multiple_of(i * 64 + u * 16, 16)
            raw = spec_ref[pl.ds(at, 16), :].astype(jnp.float32)
            dens[pl.ds(PAD + at, 16), :] = jnp.where(ends, flat[pl.ds(at, 16), :], raw)
            halo[pl.ds(at, 16), :] = jnp.zeros((16, COLS), jnp.float32)
        return carry

    lax.fori_loop(0, FLAT // 64, begin, 0)

    sub = lax.broadcasted_iota(jnp.int32, (8, COLS), 0)
    low = sub < ROWS
    depth = jnp.concatenate([depth_ref[...]] * 2, axis=0)
    wet = jnp.concatenate([wet_ref[...]] * 2, axis=0).astype(jnp.float32)
    weight = wet * fraction(jnp.concatenate([frac_ref[...]] * 2, axis=0))

    def between(d0, d1, w0, w1):
        return 0.5 * (d0 + d1) * w0 * w1

    def along(d, w):
        face = between(d, pltpu.roll(d, COLS - 1, 1), w, pltpu.roll(w, COLS - 1, 1))
        return jnp.where(lane[:8] == COLS - 1, 0.0, face)

    def wide(row):
        return jnp.broadcast_to(row, (8, COLS))

    face_x = between(depth, pltpu.roll(depth, 7, 0), weight, pltpu.roll(weight, 7, 0))
    face_x = jnp.where(sub % ROWS == ROWS - 1, 0.0, face_x)
    face_y = along(depth, weight)
    d_own = wide(jnp.where(first, depth[3:4], depth[0:1]))
    w_own = wide(jnp.where(first, weight[3:4], weight[0:1]))
    d_n1, d_n2, w_n1, w_n2, wet_n = (wide(stat_ref[i : i + 1, :]) for i in range(5))
    face_an = between(d_own, d_n1, w_own, w_n1)
    face_nb = between(d_n1, d_n2, w_n1, w_n2)
    face_n = along(d_n1, w_n1)

    def block(k, carry):
        bins = pl.multiple_of(k * BLOCK, 8)
        rows = pl.multiple_of(k * (BLOCK * ROWS), 16)
        g0, g1 = speed_ref[2 * k], speed_ref[2 * k + 1]

        def halo_flux(j):
            n1 = near[0, pl.ds(bins + 8 * j, 8), :]
            own = dens[pl.ds(PAD + rows + 32 * j + adjacent, 8, stride=ROWS), :]
            cosv = bin_block(cosb_ref, j)
            cp, cm = jnp.maximum(cosv, 0.0), jnp.minimum(cosv, 0.0)
            top, bottom = jnp.where(first, own, n1), jnp.where(first, n1, own)
            flux = face_an * (cp * top + cm * bottom)
            halo[pl.ds(rows + 32 * j + adjacent, 8, stride=ROWS), :] = sign * flux
            return n1, cp, cm, flux

        def advance(p):
            at = rows + 8 * p
            rho = dens[pl.ds(PAD + at, 8), :]
            cosv, sinv = bin_block(cos_ref, p % 18), bin_block(sin_ref, p % 18)
            after = pltpu.roll(rho, 7, 0)
            right = pltpu.roll(rho, COLS - 1, 1)
            fx = face_x * (jnp.maximum(cosv, 0.0) * rho + jnp.minimum(cosv, 0.0) * after)
            fy = face_y * (jnp.maximum(sinv, 0.0) * rho + jnp.minimum(sinv, 0.0) * right)
            change = (fx - pltpu.roll(fx, 1, 0)) + (fy - pltpu.roll(fy, 1, 1))
            change = change + halo[pl.ds(at, 8), :]
            dens[pl.ds(PAD + at, 8), :] = (rho - (g0 if p < 18 else g1) * change) * wet

        for j in range(BLOCK // 8):
            n1, cp, cm, flux = halo_flux(j)
            n2 = near[1, pl.ds(bins + 8 * j, 8), :]
            sinv = bin_block(sinb_ref, j)
            top, bottom = jnp.where(first, n1, n2), jnp.where(first, n2, n1)
            beyond = face_nb * (cp * top + cm * bottom)
            fy = face_n * (
                jnp.maximum(sinv, 0.0) * n1
                + jnp.minimum(sinv, 0.0) * pltpu.roll(n1, COLS - 1, 1)
            )
            change = sign * (beyond - flux) + (fy - pltpu.roll(fy, 1, 1))
            speed = g0 if j < 4 else (jnp.where(low, g0, g1) if j == 4 else g1)
            near[0, pl.ds(bins + 8 * j, 8), :] = (n1 - speed * change) * wet_n
        for p in range(BLOCK // 2):
            advance(p)
        for j in range(BLOCK // 8):
            halo_flux(j)
        for p in range(BLOCK // 2):
            advance(p)
        return carry

    lax.fori_loop(0, BINS // BLOCK, block, 0)

    def interact(f, carry):
        rows = pl.multiple_of(f * (ND * ROWS), 16)
        scale = 0.2 * coef_ref[f]

        def partner(ref, b):
            lower = dens[pl.ds(ref[f * ND + b], 8), :]
            upper = dens[pl.ds(ref[f * ND + b + 1] - ROWS, 8), :]
            return jnp.where(low, lower, upper)

        for g in range(ND // 4):
            done = []
            for h in range(2):
                b = 4 * g + 2 * h
                mine = dens[pl.ds(PAD + rows + 4 * b, 8), :]
                plus, minus = partner(plus_ref, b), partner(minus_ref, b)
                source = mine * (mine * (plus + minus) - 2.0 * (plus * minus))
                value = jnp.maximum(mine + scale * source, 0.0)
                evol[pl.ds(rows + 4 * b, 8), :] = value
                done.append(value)
            out_ref[pl.ds(rows + 16 * g, 16), :] = jnp.concatenate(done, axis=0).astype(jnp.bfloat16)
        return carry

    lax.fori_loop(0, NF, interact, 0)

    row = lax.broadcasted_iota(jnp.int32, (CELLS, COLS), 0)
    for r in range(ROWS):
        own = lane[:1] + r * COLS
        same = row == jnp.where(child == 1, target_ref[r : r + 1, :], own)
        hot[:, r * COLS : (r + 1) * COLS] = jnp.where(same, 1.0, 0.0).astype(jnp.bfloat16)
    inner = (((1,), (1,)), ((), ()))
    number = lax.dot_general(
        jnp.ones((16, CELLS), jnp.bfloat16), hot[...], inner, preferred_element_type=jnp.float32
    )
    share = 1.0 / jnp.maximum(number[0:1], 1.0)
    count[...] = jnp.zeros_like(count)
    for turn in range(ROWS):
        for r in range(ROWS):
            of = (turn + r) % ROWS
            here = number[0:1, of * COLS : (of + 1) * COLS].astype(jnp.int32)
            count[turn, PIECE + r : PIECE + r + 1, :] = here

    def sums(c, carry):
        base = c * (many * ROWS)
        parts = [evol[pl.ds(base + r, many, stride=ROWS), :] for r in range(ROWS)]
        value = jnp.concatenate(parts, axis=1)
        head = value.astype(jnp.bfloat16)
        tail = (value - head.astype(jnp.float32)).astype(jnp.bfloat16)
        total = lax.dot_general(head, hot[...], inner, preferred_element_type=jnp.float32)
        total += lax.dot_general(tail, hot[...], inner, preferred_element_type=jnp.float32)
        for r in range(ROWS):
            part = slice(r * COLS, (r + 1) * COLS)
            flat[pl.ds(base + r, many, stride=ROWS), :] = total[:, part] * share[:, part]
        return carry

    lax.fori_loop(0, BINS // many, sums, 0)
    row = lax.broadcasted_iota(jnp.int32, (TALL, COLS), 0)

    def cut(i, carry):
        for turn in range(ROWS):
            j = i * ROWS + turn
            mean = jnp.where(row < PIECE, flat[pl.ds(j * PIECE, TALL), :], 0.0)
            size = (jnp.max(mean, axis=0, keepdims=True) * UNIT).astype(jnp.int32) + 1
            size = jnp.minimum(size, OFFSET)
            steps = (UNIT * STEPS) / size.astype(jnp.float32)
            code = jnp.minimum((mean * steps + 0.5).astype(jnp.int32), 2 * OFFSET) - OFFSET
            rest = jnp.where(row == PIECE + ROWS, size, count[turn])
            pieces_ref[j] = jnp.where(row < PIECE, code, rest).astype(jnp.int16)
        return carry

    lax.fori_loop(0, PIECES // ROWS, cut, 0)


def evolve(*operands, interpret=False):
    smem = pl.BlockSpec(memory_space=pltpu.SMEM)
    vmem = pl.BlockSpec(memory_space=pltpu.VMEM)
    return pl.pallas_call(
        step_kernel,
        out_shape=(
            jax.ShapeDtypeStruct((FLAT, COLS), jnp.bfloat16),
            jax.ShapeDtypeStruct((PIECES, TALL, COLS), jnp.int16),
        ),
        in_specs=[smem] * 5 + [vmem] * 13,
        out_specs=(vmem, vmem),
        scratch_shapes=[
            pltpu.VMEM((FLAT + 2 * PAD, COLS), jnp.float32),
            pltpu.VMEM((FLAT + 2 * PAD, COLS), jnp.float32),
            pltpu.VMEM((FLAT, COLS), jnp.float32),
            pltpu.VMEM((FLAT, COLS), jnp.float32),
            pltpu.VMEM((2, BINS, COLS), jnp.float32),
            pltpu.VMEM((CELLS, CELLS), jnp.bfloat16),
            pltpu.VMEM((ROWS, TALL, COLS), jnp.int32),
        ],
        compiler_params=pltpu.CompilerParams(vmem_limit_bytes=VMEM_BYTES),
        cost_estimate=pl.CostEstimate(
            flops=1_400_000_000, bytes_accessed=10_000_000, transcendentals=0
        ),
        interpret=interpret,
    )(*operands)


def average_kernel(pieces_ref, out_ref):
    blocks = TALL // 8
    sub = lax.broadcasted_iota(jnp.int32, (8, COLS), 0)

    def add(i, carry):
        sums, weights, number = carry
        piece = pieces_ref[i].astype(jnp.int32).astype(jnp.float32)
        rest = piece[TALL - 8 :]
        at = PIECE % 8
        count = jnp.where(sub < ROWS, pltpu.roll(rest, 8 - at, 0), pltpu.roll(rest, ROWS - at, 0))
        weight = count * jnp.broadcast_to(rest[at + ROWS : at + ROWS + 1], (8, COLS))
        sums = tuple(sums[u] + piece[8 * u : 8 * u + 8] * weight for u in range(blocks))
        return sums, weights + weight, number + count

    zero = jnp.zeros((8, COLS), jnp.float32)
    carry = ((zero,) * blocks, zero, zero)
    sums, weights, number = lax.fori_loop(0, PIECES, add, carry)
    scale = 1.0 / (UNIT * STEPS * number)
    mean = jnp.concatenate([(part + OFFSET * weights) * scale for part in sums], axis=0)
    mean = mean.astype(jnp.bfloat16)

    def write(i, carry):
        out_ref[i] = mean
        return carry

    lax.fori_loop(0, PIECES, write, 0)


def average(pieces, interpret=False):
    vmem = pl.BlockSpec(memory_space=pltpu.VMEM)
    return pl.pallas_call(
        average_kernel,
        out_shape=jax.ShapeDtypeStruct((PIECES, TALL, COLS), jnp.bfloat16),
        in_specs=[vmem],
        out_specs=vmem,
        compiler_params=pltpu.CompilerParams(vmem_limit_bytes=VMEM_BYTES),
        interpret=interpret,
    )(pieces)


def lay_kernel(flag_ref, parts_ref, _, out_ref, wide, narrow, sem):
    @pl.when(flag_ref[1] == 0)
    def _():
        def put(j, carry):
            wide[pl.ds(j * PIECE, TALL), :] = parts_ref[j].astype(jnp.float32)
            return carry

        lax.fori_loop(0, PIECES, put, 0)

        def narrower(i, carry):
            for u in range(4):
                at = pl.multiple_of(i * 64 + u * 16, 16)
                narrow[pl.ds(at, 16), :] = wide[pl.ds(at, 16), :].astype(jnp.bfloat16)
            return carry

        lax.fori_loop(0, FLAT // 64, narrower, 0)
        copy = pltpu.make_async_copy(narrow, out_ref, sem)
        copy.start()
        copy.wait()


def lay(flags, parts, evolved):
    vmem = pl.BlockSpec(memory_space=pltpu.VMEM)
    anywhere = pl.BlockSpec(memory_space=pl.ANY)
    return pl.pallas_call(
        lay_kernel,
        out_shape=jax.ShapeDtypeStruct((FLAT, COLS), jnp.bfloat16),
        in_specs=[pl.BlockSpec(memory_space=pltpu.SMEM), vmem, anywhere],
        out_specs=anywhere,
        scratch_shapes=[
            pltpu.VMEM((FLAT + 2 * PAD, COLS), jnp.float32),
            pltpu.VMEM((FLAT, COLS), jnp.bfloat16),
            pltpu.SemaphoreType.DMA,
        ],
        input_output_aliases={2: 0},
        compiler_params=pltpu.CompilerParams(vmem_limit_bytes=VMEM_BYTES),
    )(flags, parts, evolved)


def tables():
    group_speed = 0.45 * np.exp(-math.log(1.1) * np.arange(NF))
    angles = 2.0 * math.pi / ND * np.arange(ND)

    def wide(values, times):
        return np.repeat(np.repeat(values, times)[:, None], COLS, axis=1).astype(np.float32)

    cosine, sine = np.cos(angles), np.sin(angles)
    twice = BLOCK // ND
    per_row = (wide(cosine, ROWS), wide(sine, ROWS))
    per_bin = (wide(np.tile(cosine, twice), 1), wide(np.tile(sine, twice), 1))
    return (group_speed.astype(np.float32),) + per_row + per_bin


def spots():
    source = np.arange(COLS)[:, None]
    lane = np.arange((ROWS + 2) * COLS)[None, :]
    block, column = lane // COLS, lane % COLS
    chosen = ((column == 0) & (source == 2 * block)) | (
        (column == COLS - 1) & (source == 2 * block + 1)
    )
    return chosen.astype(jnp.bfloat16)


def facing(x):
    first = lax.axis_index("cell") == 0
    return jnp.stack([jnp.where(first, x[3], x[0]), jnp.where(first, x[2], x[1])], axis=0)


def swap(x):
    return lax.ppermute(x, "cell", [(0, 1), (1, 0)])


def on_device(
    spectrum,
    depth_factor,
    wet_mask,
    frac_index,
    boundary_map,
    average_map,
    dia_plus,
    dia_minus,
    dia_coef,
):
    groups = lax.axis_size("grid")
    parent = groups - 1
    is_parent = lax.axis_index("grid") == parent
    hubs = hub_places()
    edges = 2 * ROWS
    quarter = BINS // len(hubs)
    spec = spectrum.reshape(FLAT, COLS)
    first = (lax.axis_index("cell") == 0).astype(jnp.int32)
    flags = jnp.stack([first, jnp.where(is_parent, 0, 1)]).astype(jnp.int32)
    near, near_statics, maps, *parts = prepare(
        flags, boundary_map.T, spec, depth_factor, wet_mask, frac_index
    )

    held = jnp.where(is_parent, spec[: quarter * ROWS], 0)
    for k in range(1, len(hubs)):
        held = held + lax.ppermute(parts[k - 1], "grid", [(parent, hubs[k])])
    maps = lax.all_to_all(maps, "grid", 0, 0)[:, :edges]
    near = swap(near)
    near_statics = swap(near_statics)

    pick = (
        jnp.arange(CELLS, dtype=jnp.int32)[:, None] == maps.reshape(1, groups * edges)
    ).astype(jnp.bfloat16)
    picked = jnp.dot(held.reshape(quarter, CELLS), pick, preferred_element_type=jnp.float32)
    picked = picked.astype(jnp.bfloat16).reshape(quarter, groups, edges).transpose(1, 2, 0)
    picked = lax.all_to_all(picked, "grid", 0, 0)
    picked = jnp.concatenate([picked[hub] for hub in hubs], axis=1)
    far = swap(facing(picked.reshape(ROWS, 2, BINS))).reshape(4, BINS)
    edge = jnp.concatenate(
        [picked, far, jnp.zeros((COLS - edges - 4, BINS), jnp.bfloat16)], axis=0
    ).T

    group_speed, cosine, sine, cosine_bin, sine_bin = tables()
    evolved, pieces = evolve(
        dia_plus * ROWS + PAD,
        dia_minus * ROWS + PAD,
        group_speed,
        dia_coef,
        flags,
        spec,
        near,
        edge,
        spots(),
        depth_factor,
        wet_mask,
        frac_index,
        near_statics,
        cosine,
        sine,
        cosine_bin,
        sine_bin,
        average_map,
    )
    copies = average(lax.all_to_all(pieces, "grid", 0, 0))
    gathered = lax.all_to_all(copies, "grid", 0, 0)
    return lay(flags, gathered, evolved).reshape(BINS, ROWS, COLS)


def solution(mesh):
    placed = (
        P(None, ("grid", "cell"), None),
        P(("grid", "cell"), None),
        P(("grid", "cell"), None),
        P(("grid", "cell"), None),
        P(("grid", "cell"), None),
        P(("grid", "cell"), None),
        P(),
        P(),
        P(),
    )
    return jax.shard_map(
        on_device,
        mesh=mesh,
        in_specs=placed,
        out_specs=P(None, ("grid", "cell"), None),
        check_vma=False,
    )
```

```python
import functools
import math

import jax
import jax.numpy as jnp
import numpy as np
from jax import lax
from jax.experimental import pallas as pl
from jax.experimental.pallas import tpu as pltpu
from jax.sharding import PartitionSpec as P

NF = 36
ND = 36
SIDE = 4
ROWS = 4
COLS = 128
CELLS = ROWS * COLS
BINS = NF * ND
FLAT = BINS * ROWS
PAD = 8
PIECES = SIDE**3
PIECE = FLAT // PIECES
TALL = 88
BLOCK = 72
CHUNK = 432
UNIT = 512.0
STEPS = 65534.0
OFFSET = 32767
VMEM_BYTES = 24 * 1024 * 1024
SMALL_BYTES = 10 * 1024 * 1024

FRACTIONS = (0.25, 0.5, 0.75, 1.0)


def fraction(frac_index):
    open_share = jnp.zeros(frac_index.shape, jnp.float32)
    for position, share in enumerate(FRACTIONS):
        open_share = open_share + jnp.where(frac_index == position, share, 0.0)
    return open_share


def place(z, y, x):
    return (z % SIDE * SIDE + y % SIDE) * SIDE + x % SIDE


def hub_places():
    last = SIDE - 1
    return [
        place(last, last, last),
        place(last, last, last - 1),
        place(last, last - 1, last),
        place(last - 1, last, last),
    ]


def bin_block(ref, index):
    return ref[8 * index : 8 * index + 8, :]


def prepare_kernel(
    flag_ref,
    map_ref,
    spec_ref,
    depth_ref,
    wet_ref,
    frac_ref,
    near_ref,
    stat_ref,
    maps_ref,
    part1_ref,
    part2_ref,
    part3_ref,
    dens,
):
    first = flag_ref[0] == 1
    lane = lax.broadcasted_iota(jnp.int32, (PIECES, COLS), 1)
    maps = jnp.zeros((PIECES, COLS), jnp.int32)
    for r in range(ROWS):
        for side in range(2):
            maps = jnp.where(lane == 2 * r + side, map_ref[side, r], maps)
    maps_ref[...] = maps

    wet = wet_ref[...].astype(jnp.float32)
    values = (depth_ref[...], wet * fraction(frac_ref[...]), wet)
    for i, value in enumerate(values):
        stat_ref[2 * i : 2 * i + 1, :] = jnp.where(first, value[3:4], value[0:1])
        stat_ref[2 * i + 1 : 2 * i + 2, :] = jnp.where(first, value[2:3], value[1:2])
    stat_ref[6:8, :] = jnp.zeros((2, COLS), jnp.float32)

    part = FLAT // SIDE
    for k, ref in enumerate((part1_ref, part2_ref, part3_ref)):
        ref[...] = spec_ref[(k + 1) * part : (k + 2) * part, :]

    def widen(i, carry):
        for u in range(4):
            at = pl.multiple_of(i * 64 + u * 16, 16)
            dens[pl.ds(at, 16), :] = spec_ref[pl.ds(at, 16), :].astype(jnp.float32)
        return carry

    lax.fori_loop(0, FLAT // 64, widen, 0)
    nearer = 3 * flag_ref[0]
    farther = 1 + flag_ref[0]

    def pull(i, carry):
        for u in range(3):
            at = pl.multiple_of(i * 48 + u * 16, 16)
            for n, row in enumerate((nearer, farther)):
                rows = dens[pl.ds(at * ROWS + row, 16, stride=ROWS), :]
                near_ref[n, pl.ds(at, 16), :] = rows.astype(jnp.bfloat16)
        return carry

    lax.fori_loop(0, BINS // 48, pull, 0)


def prepare(*operands, interpret=False):
    smem = pl.BlockSpec(memory_space=pltpu.SMEM)
    vmem = pl.BlockSpec(memory_space=pltpu.VMEM)
    part = jax.ShapeDtypeStruct((FLAT // SIDE, COLS), jnp.bfloat16)
    return pl.pallas_call(
        prepare_kernel,
        out_shape=(
            jax.ShapeDtypeStruct((2, BINS, COLS), jnp.bfloat16),
            jax.ShapeDtypeStruct((8, COLS), jnp.float32),
            jax.ShapeDtypeStruct((PIECES, COLS), jnp.int32),
            part,
            part,
            part,
        ),
        in_specs=[smem] * 2 + [vmem] * 4,
        out_specs=(vmem,) * 6,
        scratch_shapes=[pltpu.VMEM((FLAT, COLS), jnp.float32)],
        compiler_params=pltpu.CompilerParams(vmem_limit_bytes=SMALL_BYTES),
        interpret=interpret,
    )(*operands)


def step_kernel(
    plus_ref,
    minus_ref,
    speed_ref,
    coef_ref,
    flag_ref,
    spec_ref,
    near_ref,
    edge_ref,
    spot_ref,
    depth_ref,
    wet_ref,
    frac_ref,
    stat_ref,
    cos_ref,
    sin_ref,
    cosb_ref,
    sinb_ref,
    target_ref,
    out_ref,
    pieces_ref,
    dens,
    flat,
    halo,
    evol,
    near,
    hot,
    count,
):
    first = flag_ref[0] == 1
    child = flag_ref[1]
    adjacent = 3 * flag_ref[0]
    sign = jnp.where(first, 1.0, -1.0)
    lane = lax.broadcasted_iota(jnp.int32, (16, COLS), 1)
    ends = jnp.where((lane == 0) | (lane == COLS - 1), child, 0) > 0

    many = CHUNK
    lane_many = lax.broadcasted_iota(jnp.int32, (many, COLS), 1)
    ends_many = jnp.where((lane_many == 0) | (lane_many == COLS - 1), child, 0) > 0

    def lay_edges(c, carry):
        base = pl.multiple_of(c * many, 16)
        laid = jnp.dot(
            edge_ref[pl.ds(base, many), :], spot_ref[...], preferred_element_type=jnp.float32
        )
        for r in range(ROWS):
            flat[pl.ds(base * ROWS + r, many, stride=ROWS), :] = laid[:, r * COLS : (r + 1) * COLS]
        for n in range(2):
            raw = near_ref[n, pl.ds(base, many), :].astype(jnp.float32)
            at = (ROWS + n) * COLS
            near[n, pl.ds(base, many), :] = jnp.where(ends_many, laid[:, at : at + COLS], raw)
        return carry

    lax.fori_loop(0, BINS // many, lay_edges, 0)

    def begin(i, carry):
        for u in range(4):
            at = pl.multiple_of(i * 64 + u * 16, 16)
            raw = spec_ref[pl.ds(at, 16), :].astype(jnp.float32)
            dens[pl.ds(PAD + at, 16), :] = jnp.where(ends, flat[pl.ds(at, 16), :], raw)
            halo[pl.ds(at, 16), :] = jnp.zeros((16, COLS), jnp.float32)
        return carry

    lax.fori_loop(0, FLAT // 64, begin, 0)

    sub = lax.broadcasted_iota(jnp.int32, (8, COLS), 0)
    low = sub < ROWS
    depth = jnp.concatenate([depth_ref[...]] * 2, axis=0)
    wet = jnp.concatenate([wet_ref[...]] * 2, axis=0).astype(jnp.float32)
    weight = wet * fraction(jnp.concatenate([frac_ref[...]] * 2, axis=0))

    def between(d0, d1, w0, w1):
        return 0.5 * (d0 + d1) * w0 * w1

    def along(d, w):
        face = between(d, pltpu.roll(d, COLS - 1, 1), w, pltpu.roll(w, COLS - 1, 1))
        return jnp.where(lane[:8] == COLS - 1, 0.0, face)

    def wide(row):
        return jnp.broadcast_to(row, (8, COLS))

    face_x = between(depth, pltpu.roll(depth, 7, 0), weight, pltpu.roll(weight, 7, 0))
    face_x = jnp.where(sub % ROWS == ROWS - 1, 0.0, face_x)
    face_y = along(depth, weight)
    d_own = wide(jnp.where(first, depth[3:4], depth[0:1]))
    w_own = wide(jnp.where(first, weight[3:4], weight[0:1]))
    d_n1, d_n2, w_n1, w_n2, wet_n = (wide(stat_ref[i : i + 1, :]) for i in range(5))
    face_an = between(d_own, d_n1, w_own, w_n1)
    face_nb = between(d_n1, d_n2, w_n1, w_n2)
    face_n = along(d_n1, w_n1)

    def block(k, carry):
        bins = pl.multiple_of(k * BLOCK, 8)
        rows = pl.multiple_of(k * (BLOCK * ROWS), 16)
        g0, g1 = speed_ref[2 * k], speed_ref[2 * k + 1]

        def halo_flux(j):
            n1 = near[0, pl.ds(bins + 8 * j, 8), :]
            own = dens[pl.ds(PAD + rows + 32 * j + adjacent, 8, stride=ROWS), :]
            cosv = bin_block(cosb_ref, j)
            cp, cm = jnp.maximum(cosv, 0.0), jnp.minimum(cosv, 0.0)
            top, bottom = jnp.where(first, own, n1), jnp.where(first, n1, own)
            flux = face_an * (cp * top + cm * bottom)
            halo[pl.ds(rows + 32 * j + adjacent, 8, stride=ROWS), :] = sign * flux
            return n1, cp, cm, flux

        def advance(p):
            at = rows + 8 * p
            rho = dens[pl.ds(PAD + at, 8), :]
            cosv, sinv = bin_block(cos_ref, p % 18), bin_block(sin_ref, p % 18)
            after = pltpu.roll(rho, 7, 0)
            right = pltpu.roll(rho, COLS - 1, 1)
            fx = face_x * (jnp.maximum(cosv, 0.0) * rho + jnp.minimum(cosv, 0.0) * after)
            fy = face_y * (jnp.maximum(sinv, 0.0) * rho + jnp.minimum(sinv, 0.0) * right)
            change = (fx - pltpu.roll(fx, 1, 0)) + (fy - pltpu.roll(fy, 1, 1))
            change = change + halo[pl.ds(at, 8), :]
            dens[pl.ds(PAD + at, 8), :] = (rho - (g0 if p < 18 else g1) * change) * wet

        for j in range(BLOCK // 8):
            n1, cp, cm, flux = halo_flux(j)
            n2 = near[1, pl.ds(bins + 8 * j, 8), :]
            sinv = bin_block(sinb_ref, j)
            top, bottom = jnp.where(first, n1, n2), jnp.where(first, n2, n1)
            beyond = face_nb * (cp * top + cm * bottom)
            fy = face_n * (
                jnp.maximum(sinv, 0.0) * n1
                + jnp.minimum(sinv, 0.0) * pltpu.roll(n1, COLS - 1, 1)
            )
            change = sign * (beyond - flux) + (fy - pltpu.roll(fy, 1, 1))
            speed = g0 if j < 4 else (jnp.where(low, g0, g1) if j == 4 else g1)
            near[0, pl.ds(bins + 8 * j, 8), :] = (n1 - speed * change) * wet_n
        for p in range(BLOCK // 2):
            advance(p)
        for j in range(BLOCK // 8):
            halo_flux(j)
        for p in range(BLOCK // 2):
            advance(p)
        return carry

    lax.fori_loop(0, BINS // BLOCK, block, 0)

    def interact(f, carry):
        rows = pl.multiple_of(f * (ND * ROWS), 16)
        scale = 0.2 * coef_ref[f]

        def partner(ref, b):
            lower = dens[pl.ds(ref[f * ND + b], 8), :]
            upper = dens[pl.ds(ref[f * ND + b + 1] - ROWS, 8), :]
            return jnp.where(low, lower, upper)

        for g in range(ND // 4):
            done = []
            for h in range(2):
                b = 4 * g + 2 * h
                mine = dens[pl.ds(PAD + rows + 4 * b, 8), :]
                plus, minus = partner(plus_ref, b), partner(minus_ref, b)
                source = mine * (mine * (plus + minus) - 2.0 * (plus * minus))
                value = jnp.maximum(mine + scale * source, 0.0)
                evol[pl.ds(rows + 4 * b, 8), :] = value
                done.append(value)
            out_ref[pl.ds(rows + 16 * g, 16), :] = jnp.concatenate(done, axis=0).astype(jnp.bfloat16)
        return carry

    lax.fori_loop(0, NF, interact, 0)

    row = lax.broadcasted_iota(jnp.int32, (CELLS, COLS), 0)
    for r in range(ROWS):
        own = lane[:1] + r * COLS
        same = row == jnp.where(child == 1, target_ref[r : r + 1, :], own)
        hot[:, r * COLS : (r + 1) * COLS] = jnp.where(same, 1.0, 0.0).astype(jnp.bfloat16)
    inner = (((1,), (1,)), ((), ()))
    number = lax.dot_general(
        jnp.ones((16, CELLS), jnp.bfloat16), hot[...], inner, preferred_element_type=jnp.float32
    )
    share = 1.0 / jnp.maximum(number[0:1], 1.0)
    count[...] = jnp.zeros_like(count)
    for turn in range(ROWS):
        for r in range(ROWS):
            of = (turn + r) % ROWS
            here = number[0:1, of * COLS : (of + 1) * COLS].astype(jnp.int32)
            count[turn, PIECE + r : PIECE + r + 1, :] = here

    def sums(c, carry):
        base = c * (many * ROWS)
        parts = [evol[pl.ds(base + r, many, stride=ROWS), :] for r in range(ROWS)]
        value = jnp.concatenate(parts, axis=1)
        head = value.astype(jnp.bfloat16)
        tail = (value - head.astype(jnp.float32)).astype(jnp.bfloat16)
        total = lax.dot_general(head, hot[...], inner, preferred_element_type=jnp.float32)
        total += lax.dot_general(tail, hot[...], inner, preferred_element_type=jnp.float32)
        for r in range(ROWS):
            part = slice(r * COLS, (r + 1) * COLS)
            flat[pl.ds(base + r, many, stride=ROWS), :] = total[:, part] * share[:, part]
        return carry

    lax.fori_loop(0, BINS // many, sums, 0)
    row = lax.broadcasted_iota(jnp.int32, (TALL, COLS), 0)

    def cut(i, carry):
        for turn in range(ROWS):
            j = i * ROWS + turn
            mean = jnp.where(row < PIECE, flat[pl.ds(j * PIECE, TALL), :], 0.0)
            size = (jnp.max(mean, axis=0, keepdims=True) * UNIT).astype(jnp.int32) + 1
            size = jnp.minimum(size, OFFSET)
            steps = (UNIT * STEPS) / size.astype(jnp.float32)
            code = jnp.minimum((mean * steps + 0.5).astype(jnp.int32), 2 * OFFSET) - OFFSET
            rest = jnp.where(row == PIECE + ROWS, size, count[turn])
            pieces_ref[j] = jnp.where(row < PIECE, code, rest).astype(jnp.int16)
        return carry

    lax.fori_loop(0, PIECES // ROWS, cut, 0)


def evolve(*operands, interpret=False):
    smem = pl.BlockSpec(memory_space=pltpu.SMEM)
    vmem = pl.BlockSpec(memory_space=pltpu.VMEM)
    return pl.pallas_call(
        step_kernel,
        out_shape=(
            jax.ShapeDtypeStruct((FLAT, COLS), jnp.bfloat16),
            jax.ShapeDtypeStruct((PIECES, TALL, COLS), jnp.int16),
        ),
        in_specs=[smem] * 5 + [vmem] * 13,
        out_specs=(vmem, vmem),
        scratch_shapes=[
            pltpu.VMEM((FLAT + 2 * PAD, COLS), jnp.float32),
            pltpu.VMEM((FLAT + 2 * PAD, COLS), jnp.float32),
            pltpu.VMEM((FLAT, COLS), jnp.float32),
            pltpu.VMEM((FLAT, COLS), jnp.float32),
            pltpu.VMEM((2, BINS, COLS), jnp.float32),
            pltpu.VMEM((CELLS, CELLS), jnp.bfloat16),
            pltpu.VMEM((ROWS, TALL, COLS), jnp.int32),
        ],
        compiler_params=pltpu.CompilerParams(vmem_limit_bytes=VMEM_BYTES),
        cost_estimate=pl.CostEstimate(
            flops=1_400_000_000, bytes_accessed=10_000_000, transcendentals=0
        ),
        interpret=interpret,
    )(*operands)


def average_kernel(pieces_ref, out_ref):
    blocks = TALL // 8
    sub = lax.broadcasted_iota(jnp.int32, (8, COLS), 0)

    def add(i, carry):
        sums, weights, number = carry
        piece = pieces_ref[i].astype(jnp.int32).astype(jnp.float32)
        rest = piece[TALL - 8 :]
        at = PIECE % 8
        count = jnp.where(sub < ROWS, pltpu.roll(rest, 8 - at, 0), pltpu.roll(rest, ROWS - at, 0))
        weight = count * jnp.broadcast_to(rest[at + ROWS : at + ROWS + 1], (8, COLS))
        sums = tuple(sums[u] + piece[8 * u : 8 * u + 8] * weight for u in range(blocks))
        return sums, weights + weight, number + count

    zero = jnp.zeros((8, COLS), jnp.float32)
    carry = ((zero,) * blocks, zero, zero)
    sums, weights, number = lax.fori_loop(0, PIECES, add, carry)
    scale = 1.0 / (UNIT * STEPS * number)
    mean = jnp.concatenate([(part + OFFSET * weights) * scale for part in sums], axis=0)
    mean = mean.astype(jnp.bfloat16)

    def write(i, carry):
        out_ref[i] = mean
        return carry

    lax.fori_loop(0, PIECES, write, 0)


def average(pieces, interpret=False):
    vmem = pl.BlockSpec(memory_space=pltpu.VMEM)
    return pl.pallas_call(
        average_kernel,
        out_shape=jax.ShapeDtypeStruct((PIECES, TALL, COLS), jnp.bfloat16),
        in_specs=[vmem],
        out_specs=vmem,
        compiler_params=pltpu.CompilerParams(vmem_limit_bytes=SMALL_BYTES),
        interpret=interpret,
    )(pieces)


def lay_kernel(flag_ref, parts_ref, _, out_ref, wide, narrow, sem):
    @pl.when(flag_ref[1] == 0)
    def _():
        def put(j, carry):
            wide[pl.ds(j * PIECE, TALL), :] = parts_ref[j].astype(jnp.float32)
            return carry

        lax.fori_loop(0, PIECES, put, 0)

        def narrower(i, carry):
            for u in range(4):
                at = pl.multiple_of(i * 64 + u * 16, 16)
                narrow[pl.ds(at, 16), :] = wide[pl.ds(at, 16), :].astype(jnp.bfloat16)
            return carry

        lax.fori_loop(0, FLAT // 64, narrower, 0)
        copy = pltpu.make_async_copy(narrow, out_ref, sem)
        copy.start()
        copy.wait()


def lay(flags, parts, evolved):
    vmem = pl.BlockSpec(memory_space=pltpu.VMEM)
    anywhere = pl.BlockSpec(memory_space=pl.ANY)
    return pl.pallas_call(
        lay_kernel,
        out_shape=jax.ShapeDtypeStruct((FLAT, COLS), jnp.bfloat16),
        in_specs=[pl.BlockSpec(memory_space=pltpu.SMEM), vmem, anywhere],
        out_specs=anywhere,
        scratch_shapes=[
            pltpu.VMEM((FLAT + 2 * PAD, COLS), jnp.float32),
            pltpu.VMEM((FLAT, COLS), jnp.bfloat16),
            pltpu.SemaphoreType.DMA,
        ],
        input_output_aliases={2: 0},
        compiler_params=pltpu.CompilerParams(vmem_limit_bytes=SMALL_BYTES),
    )(flags, parts, evolved)


def tables():
    group_speed = 0.45 * np.exp(-math.log(1.1) * np.arange(NF))
    angles = 2.0 * math.pi / ND * np.arange(ND)

    def wide(values, times):
        return np.repeat(np.repeat(values, times)[:, None], COLS, axis=1).astype(np.float32)

    cosine, sine = np.cos(angles), np.sin(angles)
    twice = BLOCK // ND
    per_row = (wide(cosine, ROWS), wide(sine, ROWS))
    per_bin = (wide(np.tile(cosine, twice), 1), wide(np.tile(sine, twice), 1))
    return (group_speed.astype(np.float32),) + per_row + per_bin


def spots():
    source = np.arange(COLS)[:, None]
    lane = np.arange((ROWS + 2) * COLS)[None, :]
    block, column = lane // COLS, lane % COLS
    chosen = ((column == 0) & (source == 2 * block)) | (
        (column == COLS - 1) & (source == 2 * block + 1)
    )
    return chosen.astype(jnp.bfloat16)


def facing(x):
    first = lax.axis_index("cell") == 0
    return jnp.stack([jnp.where(first, x[3], x[0]), jnp.where(first, x[2], x[1])], axis=0)


def swap(x):
    return lax.ppermute(x, "cell", [(0, 1), (1, 0)])


def on_device(
    spectrum,
    depth_factor,
    wet_mask,
    frac_index,
    boundary_map,
    average_map,
    dia_plus,
    dia_minus,
    dia_coef,
):
    groups = lax.axis_size("grid")
    parent = groups - 1
    is_parent = lax.axis_index("grid") == parent
    hubs = hub_places()
    edges = 2 * ROWS
    quarter = BINS // len(hubs)
    spec = spectrum.reshape(FLAT, COLS)
    first = (lax.axis_index("cell") == 0).astype(jnp.int32)
    flags = jnp.stack([first, jnp.where(is_parent, 0, 1)]).astype(jnp.int32)
    near, near_statics, maps, *parts = prepare(
        flags, boundary_map.T, spec, depth_factor, wet_mask, frac_index
    )

    held = jnp.where(is_parent, spec[: quarter * ROWS], 0)
    for k in range(1, len(hubs)):
        held = held + lax.ppermute(parts[k - 1], "grid", [(parent, hubs[k])])
    maps = lax.all_to_all(maps, "grid", 0, 0)[:, :edges]
    near = swap(near)
    near_statics = swap(near_statics)

    pick = (
        jnp.arange(CELLS, dtype=jnp.int32)[:, None] == maps.reshape(1, groups * edges)
    ).astype(jnp.bfloat16)
    picked = jnp.dot(held.reshape(quarter, CELLS), pick, preferred_element_type=jnp.float32)
    picked = picked.astype(jnp.bfloat16).reshape(quarter, groups, edges).transpose(1, 2, 0)
    picked = lax.all_to_all(picked, "grid", 0, 0)
    picked = jnp.concatenate([picked[hub] for hub in hubs], axis=1)
    far = swap(facing(picked.reshape(ROWS, 2, BINS))).reshape(4, BINS)
    edge = jnp.concatenate(
        [picked, far, jnp.zeros((COLS - edges - 4, BINS), jnp.bfloat16)], axis=0
    ).T

    group_speed, cosine, sine, cosine_bin, sine_bin = tables()
    evolved, pieces = evolve(
        dia_plus * ROWS + PAD,
        dia_minus * ROWS + PAD,
        group_speed,
        dia_coef,
        flags,
        spec,
        near,
        edge,
        spots(),
        depth_factor,
        wet_mask,
        frac_index,
        near_statics,
        cosine,
        sine,
        cosine_bin,
        sine_bin,
        average_map,
    )
    copies = average(lax.all_to_all(pieces, "grid", 0, 0))
    gathered = lax.all_to_all(copies, "grid", 0, 0)
    return lay(flags, gathered, evolved).reshape(BINS, ROWS, COLS)


def solution(mesh):
    placed = (
        P(None, ("grid", "cell"), None),
        P(("grid", "cell"), None),
        P(("grid", "cell"), None),
        P(("grid", "cell"), None),
        P(("grid", "cell"), None),
        P(("grid", "cell"), None),
        P(),
        P(),
        P(),
    )
    return jax.shard_map(
        on_device,
        mesh=mesh,
        in_specs=placed,
        out_specs=P(None, ("grid", "cell"), None),
        check_vma=False,
    )
```

```python
import functools
import math

import jax
import jax.numpy as jnp
import numpy as np
from jax import lax
from jax.experimental import pallas as pl
from jax.experimental.pallas import tpu as pltpu
from jax.sharding import PartitionSpec as P

NF = 36
ND = 36
SIDE = 4
ROWS = 4
COLS = 128
CELLS = ROWS * COLS
BINS = NF * ND
FLAT = BINS * ROWS
PAD = 8
PIECES = SIDE**3
PIECE = FLAT // PIECES
TALL = 88
BLOCK = 72
CHUNK = 432
UNIT = 512.0
STEPS = 65534.0
OFFSET = 32767
SPOTS = 12
SLOT = 16
TERMS = 13
WIDE = 256
VMEM_BYTES = 24 * 1024 * 1024
SMALL_BYTES = 10 * 1024 * 1024
MIDDLE_BYTES = 14 * 1024 * 1024
LARGE_BYTES = 56 * 1024 * 1024
FIRST_BLOCKS = 6

FRACTIONS = (0.25, 0.5, 0.75, 1.0)


def fraction(frac_index):
    open_share = jnp.zeros(frac_index.shape, jnp.float32)
    for position, share in enumerate(FRACTIONS):
        open_share = open_share + jnp.where(frac_index == position, share, 0.0)
    return open_share


def place(z, y, x):
    return (z % SIDE * SIDE + y % SIDE) * SIDE + x % SIDE


def hub_places():
    last = SIDE - 1
    return [
        place(last, last, last),
        place(last, last, last - 1),
        place(last, last - 1, last),
        place(last - 1, last, last),
    ]


def bin_block(ref, index):
    return ref[8 * index : 8 * index + 8, :]


def send_kernel(map_ref, spec_ref, maps_ref, part0_ref, part1_ref, part2_ref, part3_ref, sems):
    part = FLAT // SIDE
    refs = (part0_ref, part1_ref, part2_ref, part3_ref)
    copies = [
        pltpu.make_async_copy(spec_ref.at[pl.ds(k * part, part), :], ref, sems.at[k])
        for k, ref in enumerate(refs)
    ]
    for copy in copies:
        copy.start()
    lane = lax.broadcasted_iota(jnp.int32, (PIECES, COLS), 1)
    maps = jnp.zeros((PIECES, COLS), jnp.int32)
    for r in range(ROWS):
        for side in range(2):
            maps = jnp.where(lane == 2 * r + side, map_ref[side, r], maps)
    maps_ref[...] = maps
    for copy in copies:
        copy.wait()


def send_first(maps, spec):
    anywhere = pl.BlockSpec(memory_space=pl.ANY)
    part = jax.ShapeDtypeStruct((FLAT // SIDE, COLS), jnp.bfloat16)
    return pl.pallas_call(
        send_kernel,
        out_shape=(jax.ShapeDtypeStruct((PIECES, COLS), jnp.int32),) + (part,) * SIDE,
        in_specs=[pl.BlockSpec(memory_space=pltpu.SMEM), anywhere],
        out_specs=(pl.BlockSpec(memory_space=pltpu.VMEM),) + (anywhere,) * SIDE,
        scratch_shapes=[pltpu.SemaphoreType.DMA((SIDE,))],
        compiler_params=pltpu.CompilerParams(vmem_limit_bytes=LARGE_BYTES),
    )(maps, spec)


def prepare_kernel(flag_ref, spec_ref, depth_ref, wet_ref, frac_ref, near_ref, stat_ref, dens):
    first = flag_ref[0] == 1
    wet = wet_ref[...].astype(jnp.float32)
    values = (depth_ref[...], wet * fraction(frac_ref[...]), wet)
    for i, value in enumerate(values):
        stat_ref[2 * i : 2 * i + 1, :] = jnp.where(first, value[3:4], value[0:1])
        stat_ref[2 * i + 1 : 2 * i + 2, :] = jnp.where(first, value[2:3], value[1:2])
    stat_ref[6:8, :] = jnp.zeros((2, COLS), jnp.float32)

    def widen(i, carry):
        for u in range(4):
            at = pl.multiple_of(i * 64 + u * 16, 16)
            dens[pl.ds(at, 16), :] = spec_ref[pl.ds(at, 16), :].astype(jnp.float32)
        return carry

    lax.fori_loop(0, FLAT // 64, widen, 0)
    nearer = 3 * flag_ref[0]
    farther = 1 + flag_ref[0]

    def pull(i, carry):
        for u in range(3):
            at = pl.multiple_of(i * 48 + u * 16, 16)
            for n, row in enumerate((nearer, farther)):
                rows = dens[pl.ds(at * ROWS + row, 16, stride=ROWS), :]
                near_ref[n, pl.ds(at, 16), :] = rows.astype(jnp.bfloat16)
        return carry

    lax.fori_loop(0, BINS // 48, pull, 0)


def prepare(*operands, interpret=False):
    vmem = pl.BlockSpec(memory_space=pltpu.VMEM)
    return pl.pallas_call(
        prepare_kernel,
        out_shape=(
            jax.ShapeDtypeStruct((2, BINS, COLS), jnp.bfloat16),
            jax.ShapeDtypeStruct((8, COLS), jnp.float32),
        ),
        in_specs=[pl.BlockSpec(memory_space=pltpu.SMEM)] + [vmem] * 4,
        out_specs=(vmem,) * 2,
        scratch_shapes=[pltpu.VMEM((FLAT, COLS), jnp.float32)],
        compiler_params=pltpu.CompilerParams(vmem_limit_bytes=SMALL_BYTES),
        cost_estimate=pl.CostEstimate(flops=4_000_000, bytes_accessed=5_000_000, transcendentals=0),
        interpret=interpret,
    )(*operands)


def move_kernel(
    begin_block,
    blocks,
    speed_ref,
    flag_ref,
    spec_ref,
    near_ref,
    depth_ref,
    wet_ref,
    frac_ref,
    stat_ref,
    cos_ref,
    sin_ref,
    cosb_ref,
    sinb_ref,
    dens,
    *rest,
):
    if len(rest) == 4:
        head_ref, tail_ref, halo, near = rest
    else:
        halo, near = rest
        head_ref = None
    bins0 = begin_block * BLOCK
    first = flag_ref[0] == 1
    child = flag_ref[1]
    adjacent = 3 * flag_ref[0]
    sign = jnp.where(first, 1.0, -1.0)
    lane = lax.broadcasted_iota(jnp.int32, (16, COLS), 1)
    ends = jnp.where((lane == 0) | (lane == COLS - 1), child, 0) > 0

    def begin(i, carry):
        for u in range(3):
            at = pl.multiple_of(i * 48 + u * 16, 16)
            raw = spec_ref[pl.ds(bins0 * ROWS + at, 16), :].astype(jnp.float32)
            dens[pl.ds(at, 16), :] = jnp.where(ends, 0.0, raw)
            halo[pl.ds(at, 16), :] = jnp.zeros((16, COLS), jnp.float32)
        return carry

    lax.fori_loop(0, blocks * BLOCK * ROWS // 48, begin, 0)

    def begin_near(i, carry):
        for u in range(3):
            at = pl.multiple_of(i * 48 + u * 16, 16)
            for n in range(2):
                raw = near_ref[n, pl.ds(bins0 + at, 16), :].astype(jnp.float32)
                near[n, pl.ds(at, 16), :] = jnp.where(ends, 0.0, raw)
        return carry

    lax.fori_loop(0, blocks * BLOCK // 48, begin_near, 0)

    sub = lax.broadcasted_iota(jnp.int32, (8, COLS), 0)
    lane = lane[:8]
    low = sub < ROWS
    depth = jnp.concatenate([depth_ref[...]] * 2, axis=0)
    wet = jnp.concatenate([wet_ref[...]] * 2, axis=0).astype(jnp.float32)
    weight = wet * fraction(jnp.concatenate([frac_ref[...]] * 2, axis=0))

    def between(d0, d1, w0, w1):
        return 0.5 * (d0 + d1) * w0 * w1

    def along(d, w):
        face = between(d, pltpu.roll(d, COLS - 1, 1), w, pltpu.roll(w, COLS - 1, 1))
        return jnp.where(lane == COLS - 1, 0.0, face)

    def wide(row):
        return jnp.broadcast_to(row, (8, COLS))

    face_x = between(depth, pltpu.roll(depth, 7, 0), weight, pltpu.roll(weight, 7, 0))
    face_x = jnp.where(sub % ROWS == ROWS - 1, 0.0, face_x)
    face_y = along(depth, weight)
    d_own = wide(jnp.where(first, depth[3:4], depth[0:1]))
    w_own = wide(jnp.where(first, weight[3:4], weight[0:1]))
    d_n1, d_n2, w_n1, w_n2, wet_n, wet_n2 = (wide(stat_ref[i : i + 1, :]) for i in range(6))
    face_an = between(d_own, d_n1, w_own, w_n1)
    face_nb = between(d_n1, d_n2, w_n1, w_n2)
    face_n = along(d_n1, w_n1)

    def block(k, carry):
        bins = pl.multiple_of(k * BLOCK, 8)
        rows = pl.multiple_of(k * (BLOCK * ROWS), 16)
        g0, g1 = speed_ref[2 * (begin_block + k)], speed_ref[2 * (begin_block + k) + 1]

        def halo_flux(j):
            n1 = near[0, pl.ds(bins + 8 * j, 8), :]
            own = dens[pl.ds(rows + 32 * j + adjacent, 8, stride=ROWS), :]
            cosv = bin_block(cosb_ref, j)
            cp, cm = jnp.maximum(cosv, 0.0), jnp.minimum(cosv, 0.0)
            top, bottom = jnp.where(first, own, n1), jnp.where(first, n1, own)
            flux = face_an * (cp * top + cm * bottom)
            halo[pl.ds(rows + 32 * j + adjacent, 8, stride=ROWS), :] = sign * flux
            return n1, cp, cm, flux

        def advance(p):
            at = rows + 8 * p
            rho = dens[pl.ds(at, 8), :]
            cosv, sinv = bin_block(cos_ref, p % 18), bin_block(sin_ref, p % 18)
            after = pltpu.roll(rho, 7, 0)
            right = pltpu.roll(rho, COLS - 1, 1)
            fx = face_x * (jnp.maximum(cosv, 0.0) * rho + jnp.minimum(cosv, 0.0) * after)
            fy = face_y * (jnp.maximum(sinv, 0.0) * rho + jnp.minimum(sinv, 0.0) * right)
            change = (fx - pltpu.roll(fx, 1, 0)) + (fy - pltpu.roll(fy, 1, 1))
            change = change + halo[pl.ds(at, 8), :]
            dens[pl.ds(at, 8), :] = (rho - (g0 if p < 18 else g1) * change) * wet

        for j in range(BLOCK // 8):
            n1, cp, cm, flux = halo_flux(j)
            n2 = near[1, pl.ds(bins + 8 * j, 8), :]
            sinv = bin_block(sinb_ref, j)
            top, bottom = jnp.where(first, n1, n2), jnp.where(first, n2, n1)
            beyond = face_nb * (cp * top + cm * bottom)
            fy = face_n * (
                jnp.maximum(sinv, 0.0) * n1
                + jnp.minimum(sinv, 0.0) * pltpu.roll(n1, COLS - 1, 1)
            )
            change = sign * (beyond - flux) + (fy - pltpu.roll(fy, 1, 1))
            speed = g0 if j < 4 else (jnp.where(low, g0, g1) if j == 4 else g1)
            near[0, pl.ds(bins + 8 * j, 8), :] = (n1 - speed * change) * wet_n
        for p in range(BLOCK // 2):
            advance(p)
        for j in range(BLOCK // 8):
            halo_flux(j)
        for p in range(BLOCK // 2):
            advance(p)
        return carry

    lax.fori_loop(0, blocks, block, 0)
    if head_ref is None:
        return

    at_n1, at_n2 = jnp.where(first, 4, 7), jnp.where(first, 5, 6)

    def cycle(own, n1, n2):
        return jnp.where(low, own, jnp.where(sub == at_n1, n1, jnp.where(sub == at_n2, n2, 0.0)))

    d8, w8 = cycle(depth, d_n1, d_n2), cycle(weight, w_n1, w_n2)
    wet8 = cycle(wet, wet_n, wet_n2)
    fx8 = between(d8, pltpu.roll(d8, 7, 0), w8, pltpu.roll(w8, 7, 0))
    fy8 = along(d8, w8)

    def outflow(flux, axis):
        return flux - pltpu.roll(flux, 1, axis)

    operators = (
        lambda e: outflow(fx8 * e, 0),
        lambda e: outflow(fx8 * pltpu.roll(e, 7, 0), 0),
        lambda e: outflow(fy8 * e, 1),
        lambda e: outflow(fy8 * pltpu.roll(e, COLS - 1, 1), 1),
    )

    def spread_spot(k, carry):
        n = (k - 2 * ROWS) // 2
        at = jnp.where(k < 2 * ROWS, k // 2, jnp.where(n == 0, at_n1, at_n2))
        here = (sub == at) & (lane == (k % 2) * (COLS - 1))
        unit = jnp.where(here, child, 0).astype(jnp.float32)
        once = [wet8 * op(unit) for op in operators]
        terms = [wet8 * wet8 * unit]
        for a, op in enumerate(operators):
            terms.append(-(wet8 * once[a] + wet8 * op(wet8 * unit)))
        for a in range(4):
            terms.append(wet8 * operators[a](once[a]))
        for a in range(2):
            for c in range(2, 4):
                terms.append(wet8 * (operators[a](once[c]) + operators[c](once[a])))
        for t, term in enumerate(terms):
            for r in range(ROWS):
                halo[pl.ds(r * WIDE + t * SLOT + k, 1), :] = term[r : r + 1, :]
        return carry

    halo[0 : ROWS * WIDE, :] = jnp.zeros((ROWS * WIDE, COLS), jnp.float32)
    lax.fori_loop(0, SPOTS, spread_spot, 0)
    for r in range(ROWS):
        value = halo[r * WIDE : (r + 1) * WIDE, :]
        head = value.astype(jnp.bfloat16)
        head_ref[:, r * COLS : (r + 1) * COLS] = head
        tail_ref[:, r * COLS : (r + 1) * COLS] = (value - head.astype(jnp.float32)).astype(
            jnp.bfloat16
        )


def move(begin_block, blocks, with_matrix, *operands, interpret=False):
    smem = pl.BlockSpec(memory_space=pltpu.SMEM)
    vmem = pl.BlockSpec(memory_space=pltpu.VMEM)
    rows = blocks * BLOCK * ROWS
    matrix = jax.ShapeDtypeStruct((WIDE, CELLS), jnp.bfloat16)
    out_shape = (jax.ShapeDtypeStruct((rows, COLS), jnp.float32),) + (matrix,) * (2 * with_matrix)
    return pl.pallas_call(
        functools.partial(move_kernel, begin_block, blocks),
        out_shape=out_shape,
        in_specs=[smem] * 2 + [vmem] * 10,
        out_specs=(vmem,) * len(out_shape),
        scratch_shapes=[
            pltpu.VMEM((rows, COLS), jnp.float32),
            pltpu.VMEM((2, blocks * BLOCK, COLS), jnp.float32),
        ],
        compiler_params=pltpu.CompilerParams(vmem_limit_bytes=MIDDLE_BYTES),
        cost_estimate=pl.CostEstimate(
            flops=rows * COLS * 40, bytes_accessed=rows * COLS * 30, transcendentals=0
        ),
        interpret=interpret,
    )(*operands)


def step_kernel(
    plus_ref,
    minus_ref,
    coef_ref,
    flag_ref,
    moved0_ref,
    moved1_ref,
    edge_ref,
    spot_ref,
    term_ref,
    head_ref,
    tail_ref,
    target_ref,
    out_ref,
    pieces_ref,
    dens,
    flat,
    evol,
    hot,
    count,
):
    child = flag_ref[1]
    many = CHUNK
    sub = lax.broadcasted_iota(jnp.int32, (8, COLS), 0)
    lane = lax.broadcasted_iota(jnp.int32, (8, COLS), 1)
    low = sub < ROWS

    for c in range(BINS // many):
        source = moved0_ref if c == 0 else moved1_ref
        offset = 0 if c == 0 else (c - 1) * many * ROWS
        spot = jnp.dot(
            edge_ref[c * many : (c + 1) * many, :],
            spot_ref[...],
            preferred_element_type=jnp.float32,
        )
        value = spot * term_ref[c * many : (c + 1) * many, :]
        head = value.astype(jnp.bfloat16)
        tail = (value - head.astype(jnp.float32)).astype(jnp.bfloat16)
        added = jnp.dot(head, head_ref[...], preferred_element_type=jnp.float32)
        added += jnp.dot(tail, head_ref[...], preferred_element_type=jnp.float32)
        added += jnp.dot(head, tail_ref[...], preferred_element_type=jnp.float32)
        for r in range(ROWS):
            here = source[pl.ds(offset + r, many, stride=ROWS), :]
            dens[pl.ds(PAD + c * many * ROWS + r, many, stride=ROWS), :] = (
                here + added[:, r * COLS : (r + 1) * COLS]
            )

    def interact(f, carry):
        rows = pl.multiple_of(f * (ND * ROWS), 16)
        scale = 0.2 * coef_ref[f]

        def partner(ref, b):
            lower = dens[pl.ds(ref[f * ND + b], 8), :]
            upper = dens[pl.ds(ref[f * ND + b + 1] - ROWS, 8), :]
            return jnp.where(low, lower, upper)

        for g in range(ND // 4):
            done = []
            for h in range(2):
                b = 4 * g + 2 * h
                mine = dens[pl.ds(PAD + rows + 4 * b, 8), :]
                plus, minus = partner(plus_ref, b), partner(minus_ref, b)
                source = mine * (mine * (plus + minus) - 2.0 * (plus * minus))
                value = jnp.maximum(mine + scale * source, 0.0)
                evol[pl.ds(rows + 4 * b, 8), :] = value
                done.append(value)
            out_ref[pl.ds(rows + 16 * g, 16), :] = jnp.concatenate(done, axis=0).astype(jnp.bfloat16)
        return carry

    lax.fori_loop(0, NF, interact, 0)

    row = lax.broadcasted_iota(jnp.int32, (CELLS, COLS), 0)
    for r in range(ROWS):
        own = lane[:1] + r * COLS
        same = row == jnp.where(child == 1, target_ref[r : r + 1, :], own)
        hot[:, r * COLS : (r + 1) * COLS] = jnp.where(same, 1.0, 0.0).astype(jnp.bfloat16)
    inner = (((1,), (1,)), ((), ()))
    number = lax.dot_general(
        jnp.ones((16, CELLS), jnp.bfloat16), hot[...], inner, preferred_element_type=jnp.float32
    )
    share = 1.0 / jnp.maximum(number[0:1], 1.0)
    count[...] = jnp.zeros_like(count)
    for turn in range(ROWS):
        for r in range(ROWS):
            of = (turn + r) % ROWS
            here = number[0:1, of * COLS : (of + 1) * COLS].astype(jnp.int32)
            count[turn, PIECE + r : PIECE + r + 1, :] = here

    def sums(c, carry):
        base = c * (many * ROWS)
        parts = [evol[pl.ds(base + r, many, stride=ROWS), :] for r in range(ROWS)]
        value = jnp.concatenate(parts, axis=1)
        head = value.astype(jnp.bfloat16)
        tail = (value - head.astype(jnp.float32)).astype(jnp.bfloat16)
        total = lax.dot_general(head, hot[...], inner, preferred_element_type=jnp.float32)
        total += lax.dot_general(tail, hot[...], inner, preferred_element_type=jnp.float32)
        for r in range(ROWS):
            part = slice(r * COLS, (r + 1) * COLS)
            flat[pl.ds(base + r, many, stride=ROWS), :] = total[:, part] * share[:, part]
        return carry

    lax.fori_loop(0, BINS // many, sums, 0)
    row = lax.broadcasted_iota(jnp.int32, (TALL, COLS), 0)

    def cut(i, carry):
        for turn in range(ROWS):
            j = i * ROWS + turn
            mean = jnp.where(row < PIECE, flat[pl.ds(j * PIECE, TALL), :], 0.0)
            size = (jnp.max(mean, axis=0, keepdims=True) * UNIT).astype(jnp.int32) + 1
            size = jnp.minimum(size, OFFSET)
            steps = (UNIT * STEPS) / size.astype(jnp.float32)
            code = jnp.minimum((mean * steps + 0.5).astype(jnp.int32), 2 * OFFSET) - OFFSET
            rest = jnp.where(row == PIECE + ROWS, size, count[turn])
            pieces_ref[j] = jnp.where(row < PIECE, code, rest).astype(jnp.int16)
        return carry

    lax.fori_loop(0, PIECES // ROWS, cut, 0)


def evolve(*operands, interpret=False):
    smem = pl.BlockSpec(memory_space=pltpu.SMEM)
    vmem = pl.BlockSpec(memory_space=pltpu.VMEM)
    return pl.pallas_call(
        step_kernel,
        out_shape=(
            jax.ShapeDtypeStruct((FLAT, COLS), jnp.bfloat16),
            jax.ShapeDtypeStruct((PIECES, TALL, COLS), jnp.int16),
        ),
        in_specs=[smem] * 4 + [vmem] * 8,
        out_specs=(vmem, vmem),
        scratch_shapes=[
            pltpu.VMEM((FLAT + 2 * PAD, COLS), jnp.float32),
            pltpu.VMEM((FLAT + 2 * PAD, COLS), jnp.float32),
            pltpu.VMEM((FLAT, COLS), jnp.float32),
            pltpu.VMEM((CELLS, CELLS), jnp.bfloat16),
            pltpu.VMEM((ROWS, TALL, COLS), jnp.int32),
        ],
        compiler_params=pltpu.CompilerParams(vmem_limit_bytes=VMEM_BYTES),
        cost_estimate=pl.CostEstimate(
            flops=1_400_000_000, bytes_accessed=10_000_000, transcendentals=0
        ),
        interpret=interpret,
    )(*operands)


def average_kernel(pieces_ref, out_ref):
    blocks = TALL // 8
    sub = lax.broadcasted_iota(jnp.int32, (8, COLS), 0)

    def add(i, carry):
        sums, weights, number = carry
        piece = pieces_ref[i].astype(jnp.int32).astype(jnp.float32)
        rest = piece[TALL - 8 :]
        at = PIECE % 8
        count = jnp.where(sub < ROWS, pltpu.roll(rest, 8 - at, 0), pltpu.roll(rest, ROWS - at, 0))
        weight = count * jnp.broadcast_to(rest[at + ROWS : at + ROWS + 1], (8, COLS))
        sums = tuple(sums[u] + piece[8 * u : 8 * u + 8] * weight for u in range(blocks))
        return sums, weights + weight, number + count

    zero = jnp.zeros((8, COLS), jnp.float32)
    carry = ((zero,) * blocks, zero, zero)
    sums, weights, number = lax.fori_loop(0, PIECES, add, carry)
    scale = 1.0 / (UNIT * STEPS * number)
    mean = jnp.concatenate([(part + OFFSET * weights) * scale for part in sums], axis=0)
    mean = mean.astype(jnp.bfloat16)

    def write(i, carry):
        out_ref[i] = mean
        return carry

    lax.fori_loop(0, PIECES, write, 0)


def average(pieces, interpret=False):
    vmem = pl.BlockSpec(memory_space=pltpu.VMEM)
    return pl.pallas_call(
        average_kernel,
        out_shape=jax.ShapeDtypeStruct((PIECES, TALL, COLS), jnp.bfloat16),
        in_specs=[vmem],
        out_specs=vmem,
        compiler_params=pltpu.CompilerParams(vmem_limit_bytes=SMALL_BYTES),
        interpret=interpret,
    )(pieces)


def lay_kernel(flag_ref, parts_ref, _, out_ref, wide, narrow, sem):
    @pl.when(flag_ref[1] == 0)
    def _():
        def put(j, carry):
            wide[pl.ds(j * PIECE, TALL), :] = parts_ref[j].astype(jnp.float32)
            return carry

        lax.fori_loop(0, PIECES, put, 0)

        def narrower(i, carry):
            for u in range(4):
                at = pl.multiple_of(i * 64 + u * 16, 16)
                narrow[pl.ds(at, 16), :] = wide[pl.ds(at, 16), :].astype(jnp.bfloat16)
            return carry

        lax.fori_loop(0, FLAT // 64, narrower, 0)
        copy = pltpu.make_async_copy(narrow, out_ref, sem)
        copy.start()
        copy.wait()


def lay(flags, parts, evolved):
    vmem = pl.BlockSpec(memory_space=pltpu.VMEM)
    anywhere = pl.BlockSpec(memory_space=pl.ANY)
    return pl.pallas_call(
        lay_kernel,
        out_shape=jax.ShapeDtypeStruct((FLAT, COLS), jnp.bfloat16),
        in_specs=[pl.BlockSpec(memory_space=pltpu.SMEM), vmem, anywhere],
        out_specs=anywhere,
        scratch_shapes=[
            pltpu.VMEM((FLAT + 2 * PAD, COLS), jnp.float32),
            pltpu.VMEM((FLAT, COLS), jnp.bfloat16),
            pltpu.SemaphoreType.DMA,
        ],
        input_output_aliases={2: 0},
        compiler_params=pltpu.CompilerParams(vmem_limit_bytes=SMALL_BYTES),
    )(flags, parts, evolved)


def tables():
    group_speed = 0.45 * np.exp(-math.log(1.1) * np.arange(NF))
    angles = 2.0 * math.pi / ND * np.arange(ND)

    def wide(values, times):
        return np.repeat(np.repeat(values, times)[:, None], COLS, axis=1).astype(np.float32)

    cosine, sine = np.cos(angles), np.sin(angles)
    twice = BLOCK // ND
    per_row = (wide(cosine, ROWS), wide(sine, ROWS))
    per_bin = (wide(np.tile(cosine, twice), 1), wide(np.tile(sine, twice), 1))
    return (group_speed.astype(np.float32),) + per_row + per_bin


def spots():
    repeat = np.zeros((COLS, WIDE), np.float32)
    for t in range(TERMS):
        for k in range(SPOTS):
            repeat[k, t * SLOT + k] = 1.0
    group_speed = 0.45 * np.exp(-math.log(1.1) * np.arange(NF))
    angles = 2.0 * math.pi / ND * np.arange(ND)
    along_x = (group_speed[:, None] * np.cos(angles)[None, :]).reshape(BINS)
    along_y = (group_speed[:, None] * np.sin(angles)[None, :]).reshape(BINS)
    parts = [
        np.maximum(along_x, 0.0),
        np.minimum(along_x, 0.0),
        np.maximum(along_y, 0.0),
        np.minimum(along_y, 0.0),
    ]
    factors = [np.ones(BINS)] + parts + [part * part for part in parts]
    factors += [parts[a] * parts[c] for a in range(2) for c in range(2, 4)]
    factors = np.repeat(np.stack(factors, axis=1), SLOT, axis=1)
    factors = np.pad(factors, ((0, 0), (0, WIDE - TERMS * SLOT)))
    return repeat.astype(jnp.bfloat16), factors.astype(np.float32)


def facing(x):
    first = lax.axis_index("cell") == 0
    return jnp.stack([jnp.where(first, x[3], x[0]), jnp.where(first, x[2], x[1])], axis=0)


def swap(x):
    return lax.ppermute(x, "cell", [(0, 1), (1, 0)])


def on_device(
    spectrum,
    depth_factor,
    wet_mask,
    frac_index,
    boundary_map,
    average_map,
    dia_plus,
    dia_minus,
    dia_coef,
):
    groups = lax.axis_size("grid")
    parent = groups - 1
    is_parent = lax.axis_index("grid") == parent
    hubs = hub_places()
    edges = 2 * ROWS
    quarter = BINS // len(hubs)
    spec = spectrum.reshape(FLAT, COLS)
    first = (lax.axis_index("cell") == 0).astype(jnp.int32)
    flags = jnp.stack([first, jnp.where(is_parent, 0, 1)]).astype(jnp.int32)
    maps, *parts = send_first(boundary_map.T, spec)

    held = jnp.where(is_parent, parts[0], 0)
    for k in range(1, len(hubs)):
        held = held + lax.ppermute(parts[k], "grid", [(parent, hubs[k])])
    maps = lax.all_to_all(maps, "grid", 0, 0)[:, :edges]
    near, near_statics = prepare(flags, spec, depth_factor, wet_mask, frac_index)
    near = swap(near)
    near_statics = swap(near_statics)

    pick = (
        jnp.arange(CELLS, dtype=jnp.int32)[:, None] == maps.reshape(1, groups * edges)
    ).astype(jnp.bfloat16)
    picked = jnp.dot(held.reshape(quarter, CELLS), pick, preferred_element_type=jnp.float32)
    picked = picked.astype(jnp.bfloat16).reshape(quarter, groups, edges).transpose(1, 2, 0)
    picked = lax.all_to_all(picked, "grid", 0, 0)
    picked = jnp.concatenate([picked[hub] for hub in hubs], axis=1)
    far = swap(facing(picked.reshape(ROWS, 2, BINS))).reshape(4, BINS)
    edge = jnp.concatenate(
        [picked, far, jnp.zeros((COLS - edges - 4, BINS), jnp.bfloat16)], axis=0
    ).T

    group_speed, *directions = tables()
    fields = (
        group_speed,
        flags,
        spec,
        near,
        depth_factor,
        wet_mask,
        frac_index,
        near_statics,
        *directions,
    )
    moved0, head, tail = move(0, FIRST_BLOCKS, True, *fields)
    (moved1,) = move(FIRST_BLOCKS, BINS // BLOCK - FIRST_BLOCKS, False, *fields)
    evolved, pieces = evolve(
        dia_plus * ROWS + PAD,
        dia_minus * ROWS + PAD,
        dia_coef,
        flags,
        moved0,
        moved1,
        edge,
        *spots(),
        head,
        tail,
        average_map,
    )
    pieces = lax.all_to_all(pieces, "grid", 0, 0)
    copies = average(pieces)
    gathered = lax.all_to_all(copies, "grid", 0, 0)
    return lay(flags, gathered, evolved).reshape(BINS, ROWS, COLS)


def solution(mesh):
    placed = (
        P(None, ("grid", "cell"), None),
        P(("grid", "cell"), None),
        P(("grid", "cell"), None),
        P(("grid", "cell"), None),
        P(("grid", "cell"), None),
        P(("grid", "cell"), None),
        P(),
        P(),
        P(),
    )
    return jax.shard_map(
        on_device,
        mesh=mesh,
        in_specs=placed,
        out_specs=P(None, ("grid", "cell"), None),
        check_vma=False,
    )
```

```python
import functools
import math

import jax
import jax.numpy as jnp
import numpy as np
from jax import lax
from jax.experimental import pallas as pl
from jax.experimental.pallas import tpu as pltpu
from jax.sharding import PartitionSpec as P

NF = 36
ND = 36
SIDE = 4
ROWS = 4
COLS = 128
CELLS = ROWS * COLS
BINS = NF * ND
FLAT = BINS * ROWS
PAD = 8
PIECES = SIDE**3
PIECE = FLAT // PIECES
TALL = 88
BLOCK = 72
GROUP = 3
CHUNK = 432
UNIT = 512.0
STEPS = 65534.0
OFFSET = 32767
VMEM_BYTES = 24 * 1024 * 1024
SMALL_BYTES = 10 * 1024 * 1024
LARGE_BYTES = 56 * 1024 * 1024
STACK = 16

FRACTIONS = (0.25, 0.5, 0.75, 1.0)


def fraction(frac_index):
    open_share = jnp.zeros(frac_index.shape, jnp.float32)
    for position, share in enumerate(FRACTIONS):
        open_share = open_share + jnp.where(frac_index == position, share, 0.0)
    return open_share


def place(z, y, x):
    return (z % SIDE * SIDE + y % SIDE) * SIDE + x % SIDE


def hub_places():
    last = SIDE - 1
    return [
        place(last, last, last),
        place(last, last, last - 1),
        place(last, last - 1, last),
        place(last - 1, last, last),
    ]


def blocks_of_16():
    half, last = SIDE // 2, SIDE - 1
    blocks = [
        [
            place(z, y * half + v, x * half + u)
            for z in range(SIDE)
            for v in range(half)
            for u in range(half)
        ]
        for y in range(2)
        for x in range(2)
    ]
    return blocks, [place(0, 0, 0), place(last, 0, last), place(last, last, 0), None]


def bin_block(ref, index):
    return ref[8 * index : 8 * index + 8, :]


def send_kernel(map_ref, spec_ref, maps_ref, *part_refs):
    lane = lax.broadcasted_iota(jnp.int32, (PIECES, COLS), 1)
    maps = jnp.zeros((PIECES, COLS), jnp.int32)
    for r in range(ROWS):
        for side in range(2):
            maps = jnp.where(lane == 2 * r + side, map_ref[side, r], maps)
    maps_ref[...] = maps
    part = FLAT // SIDE
    for k, ref in enumerate(part_refs):
        ref[...] = spec_ref[k * part : (k + 1) * part, :]


def send_first(maps, spec):
    vmem = pl.BlockSpec(memory_space=pltpu.VMEM)
    part = jax.ShapeDtypeStruct((FLAT // SIDE, COLS), jnp.bfloat16)
    return pl.pallas_call(
        send_kernel,
        out_shape=(jax.ShapeDtypeStruct((PIECES, COLS), jnp.int32),) + (part,) * SIDE,
        in_specs=[pl.BlockSpec(memory_space=pltpu.SMEM), vmem],
        out_specs=(vmem,) * (SIDE + 1),
        compiler_params=pltpu.CompilerParams(vmem_limit_bytes=LARGE_BYTES),
    )(maps, spec)


def pick_kernel(flag_ref, maps_ref, spec_ref, a_ref, b_ref, c_ref, out_ref, wide, turned):
    part = FLAT // SIDE
    bins = part // ROWS
    share = jnp.where(flag_ref[1] == 0, 1.0, 0.0)

    def join(i, carry):
        for u in range(3):
            at = pl.multiple_of(i * 48 + u * 16, 16)
            here = pl.ds(at, 16)
            value = spec_ref[here, :].astype(jnp.float32) * share
            for ref in (a_ref, b_ref, c_ref):
                value = value + ref[here, :].astype(jnp.float32)
            wide[here, :] = value
        return carry

    lax.fori_loop(0, part // 48, join, 0)
    wide[part:, :] = jnp.zeros((wide.shape[0] - part, COLS), jnp.float32)
    many = wide.shape[0] // ROWS
    held = [wide[pl.ds(r, many, stride=ROWS), :].astype(jnp.bfloat16) for r in range(ROWS)]
    held = jnp.concatenate(held, axis=1)
    cell = lax.broadcasted_iota(jnp.int32, (PIECES, CELLS), 1)
    for e in range(2 * ROWS):
        wanted = jnp.broadcast_to(maps_ref[:, e : e + 1], (PIECES, CELLS))
        hot = jnp.where(cell == wanted, 1.0, 0.0).astype(jnp.bfloat16)
        found = lax.dot_general(
            hot, held, (((1,), (1,)), ((), ())), preferred_element_type=jnp.float32
        )
        for t in range(many // COLS):
            lanes = slice(t * COLS, (t + 1) * COLS)
            turned[t, pl.ds(e, PIECES, stride=2 * ROWS), :] = found[:, lanes]

    def narrower(g, carry):
        at = pl.multiple_of(g * 2 * ROWS, 8)
        for t in range(many // COLS):
            lanes = min(COLS, bins - t * COLS)
            value = turned[t, pl.ds(at, 2 * ROWS), :lanes].astype(jnp.bfloat16)
            out_ref[g, :, t * COLS : t * COLS + lanes] = value
        return carry

    lax.fori_loop(0, PIECES, narrower, 0)


def pick(*operands):
    vmem = pl.BlockSpec(memory_space=pltpu.VMEM)
    part = FLAT // SIDE
    return pl.pallas_call(
        pick_kernel,
        out_shape=jax.ShapeDtypeStruct((PIECES, 2 * ROWS, part // ROWS), jnp.bfloat16),
        in_specs=[pl.BlockSpec(memory_space=pltpu.SMEM), vmem]
        + [vmem] * 4,
        out_specs=vmem,
        scratch_shapes=[
            pltpu.VMEM((3 * COLS * ROWS, COLS), jnp.float32),
            pltpu.VMEM((3, PIECES * 2 * ROWS, COLS), jnp.float32),
        ],
        compiler_params=pltpu.CompilerParams(vmem_limit_bytes=SMALL_BYTES),
    )(*operands)


def prepare_kernel(flag_ref, spec_ref, depth_ref, wet_ref, frac_ref, near_ref, stat_ref, dens):
    first = flag_ref[0] == 1
    wet = wet_ref[...].astype(jnp.float32)
    values = (depth_ref[...], wet * fraction(frac_ref[...]), wet)
    for i, value in enumerate(values):
        stat_ref[2 * i : 2 * i + 1, :] = jnp.where(first, value[3:4], value[0:1])
        stat_ref[2 * i + 1 : 2 * i + 2, :] = jnp.where(first, value[2:3], value[1:2])
    stat_ref[6:8, :] = jnp.zeros((2, COLS), jnp.float32)

    def widen(i, carry):
        for u in range(4):
            at = pl.multiple_of(i * 64 + u * 16, 16)
            dens[pl.ds(at, 16), :] = spec_ref[pl.ds(at, 16), :].astype(jnp.float32)
        return carry

    lax.fori_loop(0, FLAT // 64, widen, 0)
    nearer = 3 * flag_ref[0]
    farther = 1 + flag_ref[0]

    def pull(i, carry):
        for u in range(3):
            at = pl.multiple_of(i * 48 + u * 16, 16)
            for n, row in enumerate((nearer, farther)):
                rows = dens[pl.ds(at * ROWS + row, 16, stride=ROWS), :]
                near_ref[n, pl.ds(at, 16), :] = rows.astype(jnp.bfloat16)
        return carry

    lax.fori_loop(0, BINS // 48, pull, 0)


def prepare(*operands, interpret=False):
    vmem = pl.BlockSpec(memory_space=pltpu.VMEM)
    return pl.pallas_call(
        prepare_kernel,
        out_shape=(
            jax.ShapeDtypeStruct((2, BINS, COLS), jnp.bfloat16),
            jax.ShapeDtypeStruct((8, COLS), jnp.float32),
        ),
        in_specs=[pl.BlockSpec(memory_space=pltpu.SMEM)] + [vmem] * 4,
        out_specs=(vmem,) * 2,
        scratch_shapes=[pltpu.VMEM((FLAT, COLS), jnp.float32)],
        compiler_params=pltpu.CompilerParams(vmem_limit_bytes=LARGE_BYTES),
        cost_estimate=pl.CostEstimate(flops=4_000_000, bytes_accessed=5_000_000, transcendentals=0),
        interpret=interpret,
    )(*operands)


def step_kernel(
    plus_ref,
    minus_ref,
    speed_ref,
    coef_ref,
    flag_ref,
    spec_ref,
    near_ref,
    edge_ref,
    spot_ref,
    depth_ref,
    wet_ref,
    frac_ref,
    stat_ref,
    cos_ref,
    sin_ref,
    cosb_ref,
    sinb_ref,
    target_ref,
    out_ref,
    pieces_ref,
    dens,
    flat,
    halo,
    evol,
    near,
    hot,
    count,
    tab_x,
    tab_y,
    tab_z,
    tab_an,
    tab_nb,
    tab_n,
):
    first = flag_ref[0] == 1
    child = flag_ref[1]
    adjacent = 3 * flag_ref[0]
    sign = jnp.where(first, 1.0, -1.0)
    lane = lax.broadcasted_iota(jnp.int32, (16, COLS), 1)
    ends = jnp.where((lane == 0) | (lane == COLS - 1), child, 0) > 0

    many = CHUNK
    lane_many = lax.broadcasted_iota(jnp.int32, (many, COLS), 1)
    ends_many = jnp.where((lane_many == 0) | (lane_many == COLS - 1), child, 0) > 0

    def lay_edges(c, carry):
        base = pl.multiple_of(c * many, 16)
        laid = jnp.dot(
            edge_ref[pl.ds(base, many), :], spot_ref[...], preferred_element_type=jnp.float32
        )
        for r in range(ROWS):
            flat[pl.ds(base * ROWS + r, many, stride=ROWS), :] = laid[:, r * COLS : (r + 1) * COLS]
        for n in range(2):
            raw = near_ref[n, pl.ds(base, many), :].astype(jnp.float32)
            at = (ROWS + n) * COLS
            raw = jnp.where(ends_many, laid[:, at : at + COLS], raw)
            near[n, pl.ds(base, many), :] = raw * stat_ref[4 + n : 5 + n, :]
        return carry

    lax.fori_loop(0, BINS // many, lay_edges, 0)

    wet = jnp.concatenate([wet_ref[...]] * 2, axis=0).astype(jnp.float32)
    wet16 = jnp.concatenate([wet, wet], axis=0)

    def begin(i, carry):
        for u in range(4):
            at = pl.multiple_of(i * 64 + u * 16, 16)
            raw = spec_ref[pl.ds(at, 16), :].astype(jnp.float32)
            dens[pl.ds(PAD + at, 16), :] = jnp.where(ends, flat[pl.ds(at, 16), :], raw) * wet16
            halo[pl.ds(at, 16), :] = jnp.zeros((16, COLS), jnp.float32)
        return carry

    lax.fori_loop(0, FLAT // 64, begin, 0)

    sub = lax.broadcasted_iota(jnp.int32, (8, COLS), 0)
    low = sub < ROWS
    depth = jnp.concatenate([depth_ref[...]] * 2, axis=0)
    weight = wet * fraction(jnp.concatenate([frac_ref[...]] * 2, axis=0))

    def between(d0, d1, w0, w1):
        return 0.5 * (d0 + d1) * w0 * w1

    def along(d, w):
        face = between(d, pltpu.roll(d, COLS - 1, 1), w, pltpu.roll(w, COLS - 1, 1))
        return jnp.where(lane[:8] == COLS - 1, 0.0, face)

    def wide(row):
        return jnp.broadcast_to(row, (8, COLS))

    face_x = between(depth, pltpu.roll(depth, 7, 0), weight, pltpu.roll(weight, 7, 0))
    face_x = jnp.where(sub % ROWS == ROWS - 1, 0.0, face_x)
    face_y = along(depth, weight)
    d_own = wide(jnp.where(first, depth[3:4], depth[0:1]))
    w_own = wide(jnp.where(first, weight[3:4], weight[0:1]))
    d_n1, d_n2, w_n1, w_n2 = (wide(stat_ref[i : i + 1, :]) for i in range(4))
    face_an = between(d_own, d_n1, w_own, w_n1)
    face_nb = between(d_n1, d_n2, w_n1, w_n2)
    face_n = along(d_n1, w_n1)

    for q in range(ND // 2):
        tab_x[8 * q : 8 * q + 8, :] = face_x * bin_block(cos_ref, q)
        tab_y[8 * q : 8 * q + 8, :] = face_y * bin_block(sin_ref, q)
        if 2 * q > ND // 2:
            back = 8 * (q - ND // 4)
            tab_z[back : back + 8, :] = pltpu.roll(face_y, 1, 1) * bin_block(sin_ref, q)
    for j in range(BLOCK // 8):
        tab_an[8 * j : 8 * j + 8, :] = face_an * bin_block(cosb_ref, j)
        tab_nb[8 * j : 8 * j + 8, :] = face_nb * bin_block(cosb_ref, j)
        tab_n[8 * j : 8 * j + 8, :] = face_n * bin_block(sinb_ref, j)

    def block(k, carry):
        bins = pl.multiple_of(k * BLOCK, 8)
        rows = pl.multiple_of(k * (BLOCK * ROWS), 16)
        g0, g1 = speed_ref[2 * k], speed_ref[2 * k + 1]

        def halo_fluxes():
            many = range(BLOCK // 8)
            n1s = [near[0, pl.ds(bins + 8 * j, 8), :] for j in many]
            owns = [dens[pl.ds(PAD + rows + 32 * j + adjacent, 8, stride=ROWS), :] for j in many]
            fluxes = []
            for j in many:
                along = bin_block(tab_an, j)
                top = jnp.where(first, owns[j], n1s[j])
                bottom = jnp.where(first, n1s[j], owns[j])
                flux = jnp.maximum(along, 0.0) * top + jnp.minimum(along, 0.0) * bottom
                fluxes.append(flux)
            for j in many:
                halo[pl.ds(rows + 32 * j + adjacent, 8, stride=ROWS), :] = sign * fluxes[j]
            return n1s, fluxes

        def advance(p, rho, across):
            g = g0 if p < 18 else g1
            q = p % 18
            along_x = bin_block(tab_x, q)
            if 2 * q + 1 < ND // 4 or 2 * q > 3 * ND // 4:
                fx = along_x * rho
            else:
                after = pltpu.roll(rho, 7, 0)
                if ND // 4 < 2 * q and 2 * q + 1 < 3 * ND // 4:
                    fx = along_x * after
                else:
                    fx = jnp.maximum(along_x, 0.0) * rho + jnp.minimum(along_x, 0.0) * after
            along_y = bin_block(tab_y, q)
            if 2 * q + 1 < ND // 2:
                fy = along_y * rho
                out_y = fy - pltpu.roll(fy, 1, 1)
            elif 2 * q > ND // 2:
                out_y = along_y * pltpu.roll(rho, COLS - 1, 1) - bin_block(tab_z, q - ND // 4) * rho
            else:
                right = pltpu.roll(rho, COLS - 1, 1)
                fy = jnp.maximum(along_y, 0.0) * rho + jnp.minimum(along_y, 0.0) * right
                out_y = fy - pltpu.roll(fy, 1, 1)
            change = (fx - pltpu.roll(fx, 1, 0)) + out_y
            return rho - g * (change + across)

        def advance_all():
            for start in range(0, ND // 2, GROUP):
                group = [p + h for p in range(start, start + GROUP) for h in (0, ND // 2)]
                loaded = [
                    (dens[pl.ds(PAD + rows + 8 * p, 8), :], halo[pl.ds(rows + 8 * p, 8), :])
                    for p in group
                ]
                moved = [advance(p, *pair) for p, pair in zip(group, loaded)]
                for p, value in zip(group, moved):
                    dens[pl.ds(PAD + rows + 8 * p, 8), :] = value

        n1s, fluxes = halo_fluxes()
        n2s = [near[1, pl.ds(bins + 8 * j, 8), :] for j in range(BLOCK // 8)]
        after_near = []
        for j in range(BLOCK // 8):
            n1, n2 = n1s[j], n2s[j]
            top, bottom = jnp.where(first, n1, n2), jnp.where(first, n2, n1)
            along = bin_block(tab_nb, j)
            beyond = jnp.maximum(along, 0.0) * top + jnp.minimum(along, 0.0) * bottom
            along = bin_block(tab_n, j)
            right = pltpu.roll(n1, COLS - 1, 1)
            fy = jnp.maximum(along, 0.0) * n1 + jnp.minimum(along, 0.0) * right
            change = sign * (beyond - fluxes[j]) + (fy - pltpu.roll(fy, 1, 1))
            speed = g0 if j < 4 else (jnp.where(low, g0, g1) if j == 4 else g1)
            after_near.append(n1 - speed * change)
        for j in range(BLOCK // 8):
            near[0, pl.ds(bins + 8 * j, 8), :] = after_near[j]
        advance_all()
        halo_fluxes()
        advance_all()
        return carry

    lax.fori_loop(0, BINS // BLOCK, block, 0)

    def interact(f, carry):
        rows = pl.multiple_of(f * (ND * ROWS), 16)
        scale = 0.2 * coef_ref[f]

        def partner(ref, b):
            lower = dens[pl.ds(ref[f * ND + b], 8), :]
            upper = dens[pl.ds(ref[f * ND + b + 1] - ROWS, 8), :]
            return jnp.where(low, lower, upper)

        for g in range(ND // 4):
            done = []
            for h in range(2):
                b = 4 * g + 2 * h
                mine = dens[pl.ds(PAD + rows + 4 * b, 8), :]
                plus, minus = partner(plus_ref, b), partner(minus_ref, b)
                source = mine * (mine * (plus + minus) - 2.0 * (plus * minus))
                value = jnp.maximum(mine + scale * source, 0.0)
                evol[pl.ds(rows + 4 * b, 8), :] = value
                done.append(value)
            out_ref[pl.ds(rows + 16 * g, 16), :] = jnp.concatenate(done, axis=0).astype(jnp.bfloat16)
        return carry

    lax.fori_loop(0, NF, interact, 0)

    row = lax.broadcasted_iota(jnp.int32, (CELLS, COLS), 0)
    for r in range(ROWS):
        own = lane[:1] + r * COLS
        same = row == jnp.where(child == 1, target_ref[r : r + 1, :], own)
        hot[:, r * COLS : (r + 1) * COLS] = jnp.where(same, 1.0, 0.0).astype(jnp.bfloat16)
    inner = (((1,), (1,)), ((), ()))
    number = lax.dot_general(
        jnp.ones((16, CELLS), jnp.bfloat16), hot[...], inner, preferred_element_type=jnp.float32
    )
    share = 1.0 / jnp.maximum(number[0:1], 1.0)
    count[...] = jnp.zeros_like(count)
    for turn in range(ROWS):
        for r in range(ROWS):
            of = (turn + r) % ROWS
            here = number[0:1, of * COLS : (of + 1) * COLS].astype(jnp.int32)
            count[turn, PIECE % 8 + r : PIECE % 8 + r + 1, :] = here

    def sums(c, carry):
        base = c * (many * ROWS)
        parts = [evol[pl.ds(base + r, many, stride=ROWS), :] for r in range(ROWS)]
        value = jnp.concatenate(parts, axis=1)
        head = value.astype(jnp.bfloat16)
        tail = (value - head.astype(jnp.float32)).astype(jnp.bfloat16)
        total = lax.dot_general(head, hot[...], inner, preferred_element_type=jnp.float32)
        total += lax.dot_general(tail, hot[...], inner, preferred_element_type=jnp.float32)
        for r in range(ROWS):
            part = slice(r * COLS, (r + 1) * COLS)
            flat[pl.ds(base + r, many, stride=ROWS), :] = total[:, part] * share[:, part]
        return carry

    lax.fori_loop(0, BINS // many, sums, 0)
    main = PIECE // 8 * 8
    row = main + lax.broadcasted_iota(jnp.int32, (8, COLS), 0)

    def cut(i, carry):
        for turn in range(ROWS):
            j = i * ROWS + turn
            mean = flat[pl.ds(j * PIECE, main), :]
            last = jnp.where(row < PIECE, flat[pl.ds(j * PIECE + main, 8), :], 0.0)
            top = jnp.maximum(
                jnp.max(mean, axis=0, keepdims=True), jnp.max(last, axis=0, keepdims=True)
            )
            size = jnp.minimum((top * UNIT).astype(jnp.int32) + 1, OFFSET)
            steps = (UNIT * STEPS) / size.astype(jnp.float32)
            code = (mean * steps + 0.5).astype(jnp.int32) - OFFSET
            code_last = (last * steps + 0.5).astype(jnp.int32) - OFFSET
            rest = jnp.where(row == PIECE + ROWS, size, count[turn])
            code_last = jnp.where(row < PIECE, code_last, rest)
            code = jnp.concatenate([code, code_last], axis=0)
            pieces_ref[j] = code.astype(jnp.int16)
        return carry

    lax.fori_loop(0, PIECES // ROWS, cut, 0)


def evolve(*operands, interpret=False):
    smem = pl.BlockSpec(memory_space=pltpu.SMEM)
    vmem = pl.BlockSpec(memory_space=pltpu.VMEM)
    return pl.pallas_call(
        step_kernel,
        out_shape=(
            jax.ShapeDtypeStruct((FLAT, COLS), jnp.bfloat16),
            jax.ShapeDtypeStruct((PIECES, TALL, COLS), jnp.int16),
        ),
        in_specs=[smem] * 5 + [vmem] * 13,
        out_specs=(vmem, vmem),
        scratch_shapes=[
            pltpu.VMEM((FLAT + 2 * PAD, COLS), jnp.float32),
            pltpu.VMEM((FLAT + 2 * PAD, COLS), jnp.float32),
            pltpu.VMEM((FLAT, COLS), jnp.float32),
            pltpu.VMEM((FLAT, COLS), jnp.float32),
            pltpu.VMEM((2, BINS, COLS), jnp.float32),
            pltpu.VMEM((CELLS, CELLS), jnp.bfloat16),
            pltpu.VMEM((ROWS, 8, COLS), jnp.int32),
            pltpu.VMEM((ND * ROWS, COLS), jnp.float32),
            pltpu.VMEM((ND * ROWS, COLS), jnp.float32),
            pltpu.VMEM((ND * ROWS // 2, COLS), jnp.float32),
            pltpu.VMEM((BLOCK, COLS), jnp.float32),
            pltpu.VMEM((BLOCK, COLS), jnp.float32),
            pltpu.VMEM((BLOCK, COLS), jnp.float32),
        ],
        compiler_params=pltpu.CompilerParams(vmem_limit_bytes=VMEM_BYTES),
        cost_estimate=pl.CostEstimate(
            flops=1_400_000_000, bytes_accessed=10_000_000, transcendentals=0
        ),
        interpret=interpret,
    )(*operands)


def average_kernel(pieces_ref, out_ref):
    blocks = TALL // 8
    sub = lax.broadcasted_iota(jnp.int32, (8, COLS), 0)

    def add(i, carry):
        sums, weights, number = carry
        piece = pieces_ref[i].astype(jnp.int32).astype(jnp.float32)
        rest = piece[TALL - 8 :]
        at = PIECE % 8
        count = jnp.where(sub < ROWS, pltpu.roll(rest, 8 - at, 0), pltpu.roll(rest, ROWS - at, 0))
        weight = count * jnp.broadcast_to(rest[at + ROWS : at + ROWS + 1], (8, COLS))
        sums = tuple(sums[u] + piece[8 * u : 8 * u + 8] * weight for u in range(blocks))
        return sums, weights + weight, number + count

    zero = jnp.zeros((8, COLS), jnp.float32)
    carry = ((zero,) * blocks, zero, zero)
    sums, weights, number = lax.fori_loop(0, PIECES, add, carry)
    scale = 1.0 / (UNIT * STEPS * number)
    mean = jnp.concatenate([(part + OFFSET * weights) * scale for part in sums], axis=0)
    mean = mean.astype(jnp.bfloat16)

    def write(i, carry):
        out_ref[i] = mean
        return carry

    lax.fori_loop(0, STACK, write, 0)


def average(pieces, interpret=False):
    vmem = pl.BlockSpec(memory_space=pltpu.VMEM)
    return pl.pallas_call(
        average_kernel,
        out_shape=jax.ShapeDtypeStruct((STACK, TALL, COLS), jnp.bfloat16),
        in_specs=[vmem],
        out_specs=vmem,
        compiler_params=pltpu.CompilerParams(vmem_limit_bytes=SMALL_BYTES),
        interpret=interpret,
    )(pieces)


def lay_kernel(flag_ref, a_ref, b_ref, c_ref, d_ref, _, out_ref, wide, narrow, sem):
    main = PIECE // 8 * 8
    half = SIDE // 2

    @pl.when(flag_ref[1] == 0)
    def _():
        for k, ref in enumerate((a_ref, b_ref, c_ref, d_ref)):

            def put(i, carry):
                z, y, x = i // SIDE, k // 2 * half + i // half % half, k % 2 * half + i % half
                at = ((z * SIDE + y) * SIDE + x) * PIECE
                piece = ref[i].astype(jnp.float32)
                wide[pl.ds(at, main), :] = piece[:main]
                wide[pl.ds(at + main, 1), :] = piece[main : main + 1]
                return carry

            lax.fori_loop(0, STACK, put, 0)

        def narrower(i, carry):
            for u in range(4):
                at = pl.multiple_of(i * 64 + u * 16, 16)
                narrow[pl.ds(at, 16), :] = wide[pl.ds(at, 16), :].astype(jnp.bfloat16)
            return carry

        lax.fori_loop(0, FLAT // 64, narrower, 0)
        copy = pltpu.make_async_copy(narrow, out_ref, sem)
        copy.start()
        copy.wait()


def lay(flags, blocks, evolved):
    vmem = pl.BlockSpec(memory_space=pltpu.VMEM)
    anywhere = pl.BlockSpec(memory_space=pl.ANY)
    return pl.pallas_call(
        lay_kernel,
        out_shape=jax.ShapeDtypeStruct((FLAT, COLS), jnp.bfloat16),
        in_specs=[pl.BlockSpec(memory_space=pltpu.SMEM)] + [vmem] * SIDE + [anywhere],
        out_specs=anywhere,
        scratch_shapes=[
            pltpu.VMEM((FLAT + 2 * PAD, COLS), jnp.float32),
            pltpu.VMEM((FLAT, COLS), jnp.bfloat16),
            pltpu.SemaphoreType.DMA,
        ],
        input_output_aliases={SIDE + 1: 0},
        compiler_params=pltpu.CompilerParams(vmem_limit_bytes=SMALL_BYTES),
    )(flags, *blocks, evolved)


def tables():
    group_speed = 0.45 * np.exp(-math.log(1.1) * np.arange(NF))
    angles = 2.0 * math.pi / ND * np.arange(ND)

    def wide(values, times):
        return np.repeat(np.repeat(values, times)[:, None], COLS, axis=1).astype(np.float32)

    cosine, sine = np.cos(angles), np.sin(angles)
    twice = BLOCK // ND
    per_row = (wide(cosine, ROWS), wide(sine, ROWS))
    per_bin = (wide(np.tile(cosine, twice), 1), wide(np.tile(sine, twice), 1))
    return (group_speed.astype(np.float32),) + per_row + per_bin


def spots():
    source = np.arange(COLS)[:, None]
    lane = np.arange((ROWS + 2) * COLS)[None, :]
    block, column = lane // COLS, lane % COLS
    chosen = ((column == 0) & (source == 2 * block)) | (
        (column == COLS - 1) & (source == 2 * block + 1)
    )
    return chosen.astype(jnp.bfloat16)


def facing(x):
    first = lax.axis_index("cell") == 0
    return jnp.stack([jnp.where(first, x[3], x[0]), jnp.where(first, x[2], x[1])], axis=0)


def swap(x):
    return lax.ppermute(x, "cell", [(0, 1), (1, 0)])


def on_device(
    spectrum,
    depth_factor,
    wet_mask,
    frac_index,
    boundary_map,
    average_map,
    dia_plus,
    dia_minus,
    dia_coef,
):
    parent = lax.axis_size("grid") - 1
    is_parent = lax.axis_index("grid") == parent
    hubs = hub_places()
    edges = 2 * ROWS
    spec = spectrum.reshape(FLAT, COLS)
    first = (lax.axis_index("cell") == 0).astype(jnp.int32)
    flags = jnp.stack([first, jnp.where(is_parent, 0, 1)]).astype(jnp.int32)
    maps, *parts = send_first(boundary_map.T, spec)

    held = [lax.ppermute(part, "grid", [(parent, hub)]) for part, hub in zip(parts[1:], hubs[1:])]
    maps = lax.all_to_all(maps, "grid", 0, 0)
    near, near_statics = prepare(flags, spec, depth_factor, wet_mask, frac_index)
    near = swap(near)
    near_statics = swap(near_statics)
    maps, near = lax.optimization_barrier((maps, near))
    picked = lax.all_to_all(pick(flags, maps, parts[0], *held), "grid", 0, 0)
    picked = jnp.concatenate([picked[hub] for hub in hubs], axis=1)
    far = swap(facing(picked.reshape(ROWS, 2, BINS))).reshape(4, BINS)
    edge = jnp.concatenate(
        [picked, far, jnp.zeros((COLS - edges - 4, BINS), jnp.bfloat16)], axis=0
    ).T

    group_speed, cosine, sine, cosine_bin, sine_bin = tables()
    evolved, pieces = evolve(
        dia_plus * ROWS + PAD,
        dia_minus * ROWS + PAD,
        group_speed,
        dia_coef,
        flags,
        spec,
        near,
        edge,
        spots(),
        depth_factor,
        wet_mask,
        frac_index,
        near_statics,
        cosine,
        sine,
        cosine_bin,
        sine_bin,
        average_map,
    )
    copies = average(lax.all_to_all(pieces, "grid", 0, 0))
    blocks, senders = blocks_of_16()
    gathered = lax.all_to_all(copies, "grid", 0, 0, axis_index_groups=blocks)
    parts = [
        gathered if sender is None else lax.ppermute(gathered, "grid", [(sender, parent)])
        for sender in senders
    ]
    return lay(flags, parts, evolved).reshape(BINS, ROWS, COLS)


def solution(mesh):
    placed = (
        P(None, ("grid", "cell"), None),
        P(("grid", "cell"), None),
        P(("grid", "cell"), None),
        P(("grid", "cell"), None),
        P(("grid", "cell"), None),
        P(("grid", "cell"), None),
        P(),
        P(),
        P(),
    )
    return jax.shard_map(
        on_device,
        mesh=mesh,
        in_specs=placed,
        out_specs=P(None, ("grid", "cell"), None),
        check_vma=False,
    )
```

```python
import functools
import math

import jax
import jax.numpy as jnp
import numpy as np
from jax import lax
from jax.experimental import pallas as pl
from jax.experimental.pallas import tpu as pltpu
from jax.sharding import PartitionSpec as P

NF = 36
ND = 36
SIDE = 4
ROWS = 4
COLS = 128
CELLS = ROWS * COLS
BINS = NF * ND
FLAT = BINS * ROWS
PAD = 8
PIECES = SIDE**3
PIECE = FLAT // PIECES
TALL = 88
BLOCK = 72
GROUP = 3
CHUNK = 432
UNIT = 512.0
STEPS = 65534.0
OFFSET = 32767
VMEM_BYTES = 24 * 1024 * 1024
SMALL_BYTES = 10 * 1024 * 1024
LARGE_BYTES = 56 * 1024 * 1024
STACK = 16

FRACTIONS = (0.25, 0.5, 0.75, 1.0)


def fraction(frac_index):
    open_share = jnp.zeros(frac_index.shape, jnp.float32)
    for position, share in enumerate(FRACTIONS):
        open_share = open_share + jnp.where(frac_index == position, share, 0.0)
    return open_share


def place(z, y, x):
    return (z % SIDE * SIDE + y % SIDE) * SIDE + x % SIDE


def hub_places():
    last = SIDE - 1
    return [
        place(last, last, last),
        place(last, last, last - 1),
        place(last, last - 1, last),
        place(last - 1, last, last),
    ]


def spot_of(group, position):
    upper, inner = position // 8, position % 8
    z = 2 * upper + inner // 4
    y = 2 * ((group // 2 + upper) % 2) + inner // 2 % 2
    x = 2 * ((group % 2 + upper) % 2) + inner % 2
    return (z * SIDE + y) * SIDE + x


def groups_of_16():
    last = SIDE - 1
    groups = [[spot_of(k, i) for i in range(STACK)] for k in range(SIDE)]
    return groups, [None, place(last, last, 0), place(last, 0, last), place(0, last, last)]


def own_flags():
    return 1 - lax.axis_index("cell"), jnp.where(lax.axis_index("grid") == PIECES - 1, 0, 1)


def bin_block(ref, index):
    return ref[8 * index : 8 * index + 8, :]


def send_kernel(map_ref, spec_ref, maps_ref, *part_refs):
    lane = lax.broadcasted_iota(jnp.int32, (PIECES, COLS), 1)
    maps = jnp.zeros((PIECES, COLS), jnp.int32)
    for r in range(ROWS):
        for side in range(2):
            maps = jnp.where(lane == 2 * r + side, map_ref[side, r], maps)
    maps_ref[...] = maps
    part = FLAT // SIDE
    for k, ref in enumerate(part_refs):
        ref[...] = spec_ref[k * part : (k + 1) * part, :]


def send_first(maps, spec):
    vmem = pl.BlockSpec(memory_space=pltpu.VMEM)
    part = jax.ShapeDtypeStruct((FLAT // SIDE, COLS), jnp.bfloat16)
    return pl.pallas_call(
        send_kernel,
        out_shape=(jax.ShapeDtypeStruct((PIECES, COLS), jnp.int32),) + (part,) * SIDE,
        in_specs=[pl.BlockSpec(memory_space=pltpu.SMEM), vmem],
        out_specs=(vmem,) * (SIDE + 1),
        compiler_params=pltpu.CompilerParams(vmem_limit_bytes=LARGE_BYTES),
    )(maps, spec)


def pick_kernel(maps_ref, spec_ref, a_ref, b_ref, c_ref, out_ref, wide, turned, hot):
    part = FLAT // SIDE
    bins = part // ROWS
    share = jnp.where(own_flags()[1] == 0, 1.0, 0.0)

    def join(i, carry):
        for u in range(3):
            at = pl.multiple_of(i * 48 + u * 16, 16)
            here = pl.ds(at, 16)
            value = spec_ref[here, :].astype(jnp.float32) * share
            for ref in (a_ref, b_ref, c_ref):
                value = value + ref[here, :].astype(jnp.float32)
            wide[here, :] = value
        return carry

    lax.fori_loop(0, part // 48, join, 0)
    wide[part:, :] = jnp.zeros((wide.shape[0] - part, COLS), jnp.float32)
    many = wide.shape[0] // ROWS
    held = [wide[pl.ds(r, many, stride=ROWS), :].astype(jnp.bfloat16) for r in range(ROWS)]
    held = jnp.concatenate(held, axis=1)
    cell = lax.broadcasted_iota(jnp.int32, (PIECES, CELLS), 1)
    for e in range(2 * ROWS):
        wanted = jnp.broadcast_to(maps_ref[:, e : e + 1], (PIECES, CELLS))
        same = jnp.where(cell == wanted, 1.0, 0.0).astype(jnp.bfloat16)
        hot[e * PIECES : (e + 1) * PIECES, :] = same
    found = lax.dot_general(
        hot[...], held, (((1,), (1,)), ((), ())), preferred_element_type=jnp.float32
    )
    for e in range(2 * ROWS):
        for t in range(many // COLS):
            part = found[e * PIECES : (e + 1) * PIECES, t * COLS : (t + 1) * COLS]
            turned[t, pl.ds(e, PIECES, stride=2 * ROWS), :] = part

    def narrower(g, carry):
        at = pl.multiple_of(g * 2 * ROWS, 8)
        for t in range(many // COLS):
            lanes = min(COLS, bins - t * COLS)
            value = turned[t, pl.ds(at, 2 * ROWS), :lanes].astype(jnp.bfloat16)
            out_ref[g, :, t * COLS : t * COLS + lanes] = value
        return carry

    lax.fori_loop(0, PIECES, narrower, 0)


def pick(*operands):
    vmem = pl.BlockSpec(memory_space=pltpu.VMEM)
    part = FLAT // SIDE
    return pl.pallas_call(
        pick_kernel,
        out_shape=jax.ShapeDtypeStruct((PIECES, 2 * ROWS, part // ROWS), jnp.bfloat16),
        in_specs=[vmem] * 5,
        out_specs=vmem,
        scratch_shapes=[
            pltpu.VMEM((3 * COLS * ROWS, COLS), jnp.float32),
            pltpu.VMEM((3, PIECES * 2 * ROWS, COLS), jnp.float32),
            pltpu.VMEM((PIECES * 2 * ROWS, CELLS), jnp.bfloat16),
        ],
        compiler_params=pltpu.CompilerParams(vmem_limit_bytes=SMALL_BYTES),
    )(*operands)


def prepare_kernel(spec_ref, depth_ref, wet_ref, frac_ref, near_ref, stat_ref, dens):
    first = own_flags()[0] == 1
    wet = wet_ref[...].astype(jnp.float32)
    values = (depth_ref[...], wet * fraction(frac_ref[...]), wet)
    for i, value in enumerate(values):
        stat_ref[2 * i : 2 * i + 1, :] = jnp.where(first, value[3:4], value[0:1])
        stat_ref[2 * i + 1 : 2 * i + 2, :] = jnp.where(first, value[2:3], value[1:2])
    stat_ref[6:8, :] = jnp.zeros((2, COLS), jnp.float32)

    def widen(i, carry):
        for u in range(4):
            at = pl.multiple_of(i * 64 + u * 16, 16)
            dens[pl.ds(at, 16), :] = spec_ref[pl.ds(at, 16), :].astype(jnp.float32)
        return carry

    lax.fori_loop(0, FLAT // 64, widen, 0)
    nearer = 3 * own_flags()[0]
    farther = 1 + own_flags()[0]

    def pull(i, carry):
        for u in range(3):
            at = pl.multiple_of(i * 48 + u * 16, 16)
            for n, row in enumerate((nearer, farther)):
                rows = dens[pl.ds(at * ROWS + row, 16, stride=ROWS), :]
                near_ref[n, pl.ds(at, 16), :] = rows.astype(jnp.bfloat16)
        return carry

    lax.fori_loop(0, BINS // 48, pull, 0)


def prepare(*operands, interpret=False):
    vmem = pl.BlockSpec(memory_space=pltpu.VMEM)
    return pl.pallas_call(
        prepare_kernel,
        out_shape=(
            jax.ShapeDtypeStruct((2, BINS, COLS), jnp.bfloat16),
            jax.ShapeDtypeStruct((8, COLS), jnp.float32),
        ),
        in_specs=[vmem] * 4,
        out_specs=(vmem,) * 2,
        scratch_shapes=[pltpu.VMEM((FLAT, COLS), jnp.float32)],
        compiler_params=pltpu.CompilerParams(vmem_limit_bytes=SMALL_BYTES),
        cost_estimate=pl.CostEstimate(flops=4_000_000, bytes_accessed=5_000_000, transcendentals=0),
        interpret=interpret,
    )(*operands)


def step_kernel(
    plus_ref,
    minus_ref,
    speed_ref,
    coef_ref,
    spec_ref,
    near_ref,
    edge_ref,
    spot_ref,
    depth_ref,
    wet_ref,
    frac_ref,
    stat_ref,
    cos_ref,
    sin_ref,
    cosb_ref,
    sinb_ref,
    target_ref,
    out_ref,
    pieces_ref,
    dens,
    flat,
    halo,
    evol,
    near,
    hot,
    count,
    tab_x,
    tab_y,
    tab_z,
    tab_an,
    tab_nb,
    tab_n,
):
    first = own_flags()[0] == 1
    child = own_flags()[1]
    adjacent = 3 * own_flags()[0]
    sign = jnp.where(first, 1.0, -1.0)
    lane = lax.broadcasted_iota(jnp.int32, (16, COLS), 1)
    ends = jnp.where((lane == 0) | (lane == COLS - 1), child, 0) > 0

    many = CHUNK
    lane_many = lax.broadcasted_iota(jnp.int32, (many, COLS), 1)
    ends_many = jnp.where((lane_many == 0) | (lane_many == COLS - 1), child, 0) > 0

    def lay_edges(c, carry):
        base = pl.multiple_of(c * many, 16)
        laid = jnp.dot(
            edge_ref[pl.ds(base, many), :], spot_ref[...], preferred_element_type=jnp.float32
        )
        for r in range(ROWS):
            flat[pl.ds(base * ROWS + r, many, stride=ROWS), :] = laid[:, r * COLS : (r + 1) * COLS]
        for n in range(2):
            raw = near_ref[n, pl.ds(base, many), :].astype(jnp.float32)
            at = (ROWS + n) * COLS
            raw = jnp.where(ends_many, laid[:, at : at + COLS], raw)
            near[n, pl.ds(base, many), :] = raw * stat_ref[4 + n : 5 + n, :]
        return carry

    lax.fori_loop(0, BINS // many, lay_edges, 0)

    wet = jnp.concatenate([wet_ref[...]] * 2, axis=0).astype(jnp.float32)
    wet16 = jnp.concatenate([wet, wet], axis=0)

    def begin(i, carry):
        for u in range(4):
            at = pl.multiple_of(i * 64 + u * 16, 16)
            raw = spec_ref[pl.ds(at, 16), :].astype(jnp.float32)
            dens[pl.ds(PAD + at, 16), :] = jnp.where(ends, flat[pl.ds(at, 16), :], raw) * wet16
            halo[pl.ds(at, 16), :] = jnp.zeros((16, COLS), jnp.float32)
        return carry

    lax.fori_loop(0, FLAT // 64, begin, 0)

    sub = lax.broadcasted_iota(jnp.int32, (8, COLS), 0)
    low = sub < ROWS
    depth = jnp.concatenate([depth_ref[...]] * 2, axis=0)
    weight = wet * fraction(jnp.concatenate([frac_ref[...]] * 2, axis=0))

    def between(d0, d1, w0, w1):
        return 0.5 * (d0 + d1) * w0 * w1

    def along(d, w):
        face = between(d, pltpu.roll(d, COLS - 1, 1), w, pltpu.roll(w, COLS - 1, 1))
        return jnp.where(lane[:8] == COLS - 1, 0.0, face)

    def wide(row):
        return jnp.broadcast_to(row, (8, COLS))

    face_x = between(depth, pltpu.roll(depth, 7, 0), weight, pltpu.roll(weight, 7, 0))
    face_x = jnp.where(sub % ROWS == ROWS - 1, 0.0, face_x)
    face_y = along(depth, weight)
    d_own = wide(jnp.where(first, depth[3:4], depth[0:1]))
    w_own = wide(jnp.where(first, weight[3:4], weight[0:1]))
    d_n1, d_n2, w_n1, w_n2 = (wide(stat_ref[i : i + 1, :]) for i in range(4))
    face_an = between(d_own, d_n1, w_own, w_n1)
    face_nb = between(d_n1, d_n2, w_n1, w_n2)
    face_n = along(d_n1, w_n1)

    for q in range(ND // 2):
        tab_x[8 * q : 8 * q + 8, :] = face_x * bin_block(cos_ref, q)
        tab_y[8 * q : 8 * q + 8, :] = face_y * bin_block(sin_ref, q)
        if 2 * q > ND // 2:
            back = 8 * (q - ND // 4)
            tab_z[back : back + 8, :] = pltpu.roll(face_y, 1, 1) * bin_block(sin_ref, q)
    for j in range(BLOCK // 8):
        tab_an[8 * j : 8 * j + 8, :] = face_an * bin_block(cosb_ref, j)
        tab_nb[8 * j : 8 * j + 8, :] = face_nb * bin_block(cosb_ref, j)
        tab_n[8 * j : 8 * j + 8, :] = face_n * bin_block(sinb_ref, j)

    def block(k, carry):
        bins = pl.multiple_of(k * BLOCK, 8)
        rows = pl.multiple_of(k * (BLOCK * ROWS), 16)
        g0, g1 = speed_ref[2 * k], speed_ref[2 * k + 1]

        def halo_fluxes():
            many = range(BLOCK // 8)
            n1s = [near[0, pl.ds(bins + 8 * j, 8), :] for j in many]
            owns = [dens[pl.ds(PAD + rows + 32 * j + adjacent, 8, stride=ROWS), :] for j in many]
            fluxes = []
            for j in many:
                along = bin_block(tab_an, j)
                top = jnp.where(first, owns[j], n1s[j])
                bottom = jnp.where(first, n1s[j], owns[j])
                flux = jnp.maximum(along, 0.0) * top + jnp.minimum(along, 0.0) * bottom
                fluxes.append(flux)
            for j in many:
                halo[pl.ds(rows + 32 * j + adjacent, 8, stride=ROWS), :] = sign * fluxes[j]
            return n1s, fluxes

        def advance(p, rho, across):
            g = g0 if p < 18 else g1
            q = p % 18
            along_x = bin_block(tab_x, q)
            if 2 * q + 1 < ND // 4 or 2 * q > 3 * ND // 4:
                fx = along_x * rho
            else:
                after = pltpu.roll(rho, 7, 0)
                if ND // 4 < 2 * q and 2 * q + 1 < 3 * ND // 4:
                    fx = along_x * after
                else:
                    fx = jnp.maximum(along_x, 0.0) * rho + jnp.minimum(along_x, 0.0) * after
            along_y = bin_block(tab_y, q)
            if 2 * q + 1 < ND // 2:
                fy = along_y * rho
                out_y = fy - pltpu.roll(fy, 1, 1)
            elif 2 * q > ND // 2:
                out_y = along_y * pltpu.roll(rho, COLS - 1, 1) - bin_block(tab_z, q - ND // 4) * rho
            else:
                right = pltpu.roll(rho, COLS - 1, 1)
                fy = jnp.maximum(along_y, 0.0) * rho + jnp.minimum(along_y, 0.0) * right
                out_y = fy - pltpu.roll(fy, 1, 1)
            change = (fx - pltpu.roll(fx, 1, 0)) + out_y
            return rho - g * (change + across)

        def advance_all():
            for start in range(0, ND // 2, GROUP):
                group = [p + h for p in range(start, start + GROUP) for h in (0, ND // 2)]
                loaded = [
                    (dens[pl.ds(PAD + rows + 8 * p, 8), :], halo[pl.ds(rows + 8 * p, 8), :])
                    for p in group
                ]
                moved = [advance(p, *pair) for p, pair in zip(group, loaded)]
                for p, value in zip(group, moved):
                    dens[pl.ds(PAD + rows + 8 * p, 8), :] = value

        n1s, fluxes = halo_fluxes()
        n2s = [near[1, pl.ds(bins + 8 * j, 8), :] for j in range(BLOCK // 8)]
        after_near = []
        for j in range(BLOCK // 8):
            n1, n2 = n1s[j], n2s[j]
            top, bottom = jnp.where(first, n1, n2), jnp.where(first, n2, n1)
            along = bin_block(tab_nb, j)
            beyond = jnp.maximum(along, 0.0) * top + jnp.minimum(along, 0.0) * bottom
            along = bin_block(tab_n, j)
            right = pltpu.roll(n1, COLS - 1, 1)
            fy = jnp.maximum(along, 0.0) * n1 + jnp.minimum(along, 0.0) * right
            change = sign * (beyond - fluxes[j]) + (fy - pltpu.roll(fy, 1, 1))
            speed = g0 if j < 4 else (jnp.where(low, g0, g1) if j == 4 else g1)
            after_near.append(n1 - speed * change)
        for j in range(BLOCK // 8):
            near[0, pl.ds(bins + 8 * j, 8), :] = after_near[j]
        advance_all()
        halo_fluxes()
        advance_all()
        return carry

    lax.fori_loop(0, BINS // BLOCK, block, 0)

    def interact(f, carry):
        rows = pl.multiple_of(f * (ND * ROWS), 16)
        scale = 0.2 * coef_ref[f]

        def partner(ref, b):
            lower = dens[pl.ds(ref[f * ND + b], 8), :]
            upper = dens[pl.ds(ref[f * ND + b + 1] - ROWS, 8), :]
            return jnp.where(low, lower, upper)

        for g in range(ND // 4):
            done = []
            for h in range(2):
                b = 4 * g + 2 * h
                mine = dens[pl.ds(PAD + rows + 4 * b, 8), :]
                plus, minus = partner(plus_ref, b), partner(minus_ref, b)
                source = mine * (mine * (plus + minus) - 2.0 * (plus * minus))
                value = jnp.maximum(mine + scale * source, 0.0)
                evol[pl.ds(rows + 4 * b, 8), :] = value
                done.append(value)
            out_ref[pl.ds(rows + 16 * g, 16), :] = jnp.concatenate(done, axis=0).astype(jnp.bfloat16)
        return carry

    lax.fori_loop(0, NF, interact, 0)

    row = lax.broadcasted_iota(jnp.int32, (CELLS, COLS), 0)
    for r in range(ROWS):
        own = lane[:1] + r * COLS
        same = row == jnp.where(child == 1, target_ref[r : r + 1, :], own)
        hot[:, r * COLS : (r + 1) * COLS] = jnp.where(same, 1.0, 0.0).astype(jnp.bfloat16)
    inner = (((1,), (1,)), ((), ()))
    number = lax.dot_general(
        jnp.ones((16, CELLS), jnp.bfloat16), hot[...], inner, preferred_element_type=jnp.float32
    )
    share = 1.0 / jnp.maximum(number[0:1], 1.0)
    count[...] = jnp.zeros_like(count)
    for turn in range(ROWS):
        for r in range(ROWS):
            of = (turn + r) % ROWS
            here = number[0:1, of * COLS : (of + 1) * COLS].astype(jnp.int32)
            count[turn, PIECE % 8 + r : PIECE % 8 + r + 1, :] = here

    def sums(c, carry):
        base = c * (many * ROWS)
        parts = [evol[pl.ds(base + r, many, stride=ROWS), :] for r in range(ROWS)]
        value = jnp.concatenate(parts, axis=1)
        head = value.astype(jnp.bfloat16)
        tail = (value - head.astype(jnp.float32)).astype(jnp.bfloat16)
        total = lax.dot_general(head, hot[...], inner, preferred_element_type=jnp.float32)
        total += lax.dot_general(tail, hot[...], inner, preferred_element_type=jnp.float32)
        for r in range(ROWS):
            part = slice(r * COLS, (r + 1) * COLS)
            flat[pl.ds(base + r, many, stride=ROWS), :] = total[:, part] * share[:, part]
        return carry

    lax.fori_loop(0, BINS // many, sums, 0)
    main = PIECE // 8 * 8
    row = main + lax.broadcasted_iota(jnp.int32, (8, COLS), 0)

    def cut(i, carry):
        for turn in range(ROWS):
            j = i * ROWS + turn
            mean = flat[pl.ds(j * PIECE, main), :]
            last = jnp.where(row < PIECE, flat[pl.ds(j * PIECE + main, 8), :], 0.0)
            top = jnp.maximum(
                jnp.max(mean, axis=0, keepdims=True), jnp.max(last, axis=0, keepdims=True)
            )
            size = jnp.minimum((top * UNIT).astype(jnp.int32) + 1, OFFSET)
            steps = (UNIT * STEPS) / size.astype(jnp.float32)
            code = (mean * steps + 0.5).astype(jnp.int32) - OFFSET
            code_last = (last * steps + 0.5).astype(jnp.int32) - OFFSET
            rest = jnp.where(row == PIECE + ROWS, size, count[turn])
            code_last = jnp.where(row < PIECE, code_last, rest)
            code = jnp.concatenate([code, code_last], axis=0)
            pieces_ref[j] = code.astype(jnp.int16)
        return carry

    lax.fori_loop(0, PIECES // ROWS, cut, 0)


def evolve(*operands, interpret=False):
    smem = pl.BlockSpec(memory_space=pltpu.SMEM)
    vmem = pl.BlockSpec(memory_space=pltpu.VMEM)
    return pl.pallas_call(
        step_kernel,
        out_shape=(
            jax.ShapeDtypeStruct((FLAT, COLS), jnp.bfloat16),
            jax.ShapeDtypeStruct((PIECES, TALL, COLS), jnp.int16),
        ),
        in_specs=[smem] * 4 + [vmem] * 13,
        out_specs=(vmem, vmem),
        scratch_shapes=[
            pltpu.VMEM((FLAT + 2 * PAD, COLS), jnp.float32),
            pltpu.VMEM((FLAT + 2 * PAD, COLS), jnp.float32),
            pltpu.VMEM((FLAT, COLS), jnp.float32),
            pltpu.VMEM((FLAT, COLS), jnp.float32),
            pltpu.VMEM((2, BINS, COLS), jnp.float32),
            pltpu.VMEM((CELLS, CELLS), jnp.bfloat16),
            pltpu.VMEM((ROWS, 8, COLS), jnp.int32),
            pltpu.VMEM((ND * ROWS, COLS), jnp.float32),
            pltpu.VMEM((ND * ROWS, COLS), jnp.float32),
            pltpu.VMEM((ND * ROWS // 2, COLS), jnp.float32),
            pltpu.VMEM((BLOCK, COLS), jnp.float32),
            pltpu.VMEM((BLOCK, COLS), jnp.float32),
            pltpu.VMEM((BLOCK, COLS), jnp.float32),
        ],
        compiler_params=pltpu.CompilerParams(vmem_limit_bytes=VMEM_BYTES),
        cost_estimate=pl.CostEstimate(
            flops=1_400_000_000, bytes_accessed=10_000_000, transcendentals=0
        ),
        interpret=interpret,
    )(*operands)


def average_kernel(pieces_ref, out_ref):
    blocks = TALL // 8
    sub = lax.broadcasted_iota(jnp.int32, (8, COLS), 0)

    def add(i, carry):
        sums, weights, number = carry
        piece = pieces_ref[i].astype(jnp.int32).astype(jnp.float32)
        rest = piece[TALL - 8 :]
        at = PIECE % 8
        count = jnp.where(sub < ROWS, pltpu.roll(rest, 8 - at, 0), pltpu.roll(rest, ROWS - at, 0))
        weight = count * jnp.broadcast_to(rest[at + ROWS : at + ROWS + 1], (8, COLS))
        sums = tuple(sums[u] + piece[8 * u : 8 * u + 8] * weight for u in range(blocks))
        return sums, weights + weight, number + count

    zero = jnp.zeros((8, COLS), jnp.float32)
    carry = ((zero,) * blocks, zero, zero)
    sums, weights, number = lax.fori_loop(0, PIECES, add, carry)
    scale = 1.0 / (UNIT * STEPS * number)
    mean = jnp.concatenate([(part + OFFSET * weights) * scale for part in sums], axis=0)
    mean = mean.astype(jnp.bfloat16)

    def write(i, carry):
        out_ref[i] = mean
        return carry

    lax.fori_loop(0, STACK, write, 0)


def average(pieces, interpret=False):
    vmem = pl.BlockSpec(memory_space=pltpu.VMEM)
    return pl.pallas_call(
        average_kernel,
        out_shape=jax.ShapeDtypeStruct((STACK, TALL, COLS), jnp.bfloat16),
        in_specs=[vmem],
        out_specs=vmem,
        compiler_params=pltpu.CompilerParams(vmem_limit_bytes=SMALL_BYTES),
        interpret=interpret,
    )(pieces)


def lay_kernel(a_ref, b_ref, c_ref, d_ref, _, out_ref, wide, narrow, sems):
    main = PIECE // 8 * 8

    @pl.when(own_flags()[1] == 0)
    def _():
        for k, ref in enumerate((a_ref, b_ref, c_ref, d_ref)):

            def put(i, carry):
                at = spot_of(k, i) * PIECE
                piece = ref[i].astype(jnp.float32)
                wide[pl.ds(at, main), :] = piece[:main]
                wide[pl.ds(at + main, 1), :] = piece[main : main + 1]
                return carry

            lax.fori_loop(0, STACK, put, 0)

        part = FLAT // SIDE
        copies = []
        for k in range(SIDE):

            def narrower(i, carry):
                for u in range(3):
                    at = pl.multiple_of(k * part + i * 48 + u * 16, 16)
                    narrow[pl.ds(at, 16), :] = wide[pl.ds(at, 16), :].astype(jnp.bfloat16)
                return carry

            lax.fori_loop(0, part // 48, narrower, 0)
            here = pl.ds(k * part, part)
            copies.append(pltpu.make_async_copy(narrow.at[here], out_ref.at[here], sems.at[k]))
            copies[k].start()
        for copy in copies:
            copy.wait()


def lay(blocks, evolved):
    vmem = pl.BlockSpec(memory_space=pltpu.VMEM)
    anywhere = pl.BlockSpec(memory_space=pl.ANY)
    return pl.pallas_call(
        lay_kernel,
        out_shape=jax.ShapeDtypeStruct((FLAT, COLS), jnp.bfloat16),
        in_specs=[vmem] * SIDE + [anywhere],
        out_specs=anywhere,
        scratch_shapes=[
            pltpu.VMEM((FLAT + 2 * PAD, COLS), jnp.float32),
            pltpu.VMEM((FLAT, COLS), jnp.bfloat16),
            pltpu.SemaphoreType.DMA((SIDE,)),
        ],
        input_output_aliases={SIDE: 0},
        compiler_params=pltpu.CompilerParams(vmem_limit_bytes=SMALL_BYTES),
    )(*blocks, evolved)


def tables():
    group_speed = 0.45 * np.exp(-math.log(1.1) * np.arange(NF))
    angles = 2.0 * math.pi / ND * np.arange(ND)

    def wide(values, times):
        return np.repeat(np.repeat(values, times)[:, None], COLS, axis=1).astype(np.float32)

    cosine, sine = np.cos(angles), np.sin(angles)
    twice = BLOCK // ND
    per_row = (wide(cosine, ROWS), wide(sine, ROWS))
    per_bin = (wide(np.tile(cosine, twice), 1), wide(np.tile(sine, twice), 1))
    return (group_speed.astype(np.float32),) + per_row + per_bin


def spots():
    source = np.arange(COLS)[:, None]
    lane = np.arange((ROWS + 2) * COLS)[None, :]
    block, column = lane // COLS, lane % COLS
    chosen = ((column == 0) & (source == 2 * block)) | (
        (column == COLS - 1) & (source == 2 * block + 1)
    )
    return chosen.astype(jnp.bfloat16)


def facing(x):
    first = lax.axis_index("cell") == 0
    return jnp.stack([jnp.where(first, x[3], x[0]), jnp.where(first, x[2], x[1])], axis=0)


def swap(x):
    return lax.ppermute(x, "cell", [(0, 1), (1, 0)])


def on_device(
    spectrum,
    depth_factor,
    wet_mask,
    frac_index,
    boundary_map,
    average_map,
    dia_plus,
    dia_minus,
    dia_coef,
):
    parent = lax.axis_size("grid") - 1
    hubs = hub_places()
    edges = 2 * ROWS
    spec = spectrum.reshape(FLAT, COLS)
    maps, *parts = send_first(boundary_map.T, spec)

    held = [lax.ppermute(part, "grid", [(parent, hub)]) for part, hub in zip(parts[1:], hubs[1:])]
    maps = lax.all_to_all(maps, "grid", 0, 0)
    near, near_statics = prepare(spec, depth_factor, wet_mask, frac_index)
    near = swap(near)
    near_statics = swap(near_statics)
    picked = lax.all_to_all(pick(maps, parts[0], *held), "grid", 0, 0)
    picked = jnp.concatenate([picked[hub] for hub in hubs], axis=1)
    far = swap(facing(picked.reshape(ROWS, 2, BINS))).reshape(4, BINS)
    edge = jnp.concatenate(
        [picked, far, jnp.zeros((COLS - edges - 4, BINS), jnp.bfloat16)], axis=0
    ).T

    group_speed, cosine, sine, cosine_bin, sine_bin = tables()
    evolved, pieces = evolve(
        dia_plus * ROWS + PAD,
        dia_minus * ROWS + PAD,
        group_speed,
        dia_coef,
        spec,
        near,
        edge,
        spots(),
        depth_factor,
        wet_mask,
        frac_index,
        near_statics,
        cosine,
        sine,
        cosine_bin,
        sine_bin,
        average_map,
    )
    copies = average(lax.all_to_all(pieces, "grid", 0, 0))
    members, senders = groups_of_16()
    gathered = lax.all_to_all(copies, "grid", 0, 0, axis_index_groups=members)
    parts = [
        gathered if sender is None else lax.ppermute(gathered, "grid", [(sender, parent)])
        for sender in senders
    ]
    return lay(parts, evolved).reshape(BINS, ROWS, COLS)


def solution(mesh):
    placed = (
        P(None, ("grid", "cell"), None),
        P(("grid", "cell"), None),
        P(("grid", "cell"), None),
        P(("grid", "cell"), None),
        P(("grid", "cell"), None),
        P(("grid", "cell"), None),
        P(),
        P(),
        P(),
    )
    return jax.shard_map(
        on_device,
        mesh=mesh,
        in_specs=placed,
        out_specs=P(None, ("grid", "cell"), None),
        check_vma=False,
    )
```

```python
import functools
import math

import jax
import jax.numpy as jnp
import numpy as np
from jax import lax
from jax.experimental import pallas as pl
from jax.experimental.pallas import tpu as pltpu
from jax.sharding import PartitionSpec as P

NF = 36
ND = 36
SIDE = 4
ROWS = 4
COLS = 128
CELLS = ROWS * COLS
BINS = NF * ND
FLAT = BINS * ROWS
PAD = 8
PIECES = SIDE**3
PIECE = FLAT // PIECES
TALL = 88
BLOCK = 72
GROUP = 3
CHUNK = 432
WIDTH = 512
UNIT = 512.0
STEPS = 65534.0
OFFSET = 32767
VMEM_BYTES = 24 * 1024 * 1024
SMALL_BYTES = 10 * 1024 * 1024
LARGE_BYTES = 56 * 1024 * 1024
STACK = 8

FRACTIONS = (0.25, 0.5, 0.75, 1.0)


def fraction(frac_index):
    open_share = jnp.zeros(frac_index.shape, jnp.float32)
    for position, share in enumerate(FRACTIONS):
        open_share = open_share + jnp.where(frac_index == position, share, 0.0)
    return open_share


def place(z, y, x):
    return (z % SIDE * SIDE + y % SIDE) * SIDE + x % SIDE


def hub_places():
    last = SIDE - 1
    return [
        place(last, last, last),
        place(last, last, last - 1),
        place(last, last - 1, last),
        place(last - 1, last, last),
    ]


def cube_member(cube, position):
    zyx = [2 * (cube // d % 2) + position // d % 2 for d in (4, 2, 1)]
    return (zyx[0] * SIDE + zyx[1]) * SIDE + zyx[2]


CUBES = 8
DIRECT = (6, 5, 3)
PASSED = (4, 1, 2)
OWN, OPPOSITE = 7, 0


def own_flags():
    return 1 - lax.axis_index("cell"), jnp.where(lax.axis_index("grid") == PIECES - 1, 0, 1)


def bin_block(ref, index):
    return ref[8 * index : 8 * index + 8, :]


def send_kernel(map_ref, spec_ref, maps_ref, *part_refs):
    lane = lax.broadcasted_iota(jnp.int32, (PIECES, COLS), 1)
    maps = jnp.zeros((PIECES, COLS), jnp.int32)
    for r in range(ROWS):
        for side in range(2):
            maps = jnp.where(lane == 2 * r + side, map_ref[side, r], maps)
    maps_ref[...] = maps
    part = FLAT // SIDE
    for k, ref in enumerate(part_refs):
        ref[...] = spec_ref[(k + 1) * part : (k + 2) * part, :]


def send_first(maps, spec):
    vmem = pl.BlockSpec(memory_space=pltpu.VMEM)
    part = jax.ShapeDtypeStruct((FLAT // SIDE, COLS), jnp.bfloat16)
    return pl.pallas_call(
        send_kernel,
        out_shape=(jax.ShapeDtypeStruct((PIECES, COLS), jnp.int32),) + (part,) * (SIDE - 1),
        in_specs=[pl.BlockSpec(memory_space=pltpu.SMEM), vmem],
        out_specs=(vmem,) * SIDE,
        compiler_params=pltpu.CompilerParams(vmem_limit_bytes=LARGE_BYTES),
    )(maps, spec)


def pick_kernel(maps_ref, spec_ref, a_ref, b_ref, c_ref, out_ref, wide, turned, hot, mine, sem):
    part = FLAT // SIDE
    bins = part // ROWS
    share = jnp.where(own_flags()[1] == 0, 1.0, 0.0)
    copy = pltpu.make_async_copy(spec_ref.at[pl.ds(0, part), :], mine, sem)
    copy.start()
    cell = lax.broadcasted_iota(jnp.int32, (PIECES, CELLS), 1)
    for e in range(2 * ROWS):
        wanted = jnp.broadcast_to(maps_ref[:, e : e + 1], (PIECES, CELLS))
        same = jnp.where(cell == wanted, 1.0, 0.0).astype(jnp.bfloat16)
        hot[e * PIECES : (e + 1) * PIECES, :] = same
    copy.wait()

    def join(i, carry):
        for u in range(3):
            at = pl.multiple_of(i * 48 + u * 16, 16)
            here = pl.ds(at, 16)
            value = mine[here, :].astype(jnp.float32) * share
            for ref in (a_ref, b_ref, c_ref):
                value = value + ref[here, :].astype(jnp.float32)
            wide[here, :] = value
        return carry

    lax.fori_loop(0, part // 48, join, 0)
    wide[part:, :] = jnp.zeros((wide.shape[0] - part, COLS), jnp.float32)
    many = wide.shape[0] // ROWS
    held = [wide[pl.ds(r, many, stride=ROWS), :].astype(jnp.bfloat16) for r in range(ROWS)]
    held = jnp.concatenate(held, axis=1)
    found = lax.dot_general(
        hot[...], held, (((1,), (1,)), ((), ())), preferred_element_type=jnp.float32
    )
    for e in range(2 * ROWS):
        for t in range(many // COLS):
            part = found[e * PIECES : (e + 1) * PIECES, t * COLS : (t + 1) * COLS]
            turned[t, pl.ds(e, PIECES, stride=2 * ROWS), :] = part

    def narrower(g, carry):
        at = pl.multiple_of(g * 2 * ROWS, 8)
        for t in range(many // COLS):
            lanes = min(COLS, bins - t * COLS)
            value = turned[t, pl.ds(at, 2 * ROWS), :lanes].astype(jnp.bfloat16)
            out_ref[g, :, t * COLS : t * COLS + lanes] = value
        return carry

    lax.fori_loop(0, PIECES, narrower, 0)


def pick(*operands):
    vmem = pl.BlockSpec(memory_space=pltpu.VMEM)
    part = FLAT // SIDE
    return pl.pallas_call(
        pick_kernel,
        out_shape=jax.ShapeDtypeStruct((PIECES, 2 * ROWS, part // ROWS), jnp.bfloat16),
        in_specs=[vmem, pl.BlockSpec(memory_space=pl.ANY)] + [vmem] * 3,
        out_specs=vmem,
        scratch_shapes=[
            pltpu.VMEM((3 * COLS * ROWS, COLS), jnp.float32),
            pltpu.VMEM((3, PIECES * 2 * ROWS, COLS), jnp.float32),
            pltpu.VMEM((PIECES * 2 * ROWS, CELLS), jnp.bfloat16),
            pltpu.VMEM((part, COLS), jnp.bfloat16),
            pltpu.SemaphoreType.DMA,
        ],
        compiler_params=pltpu.CompilerParams(vmem_limit_bytes=SMALL_BYTES),
    )(*operands)


def prepare_kernel(spec_ref, depth_ref, wet_ref, frac_ref, near_ref, stat_ref, dens):
    first = own_flags()[0] == 1
    wet = wet_ref[...].astype(jnp.float32)
    values = (depth_ref[...], wet * fraction(frac_ref[...]), wet)
    for i, value in enumerate(values):
        stat_ref[2 * i : 2 * i + 1, :] = jnp.where(first, value[3:4], value[0:1])
        stat_ref[2 * i + 1 : 2 * i + 2, :] = jnp.where(first, value[2:3], value[1:2])
    stat_ref[6:8, :] = jnp.zeros((2, COLS), jnp.float32)

    def widen(i, carry):
        for u in range(4):
            at = pl.multiple_of(i * 64 + u * 16, 16)
            dens[pl.ds(at, 16), :] = spec_ref[pl.ds(at, 16), :].astype(jnp.float32)
        return carry

    lax.fori_loop(0, FLAT // 64, widen, 0)
    nearer = 3 * own_flags()[0]
    farther = 1 + own_flags()[0]

    def pull(i, carry):
        for u in range(3):
            at = pl.multiple_of(i * 48 + u * 16, 16)
            for n, row in enumerate((nearer, farther)):
                rows = dens[pl.ds(at * ROWS + row, 16, stride=ROWS), :]
                near_ref[n, pl.ds(at, 16), :] = rows.astype(jnp.bfloat16)
        return carry

    lax.fori_loop(0, BINS // 48, pull, 0)


def prepare(*operands, interpret=False):
    vmem = pl.BlockSpec(memory_space=pltpu.VMEM)
    return pl.pallas_call(
        prepare_kernel,
        out_shape=(
            jax.ShapeDtypeStruct((2, BINS, COLS), jnp.bfloat16),
            jax.ShapeDtypeStruct((8, COLS), jnp.float32),
        ),
        in_specs=[vmem] * 4,
        out_specs=(vmem,) * 2,
        scratch_shapes=[pltpu.VMEM((FLAT, COLS), jnp.float32)],
        compiler_params=pltpu.CompilerParams(vmem_limit_bytes=SMALL_BYTES),
        cost_estimate=pl.CostEstimate(flops=4_000_000, bytes_accessed=5_000_000, transcendentals=0),
        interpret=interpret,
    )(*operands)


def step_kernel(
    plus_ref,
    minus_ref,
    speed_ref,
    coef_ref,
    spec_ref,
    near_ref,
    edge_ref,
    far_ref,
    spot_ref,
    depth_ref,
    wet_ref,
    frac_ref,
    stat_ref,
    cos_ref,
    sin_ref,
    cosb_ref,
    sinb_ref,
    target_ref,
    out_ref,
    pieces_ref,
    dens,
    flat,
    halo,
    evol,
    near,
    hot,
    count,
    tab_x,
    tab_y,
    tab_z,
    tab_an,
    tab_nb,
    tab_n,
):
    first = own_flags()[0] == 1
    child = own_flags()[1]
    adjacent = 3 * own_flags()[0]
    sign = jnp.where(first, 1.0, -1.0)
    lane = lax.broadcasted_iota(jnp.int32, (16, COLS), 1)
    ends = jnp.where((lane == 0) | (lane == COLS - 1), child, 0) > 0

    values = jnp.concatenate([edge_ref[...], far_ref[...]], axis=0)
    spot = spot_ref[1 - own_flags()[0]]
    for base in range(0, BINS, WIDTH):
        wide_rows = min(WIDTH, BINS - base)
        laid = lax.dot_general(
            values[:, base : base + wide_rows],
            spot,
            (((0,), (0,)), ((), ())),
            preferred_element_type=jnp.float32,
        )
        lanes = lax.broadcasted_iota(jnp.int32, (wide_rows, COLS), 1)
        ends_wide = jnp.where((lanes == 0) | (lanes == COLS - 1), child, 0) > 0
        for r in range(ROWS):
            here = pl.ds(base * ROWS + r, wide_rows, stride=ROWS)
            flat[here, :] = laid[:, r * COLS : (r + 1) * COLS]
        for n in range(2):
            raw = near_ref[n, base : base + wide_rows, :].astype(jnp.float32)
            at = (ROWS + n) * COLS
            raw = jnp.where(ends_wide, laid[:, at : at + COLS], raw)
            near[n, base : base + wide_rows, :] = raw * stat_ref[4 + n : 5 + n, :]

    wet = jnp.concatenate([wet_ref[...]] * 2, axis=0).astype(jnp.float32)
    wet16 = jnp.concatenate([wet, wet], axis=0)

    def begin(i, carry):
        for u in range(4):
            at = pl.multiple_of(i * 64 + u * 16, 16)
            raw = spec_ref[pl.ds(at, 16), :].astype(jnp.float32)
            dens[pl.ds(PAD + at, 16), :] = jnp.where(ends, flat[pl.ds(at, 16), :], raw) * wet16
            halo[pl.ds(at, 16), :] = jnp.zeros((16, COLS), jnp.float32)
        return carry

    lax.fori_loop(0, FLAT // 64, begin, 0)

    sub = lax.broadcasted_iota(jnp.int32, (8, COLS), 0)
    low = sub < ROWS
    depth = jnp.concatenate([depth_ref[...]] * 2, axis=0)
    weight = wet * fraction(jnp.concatenate([frac_ref[...]] * 2, axis=0))

    def between(d0, d1, w0, w1):
        return 0.5 * (d0 + d1) * w0 * w1

    def along(d, w):
        face = between(d, pltpu.roll(d, COLS - 1, 1), w, pltpu.roll(w, COLS - 1, 1))
        return jnp.where(lane[:8] == COLS - 1, 0.0, face)

    def wide(row):
        return jnp.broadcast_to(row, (8, COLS))

    face_x = between(depth, pltpu.roll(depth, 7, 0), weight, pltpu.roll(weight, 7, 0))
    face_x = jnp.where(sub % ROWS == ROWS - 1, 0.0, face_x)
    face_y = along(depth, weight)
    d_own = wide(jnp.where(first, depth[3:4], depth[0:1]))
    w_own = wide(jnp.where(first, weight[3:4], weight[0:1]))
    d_n1, d_n2, w_n1, w_n2 = (wide(stat_ref[i : i + 1, :]) for i in range(4))
    face_an = between(d_own, d_n1, w_own, w_n1)
    face_nb = between(d_n1, d_n2, w_n1, w_n2)
    face_n = along(d_n1, w_n1)

    for q in range(ND // 2):
        tab_x[8 * q : 8 * q + 8, :] = face_x * bin_block(cos_ref, q)
        tab_y[8 * q : 8 * q + 8, :] = face_y * bin_block(sin_ref, q)
        if 2 * q > ND // 2:
            back = 8 * (q - ND // 4)
            tab_z[back : back + 8, :] = pltpu.roll(face_y, 1, 1) * bin_block(sin_ref, q)
    for j in range(BLOCK // 8):
        tab_an[8 * j : 8 * j + 8, :] = face_an * bin_block(cosb_ref, j)
        tab_nb[8 * j : 8 * j + 8, :] = face_nb * bin_block(cosb_ref, j)
        tab_n[8 * j : 8 * j + 8, :] = face_n * bin_block(sinb_ref, j)

    def block(k, carry):
        bins = pl.multiple_of(k * BLOCK, 8)
        rows = pl.multiple_of(k * (BLOCK * ROWS), 16)
        g0, g1 = speed_ref[2 * k], speed_ref[2 * k + 1]

        def halo_fluxes():
            many = range(BLOCK // 8)
            n1s = [near[0, pl.ds(bins + 8 * j, 8), :] for j in many]
            owns = [dens[pl.ds(PAD + rows + 32 * j + adjacent, 8, stride=ROWS), :] for j in many]
            fluxes = []
            for j in many:
                along = bin_block(tab_an, j)
                top = jnp.where(first, owns[j], n1s[j])
                bottom = jnp.where(first, n1s[j], owns[j])
                flux = jnp.maximum(along, 0.0) * top + jnp.minimum(along, 0.0) * bottom
                fluxes.append(flux)
            for j in many:
                halo[pl.ds(rows + 32 * j + adjacent, 8, stride=ROWS), :] = sign * fluxes[j]
            return n1s, fluxes

        def advance(p, rho, across):
            g = g0 if p < 18 else g1
            q = p % 18
            along_x = bin_block(tab_x, q)
            if 2 * q + 1 < ND // 4 or 2 * q > 3 * ND // 4:
                fx = along_x * rho
            else:
                after = pltpu.roll(rho, 7, 0)
                if ND // 4 < 2 * q and 2 * q + 1 < 3 * ND // 4:
                    fx = along_x * after
                else:
                    fx = jnp.maximum(along_x, 0.0) * rho + jnp.minimum(along_x, 0.0) * after
            along_y = bin_block(tab_y, q)
            if 2 * q + 1 < ND // 2:
                fy = along_y * rho
                out_y = fy - pltpu.roll(fy, 1, 1)
            elif 2 * q > ND // 2:
                out_y = along_y * pltpu.roll(rho, COLS - 1, 1) - bin_block(tab_z, q - ND // 4) * rho
            else:
                right = pltpu.roll(rho, COLS - 1, 1)
                fy = jnp.maximum(along_y, 0.0) * rho + jnp.minimum(along_y, 0.0) * right
                out_y = fy - pltpu.roll(fy, 1, 1)
            change = (fx - pltpu.roll(fx, 1, 0)) + out_y
            return rho - g * (change + across)

        def advance_all():
            for start in range(0, ND // 2, GROUP):
                group = [p + h for p in range(start, start + GROUP) for h in (0, ND // 2)]
                loaded = [
                    (dens[pl.ds(PAD + rows + 8 * p, 8), :], halo[pl.ds(rows + 8 * p, 8), :])
                    for p in group
                ]
                moved = [advance(p, *pair) for p, pair in zip(group, loaded)]
                for p, value in zip(group, moved):
                    dens[pl.ds(PAD + rows + 8 * p, 8), :] = value

        n1s, fluxes = halo_fluxes()
        n2s = [near[1, pl.ds(bins + 8 * j, 8), :] for j in range(BLOCK // 8)]
        after_near = []
        for j in range(BLOCK // 8):
            n1, n2 = n1s[j], n2s[j]
            top, bottom = jnp.where(first, n1, n2), jnp.where(first, n2, n1)
            along = bin_block(tab_nb, j)
            beyond = jnp.maximum(along, 0.0) * top + jnp.minimum(along, 0.0) * bottom
            along = bin_block(tab_n, j)
            right = pltpu.roll(n1, COLS - 1, 1)
            fy = jnp.maximum(along, 0.0) * n1 + jnp.minimum(along, 0.0) * right
            change = sign * (beyond - fluxes[j]) + (fy - pltpu.roll(fy, 1, 1))
            speed = g0 if j < 4 else (jnp.where(low, g0, g1) if j == 4 else g1)
            after_near.append(n1 - speed * change)
        for j in range(BLOCK // 8):
            near[0, pl.ds(bins + 8 * j, 8), :] = after_near[j]
        advance_all()
        halo_fluxes()
        advance_all()
        return carry

    lax.fori_loop(0, BINS // BLOCK, block, 0)

    def interact(f, carry):
        rows = pl.multiple_of(f * (ND * ROWS), 16)
        scale = 0.2 * coef_ref[f]

        def partner(ref, b):
            lower = dens[pl.ds(ref[f * ND + b], 8), :]
            upper = dens[pl.ds(ref[f * ND + b + 1] - ROWS, 8), :]
            return jnp.where(low, lower, upper)

        for g in range(ND // 4):
            done = []
            for h in range(2):
                b = 4 * g + 2 * h
                mine = dens[pl.ds(PAD + rows + 4 * b, 8), :]
                plus, minus = partner(plus_ref, b), partner(minus_ref, b)
                source = mine * (mine * (plus + minus) - 2.0 * (plus * minus))
                value = jnp.maximum(mine + scale * source, 0.0)
                evol[pl.ds(rows + 4 * b, 8), :] = value
                done.append(value)
            out_ref[pl.ds(rows + 16 * g, 16), :] = jnp.concatenate(done, axis=0).astype(jnp.bfloat16)
        return carry

    lax.fori_loop(0, NF, interact, 0)

    row = lax.broadcasted_iota(jnp.int32, (CELLS, COLS), 0)
    for r in range(ROWS):
        own = lane[:1] + r * COLS
        same = row == jnp.where(child == 1, target_ref[r : r + 1, :], own)
        hot[:, r * COLS : (r + 1) * COLS] = jnp.where(same, 1.0, 0.0).astype(jnp.bfloat16)
    inner = (((1,), (1,)), ((), ()))
    number = lax.dot_general(
        jnp.ones((16, CELLS), jnp.bfloat16), hot[...], inner, preferred_element_type=jnp.float32
    )
    share = 1.0 / jnp.maximum(number[0:1], 1.0)
    count[...] = jnp.zeros_like(count)
    for turn in range(ROWS):
        for r in range(ROWS):
            of = (turn + r) % ROWS
            here = number[0:1, of * COLS : (of + 1) * COLS].astype(jnp.int32)
            count[turn, PIECE % 8 + r : PIECE % 8 + r + 1, :] = here

    many = CHUNK

    def sums(c, carry):
        base = c * (many * ROWS)
        parts = [evol[pl.ds(base + r, many, stride=ROWS), :] for r in range(ROWS)]
        value = jnp.concatenate(parts, axis=1)
        head = value.astype(jnp.bfloat16)
        tail = (value - head.astype(jnp.float32)).astype(jnp.bfloat16)
        total = lax.dot_general(head, hot[...], inner, preferred_element_type=jnp.float32)
        total += lax.dot_general(tail, hot[...], inner, preferred_element_type=jnp.float32)
        for r in range(ROWS):
            part = slice(r * COLS, (r + 1) * COLS)
            flat[pl.ds(base + r, many, stride=ROWS), :] = total[:, part] * share[:, part]
        return carry

    lax.fori_loop(0, BINS // many, sums, 0)
    main = PIECE // 8 * 8
    row = main + lax.broadcasted_iota(jnp.int32, (8, COLS), 0)

    def cut(i, carry):
        for turn in range(ROWS):
            j = i * ROWS + turn
            mean = flat[pl.ds(j * PIECE, main), :]
            last = jnp.where(row < PIECE, flat[pl.ds(j * PIECE + main, 8), :], 0.0)
            top = jnp.maximum(
                jnp.max(mean, axis=0, keepdims=True), jnp.max(last, axis=0, keepdims=True)
            )
            size = jnp.minimum((top * UNIT).astype(jnp.int32) + 1, OFFSET)
            steps = (UNIT * STEPS) / size.astype(jnp.float32)
            code = (mean * steps + 0.5).astype(jnp.int32) - OFFSET
            code_last = (last * steps + 0.5).astype(jnp.int32) - OFFSET
            rest = jnp.where(row == PIECE + ROWS, size, count[turn])
            code_last = jnp.where(row < PIECE, code_last, rest)
            code = jnp.concatenate([code, code_last], axis=0)
            pieces_ref[j] = code.astype(jnp.int16)
        return carry

    lax.fori_loop(0, PIECES // ROWS, cut, 0)


def evolve(*operands, interpret=False):
    smem = pl.BlockSpec(memory_space=pltpu.SMEM)
    vmem = pl.BlockSpec(memory_space=pltpu.VMEM)
    return pl.pallas_call(
        step_kernel,
        out_shape=(
            jax.ShapeDtypeStruct((FLAT, COLS), jnp.bfloat16),
            jax.ShapeDtypeStruct((PIECES, TALL, COLS), jnp.int16),
        ),
        in_specs=[smem] * 4 + [vmem] * 14,
        out_specs=(vmem, vmem),
        scratch_shapes=[
            pltpu.VMEM((FLAT + 2 * PAD, COLS), jnp.float32),
            pltpu.VMEM((FLAT + 2 * PAD, COLS), jnp.float32),
            pltpu.VMEM((FLAT, COLS), jnp.float32),
            pltpu.VMEM((FLAT, COLS), jnp.float32),
            pltpu.VMEM((2, BINS, COLS), jnp.float32),
            pltpu.VMEM((CELLS, CELLS), jnp.bfloat16),
            pltpu.VMEM((ROWS, 8, COLS), jnp.int32),
            pltpu.VMEM((ND * ROWS, COLS), jnp.float32),
            pltpu.VMEM((ND * ROWS, COLS), jnp.float32),
            pltpu.VMEM((ND * ROWS // 2, COLS), jnp.float32),
            pltpu.VMEM((BLOCK, COLS), jnp.float32),
            pltpu.VMEM((BLOCK, COLS), jnp.float32),
            pltpu.VMEM((BLOCK, COLS), jnp.float32),
        ],
        compiler_params=pltpu.CompilerParams(vmem_limit_bytes=VMEM_BYTES),
        cost_estimate=pl.CostEstimate(
            flops=1_400_000_000, bytes_accessed=10_000_000, transcendentals=0
        ),
        interpret=interpret,
    )(*operands)


def average_kernel(pieces_ref, out_ref):
    blocks = TALL // 8
    sub = lax.broadcasted_iota(jnp.int32, (8, COLS), 0)

    def add(i, carry):
        sums, weights, number = carry
        piece = pieces_ref[i].astype(jnp.int32).astype(jnp.float32)
        rest = piece[TALL - 8 :]
        at = PIECE % 8
        count = jnp.where(sub < ROWS, pltpu.roll(rest, 8 - at, 0), pltpu.roll(rest, ROWS - at, 0))
        weight = count * jnp.broadcast_to(rest[at + ROWS : at + ROWS + 1], (8, COLS))
        sums = tuple(sums[u] + piece[8 * u : 8 * u + 8] * weight for u in range(blocks))
        return sums, weights + weight, number + count

    zero = jnp.zeros((8, COLS), jnp.float32)
    carry = ((zero,) * blocks, zero, zero)
    sums, weights, number = lax.fori_loop(0, PIECES, add, carry)
    scale = 1.0 / (UNIT * STEPS * number)
    mean = jnp.concatenate([(part + OFFSET * weights) * scale for part in sums], axis=0)
    mean = mean.astype(jnp.bfloat16)

    def write(i, carry):
        out_ref[i] = mean
        return carry

    lax.fori_loop(0, STACK, write, 0)


def average(pieces, interpret=False):
    vmem = pl.BlockSpec(memory_space=pltpu.VMEM)
    return pl.pallas_call(
        average_kernel,
        out_shape=jax.ShapeDtypeStruct((STACK, TALL, COLS), jnp.bfloat16),
        in_specs=[vmem],
        out_specs=vmem,
        compiler_params=pltpu.CompilerParams(vmem_limit_bytes=SMALL_BYTES),
        interpret=interpret,
    )(pieces)


def lay_kernel(*refs):
    parts, (_, out_ref, wide, narrow, sems) = refs[:CUBES], refs[CUBES:]
    main = PIECE // 8 * 8

    @pl.when(own_flags()[1] == 0)
    def _():
        for cube, ref in zip((OWN, OPPOSITE) + DIRECT + PASSED, parts):
            for i in range(STACK):
                at = cube_member(cube, i) * PIECE
                piece = ref[i].astype(jnp.float32)
                wide[at : at + main, :] = piece[:main]
                wide[at + main : at + PIECE, :] = piece[main:PIECE]

        part = FLAT // SIDE
        copies = []
        for k in range(SIDE):

            def narrower(i, carry):
                for u in range(3):
                    at = pl.multiple_of(k * part + i * 48 + u * 16, 16)
                    narrow[pl.ds(at, 16), :] = wide[pl.ds(at, 16), :].astype(jnp.bfloat16)
                return carry

            lax.fori_loop(0, part // 48, narrower, 0)
            here = pl.ds(k * part, part)
            copies.append(pltpu.make_async_copy(narrow.at[here], out_ref.at[here], sems.at[k]))
            copies[k].start()
        for copy in copies:
            copy.wait()


def lay(parts, evolved):
    vmem = pl.BlockSpec(memory_space=pltpu.VMEM)
    anywhere = pl.BlockSpec(memory_space=pl.ANY)
    return pl.pallas_call(
        lay_kernel,
        out_shape=jax.ShapeDtypeStruct((FLAT, COLS), jnp.bfloat16),
        in_specs=[vmem] * CUBES + [anywhere],
        out_specs=anywhere,
        scratch_shapes=[
            pltpu.VMEM((FLAT + 2 * PAD, COLS), jnp.float32),
            pltpu.VMEM((FLAT, COLS), jnp.bfloat16),
            pltpu.SemaphoreType.DMA((SIDE,)),
        ],
        input_output_aliases={CUBES: 0},
        compiler_params=pltpu.CompilerParams(vmem_limit_bytes=SMALL_BYTES),
    )(*parts, evolved)


def tables():
    group_speed = 0.45 * np.exp(-math.log(1.1) * np.arange(NF))
    angles = 2.0 * math.pi / ND * np.arange(ND)

    def wide(values, times):
        return np.repeat(np.repeat(values, times)[:, None], COLS, axis=1).astype(np.float32)

    cosine, sine = np.cos(angles), np.sin(angles)
    twice = BLOCK // ND
    per_row = (wide(cosine, ROWS), wide(sine, ROWS))
    per_bin = (wide(np.tile(cosine, twice), 1), wide(np.tile(sine, twice), 1))
    return (group_speed.astype(np.float32),) + per_row + per_bin


def spots():
    both = []
    for cell in range(2):
        chosen = np.zeros((4 * ROWS, (ROWS + 2) * COLS), np.float32)
        near = (ROWS - 1, ROWS - 2) if cell else (0, 1)
        for block, source in enumerate(tuple(range(ROWS)) + tuple(ROWS + row for row in near)):
            chosen[2 * source, block * COLS] = 1.0
            chosen[2 * source + 1, (block + 1) * COLS - 1] = 1.0
        both.append(chosen)
    return np.stack(both).astype(jnp.bfloat16)


def swap(x):
    return lax.ppermute(x, "cell", [(0, 1), (1, 0)])


def on_device(
    spectrum,
    depth_factor,
    wet_mask,
    frac_index,
    boundary_map,
    average_map,
    dia_plus,
    dia_minus,
    dia_coef,
):
    parent = lax.axis_size("grid") - 1
    hubs = hub_places()
    spec = spectrum.reshape(FLAT, COLS)
    maps, *parts = send_first(boundary_map.T, spec)

    held = [lax.ppermute(part, "grid", [(parent, hub)]) for part, hub in zip(parts, hubs[1:])]
    maps = lax.all_to_all(maps, "grid", 0, 0)
    near, near_statics = prepare(spec, depth_factor, wet_mask, frac_index)
    near = swap(near)
    near_statics = swap(near_statics)
    picked = lax.all_to_all(pick(maps, spec, *held), "grid", 0, 0)
    picked = jnp.concatenate([picked[hub] for hub in hubs], axis=1)
    far = swap(picked)

    group_speed, cosine, sine, cosine_bin, sine_bin = tables()
    evolved, pieces = evolve(
        dia_plus * ROWS + PAD,
        dia_minus * ROWS + PAD,
        group_speed,
        dia_coef,
        spec,
        near,
        picked,
        far,
        spots(),
        depth_factor,
        wet_mask,
        frac_index,
        near_statics,
        cosine,
        sine,
        cosine_bin,
        sine_bin,
        average_map,
    )
    copies = average(lax.all_to_all(pieces, "grid", 0, 0))
    last = SIDE - 1
    cubes = [[cube_member(k, i) for i in range(STACK)] for k in range(CUBES)]
    gathered = lax.all_to_all(copies, "grid", 0, 0, axis_index_groups=cubes)
    passing = [place(last, last, 0), place(last, 0, last), place(0, last, last)]
    far = [place(last, 0, 0), place(0, 0, last), place(0, last, 0)]
    relayed = lax.ppermute(
        gathered, "grid", list(zip(far, passing)) + [(place(0, 0, 0), parent)]
    )
    parts = [gathered, relayed]
    for value in (gathered, relayed):
        parts += [lax.ppermute(value, "grid", [(device, parent)]) for device in passing]
    return lay(parts, evolved).reshape(BINS, ROWS, COLS)


def solution(mesh):
    placed = (
        P(None, ("grid", "cell"), None),
        P(("grid", "cell"), None),
        P(("grid", "cell"), None),
        P(("grid", "cell"), None),
        P(("grid", "cell"), None),
        P(("grid", "cell"), None),
        P(),
        P(),
        P(),
    )
    return jax.shard_map(
        on_device,
        mesh=mesh,
        in_specs=placed,
        out_specs=P(None, ("grid", "cell"), None),
        check_vma=False,
    )
```

```python
import functools
import math

import jax
import jax.numpy as jnp
import numpy as np
from jax import lax
from jax.experimental import pallas as pl
from jax.experimental.pallas import tpu as pltpu
from jax.sharding import PartitionSpec as P

NF = 36
ND = 36
SIDE = 4
ROWS = 4
COLS = 128
CELLS = ROWS * COLS
BINS = NF * ND
FLAT = BINS * ROWS
PAD = 8
PIECES = SIDE**3
PIECE = FLAT // PIECES
TALL = 88
BLOCK = 72
GROUP = 3
CHUNK = 432
WIDTH = 512
UNIT = 512.0
STEPS = 65534.0
OFFSET = 32767
VMEM_BYTES = 24 * 1024 * 1024
SMALL_BYTES = 10 * 1024 * 1024
LARGE_BYTES = 56 * 1024 * 1024
STACK = 8

FRACTIONS = (0.25, 0.5, 0.75, 1.0)


def fraction(frac_index):
    open_share = jnp.zeros(frac_index.shape, jnp.float32)
    for position, share in enumerate(FRACTIONS):
        open_share = open_share + jnp.where(frac_index == position, share, 0.0)
    return open_share


def place(z, y, x):
    return (z % SIDE * SIDE + y % SIDE) * SIDE + x % SIDE


def hub_places():
    last = SIDE - 1
    return [
        place(last, last, last),
        place(last, last, last - 1),
        place(last, last - 1, last),
        place(last - 1, last, last),
    ]


def cube_member(cube, position):
    zyx = [2 * (cube // d % 2) + position // d % 2 for d in (4, 2, 1)]
    return (zyx[0] * SIDE + zyx[1]) * SIDE + zyx[2]


CUBES = 8
DIRECT = (6, 5, 3)
PASSED = (4, 1, 2)
OWN, OPPOSITE = 7, 0


def own_flags():
    return 1 - lax.axis_index("cell"), jnp.where(lax.axis_index("grid") == PIECES - 1, 0, 1)


def bin_block(ref, index):
    return ref[8 * index : 8 * index + 8, :]


def send_kernel(map_ref, spec_ref, maps_ref, part1_ref, part2_ref, part3_ref, held, sems):
    part = FLAT // SIDE
    parts = (part1_ref, part2_ref, part3_ref)
    there = [
        pltpu.make_async_copy(spec_ref.at[pl.ds((k + 1) * part, part), :], held.at[k], sems.at[k])
        for k in range(SIDE - 1)
    ]
    back = [
        pltpu.make_async_copy(held.at[k], ref, sems.at[SIDE - 1 + k]) for k, ref in enumerate(parts)
    ]
    for copy in there:
        copy.start()
    lane = lax.broadcasted_iota(jnp.int32, (PIECES, COLS), 1)
    maps = jnp.zeros((PIECES, COLS), jnp.int32)
    for r in range(ROWS):
        for side in range(2):
            maps = jnp.where(lane == 2 * r + side, map_ref[side, r], maps)
    maps_ref[...] = maps
    for copy, onward in zip(there, back):
        copy.wait()
        onward.start()
    for onward in back:
        onward.wait()


def send_first(maps, spec):
    anywhere = pl.BlockSpec(memory_space=pl.ANY)
    part = jax.ShapeDtypeStruct((FLAT // SIDE, COLS), jnp.bfloat16)
    return pl.pallas_call(
        send_kernel,
        out_shape=(jax.ShapeDtypeStruct((PIECES, COLS), jnp.int32),) + (part,) * (SIDE - 1),
        in_specs=[pl.BlockSpec(memory_space=pltpu.SMEM), anywhere],
        out_specs=(pl.BlockSpec(memory_space=pltpu.VMEM),) + (anywhere,) * (SIDE - 1),
        scratch_shapes=[
            pltpu.VMEM((SIDE - 1, FLAT // SIDE, COLS), jnp.bfloat16),
            pltpu.SemaphoreType.DMA((2 * SIDE - 2,)),
        ],
        compiler_params=pltpu.CompilerParams(vmem_limit_bytes=LARGE_BYTES),
    )(maps, spec)


def pick_kernel(maps_ref, spec_ref, a_ref, b_ref, c_ref, out_ref, wide, turned, hot, mine, sem):
    part = FLAT // SIDE
    bins = part // ROWS
    share = jnp.where(own_flags()[1] == 0, 1.0, 0.0)
    copy = pltpu.make_async_copy(spec_ref.at[pl.ds(0, part), :], mine, sem)
    copy.start()
    cell = lax.broadcasted_iota(jnp.int32, (PIECES, CELLS), 1)
    for e in range(2 * ROWS):
        wanted = jnp.broadcast_to(maps_ref[:, e : e + 1], (PIECES, CELLS))
        same = jnp.where(cell == wanted, 1.0, 0.0).astype(jnp.bfloat16)
        hot[e * PIECES : (e + 1) * PIECES, :] = same
    copy.wait()

    def join(i, carry):
        for u in range(3):
            at = pl.multiple_of(i * 48 + u * 16, 16)
            here = pl.ds(at, 16)
            value = mine[here, :].astype(jnp.float32) * share
            for ref in (a_ref, b_ref, c_ref):
                value = value + ref[here, :].astype(jnp.float32)
            wide[here, :] = value
        return carry

    lax.fori_loop(0, part // 48, join, 0)
    wide[part:, :] = jnp.zeros((wide.shape[0] - part, COLS), jnp.float32)
    many = wide.shape[0] // ROWS
    held = [wide[pl.ds(r, many, stride=ROWS), :].astype(jnp.bfloat16) for r in range(ROWS)]
    held = jnp.concatenate(held, axis=1)
    found = lax.dot_general(
        hot[...], held, (((1,), (1,)), ((), ())), preferred_element_type=jnp.float32
    )
    for e in range(2 * ROWS):
        for t in range(many // COLS):
            part = found[e * PIECES : (e + 1) * PIECES, t * COLS : (t + 1) * COLS]
            turned[t, pl.ds(e, PIECES, stride=2 * ROWS), :] = part

    def narrower(g, carry):
        at = pl.multiple_of(g * 2 * ROWS, 8)
        for t in range(many // COLS):
            lanes = min(COLS, bins - t * COLS)
            value = turned[t, pl.ds(at, 2 * ROWS), :lanes].astype(jnp.bfloat16)
            out_ref[g, :, t * COLS : t * COLS + lanes] = value
        return carry

    lax.fori_loop(0, PIECES, narrower, 0)


def pick(*operands):
    vmem = pl.BlockSpec(memory_space=pltpu.VMEM)
    part = FLAT // SIDE
    return pl.pallas_call(
        pick_kernel,
        out_shape=jax.ShapeDtypeStruct((PIECES, 2 * ROWS, part // ROWS), jnp.bfloat16),
        in_specs=[vmem, pl.BlockSpec(memory_space=pl.ANY)] + [vmem] * 3,
        out_specs=vmem,
        scratch_shapes=[
            pltpu.VMEM((3 * COLS * ROWS, COLS), jnp.float32),
            pltpu.VMEM((3, PIECES * 2 * ROWS, COLS), jnp.float32),
            pltpu.VMEM((PIECES * 2 * ROWS, CELLS), jnp.bfloat16),
            pltpu.VMEM((part, COLS), jnp.bfloat16),
            pltpu.SemaphoreType.DMA,
        ],
        compiler_params=pltpu.CompilerParams(vmem_limit_bytes=SMALL_BYTES),
    )(*operands)


def prepare_kernel(spec_ref, depth_ref, wet_ref, frac_ref, near_ref, stat_ref, dens):
    first = own_flags()[0] == 1
    wet = wet_ref[...].astype(jnp.float32)
    values = (depth_ref[...], wet * fraction(frac_ref[...]), wet)
    for i, value in enumerate(values):
        stat_ref[2 * i : 2 * i + 1, :] = jnp.where(first, value[3:4], value[0:1])
        stat_ref[2 * i + 1 : 2 * i + 2, :] = jnp.where(first, value[2:3], value[1:2])
    stat_ref[6:8, :] = jnp.zeros((2, COLS), jnp.float32)

    def widen(i, carry):
        for u in range(4):
            at = pl.multiple_of(i * 64 + u * 16, 16)
            dens[pl.ds(at, 16), :] = spec_ref[pl.ds(at, 16), :].astype(jnp.float32)
        return carry

    lax.fori_loop(0, FLAT // 64, widen, 0)
    nearer = 3 * own_flags()[0]
    farther = 1 + own_flags()[0]

    def pull(i, carry):
        for u in range(3):
            at = pl.multiple_of(i * 48 + u * 16, 16)
            for n, row in enumerate((nearer, farther)):
                rows = dens[pl.ds(at * ROWS + row, 16, stride=ROWS), :]
                near_ref[n, pl.ds(at, 16), :] = rows.astype(jnp.bfloat16)
        return carry

    lax.fori_loop(0, BINS // 48, pull, 0)


def prepare(*operands, interpret=False):
    vmem = pl.BlockSpec(memory_space=pltpu.VMEM)
    return pl.pallas_call(
        prepare_kernel,
        out_shape=(
            jax.ShapeDtypeStruct((2, BINS, COLS), jnp.bfloat16),
            jax.ShapeDtypeStruct((8, COLS), jnp.float32),
        ),
        in_specs=[vmem] * 4,
        out_specs=(vmem,) * 2,
        scratch_shapes=[pltpu.VMEM((FLAT, COLS), jnp.float32)],
        compiler_params=pltpu.CompilerParams(vmem_limit_bytes=SMALL_BYTES),
        cost_estimate=pl.CostEstimate(flops=4_000_000, bytes_accessed=5_000_000, transcendentals=0),
        interpret=interpret,
    )(*operands)


def step_kernel(
    plus_ref,
    minus_ref,
    speed_ref,
    coef_ref,
    spec_ref,
    near_ref,
    edge_ref,
    far_ref,
    spot_ref,
    depth_ref,
    wet_ref,
    frac_ref,
    stat_ref,
    cos_ref,
    sin_ref,
    cosb_ref,
    sinb_ref,
    target_ref,
    out_ref,
    pieces_ref,
    dens,
    flat,
    halo,
    evol,
    near,
    hot,
    count,
    tab_x,
    tab_y,
    tab_z,
    tab_an,
    tab_nb,
    tab_n,
    done_out,
    out_sem,
):
    first = own_flags()[0] == 1
    child = own_flags()[1]
    adjacent = 3 * own_flags()[0]
    sign = jnp.where(first, 1.0, -1.0)
    lane = lax.broadcasted_iota(jnp.int32, (16, COLS), 1)
    ends = jnp.where((lane == 0) | (lane == COLS - 1), child, 0) > 0

    values = jnp.concatenate([edge_ref[...], far_ref[...]], axis=0)
    spot = spot_ref[1 - own_flags()[0]]
    for base in range(0, BINS, WIDTH):
        wide_rows = min(WIDTH, BINS - base)
        laid = lax.dot_general(
            values[:, base : base + wide_rows],
            spot,
            (((0,), (0,)), ((), ())),
            preferred_element_type=jnp.float32,
        )
        lanes = lax.broadcasted_iota(jnp.int32, (wide_rows, COLS), 1)
        ends_wide = jnp.where((lanes == 0) | (lanes == COLS - 1), child, 0) > 0
        for r in range(ROWS):
            here = pl.ds(base * ROWS + r, wide_rows, stride=ROWS)
            flat[here, :] = laid[:, r * COLS : (r + 1) * COLS]
        for n in range(2):
            raw = near_ref[n, base : base + wide_rows, :].astype(jnp.float32)
            at = (ROWS + n) * COLS
            raw = jnp.where(ends_wide, laid[:, at : at + COLS], raw)
            near[n, base : base + wide_rows, :] = raw * stat_ref[4 + n : 5 + n, :]

    wet = jnp.concatenate([wet_ref[...]] * 2, axis=0).astype(jnp.float32)
    wet16 = jnp.concatenate([wet, wet], axis=0)

    def begin(i, carry):
        for u in range(4):
            at = pl.multiple_of(i * 64 + u * 16, 16)
            raw = spec_ref[pl.ds(at, 16), :].astype(jnp.float32)
            dens[pl.ds(PAD + at, 16), :] = jnp.where(ends, flat[pl.ds(at, 16), :], raw) * wet16
            halo[pl.ds(at, 16), :] = jnp.zeros((16, COLS), jnp.float32)
        return carry

    lax.fori_loop(0, FLAT // 64, begin, 0)

    sub = lax.broadcasted_iota(jnp.int32, (8, COLS), 0)
    low = sub < ROWS
    depth = jnp.concatenate([depth_ref[...]] * 2, axis=0)
    weight = wet * fraction(jnp.concatenate([frac_ref[...]] * 2, axis=0))

    def between(d0, d1, w0, w1):
        return 0.5 * (d0 + d1) * w0 * w1

    def along(d, w):
        face = between(d, pltpu.roll(d, COLS - 1, 1), w, pltpu.roll(w, COLS - 1, 1))
        return jnp.where(lane[:8] == COLS - 1, 0.0, face)

    def wide(row):
        return jnp.broadcast_to(row, (8, COLS))

    face_x = between(depth, pltpu.roll(depth, 7, 0), weight, pltpu.roll(weight, 7, 0))
    face_x = jnp.where(sub % ROWS == ROWS - 1, 0.0, face_x)
    face_y = along(depth, weight)
    d_own = wide(jnp.where(first, depth[3:4], depth[0:1]))
    w_own = wide(jnp.where(first, weight[3:4], weight[0:1]))
    d_n1, d_n2, w_n1, w_n2 = (wide(stat_ref[i : i + 1, :]) for i in range(4))
    face_an = between(d_own, d_n1, w_own, w_n1)
    face_nb = between(d_n1, d_n2, w_n1, w_n2)
    face_n = along(d_n1, w_n1)

    for q in range(ND // 2):
        tab_x[8 * q : 8 * q + 8, :] = face_x * bin_block(cos_ref, q)
        tab_y[8 * q : 8 * q + 8, :] = face_y * bin_block(sin_ref, q)
        if 2 * q > ND // 2:
            back = 8 * (q - ND // 4)
            tab_z[back : back + 8, :] = pltpu.roll(face_y, 1, 1) * bin_block(sin_ref, q)
    for j in range(BLOCK // 8):
        tab_an[8 * j : 8 * j + 8, :] = face_an * bin_block(cosb_ref, j)
        tab_nb[8 * j : 8 * j + 8, :] = face_nb * bin_block(cosb_ref, j)
        tab_n[8 * j : 8 * j + 8, :] = face_n * bin_block(sinb_ref, j)

    def block(k, carry):
        bins = pl.multiple_of(k * BLOCK, 8)
        rows = pl.multiple_of(k * (BLOCK * ROWS), 16)
        g0, g1 = speed_ref[2 * k], speed_ref[2 * k + 1]

        def halo_fluxes():
            many = range(BLOCK // 8)
            n1s = [near[0, pl.ds(bins + 8 * j, 8), :] for j in many]
            owns = [dens[pl.ds(PAD + rows + 32 * j + adjacent, 8, stride=ROWS), :] for j in many]
            fluxes = []
            for j in many:
                along = bin_block(tab_an, j)
                top = jnp.where(first, owns[j], n1s[j])
                bottom = jnp.where(first, n1s[j], owns[j])
                flux = jnp.maximum(along, 0.0) * top + jnp.minimum(along, 0.0) * bottom
                fluxes.append(flux)
            for j in many:
                halo[pl.ds(rows + 32 * j + adjacent, 8, stride=ROWS), :] = sign * fluxes[j]
            return n1s, fluxes

        def advance(p, rho, across):
            g = g0 if p < 18 else g1
            q = p % 18
            along_x = bin_block(tab_x, q)
            if 2 * q + 1 < ND // 4 or 2 * q > 3 * ND // 4:
                fx = along_x * rho
            else:
                after = pltpu.roll(rho, 7, 0)
                if ND // 4 < 2 * q and 2 * q + 1 < 3 * ND // 4:
                    fx = along_x * after
                else:
                    fx = jnp.maximum(along_x, 0.0) * rho + jnp.minimum(along_x, 0.0) * after
            along_y = bin_block(tab_y, q)
            if 2 * q + 1 < ND // 2:
                fy = along_y * rho
                out_y = fy - pltpu.roll(fy, 1, 1)
            elif 2 * q > ND // 2:
                out_y = along_y * pltpu.roll(rho, COLS - 1, 1) - bin_block(tab_z, q - ND // 4) * rho
            else:
                right = pltpu.roll(rho, COLS - 1, 1)
                fy = jnp.maximum(along_y, 0.0) * rho + jnp.minimum(along_y, 0.0) * right
                out_y = fy - pltpu.roll(fy, 1, 1)
            change = (fx - pltpu.roll(fx, 1, 0)) + out_y
            return rho - g * (change + across)

        def advance_all():
            for start in range(0, ND // 2, GROUP):
                group = [p + h for p in range(start, start + GROUP) for h in (0, ND // 2)]
                loaded = [
                    (dens[pl.ds(PAD + rows + 8 * p, 8), :], halo[pl.ds(rows + 8 * p, 8), :])
                    for p in group
                ]
                moved = [advance(p, *pair) for p, pair in zip(group, loaded)]
                for p, value in zip(group, moved):
                    dens[pl.ds(PAD + rows + 8 * p, 8), :] = value

        n1s, fluxes = halo_fluxes()
        n2s = [near[1, pl.ds(bins + 8 * j, 8), :] for j in range(BLOCK // 8)]
        after_near = []
        for j in range(BLOCK // 8):
            n1, n2 = n1s[j], n2s[j]
            top, bottom = jnp.where(first, n1, n2), jnp.where(first, n2, n1)
            along = bin_block(tab_nb, j)
            beyond = jnp.maximum(along, 0.0) * top + jnp.minimum(along, 0.0) * bottom
            along = bin_block(tab_n, j)
            right = pltpu.roll(n1, COLS - 1, 1)
            fy = jnp.maximum(along, 0.0) * n1 + jnp.minimum(along, 0.0) * right
            change = sign * (beyond - fluxes[j]) + (fy - pltpu.roll(fy, 1, 1))
            speed = g0 if j < 4 else (jnp.where(low, g0, g1) if j == 4 else g1)
            after_near.append(n1 - speed * change)
        for j in range(BLOCK // 8):
            near[0, pl.ds(bins + 8 * j, 8), :] = after_near[j]
        advance_all()
        halo_fluxes()
        advance_all()
        return carry

    lax.fori_loop(0, BINS // BLOCK, block, 0)

    def interact(f, carry):
        rows = pl.multiple_of(f * (ND * ROWS), 16)
        scale = 0.2 * coef_ref[f]

        def partner(ref, b):
            lower = dens[pl.ds(ref[f * ND + b], 8), :]
            upper = dens[pl.ds(ref[f * ND + b + 1] - ROWS, 8), :]
            return jnp.where(low, lower, upper)

        for g in range(ND // 4):
            done = []
            for h in range(2):
                b = 4 * g + 2 * h
                mine = dens[pl.ds(PAD + rows + 4 * b, 8), :]
                plus, minus = partner(plus_ref, b), partner(minus_ref, b)
                source = mine * (mine * (plus + minus) - 2.0 * (plus * minus))
                value = jnp.maximum(mine + scale * source, 0.0)
                evol[pl.ds(rows + 4 * b, 8), :] = value
                done.append(value)
            done_out[pl.ds(rows + 16 * g, 16), :] = jnp.concatenate(done, axis=0).astype(jnp.bfloat16)
        return carry

    lax.fori_loop(0, NF, interact, 0)
    leaving = pltpu.make_async_copy(done_out, out_ref, out_sem)
    leaving.start()

    row = lax.broadcasted_iota(jnp.int32, (CELLS, COLS), 0)
    for r in range(ROWS):
        own = lane[:1] + r * COLS
        same = row == jnp.where(child == 1, target_ref[r : r + 1, :], own)
        hot[:, r * COLS : (r + 1) * COLS] = jnp.where(same, 1.0, 0.0).astype(jnp.bfloat16)
    inner = (((1,), (1,)), ((), ()))
    number = lax.dot_general(
        jnp.ones((16, CELLS), jnp.bfloat16), hot[...], inner, preferred_element_type=jnp.float32
    )
    share = 1.0 / jnp.maximum(number[0:1], 1.0)
    count[...] = jnp.zeros_like(count)
    for turn in range(ROWS):
        for r in range(ROWS):
            of = (turn + r) % ROWS
            here = number[0:1, of * COLS : (of + 1) * COLS].astype(jnp.int32)
            count[turn, PIECE % 8 + r : PIECE % 8 + r + 1, :] = here

    many = CHUNK

    def sums(c, carry):
        base = c * (many * ROWS)
        parts = [evol[pl.ds(base + r, many, stride=ROWS), :] for r in range(ROWS)]
        value = jnp.concatenate(parts, axis=1)
        head = value.astype(jnp.bfloat16)
        tail = (value - head.astype(jnp.float32)).astype(jnp.bfloat16)
        total = lax.dot_general(head, hot[...], inner, preferred_element_type=jnp.float32)
        total += lax.dot_general(tail, hot[...], inner, preferred_element_type=jnp.float32)
        for r in range(ROWS):
            part = slice(r * COLS, (r + 1) * COLS)
            flat[pl.ds(base + r, many, stride=ROWS), :] = total[:, part] * share[:, part]
        return carry

    lax.fori_loop(0, BINS // many, sums, 0)
    main = PIECE // 8 * 8
    row = main + lax.broadcasted_iota(jnp.int32, (8, COLS), 0)

    def cut(i, carry):
        for turn in range(ROWS):
            j = i * ROWS + turn
            mean = flat[pl.ds(j * PIECE, main), :]
            last = jnp.where(row < PIECE, flat[pl.ds(j * PIECE + main, 8), :], 0.0)
            top = jnp.maximum(
                jnp.max(mean, axis=0, keepdims=True), jnp.max(last, axis=0, keepdims=True)
            )
            size = jnp.minimum((top * UNIT).astype(jnp.int32) + 1, OFFSET)
            steps = (UNIT * STEPS) / size.astype(jnp.float32)
            code = (mean * steps + 0.5).astype(jnp.int32) - OFFSET
            code_last = (last * steps + 0.5).astype(jnp.int32) - OFFSET
            rest = jnp.where(row == PIECE + ROWS, size, count[turn])
            code_last = jnp.where(row < PIECE, code_last, rest)
            code = jnp.concatenate([code, code_last], axis=0)
            pieces_ref[j] = code.astype(jnp.int16)
        return carry

    lax.fori_loop(0, PIECES // ROWS, cut, 0)
    leaving.wait()


def evolve(*operands, interpret=False):
    smem = pl.BlockSpec(memory_space=pltpu.SMEM)
    vmem = pl.BlockSpec(memory_space=pltpu.VMEM)
    return pl.pallas_call(
        step_kernel,
        out_shape=(
            jax.ShapeDtypeStruct((FLAT, COLS), jnp.bfloat16),
            jax.ShapeDtypeStruct((PIECES, TALL, COLS), jnp.int16),
        ),
        in_specs=[smem] * 4 + [vmem] * 14,
        out_specs=(pl.BlockSpec(memory_space=pl.ANY), vmem),
        scratch_shapes=[
            pltpu.VMEM((FLAT + 2 * PAD, COLS), jnp.float32),
            pltpu.VMEM((FLAT + 2 * PAD, COLS), jnp.float32),
            pltpu.VMEM((FLAT, COLS), jnp.float32),
            pltpu.VMEM((FLAT, COLS), jnp.float32),
            pltpu.VMEM((2, BINS, COLS), jnp.float32),
            pltpu.VMEM((CELLS, CELLS), jnp.bfloat16),
            pltpu.VMEM((ROWS, 8, COLS), jnp.int32),
            pltpu.VMEM((ND * ROWS, COLS), jnp.float32),
            pltpu.VMEM((ND * ROWS, COLS), jnp.float32),
            pltpu.VMEM((ND * ROWS // 2, COLS), jnp.float32),
            pltpu.VMEM((BLOCK, COLS), jnp.float32),
            pltpu.VMEM((BLOCK, COLS), jnp.float32),
            pltpu.VMEM((BLOCK, COLS), jnp.float32),
            pltpu.VMEM((FLAT, COLS), jnp.bfloat16),
            pltpu.SemaphoreType.DMA,
        ],
        compiler_params=pltpu.CompilerParams(vmem_limit_bytes=VMEM_BYTES),
        cost_estimate=pl.CostEstimate(
            flops=1_400_000_000, bytes_accessed=10_000_000, transcendentals=0
        ),
        interpret=interpret,
    )(*operands)


def average_kernel(pieces_ref, out_ref):
    blocks = TALL // 8
    sub = lax.broadcasted_iota(jnp.int32, (8, COLS), 0)

    def add(i, carry):
        sums, weights, number = carry
        piece = pieces_ref[i].astype(jnp.int32).astype(jnp.float32)
        rest = piece[TALL - 8 :]
        at = PIECE % 8
        count = jnp.where(sub < ROWS, pltpu.roll(rest, 8 - at, 0), pltpu.roll(rest, ROWS - at, 0))
        weight = count * jnp.broadcast_to(rest[at + ROWS : at + ROWS + 1], (8, COLS))
        sums = tuple(sums[u] + piece[8 * u : 8 * u + 8] * weight for u in range(blocks))
        return sums, weights + weight, number + count

    zero = jnp.zeros((8, COLS), jnp.float32)
    carry = ((zero,) * blocks, zero, zero)
    sums, weights, number = lax.fori_loop(0, PIECES, add, carry)
    scale = 1.0 / (UNIT * STEPS * number)
    mean = jnp.concatenate([(part + OFFSET * weights) * scale for part in sums], axis=0)
    mean = mean.astype(jnp.bfloat16)

    def write(i, carry):
        out_ref[i] = mean
        return carry

    lax.fori_loop(0, STACK, write, 0)


def average(pieces, interpret=False):
    vmem = pl.BlockSpec(memory_space=pltpu.VMEM)
    return pl.pallas_call(
        average_kernel,
        out_shape=jax.ShapeDtypeStruct((STACK, TALL, COLS), jnp.bfloat16),
        in_specs=[vmem],
        out_specs=vmem,
        compiler_params=pltpu.CompilerParams(vmem_limit_bytes=SMALL_BYTES),
        interpret=interpret,
    )(pieces)


def lay_kernel(*refs):
    parts, (_, out_ref, wide, narrow, sems) = refs[:CUBES], refs[CUBES:]
    main = PIECE // 8 * 8

    @pl.when(own_flags()[1] == 0)
    def _():
        for cube, ref in zip((OWN, OPPOSITE) + DIRECT + PASSED, parts):
            for i in range(STACK):
                at = cube_member(cube, i) * PIECE
                piece = ref[i].astype(jnp.float32)
                wide[at : at + main, :] = piece[:main]
                wide[at + main : at + PIECE, :] = piece[main:PIECE]

        part = FLAT // SIDE
        copies = []
        for k in range(SIDE):

            def narrower(i, carry):
                for u in range(3):
                    at = pl.multiple_of(k * part + i * 48 + u * 16, 16)
                    narrow[pl.ds(at, 16), :] = wide[pl.ds(at, 16), :].astype(jnp.bfloat16)
                return carry

            lax.fori_loop(0, part // 48, narrower, 0)
            here = pl.ds(k * part, part)
            copies.append(pltpu.make_async_copy(narrow.at[here], out_ref.at[here], sems.at[k]))
            copies[k].start()
        for copy in copies:
            copy.wait()


def lay(parts, evolved):
    vmem = pl.BlockSpec(memory_space=pltpu.VMEM)
    anywhere = pl.BlockSpec(memory_space=pl.ANY)
    return pl.pallas_call(
        lay_kernel,
        out_shape=jax.ShapeDtypeStruct((FLAT, COLS), jnp.bfloat16),
        in_specs=[vmem] * CUBES + [anywhere],
        out_specs=anywhere,
        scratch_shapes=[
            pltpu.VMEM((FLAT + 2 * PAD, COLS), jnp.float32),
            pltpu.VMEM((FLAT, COLS), jnp.bfloat16),
            pltpu.SemaphoreType.DMA((SIDE,)),
        ],
        input_output_aliases={CUBES: 0},
        compiler_params=pltpu.CompilerParams(vmem_limit_bytes=SMALL_BYTES),
    )(*parts, evolved)


def tables():
    group_speed = 0.45 * np.exp(-math.log(1.1) * np.arange(NF))
    angles = 2.0 * math.pi / ND * np.arange(ND)

    def wide(values, times):
        return np.repeat(np.repeat(values, times)[:, None], COLS, axis=1).astype(np.float32)

    cosine, sine = np.cos(angles), np.sin(angles)
    twice = BLOCK // ND
    per_row = (wide(cosine, ROWS), wide(sine, ROWS))
    per_bin = (wide(np.tile(cosine, twice), 1), wide(np.tile(sine, twice), 1))
    return (group_speed.astype(np.float32),) + per_row + per_bin


def spots():
    both = []
    for cell in range(2):
        chosen = np.zeros((4 * ROWS, (ROWS + 2) * COLS), np.float32)
        near = (ROWS - 1, ROWS - 2) if cell else (0, 1)
        for block, source in enumerate(tuple(range(ROWS)) + tuple(ROWS + row for row in near)):
            chosen[2 * source, block * COLS] = 1.0
            chosen[2 * source + 1, (block + 1) * COLS - 1] = 1.0
        both.append(chosen)
    return np.stack(both).astype(jnp.bfloat16)


def swap(x):
    return lax.ppermute(x, "cell", [(0, 1), (1, 0)])


def on_device(
    spectrum,
    depth_factor,
    wet_mask,
    frac_index,
    boundary_map,
    average_map,
    dia_plus,
    dia_minus,
    dia_coef,
):
    parent = lax.axis_size("grid") - 1
    hubs = hub_places()
    spec = spectrum.reshape(FLAT, COLS)
    maps, *parts = send_first(boundary_map.T, spec)

    held = [lax.ppermute(part, "grid", [(parent, hub)]) for part, hub in zip(parts, hubs[1:])]
    maps = lax.all_to_all(maps, "grid", 0, 0)
    near, near_statics = prepare(spec, depth_factor, wet_mask, frac_index)
    near = swap(near)
    near_statics = swap(near_statics)
    picked = lax.all_to_all(pick(maps, spec, *held), "grid", 0, 0)
    picked = jnp.concatenate([picked[hub] for hub in hubs], axis=1)
    far = swap(picked)

    group_speed, cosine, sine, cosine_bin, sine_bin = tables()
    evolved, pieces = evolve(
        dia_plus * ROWS + PAD,
        dia_minus * ROWS + PAD,
        group_speed,
        dia_coef,
        spec,
        near,
        picked,
        far,
        spots(),
        depth_factor,
        wet_mask,
        frac_index,
        near_statics,
        cosine,
        sine,
        cosine_bin,
        sine_bin,
        average_map,
    )
    copies = average(lax.all_to_all(pieces, "grid", 0, 0))
    last = SIDE - 1
    cubes = [[cube_member(k, i) for i in range(STACK)] for k in range(CUBES)]
    gathered = lax.all_to_all(copies, "grid", 0, 0, axis_index_groups=cubes)
    wrapping = [place(last, last, 0), place(last, 0, last), place(0, last, last)]
    inside = [place(last, last, last - 1), place(last, last - 1, last), place(last - 1, last, last)]
    far = [place(last, 0, 1), place(0, 1, last), place(1, last, 0)]
    relayed = lax.ppermute(gathered, "grid", list(zip(far, inside)))
    parts = [gathered, lax.ppermute(gathered, "grid", [(place(0, 0, 0), parent)])]
    parts += [lax.ppermute(gathered, "grid", [(device, parent)]) for device in wrapping]
    parts += [lax.ppermute(relayed, "grid", [(device, parent)]) for device in inside]
    return lay(parts, evolved).reshape(BINS, ROWS, COLS)


def solution(mesh):
    placed = (
        P(None, ("grid", "cell"), None),
        P(("grid", "cell"), None),
        P(("grid", "cell"), None),
        P(("grid", "cell"), None),
        P(("grid", "cell"), None),
        P(("grid", "cell"), None),
        P(),
        P(),
        P(),
    )
    return jax.shard_map(
        on_device,
        mesh=mesh,
        in_specs=placed,
        out_specs=P(None, ("grid", "cell"), None),
        check_vma=False,
    )
```

```python
import functools
import math

import jax
import jax.numpy as jnp
import numpy as np
from jax import lax
from jax.experimental import pallas as pl
from jax.experimental.pallas import tpu as pltpu
from jax.sharding import PartitionSpec as P

NF = 36
ND = 36
SIDE = 4
ROWS = 4
COLS = 128
CELLS = ROWS * COLS
BINS = NF * ND
FLAT = BINS * ROWS
PAD = 8
PIECES = SIDE**3
TOGETHER = 3
PIECE = FLAT // PIECES
TALL = 88
BLOCK = 72
GROUP = 3
CHUNK = 432
WIDTH = 512
UNIT = 512.0
STEPS = 65534.0
OFFSET = 32767
VMEM_BYTES = 24 * 1024 * 1024
SMALL_BYTES = 10 * 1024 * 1024
LARGE_BYTES = 56 * 1024 * 1024
STACK = 8

FRACTIONS = (0.25, 0.5, 0.75, 1.0)


def fraction(frac_index):
    open_share = jnp.zeros(frac_index.shape, jnp.float32)
    for position, share in enumerate(FRACTIONS):
        open_share = open_share + jnp.where(frac_index == position, share, 0.0)
    return open_share


def place(z, y, x):
    return (z % SIDE * SIDE + y % SIDE) * SIDE + x % SIDE


def hub_places():
    last = SIDE - 1
    return [
        place(last, last, last),
        place(last, last, last - 1),
        place(last, last - 1, last),
        place(last - 1, last, last),
    ]


def cube_member(cube, position):
    zyx = [2 * (cube // d % 2) + position // d % 2 for d in (4, 2, 1)]
    return (zyx[0] * SIDE + zyx[1]) * SIDE + zyx[2]


CUBES = 8
DIRECT = (6, 5, 3)
PASSED = (4, 1, 2)
OWN, OPPOSITE = 7, 0


def own_flags():
    return 1 - lax.axis_index("cell"), jnp.where(lax.axis_index("grid") == PIECES - 1, 0, 1)


def bin_block(ref, index):
    return ref[8 * index : 8 * index + 8, :]


def send_kernel(map_ref, spec_ref, maps_ref, *part_refs):
    lane = lax.broadcasted_iota(jnp.int32, (PIECES, COLS), 1)
    maps = jnp.zeros((PIECES, COLS), jnp.int32)
    for r in range(ROWS):
        for side in range(2):
            maps = jnp.where(lane == 2 * r + side, map_ref[side, r], maps)
    maps_ref[...] = maps
    part = FLAT // SIDE
    for k, ref in enumerate(part_refs):
        ref[...] = spec_ref[(k + 1) * part : (k + 2) * part, :]


def send_first(maps, spec):
    vmem = pl.BlockSpec(memory_space=pltpu.VMEM)
    part = jax.ShapeDtypeStruct((FLAT // SIDE, COLS), jnp.bfloat16)
    return pl.pallas_call(
        send_kernel,
        out_shape=(jax.ShapeDtypeStruct((PIECES, COLS), jnp.int32),) + (part,) * (SIDE - 1),
        in_specs=[pl.BlockSpec(memory_space=pltpu.SMEM), vmem],
        out_specs=(vmem,) * SIDE,
        compiler_params=pltpu.CompilerParams(vmem_limit_bytes=LARGE_BYTES),
    )(maps, spec)


def pick_kernel(maps_ref, spec_ref, a_ref, b_ref, c_ref, out_ref, wide, turned, hot, mine, sem):
    part = FLAT // SIDE
    bins = part // ROWS
    share = jnp.where(own_flags()[1] == 0, 1.0, 0.0)
    copy = pltpu.make_async_copy(spec_ref.at[pl.ds(0, part), :], mine, sem)
    copy.start()
    cell = lax.broadcasted_iota(jnp.int32, (PIECES, CELLS), 1)
    for e in range(2 * ROWS):
        wanted = jnp.broadcast_to(maps_ref[:, e : e + 1], (PIECES, CELLS))
        same = jnp.where(cell == wanted, 1.0, 0.0).astype(jnp.bfloat16)
        hot[e * PIECES : (e + 1) * PIECES, :] = same
    copy.wait()

    def join(i, carry):
        for u in range(9):
            at = pl.multiple_of(i * 144 + u * 16, 16)
            here = pl.ds(at, 16)
            value = mine[here, :].astype(jnp.float32) * share
            for ref in (a_ref, b_ref, c_ref):
                value = value + ref[here, :].astype(jnp.float32)
            wide[here, :] = value
        return carry

    lax.fori_loop(0, part // 144, join, 0)
    wide[part:, :] = jnp.zeros((wide.shape[0] - part, COLS), jnp.float32)
    many = wide.shape[0] // ROWS
    held = [wide[pl.ds(r, many, stride=ROWS), :].astype(jnp.bfloat16) for r in range(ROWS)]
    held = jnp.concatenate(held, axis=1)
    found = lax.dot_general(
        hot[...], held, (((1,), (1,)), ((), ())), preferred_element_type=jnp.float32
    )
    for e in range(2 * ROWS):
        for t in range(many // COLS):
            part = found[e * PIECES : (e + 1) * PIECES, t * COLS : (t + 1) * COLS]
            turned[t, pl.ds(e, PIECES, stride=2 * ROWS), :] = part

    def narrower(i, carry):
        for u in range(8):
            g = i * 8 + u
            at = pl.multiple_of(g * 2 * ROWS, 8)
            for t in range(many // COLS):
                lanes = min(COLS, bins - t * COLS)
                value = turned[t, pl.ds(at, 2 * ROWS), :lanes].astype(jnp.bfloat16)
                out_ref[g, :, t * COLS : t * COLS + lanes] = value
        return carry

    lax.fori_loop(0, PIECES // 8, narrower, 0)


def pick(*operands):
    vmem = pl.BlockSpec(memory_space=pltpu.VMEM)
    part = FLAT // SIDE
    return pl.pallas_call(
        pick_kernel,
        out_shape=jax.ShapeDtypeStruct((PIECES, 2 * ROWS, part // ROWS), jnp.bfloat16),
        in_specs=[vmem, pl.BlockSpec(memory_space=pl.ANY)] + [vmem] * 3,
        out_specs=vmem,
        scratch_shapes=[
            pltpu.VMEM((3 * COLS * ROWS, COLS), jnp.float32),
            pltpu.VMEM((3, PIECES * 2 * ROWS, COLS), jnp.float32),
            pltpu.VMEM((PIECES * 2 * ROWS, CELLS), jnp.bfloat16),
            pltpu.VMEM((part, COLS), jnp.bfloat16),
            pltpu.SemaphoreType.DMA,
        ],
        compiler_params=pltpu.CompilerParams(vmem_limit_bytes=SMALL_BYTES),
    )(*operands)


def prepare_kernel(spec_ref, depth_ref, wet_ref, frac_ref, near_ref, stat_ref, dens):
    first = own_flags()[0] == 1
    wet = wet_ref[...].astype(jnp.float32)
    values = (depth_ref[...], wet * fraction(frac_ref[...]), wet)
    for i, value in enumerate(values):
        stat_ref[2 * i : 2 * i + 1, :] = jnp.where(first, value[3:4], value[0:1])
        stat_ref[2 * i + 1 : 2 * i + 2, :] = jnp.where(first, value[2:3], value[1:2])
    stat_ref[6:8, :] = jnp.zeros((2, COLS), jnp.float32)

    def widen(i, carry):
        for u in range(12):
            at = pl.multiple_of(i * 192 + u * 16, 16)
            dens[pl.ds(at, 16), :] = spec_ref[pl.ds(at, 16), :].astype(jnp.float32)
        return carry

    lax.fori_loop(0, FLAT // 192, widen, 0)
    nearer = 3 * own_flags()[0]
    farther = 1 + own_flags()[0]

    def pull(i, carry):
        for u in range(9):
            at = pl.multiple_of(i * 144 + u * 16, 16)
            for n, row in enumerate((nearer, farther)):
                rows = dens[pl.ds(at * ROWS + row, 16, stride=ROWS), :]
                near_ref[n, pl.ds(at, 16), :] = rows.astype(jnp.bfloat16)
        return carry

    lax.fori_loop(0, BINS // 144, pull, 0)


def prepare(*operands, interpret=False):
    vmem = pl.BlockSpec(memory_space=pltpu.VMEM)
    return pl.pallas_call(
        prepare_kernel,
        out_shape=(
            jax.ShapeDtypeStruct((2, BINS, COLS), jnp.bfloat16),
            jax.ShapeDtypeStruct((8, COLS), jnp.float32),
        ),
        in_specs=[vmem] * 4,
        out_specs=(vmem,) * 2,
        scratch_shapes=[pltpu.VMEM((FLAT, COLS), jnp.float32)],
        compiler_params=pltpu.CompilerParams(vmem_limit_bytes=SMALL_BYTES),
        cost_estimate=pl.CostEstimate(flops=4_000_000, bytes_accessed=5_000_000, transcendentals=0),
        interpret=interpret,
    )(*operands)


def step_kernel(
    plus_ref,
    minus_ref,
    speed_ref,
    coef_ref,
    spec_ref,
    near_ref,
    edge_ref,
    far_ref,
    spot_ref,
    depth_ref,
    wet_ref,
    frac_ref,
    stat_ref,
    cos_ref,
    sin_ref,
    cosb_ref,
    sinb_ref,
    target_ref,
    out_ref,
    pieces_ref,
    dens,
    flat,
    halo,
    evol,
    near,
    hot,
    count,
    tab_x,
    tab_y,
    tab_z,
    tab_an,
    tab_nb,
    tab_n,
    done_out,
    out_sem,
):
    first = own_flags()[0] == 1
    child = own_flags()[1]
    adjacent = 3 * own_flags()[0]
    sign = jnp.where(first, 1.0, -1.0)
    lane = lax.broadcasted_iota(jnp.int32, (16, COLS), 1)
    ends = jnp.where((lane == 0) | (lane == COLS - 1), child, 0) > 0

    values = jnp.concatenate([edge_ref[...], far_ref[...]], axis=0)
    spot = spot_ref[1 - own_flags()[0]]
    for base in range(0, BINS, WIDTH):
        wide_rows = min(WIDTH, BINS - base)
        laid = lax.dot_general(
            values[:, base : base + wide_rows],
            spot,
            (((0,), (0,)), ((), ())),
            preferred_element_type=jnp.float32,
        )
        lanes = lax.broadcasted_iota(jnp.int32, (wide_rows, COLS), 1)
        ends_wide = jnp.where((lanes == 0) | (lanes == COLS - 1), child, 0) > 0
        for r in range(ROWS):
            here = pl.ds(base * ROWS + r, wide_rows, stride=ROWS)
            flat[here, :] = laid[:, r * COLS : (r + 1) * COLS]
        for n in range(2):
            raw = near_ref[n, base : base + wide_rows, :].astype(jnp.float32)
            at = (ROWS + n) * COLS
            raw = jnp.where(ends_wide, laid[:, at : at + COLS], raw)
            near[n, base : base + wide_rows, :] = raw * stat_ref[4 + n : 5 + n, :]

    wet = jnp.concatenate([wet_ref[...]] * 2, axis=0).astype(jnp.float32)
    wet16 = jnp.concatenate([wet, wet], axis=0)

    def begin(i, carry):
        for u in range(12):
            at = pl.multiple_of(i * 192 + u * 16, 16)
            raw = spec_ref[pl.ds(at, 16), :].astype(jnp.float32)
            dens[pl.ds(PAD + at, 16), :] = jnp.where(ends, flat[pl.ds(at, 16), :], raw) * wet16
            halo[pl.ds(at, 16), :] = jnp.zeros((16, COLS), jnp.float32)
        return carry

    lax.fori_loop(0, FLAT // 192, begin, 0)

    sub = lax.broadcasted_iota(jnp.int32, (8, COLS), 0)
    low = sub < ROWS
    depth = jnp.concatenate([depth_ref[...]] * 2, axis=0)
    weight = wet * fraction(jnp.concatenate([frac_ref[...]] * 2, axis=0))

    def between(d0, d1, w0, w1):
        return 0.5 * (d0 + d1) * w0 * w1

    def along(d, w):
        face = between(d, pltpu.roll(d, COLS - 1, 1), w, pltpu.roll(w, COLS - 1, 1))
        return jnp.where(lane[:8] == COLS - 1, 0.0, face)

    def wide(row):
        return jnp.broadcast_to(row, (8, COLS))

    face_x = between(depth, pltpu.roll(depth, 7, 0), weight, pltpu.roll(weight, 7, 0))
    face_x = jnp.where(sub % ROWS == ROWS - 1, 0.0, face_x)
    face_y = along(depth, weight)
    d_own = wide(jnp.where(first, depth[3:4], depth[0:1]))
    w_own = wide(jnp.where(first, weight[3:4], weight[0:1]))
    d_n1, d_n2, w_n1, w_n2 = (wide(stat_ref[i : i + 1, :]) for i in range(4))
    face_an = between(d_own, d_n1, w_own, w_n1)
    face_nb = between(d_n1, d_n2, w_n1, w_n2)
    face_n = along(d_n1, w_n1)

    for q in range(ND // 2):
        tab_x[8 * q : 8 * q + 8, :] = face_x * bin_block(cos_ref, q)
        tab_y[8 * q : 8 * q + 8, :] = face_y * bin_block(sin_ref, q)
        if 2 * q > ND // 2:
            back = 8 * (q - ND // 4)
            tab_z[back : back + 8, :] = pltpu.roll(face_y, 1, 1) * bin_block(sin_ref, q)
    for j in range(BLOCK // 8):
        tab_an[8 * j : 8 * j + 8, :] = face_an * bin_block(cosb_ref, j)
        tab_nb[8 * j : 8 * j + 8, :] = face_nb * bin_block(cosb_ref, j)
        tab_n[8 * j : 8 * j + 8, :] = face_n * bin_block(sinb_ref, j)

    def halo_fluxes(bins, rows):
        many = range(BLOCK // 8)
        n1s = [near[0, pl.ds(bins + 8 * j, 8), :] for j in many]
        owns = [dens[pl.ds(PAD + rows + 32 * j + adjacent, 8, stride=ROWS), :] for j in many]
        fluxes = []
        for j in many:
            along = bin_block(tab_an, j)
            top = jnp.where(first, owns[j], n1s[j])
            bottom = jnp.where(first, n1s[j], owns[j])
            fluxes.append(jnp.maximum(along, 0.0) * top + jnp.minimum(along, 0.0) * bottom)
        for j in many:
            halo[pl.ds(rows + 32 * j + adjacent, 8, stride=ROWS), :] = sign * fluxes[j]
        return n1s, fluxes

    def advance_near(bins, speeds, n1s, fluxes):
        n2s = [near[1, pl.ds(bins + 8 * j, 8), :] for j in range(BLOCK // 8)]
        after_near = []
        for j in range(BLOCK // 8):
            n1, n2 = n1s[j], n2s[j]
            top, bottom = jnp.where(first, n1, n2), jnp.where(first, n2, n1)
            along = bin_block(tab_nb, j)
            beyond = jnp.maximum(along, 0.0) * top + jnp.minimum(along, 0.0) * bottom
            along = bin_block(tab_n, j)
            right = pltpu.roll(n1, COLS - 1, 1)
            fy = jnp.maximum(along, 0.0) * n1 + jnp.minimum(along, 0.0) * right
            change = sign * (beyond - fluxes[j]) + (fy - pltpu.roll(fy, 1, 1))
            speed = speeds[0] if j < 4 else (jnp.where(low, *speeds) if j == 4 else speeds[1])
            after_near.append(n1 - speed * change)
        for j in range(BLOCK // 8):
            near[0, pl.ds(bins + 8 * j, 8), :] = after_near[j]

    def advance(q, speed, rho, across):
        along_x = bin_block(tab_x, q)
        if 2 * q + 1 < ND // 4 or 2 * q > 3 * ND // 4:
            fx = along_x * rho
        else:
            after = pltpu.roll(rho, 7, 0)
            if ND // 4 < 2 * q and 2 * q + 1 < 3 * ND // 4:
                fx = along_x * after
            else:
                fx = jnp.maximum(along_x, 0.0) * rho + jnp.minimum(along_x, 0.0) * after
        along_y = bin_block(tab_y, q)
        if 2 * q + 1 < ND // 2:
            fy = along_y * rho
            out_y = fy - pltpu.roll(fy, 1, 1)
        elif 2 * q > ND // 2:
            out_y = along_y * pltpu.roll(rho, COLS - 1, 1) - bin_block(tab_z, q - ND // 4) * rho
        else:
            right = pltpu.roll(rho, COLS - 1, 1)
            fy = jnp.maximum(along_y, 0.0) * rho + jnp.minimum(along_y, 0.0) * right
            out_y = fy - pltpu.roll(fy, 1, 1)
        change = (fx - pltpu.roll(fx, 1, 0)) + out_y
        return rho - speed * (change + across)

    def advance_all(starts, speeds):
        for q in range(0, ND // 2, GROUP):
            group = [
                (p, rows + 8 * (p + h * ND // 2), speed[h])
                for p in range(q, q + GROUP)
                for rows, speed in zip(starts, speeds)
                for h in range(2)
            ]
            loaded = [(dens[pl.ds(PAD + at, 8), :], halo[pl.ds(at, 8), :]) for _, at, _ in group]
            moved = [advance(p, speed, *pair) for (p, _, speed), pair in zip(group, loaded)]
            for (_, at, _), value in zip(group, moved):
                dens[pl.ds(PAD + at, 8), :] = value

    def blocks(i, carry):
        ks = [i * TOGETHER + u for u in range(TOGETHER)]
        bins = [pl.multiple_of(k * BLOCK, 8) for k in ks]
        rows = [pl.multiple_of(k * (BLOCK * ROWS), 16) for k in ks]
        speeds = [(speed_ref[2 * k], speed_ref[2 * k + 1]) for k in ks]
        halos = [halo_fluxes(*pair) for pair in zip(bins, rows)]
        for start, speed, values in zip(bins, speeds, halos):
            advance_near(start, speed, *values)
        advance_all(rows, speeds)
        for pair in zip(bins, rows):
            halo_fluxes(*pair)
        advance_all(rows, speeds)
        return carry

    lax.fori_loop(0, BINS // BLOCK // TOGETHER, blocks, 0)

    def interact(f, carry):
        rows = pl.multiple_of(f * (ND * ROWS), 16)
        scale = 0.2 * coef_ref[f]

        def partner(ref, b):
            lower = dens[pl.ds(ref[f * ND + b], 8), :]
            upper = dens[pl.ds(ref[f * ND + b + 1] - ROWS, 8), :]
            return jnp.where(low, lower, upper)

        for g in range(ND // 4):
            done = []
            for h in range(2):
                b = 4 * g + 2 * h
                mine = dens[pl.ds(PAD + rows + 4 * b, 8), :]
                plus, minus = partner(plus_ref, b), partner(minus_ref, b)
                source = mine * (mine * (plus + minus) - 2.0 * (plus * minus))
                value = jnp.maximum(mine + scale * source, 0.0)
                evol[pl.ds(rows + 4 * b, 8), :] = value
                done.append(value)
            done_out[pl.ds(rows + 16 * g, 16), :] = jnp.concatenate(done, axis=0).astype(jnp.bfloat16)
        return carry

    lax.fori_loop(0, NF, interact, 0)
    leaving = pltpu.make_async_copy(done_out, out_ref, out_sem)
    leaving.start()

    row = lax.broadcasted_iota(jnp.int32, (CELLS, COLS), 0)
    for r in range(ROWS):
        own = lane[:1] + r * COLS
        same = row == jnp.where(child == 1, target_ref[r : r + 1, :], own)
        hot[:, r * COLS : (r + 1) * COLS] = jnp.where(same, 1.0, 0.0).astype(jnp.bfloat16)
    inner = (((1,), (1,)), ((), ()))
    number = lax.dot_general(
        jnp.ones((16, CELLS), jnp.bfloat16), hot[...], inner, preferred_element_type=jnp.float32
    )
    share = 1.0 / jnp.maximum(number[0:1], 1.0)
    count[...] = jnp.zeros_like(count)
    for turn in range(ROWS):
        for r in range(ROWS):
            of = (turn + r) % ROWS
            here = number[0:1, of * COLS : (of + 1) * COLS].astype(jnp.int32)
            count[turn, PIECE % 8 + r : PIECE % 8 + r + 1, :] = here

    many = CHUNK

    def sums(c, carry):
        base = c * (many * ROWS)
        parts = [evol[pl.ds(base + r, many, stride=ROWS), :] for r in range(ROWS)]
        value = jnp.concatenate(parts, axis=1)
        head = value.astype(jnp.bfloat16)
        tail = (value - head.astype(jnp.float32)).astype(jnp.bfloat16)
        total = lax.dot_general(head, hot[...], inner, preferred_element_type=jnp.float32)
        total += lax.dot_general(tail, hot[...], inner, preferred_element_type=jnp.float32)
        for r in range(ROWS):
            part = slice(r * COLS, (r + 1) * COLS)
            flat[pl.ds(base + r, many, stride=ROWS), :] = total[:, part] * share[:, part]
        return carry

    lax.fori_loop(0, BINS // many, sums, 0)
    main = PIECE // 8 * 8
    row = main + lax.broadcasted_iota(jnp.int32, (8, COLS), 0)

    def cut(i, carry):
        for turn in range(ROWS):
            j = i * ROWS + turn
            mean = flat[pl.ds(j * PIECE, main), :]
            last = jnp.where(row < PIECE, flat[pl.ds(j * PIECE + main, 8), :], 0.0)
            top = jnp.maximum(
                jnp.max(mean, axis=0, keepdims=True), jnp.max(last, axis=0, keepdims=True)
            )
            size = jnp.minimum((top * UNIT).astype(jnp.int32) + 1, OFFSET)
            steps = (UNIT * STEPS) / size.astype(jnp.float32)
            code = (mean * steps + 0.5).astype(jnp.int32) - OFFSET
            code_last = (last * steps + 0.5).astype(jnp.int32) - OFFSET
            rest = jnp.where(row == PIECE + ROWS, size, count[turn])
            code_last = jnp.where(row < PIECE, code_last, rest)
            code = jnp.concatenate([code, code_last], axis=0)
            pieces_ref[j] = code.astype(jnp.int16)
        return carry

    lax.fori_loop(0, PIECES // ROWS, cut, 0)
    leaving.wait()


def evolve(*operands, interpret=False):
    smem = pl.BlockSpec(memory_space=pltpu.SMEM)
    vmem = pl.BlockSpec(memory_space=pltpu.VMEM)
    return pl.pallas_call(
        step_kernel,
        out_shape=(
            jax.ShapeDtypeStruct((FLAT, COLS), jnp.bfloat16),
            jax.ShapeDtypeStruct((PIECES, TALL, COLS), jnp.int16),
        ),
        in_specs=[smem] * 4 + [vmem] * 14,
        out_specs=(pl.BlockSpec(memory_space=pl.ANY), vmem),
        scratch_shapes=[
            pltpu.VMEM((FLAT + 2 * PAD, COLS), jnp.float32),
            pltpu.VMEM((FLAT + 2 * PAD, COLS), jnp.float32),
            pltpu.VMEM((FLAT, COLS), jnp.float32),
            pltpu.VMEM((FLAT, COLS), jnp.float32),
            pltpu.VMEM((2, BINS, COLS), jnp.float32),
            pltpu.VMEM((CELLS, CELLS), jnp.bfloat16),
            pltpu.VMEM((ROWS, 8, COLS), jnp.int32),
            pltpu.VMEM((ND * ROWS, COLS), jnp.float32),
            pltpu.VMEM((ND * ROWS, COLS), jnp.float32),
            pltpu.VMEM((ND * ROWS // 2, COLS), jnp.float32),
            pltpu.VMEM((BLOCK, COLS), jnp.float32),
            pltpu.VMEM((BLOCK, COLS), jnp.float32),
            pltpu.VMEM((BLOCK, COLS), jnp.float32),
            pltpu.VMEM((FLAT, COLS), jnp.bfloat16),
            pltpu.SemaphoreType.DMA,
        ],
        compiler_params=pltpu.CompilerParams(vmem_limit_bytes=VMEM_BYTES),
        cost_estimate=pl.CostEstimate(
            flops=1_400_000_000, bytes_accessed=10_000_000, transcendentals=0
        ),
        interpret=interpret,
    )(*operands)


def average_kernel(pieces_ref, out_ref):
    blocks = TALL // 8
    sub = lax.broadcasted_iota(jnp.int32, (8, COLS), 0)

    def add(i, carry):
        sums, weights, number = carry
        for u in range(4):
            piece = pieces_ref[4 * i + u].astype(jnp.int32).astype(jnp.float32)
            rest = piece[TALL - 8 :]
            at = PIECE % 8
            turned = [pltpu.roll(rest, shift - at, 0) for shift in (8, ROWS)]
            count = jnp.where(sub < ROWS, *turned)
            weight = count * jnp.broadcast_to(rest[at + ROWS : at + ROWS + 1], (8, COLS))
            sums = tuple(sums[b] + piece[8 * b : 8 * b + 8] * weight for b in range(blocks))
            weights, number = weights + weight, number + count
        return sums, weights, number

    zero = jnp.zeros((8, COLS), jnp.float32)
    carry = ((zero,) * blocks, zero, zero)
    sums, weights, number = lax.fori_loop(0, PIECES // 4, add, carry)
    scale = 1.0 / (UNIT * STEPS * number)
    mean = jnp.concatenate([(part + OFFSET * weights) * scale for part in sums], axis=0)
    mean = mean.astype(jnp.bfloat16)

    def write(i, carry):
        out_ref[i] = mean
        return carry

    lax.fori_loop(0, STACK, write, 0)


def average(pieces, interpret=False):
    vmem = pl.BlockSpec(memory_space=pltpu.VMEM)
    return pl.pallas_call(
        average_kernel,
        out_shape=jax.ShapeDtypeStruct((STACK, TALL, COLS), jnp.bfloat16),
        in_specs=[vmem],
        out_specs=vmem,
        compiler_params=pltpu.CompilerParams(vmem_limit_bytes=SMALL_BYTES),
        interpret=interpret,
    )(pieces)


def lay_kernel(*refs):
    parts, (_, out_ref, wide, narrow, sems) = refs[:CUBES], refs[CUBES:]
    main = PIECE // 8 * 8

    @pl.when(own_flags()[1] == 0)
    def _():
        for cube, ref in zip((OWN,) + DIRECT + (OPPOSITE,) + PASSED, parts):
            for i in range(STACK):
                at = cube_member(cube, i) * PIECE
                piece = ref[i].astype(jnp.float32)
                wide[at : at + main, :] = piece[:main]
                wide[at + main : at + PIECE, :] = piece[main:PIECE]

        part = FLAT // SIDE
        copies = []
        for k in range(SIDE):

            def narrower(i, carry):
                for u in range(9):
                    at = pl.multiple_of(k * part + i * 144 + u * 16, 16)
                    narrow[pl.ds(at, 16), :] = wide[pl.ds(at, 16), :].astype(jnp.bfloat16)
                return carry

            lax.fori_loop(0, part // 144, narrower, 0)
            here = pl.ds(k * part, part)
            copies.append(pltpu.make_async_copy(narrow.at[here], out_ref.at[here], sems.at[k]))
            copies[k].start()
        for copy in copies:
            copy.wait()


def lay(parts, evolved):
    vmem = pl.BlockSpec(memory_space=pltpu.VMEM)
    anywhere = pl.BlockSpec(memory_space=pl.ANY)
    return pl.pallas_call(
        lay_kernel,
        out_shape=jax.ShapeDtypeStruct((FLAT, COLS), jnp.bfloat16),
        in_specs=[vmem] * CUBES + [anywhere],
        out_specs=anywhere,
        scratch_shapes=[
            pltpu.VMEM((FLAT + 2 * PAD, COLS), jnp.float32),
            pltpu.VMEM((FLAT, COLS), jnp.bfloat16),
            pltpu.SemaphoreType.DMA((SIDE,)),
        ],
        input_output_aliases={CUBES: 0},
        compiler_params=pltpu.CompilerParams(vmem_limit_bytes=SMALL_BYTES),
    )(*parts, evolved)


def tables():
    group_speed = 0.45 * np.exp(-math.log(1.1) * np.arange(NF))
    angles = 2.0 * math.pi / ND * np.arange(ND)

    def wide(values, times):
        return np.repeat(np.repeat(values, times)[:, None], COLS, axis=1).astype(np.float32)

    cosine, sine = np.cos(angles), np.sin(angles)
    twice = BLOCK // ND
    per_row = (wide(cosine, ROWS), wide(sine, ROWS))
    per_bin = (wide(np.tile(cosine, twice), 1), wide(np.tile(sine, twice), 1))
    return (group_speed.astype(np.float32),) + per_row + per_bin


def spots():
    both = []
    for cell in range(2):
        chosen = np.zeros((4 * ROWS, (ROWS + 2) * COLS), np.float32)
        near = (ROWS - 1, ROWS - 2) if cell else (0, 1)
        for block, source in enumerate(tuple(range(ROWS)) + tuple(ROWS + row for row in near)):
            chosen[2 * source, block * COLS] = 1.0
            chosen[2 * source + 1, (block + 1) * COLS - 1] = 1.0
        both.append(chosen)
    return np.stack(both).astype(jnp.bfloat16)


def swap(x):
    return lax.ppermute(x, "cell", [(0, 1), (1, 0)])


def on_device(
    spectrum,
    depth_factor,
    wet_mask,
    frac_index,
    boundary_map,
    average_map,
    dia_plus,
    dia_minus,
    dia_coef,
):
    parent = lax.axis_size("grid") - 1
    hubs = hub_places()
    spec = spectrum.reshape(FLAT, COLS)
    maps, *parts = send_first(boundary_map.T, spec)

    held = [lax.ppermute(part, "grid", [(parent, hub)]) for part, hub in zip(parts, hubs[1:])]
    maps = lax.all_to_all(maps, "grid", 0, 0)
    near, near_statics = prepare(spec, depth_factor, wet_mask, frac_index)
    near = swap(near)
    near_statics = swap(near_statics)
    picked = lax.all_to_all(pick(maps, spec, *held), "grid", 0, 0)
    picked = jnp.concatenate([picked[hub] for hub in hubs], axis=1)
    far = swap(picked)

    group_speed, cosine, sine, cosine_bin, sine_bin = tables()
    evolved, pieces = evolve(
        dia_plus * ROWS + PAD,
        dia_minus * ROWS + PAD,
        group_speed,
        dia_coef,
        spec,
        near,
        picked,
        far,
        spots(),
        depth_factor,
        wet_mask,
        frac_index,
        near_statics,
        cosine,
        sine,
        cosine_bin,
        sine_bin,
        average_map,
    )
    copies = average(lax.all_to_all(pieces, "grid", 0, 0))
    last = SIDE - 1
    cubes = [[cube_member(k, i) for i in range(STACK)] for k in range(CUBES)]
    gathered = lax.all_to_all(copies, "grid", 0, 0, axis_index_groups=cubes)
    wrapping = [place(last, last, 0), place(last, 0, last), place(0, last, last)]
    inside = [place(last, last, last - 1), place(last, last - 1, last), place(last - 1, last, last)]
    far = [place(last, 0, 1), place(0, 1, last), place(1, last, 0)]
    relayed = lax.ppermute(gathered, "grid", list(zip(far, inside)))
    near_by = wrapping + [place(0, 0, 0)]
    parts = [lax.ppermute(gathered, "grid", [(device, parent)]) for device in near_by]
    parts += [lax.ppermute(relayed, "grid", [(device, parent)]) for device in inside]
    parts = [gathered] + parts
    return lay(parts, evolved).reshape(BINS, ROWS, COLS)


def solution(mesh):
    placed = (
        P(None, ("grid", "cell"), None),
        P(("grid", "cell"), None),
        P(("grid", "cell"), None),
        P(("grid", "cell"), None),
        P(("grid", "cell"), None),
        P(("grid", "cell"), None),
        P(),
        P(),
        P(),
    )
    return jax.shard_map(
        on_device,
        mesh=mesh,
        in_specs=placed,
        out_specs=P(None, ("grid", "cell"), None),
        check_vma=False,
    )
```

```python
import functools
import math

import jax
import jax.numpy as jnp
import numpy as np
from jax import lax
from jax.experimental import pallas as pl
from jax.experimental.pallas import tpu as pltpu
from jax.sharding import PartitionSpec as P

NF = 36
ND = 36
SIDE = 4
ROWS = 4
COLS = 128
CELLS = ROWS * COLS
BINS = NF * ND
FLAT = BINS * ROWS
PAD = 8
PIECES = SIDE**3
TOGETHER = 3
PIECE = FLAT // PIECES
TALL = 88
BLOCK = 72
GROUP = 3
CHUNK = 432
WIDTH = 512
UNIT = 512.0
STEPS = 65534.0
OFFSET = 32767
VMEM_BYTES = 24 * 1024 * 1024
SMALL_BYTES = 10 * 1024 * 1024
LARGE_BYTES = 56 * 1024 * 1024
STACK = 8

FRACTIONS = (0.25, 0.5, 0.75, 1.0)


def fraction(frac_index):
    open_share = jnp.zeros(frac_index.shape, jnp.float32)
    for position, share in enumerate(FRACTIONS):
        open_share = open_share + jnp.where(frac_index == position, share, 0.0)
    return open_share


def place(z, y, x):
    return (z % SIDE * SIDE + y % SIDE) * SIDE + x % SIDE


def hub_places():
    last = SIDE - 1
    return [
        place(last, last, last),
        place(last, last, last - 1),
        place(last, last - 1, last),
        place(last - 1, last, last),
    ]


def cube_member(cube, position):
    zyx = [2 * (cube // d % 2) + position // d % 2 for d in (4, 2, 1)]
    return (zyx[0] * SIDE + zyx[1]) * SIDE + zyx[2]


CUBES = 8
DIRECT = (6, 5, 3)
PASSED = (4, 1, 2, 0)
OWN = 7


def own_flags():
    return 1 - lax.axis_index("cell"), jnp.where(lax.axis_index("grid") == PIECES - 1, 0, 1)


def bin_block(ref, index):
    return ref[8 * index : 8 * index + 8, :]


def send_kernel(map_ref, spec_ref, maps_ref, *part_refs):
    lane = lax.broadcasted_iota(jnp.int32, (PIECES, COLS), 1)
    maps = jnp.zeros((PIECES, COLS), jnp.int32)
    for r in range(ROWS):
        for side in range(2):
            maps = jnp.where(lane == 2 * r + side, map_ref[side, r], maps)
    maps_ref[...] = maps
    part = FLAT // SIDE
    for k, ref in enumerate(part_refs):
        ref[...] = spec_ref[(k + 1) * part : (k + 2) * part, :]


def send_first(maps, spec):
    vmem = pl.BlockSpec(memory_space=pltpu.VMEM)
    part = jax.ShapeDtypeStruct((FLAT // SIDE, COLS), jnp.bfloat16)
    return pl.pallas_call(
        send_kernel,
        out_shape=(jax.ShapeDtypeStruct((PIECES, COLS), jnp.int32),) + (part,) * (SIDE - 1),
        in_specs=[pl.BlockSpec(memory_space=pltpu.SMEM), vmem],
        out_specs=(vmem,) * SIDE,
        compiler_params=pltpu.CompilerParams(vmem_limit_bytes=LARGE_BYTES),
    )(maps, spec)


def pick_kernel(maps_ref, spec_ref, a_ref, b_ref, c_ref, out_ref, wide, turned, hot, mine, sem):
    part = FLAT // SIDE
    bins = part // ROWS
    share = jnp.where(own_flags()[1] == 0, 1.0, 0.0)
    copy = pltpu.make_async_copy(spec_ref.at[pl.ds(0, part), :], mine, sem)
    copy.start()
    cell = lax.broadcasted_iota(jnp.int32, (PIECES, CELLS), 1)
    for e in range(2 * ROWS):
        wanted = jnp.broadcast_to(maps_ref[:, e : e + 1], (PIECES, CELLS))
        same = jnp.where(cell == wanted, 1.0, 0.0).astype(jnp.bfloat16)
        hot[e * PIECES : (e + 1) * PIECES, :] = same
    copy.wait()

    def join(i, carry):
        for u in range(9):
            at = pl.multiple_of(i * 144 + u * 16, 16)
            here = pl.ds(at, 16)
            value = mine[here, :].astype(jnp.float32) * share
            for ref in (a_ref, b_ref, c_ref):
                value = value + ref[here, :].astype(jnp.float32)
            wide[here, :] = value
        return carry

    lax.fori_loop(0, part // 144, join, 0)
    wide[part:, :] = jnp.zeros((wide.shape[0] - part, COLS), jnp.float32)
    many = wide.shape[0] // ROWS
    held = [wide[pl.ds(r, many, stride=ROWS), :].astype(jnp.bfloat16) for r in range(ROWS)]
    held = jnp.concatenate(held, axis=1)
    found = lax.dot_general(
        hot[...], held, (((1,), (1,)), ((), ())), preferred_element_type=jnp.float32
    )
    for e in range(2 * ROWS):
        for t in range(many // COLS):
            part = found[e * PIECES : (e + 1) * PIECES, t * COLS : (t + 1) * COLS]
            turned[t, pl.ds(e, PIECES, stride=2 * ROWS), :] = part

    def narrower(i, carry):
        for u in range(8):
            g = i * 8 + u
            at = pl.multiple_of(g * 2 * ROWS, 8)
            for t in range(many // COLS):
                lanes = min(COLS, bins - t * COLS)
                value = turned[t, pl.ds(at, 2 * ROWS), :lanes].astype(jnp.bfloat16)
                out_ref[g, :, t * COLS : t * COLS + lanes] = value
        return carry

    lax.fori_loop(0, PIECES // 8, narrower, 0)


def pick(*operands):
    vmem = pl.BlockSpec(memory_space=pltpu.VMEM)
    part = FLAT // SIDE
    return pl.pallas_call(
        pick_kernel,
        out_shape=jax.ShapeDtypeStruct((PIECES, 2 * ROWS, part // ROWS), jnp.bfloat16),
        in_specs=[vmem, pl.BlockSpec(memory_space=pl.ANY)] + [vmem] * 3,
        out_specs=vmem,
        scratch_shapes=[
            pltpu.VMEM((3 * COLS * ROWS, COLS), jnp.float32),
            pltpu.VMEM((3, PIECES * 2 * ROWS, COLS), jnp.float32),
            pltpu.VMEM((PIECES * 2 * ROWS, CELLS), jnp.bfloat16),
            pltpu.VMEM((part, COLS), jnp.bfloat16),
            pltpu.SemaphoreType.DMA,
        ],
        compiler_params=pltpu.CompilerParams(vmem_limit_bytes=SMALL_BYTES),
    )(*operands)


def prepare_kernel(spec_ref, depth_ref, wet_ref, frac_ref, near_ref, stat_ref, dens):
    first = own_flags()[0] == 1
    wet = wet_ref[...].astype(jnp.float32)
    values = (depth_ref[...], wet * fraction(frac_ref[...]), wet)
    for i, value in enumerate(values):
        stat_ref[2 * i : 2 * i + 1, :] = jnp.where(first, value[3:4], value[0:1])
        stat_ref[2 * i + 1 : 2 * i + 2, :] = jnp.where(first, value[2:3], value[1:2])
    stat_ref[6:8, :] = jnp.zeros((2, COLS), jnp.float32)

    def widen(i, carry):
        for u in range(12):
            at = pl.multiple_of(i * 192 + u * 16, 16)
            dens[pl.ds(at, 16), :] = spec_ref[pl.ds(at, 16), :].astype(jnp.float32)
        return carry

    lax.fori_loop(0, FLAT // 192, widen, 0)
    nearer = 3 * own_flags()[0]
    farther = 1 + own_flags()[0]

    def pull(i, carry):
        for u in range(9):
            at = pl.multiple_of(i * 144 + u * 16, 16)
            for n, row in enumerate((nearer, farther)):
                rows = dens[pl.ds(at * ROWS + row, 16, stride=ROWS), :]
                near_ref[n, pl.ds(at, 16), :] = rows.astype(jnp.bfloat16)
        return carry

    lax.fori_loop(0, BINS // 144, pull, 0)


def prepare(*operands, interpret=False):
    vmem = pl.BlockSpec(memory_space=pltpu.VMEM)
    return pl.pallas_call(
        prepare_kernel,
        out_shape=(
            jax.ShapeDtypeStruct((2, BINS, COLS), jnp.bfloat16),
            jax.ShapeDtypeStruct((8, COLS), jnp.float32),
        ),
        in_specs=[vmem] * 4,
        out_specs=(vmem,) * 2,
        scratch_shapes=[pltpu.VMEM((FLAT, COLS), jnp.float32)],
        compiler_params=pltpu.CompilerParams(vmem_limit_bytes=SMALL_BYTES),
        cost_estimate=pl.CostEstimate(flops=4_000_000, bytes_accessed=5_000_000, transcendentals=0),
        interpret=interpret,
    )(*operands)


def step_kernel(
    plus_ref,
    minus_ref,
    speed_ref,
    coef_ref,
    spec_ref,
    near_ref,
    edge_ref,
    far_ref,
    spot_ref,
    depth_ref,
    wet_ref,
    frac_ref,
    stat_ref,
    cos_ref,
    sin_ref,
    cosb_ref,
    sinb_ref,
    target_ref,
    out_ref,
    pieces_ref,
    dens,
    flat,
    halo,
    evol,
    near,
    hot,
    count,
    tab_x,
    tab_y,
    tab_z,
    tab_an,
    tab_nb,
    tab_n,
    done_out,
    out_sem,
):
    first = own_flags()[0] == 1
    child = own_flags()[1]
    adjacent = 3 * own_flags()[0]
    sign = jnp.where(first, 1.0, -1.0)
    lane = lax.broadcasted_iota(jnp.int32, (16, COLS), 1)
    ends = jnp.where((lane == 0) | (lane == COLS - 1), child, 0) > 0

    values = jnp.concatenate([edge_ref[...], far_ref[...]], axis=0)
    spot = spot_ref[1 - own_flags()[0]]
    for base in range(0, BINS, WIDTH):
        wide_rows = min(WIDTH, BINS - base)
        laid = lax.dot_general(
            values[:, base : base + wide_rows],
            spot,
            (((0,), (0,)), ((), ())),
            preferred_element_type=jnp.float32,
        )
        lanes = lax.broadcasted_iota(jnp.int32, (wide_rows, COLS), 1)
        ends_wide = jnp.where((lanes == 0) | (lanes == COLS - 1), child, 0) > 0
        for r in range(ROWS):
            here = pl.ds(base * ROWS + r, wide_rows, stride=ROWS)
            flat[here, :] = laid[:, r * COLS : (r + 1) * COLS]
        for n in range(2):
            raw = near_ref[n, base : base + wide_rows, :].astype(jnp.float32)
            at = (ROWS + n) * COLS
            raw = jnp.where(ends_wide, laid[:, at : at + COLS], raw)
            near[n, base : base + wide_rows, :] = raw * stat_ref[4 + n : 5 + n, :]

    wet = jnp.concatenate([wet_ref[...]] * 2, axis=0).astype(jnp.float32)
    wet16 = jnp.concatenate([wet, wet], axis=0)

    def begin(i, carry):
        for u in range(12):
            at = pl.multiple_of(i * 192 + u * 16, 16)
            raw = spec_ref[pl.ds(at, 16), :].astype(jnp.float32)
            dens[pl.ds(PAD + at, 16), :] = jnp.where(ends, flat[pl.ds(at, 16), :], raw) * wet16
            halo[pl.ds(at, 16), :] = jnp.zeros((16, COLS), jnp.float32)
        return carry

    lax.fori_loop(0, FLAT // 192, begin, 0)

    sub = lax.broadcasted_iota(jnp.int32, (8, COLS), 0)
    low = sub < ROWS
    depth = jnp.concatenate([depth_ref[...]] * 2, axis=0)
    weight = wet * fraction(jnp.concatenate([frac_ref[...]] * 2, axis=0))

    def between(d0, d1, w0, w1):
        return 0.5 * (d0 + d1) * w0 * w1

    def along(d, w):
        face = between(d, pltpu.roll(d, COLS - 1, 1), w, pltpu.roll(w, COLS - 1, 1))
        return jnp.where(lane[:8] == COLS - 1, 0.0, face)

    def wide(row):
        return jnp.broadcast_to(row, (8, COLS))

    face_x = between(depth, pltpu.roll(depth, 7, 0), weight, pltpu.roll(weight, 7, 0))
    face_x = jnp.where(sub % ROWS == ROWS - 1, 0.0, face_x)
    face_y = along(depth, weight)
    d_own = wide(jnp.where(first, depth[3:4], depth[0:1]))
    w_own = wide(jnp.where(first, weight[3:4], weight[0:1]))
    d_n1, d_n2, w_n1, w_n2 = (wide(stat_ref[i : i + 1, :]) for i in range(4))
    face_an = between(d_own, d_n1, w_own, w_n1)
    face_nb = between(d_n1, d_n2, w_n1, w_n2)
    face_n = along(d_n1, w_n1)

    for q in range(ND // 2):
        tab_x[8 * q : 8 * q + 8, :] = face_x * bin_block(cos_ref, q)
        tab_y[8 * q : 8 * q + 8, :] = face_y * bin_block(sin_ref, q)
        if 2 * q > ND // 2:
            back = 8 * (q - ND // 4)
            tab_z[back : back + 8, :] = pltpu.roll(face_y, 1, 1) * bin_block(sin_ref, q)
    for j in range(BLOCK // 8):
        tab_an[8 * j : 8 * j + 8, :] = face_an * bin_block(cosb_ref, j)
        tab_nb[8 * j : 8 * j + 8, :] = face_nb * bin_block(cosb_ref, j)
        tab_n[8 * j : 8 * j + 8, :] = face_n * bin_block(sinb_ref, j)

    def halo_fluxes(bins, rows):
        many = range(BLOCK // 8)
        n1s = [near[0, pl.ds(bins + 8 * j, 8), :] for j in many]
        owns = [dens[pl.ds(PAD + rows + 32 * j + adjacent, 8, stride=ROWS), :] for j in many]
        fluxes = []
        for j in many:
            along = bin_block(tab_an, j)
            top = jnp.where(first, owns[j], n1s[j])
            bottom = jnp.where(first, n1s[j], owns[j])
            fluxes.append(jnp.maximum(along, 0.0) * top + jnp.minimum(along, 0.0) * bottom)
        for j in many:
            halo[pl.ds(rows + 32 * j + adjacent, 8, stride=ROWS), :] = sign * fluxes[j]
        return n1s, fluxes

    def advance_near(bins, speeds, n1s, fluxes):
        n2s = [near[1, pl.ds(bins + 8 * j, 8), :] for j in range(BLOCK // 8)]
        after_near = []
        for j in range(BLOCK // 8):
            n1, n2 = n1s[j], n2s[j]
            top, bottom = jnp.where(first, n1, n2), jnp.where(first, n2, n1)
            along = bin_block(tab_nb, j)
            beyond = jnp.maximum(along, 0.0) * top + jnp.minimum(along, 0.0) * bottom
            along = bin_block(tab_n, j)
            right = pltpu.roll(n1, COLS - 1, 1)
            fy = jnp.maximum(along, 0.0) * n1 + jnp.minimum(along, 0.0) * right
            change = sign * (beyond - fluxes[j]) + (fy - pltpu.roll(fy, 1, 1))
            speed = speeds[0] if j < 4 else (jnp.where(low, *speeds) if j == 4 else speeds[1])
            after_near.append(n1 - speed * change)
        for j in range(BLOCK // 8):
            near[0, pl.ds(bins + 8 * j, 8), :] = after_near[j]

    def advance(q, speed, rho, across):
        along_x = bin_block(tab_x, q)
        if 2 * q + 1 < ND // 4 or 2 * q > 3 * ND // 4:
            fx = along_x * rho
        else:
            after = pltpu.roll(rho, 7, 0)
            if ND // 4 < 2 * q and 2 * q + 1 < 3 * ND // 4:
                fx = along_x * after
            else:
                fx = jnp.maximum(along_x, 0.0) * rho + jnp.minimum(along_x, 0.0) * after
        along_y = bin_block(tab_y, q)
        if 2 * q + 1 < ND // 2:
            fy = along_y * rho
            out_y = fy - pltpu.roll(fy, 1, 1)
        elif 2 * q > ND // 2:
            out_y = along_y * pltpu.roll(rho, COLS - 1, 1) - bin_block(tab_z, q - ND // 4) * rho
        else:
            right = pltpu.roll(rho, COLS - 1, 1)
            fy = jnp.maximum(along_y, 0.0) * rho + jnp.minimum(along_y, 0.0) * right
            out_y = fy - pltpu.roll(fy, 1, 1)
        change = (fx - pltpu.roll(fx, 1, 0)) + out_y
        return rho - speed * (change + across)

    def advance_all(starts, speeds):
        for q in range(0, ND // 2, GROUP):
            group = [
                (p, rows + 8 * (p + h * ND // 2), speed[h])
                for p in range(q, q + GROUP)
                for rows, speed in zip(starts, speeds)
                for h in range(2)
            ]
            loaded = [(dens[pl.ds(PAD + at, 8), :], halo[pl.ds(at, 8), :]) for _, at, _ in group]
            moved = [advance(p, speed, *pair) for (p, _, speed), pair in zip(group, loaded)]
            for (_, at, _), value in zip(group, moved):
                dens[pl.ds(PAD + at, 8), :] = value

    def blocks(i, carry):
        ks = [i * TOGETHER + u for u in range(TOGETHER)]
        bins = [pl.multiple_of(k * BLOCK, 8) for k in ks]
        rows = [pl.multiple_of(k * (BLOCK * ROWS), 16) for k in ks]
        speeds = [(speed_ref[2 * k], speed_ref[2 * k + 1]) for k in ks]
        halos = [halo_fluxes(*pair) for pair in zip(bins, rows)]
        for start, speed, values in zip(bins, speeds, halos):
            advance_near(start, speed, *values)
        advance_all(rows, speeds)
        for pair in zip(bins, rows):
            halo_fluxes(*pair)
        advance_all(rows, speeds)
        return carry

    lax.fori_loop(0, BINS // BLOCK // TOGETHER, blocks, 0)

    def interact(f, carry):
        rows = pl.multiple_of(f * (ND * ROWS), 16)
        scale = 0.2 * coef_ref[f]

        def partner(ref, b):
            lower = dens[pl.ds(ref[f * ND + b], 8), :]
            upper = dens[pl.ds(ref[f * ND + b + 1] - ROWS, 8), :]
            return jnp.where(low, lower, upper)

        for g in range(ND // 4):
            done = []
            for h in range(2):
                b = 4 * g + 2 * h
                mine = dens[pl.ds(PAD + rows + 4 * b, 8), :]
                plus, minus = partner(plus_ref, b), partner(minus_ref, b)
                source = mine * (mine * (plus + minus) - 2.0 * (plus * minus))
                value = jnp.maximum(mine + scale * source, 0.0)
                evol[pl.ds(rows + 4 * b, 8), :] = value
                done.append(value)
            done_out[pl.ds(rows + 16 * g, 16), :] = jnp.concatenate(done, axis=0).astype(jnp.bfloat16)
        return carry

    lax.fori_loop(0, NF, interact, 0)
    leaving = pltpu.make_async_copy(done_out, out_ref, out_sem)
    leaving.start()

    row = lax.broadcasted_iota(jnp.int32, (CELLS, COLS), 0)
    for r in range(ROWS):
        own = lane[:1] + r * COLS
        same = row == jnp.where(child == 1, target_ref[r : r + 1, :], own)
        hot[:, r * COLS : (r + 1) * COLS] = jnp.where(same, 1.0, 0.0).astype(jnp.bfloat16)
    inner = (((1,), (1,)), ((), ()))
    number = lax.dot_general(
        jnp.ones((16, CELLS), jnp.bfloat16), hot[...], inner, preferred_element_type=jnp.float32
    )
    share = 1.0 / jnp.maximum(number[0:1], 1.0)
    count[...] = jnp.zeros_like(count)
    for turn in range(ROWS):
        for r in range(ROWS):
            of = (turn + r) % ROWS
            here = number[0:1, of * COLS : (of + 1) * COLS].astype(jnp.int32)
            count[turn, PIECE % 8 + r : PIECE % 8 + r + 1, :] = here

    many = CHUNK

    def sums(c, carry):
        base = c * (many * ROWS)
        parts = [evol[pl.ds(base + r, many, stride=ROWS), :] for r in range(ROWS)]
        value = jnp.concatenate(parts, axis=1)
        head = value.astype(jnp.bfloat16)
        tail = (value - head.astype(jnp.float32)).astype(jnp.bfloat16)
        total = lax.dot_general(head, hot[...], inner, preferred_element_type=jnp.float32)
        total += lax.dot_general(tail, hot[...], inner, preferred_element_type=jnp.float32)
        for r in range(ROWS):
            part = slice(r * COLS, (r + 1) * COLS)
            flat[pl.ds(base + r, many, stride=ROWS), :] = total[:, part] * share[:, part]
        return carry

    lax.fori_loop(0, BINS // many, sums, 0)
    main = PIECE // 8 * 8
    row = main + lax.broadcasted_iota(jnp.int32, (8, COLS), 0)

    def cut(i, carry):
        for turn in range(ROWS):
            j = i * ROWS + turn
            mean = flat[pl.ds(j * PIECE, main), :]
            last = jnp.where(row < PIECE, flat[pl.ds(j * PIECE + main, 8), :], 0.0)
            top = jnp.maximum(
                jnp.max(mean, axis=0, keepdims=True), jnp.max(last, axis=0, keepdims=True)
            )
            size = jnp.minimum((top * UNIT).astype(jnp.int32) + 1, OFFSET)
            steps = (UNIT * STEPS) / size.astype(jnp.float32)
            code = (mean * steps + 0.5).astype(jnp.int32) - OFFSET
            code_last = (last * steps + 0.5).astype(jnp.int32) - OFFSET
            rest = jnp.where(row == PIECE + ROWS, size, count[turn])
            code_last = jnp.where(row < PIECE, code_last, rest)
            code = jnp.concatenate([code, code_last], axis=0)
            pieces_ref[j] = code.astype(jnp.int16)
        return carry

    lax.fori_loop(0, PIECES // ROWS, cut, 0)
    leaving.wait()


def evolve(*operands, interpret=False):
    smem = pl.BlockSpec(memory_space=pltpu.SMEM)
    vmem = pl.BlockSpec(memory_space=pltpu.VMEM)
    return pl.pallas_call(
        step_kernel,
        out_shape=(
            jax.ShapeDtypeStruct((FLAT, COLS), jnp.bfloat16),
            jax.ShapeDtypeStruct((PIECES, TALL, COLS), jnp.int16),
        ),
        in_specs=[smem] * 4 + [vmem] * 14,
        out_specs=(pl.BlockSpec(memory_space=pl.ANY), vmem),
        scratch_shapes=[
            pltpu.VMEM((FLAT + 2 * PAD, COLS), jnp.float32),
            pltpu.VMEM((FLAT + 2 * PAD, COLS), jnp.float32),
            pltpu.VMEM((FLAT, COLS), jnp.float32),
            pltpu.VMEM((FLAT, COLS), jnp.float32),
            pltpu.VMEM((2, BINS, COLS), jnp.float32),
            pltpu.VMEM((CELLS, CELLS), jnp.bfloat16),
            pltpu.VMEM((ROWS, 8, COLS), jnp.int32),
            pltpu.VMEM((ND * ROWS, COLS), jnp.float32),
            pltpu.VMEM((ND * ROWS, COLS), jnp.float32),
            pltpu.VMEM((ND * ROWS // 2, COLS), jnp.float32),
            pltpu.VMEM((BLOCK, COLS), jnp.float32),
            pltpu.VMEM((BLOCK, COLS), jnp.float32),
            pltpu.VMEM((BLOCK, COLS), jnp.float32),
            pltpu.VMEM((FLAT, COLS), jnp.bfloat16),
            pltpu.SemaphoreType.DMA,
        ],
        compiler_params=pltpu.CompilerParams(vmem_limit_bytes=VMEM_BYTES),
        cost_estimate=pl.CostEstimate(
            flops=1_400_000_000, bytes_accessed=10_000_000, transcendentals=0
        ),
        interpret=interpret,
    )(*operands)


def average_kernel(pieces_ref, out_ref):
    blocks = TALL // 8
    sub = lax.broadcasted_iota(jnp.int32, (8, COLS), 0)

    def add(i, carry):
        sums, weights, number = carry
        for u in range(4):
            piece = pieces_ref[4 * i + u].astype(jnp.int32).astype(jnp.float32)
            rest = piece[TALL - 8 :]
            at = PIECE % 8
            turned = [pltpu.roll(rest, shift - at, 0) for shift in (8, ROWS)]
            count = jnp.where(sub < ROWS, *turned)
            weight = count * jnp.broadcast_to(rest[at + ROWS : at + ROWS + 1], (8, COLS))
            sums = tuple(sums[b] + piece[8 * b : 8 * b + 8] * weight for b in range(blocks))
            weights, number = weights + weight, number + count
        return sums, weights, number

    zero = jnp.zeros((8, COLS), jnp.float32)
    carry = ((zero,) * blocks, zero, zero)
    sums, weights, number = lax.fori_loop(0, PIECES // 4, add, carry)
    scale = 1.0 / (UNIT * STEPS * number)
    mean = jnp.concatenate([(part + OFFSET * weights) * scale for part in sums], axis=0)
    mean = mean.astype(jnp.bfloat16)

    def write(i, carry):
        out_ref[i] = mean
        return carry

    lax.fori_loop(0, STACK, write, 0)


def average(pieces, interpret=False):
    vmem = pl.BlockSpec(memory_space=pltpu.VMEM)
    return pl.pallas_call(
        average_kernel,
        out_shape=jax.ShapeDtypeStruct((STACK, TALL, COLS), jnp.bfloat16),
        in_specs=[vmem],
        out_specs=vmem,
        compiler_params=pltpu.CompilerParams(vmem_limit_bytes=SMALL_BYTES),
        interpret=interpret,
    )(pieces)


def lay_kernel(*refs):
    parts, (_, out_ref, wide, narrow, sems) = refs[:CUBES], refs[CUBES:]
    main = PIECE // 8 * 8

    @pl.when(own_flags()[1] == 0)
    def _():
        for cube, ref in zip((OWN,) + DIRECT + PASSED, parts):
            for i in range(STACK):
                at = cube_member(cube, i) * PIECE
                piece = ref[i].astype(jnp.float32)
                wide[at : at + main, :] = piece[:main]
                wide[at + main : at + PIECE, :] = piece[main:PIECE]

        part = FLAT // SIDE
        copies = []
        for k in range(SIDE):

            def narrower(i, carry):
                for u in range(9):
                    at = pl.multiple_of(k * part + i * 144 + u * 16, 16)
                    narrow[pl.ds(at, 16), :] = wide[pl.ds(at, 16), :].astype(jnp.bfloat16)
                return carry

            lax.fori_loop(0, part // 144, narrower, 0)
            here = pl.ds(k * part, part)
            copies.append(pltpu.make_async_copy(narrow.at[here], out_ref.at[here], sems.at[k]))
            copies[k].start()
        for copy in copies:
            copy.wait()


def lay(parts, evolved):
    vmem = pl.BlockSpec(memory_space=pltpu.VMEM)
    anywhere = pl.BlockSpec(memory_space=pl.ANY)
    return pl.pallas_call(
        lay_kernel,
        out_shape=jax.ShapeDtypeStruct((FLAT, COLS), jnp.bfloat16),
        in_specs=[vmem] * CUBES + [anywhere],
        out_specs=anywhere,
        scratch_shapes=[
            pltpu.VMEM((FLAT + 2 * PAD, COLS), jnp.float32),
            pltpu.VMEM((FLAT, COLS), jnp.bfloat16),
            pltpu.SemaphoreType.DMA((SIDE,)),
        ],
        input_output_aliases={CUBES: 0},
        compiler_params=pltpu.CompilerParams(vmem_limit_bytes=SMALL_BYTES),
    )(*parts, evolved)


def tables():
    group_speed = 0.45 * np.exp(-math.log(1.1) * np.arange(NF))
    angles = 2.0 * math.pi / ND * np.arange(ND)

    def wide(values, times):
        return np.repeat(np.repeat(values, times)[:, None], COLS, axis=1).astype(np.float32)

    cosine, sine = np.cos(angles), np.sin(angles)
    twice = BLOCK // ND
    per_row = (wide(cosine, ROWS), wide(sine, ROWS))
    per_bin = (wide(np.tile(cosine, twice), 1), wide(np.tile(sine, twice), 1))
    return (group_speed.astype(np.float32),) + per_row + per_bin


def spots():
    both = []
    for cell in range(2):
        chosen = np.zeros((4 * ROWS, (ROWS + 2) * COLS), np.float32)
        near = (ROWS - 1, ROWS - 2) if cell else (0, 1)
        for block, source in enumerate(tuple(range(ROWS)) + tuple(ROWS + row for row in near)):
            chosen[2 * source, block * COLS] = 1.0
            chosen[2 * source + 1, (block + 1) * COLS - 1] = 1.0
        both.append(chosen)
    return np.stack(both).astype(jnp.bfloat16)


def swap(x):
    return lax.ppermute(x, "cell", [(0, 1), (1, 0)])


def on_device(
    spectrum,
    depth_factor,
    wet_mask,
    frac_index,
    boundary_map,
    average_map,
    dia_plus,
    dia_minus,
    dia_coef,
):
    parent = lax.axis_size("grid") - 1
    hubs = hub_places()
    spec = spectrum.reshape(FLAT, COLS)
    maps, *parts = send_first(boundary_map.T, spec)

    held = [lax.ppermute(part, "grid", [(parent, hub)]) for part, hub in zip(parts, hubs[1:])]
    maps = lax.all_to_all(maps, "grid", 0, 0)
    near, near_statics = prepare(spec, depth_factor, wet_mask, frac_index)
    near = swap(near)
    near_statics = swap(near_statics)
    picked = lax.all_to_all(pick(maps, spec, *held), "grid", 0, 0)
    picked = jnp.concatenate([picked[hub] for hub in hubs], axis=1)
    far = swap(picked)

    group_speed, cosine, sine, cosine_bin, sine_bin = tables()
    evolved, pieces = evolve(
        dia_plus * ROWS + PAD,
        dia_minus * ROWS + PAD,
        group_speed,
        dia_coef,
        spec,
        near,
        picked,
        far,
        spots(),
        depth_factor,
        wet_mask,
        frac_index,
        near_statics,
        cosine,
        sine,
        cosine_bin,
        sine_bin,
        average_map,
    )
    copies = average(lax.all_to_all(pieces, "grid", 0, 0))
    last = SIDE - 1
    cubes = [[cube_member(k, i) for i in range(STACK)] for k in range(CUBES)]
    gathered = lax.all_to_all(copies, "grid", 0, 0, axis_index_groups=cubes)
    wrapping = [place(last, last, 0), place(last, 0, last), place(0, last, last)]
    relays = [place(last, last, last - 1), place(last, last - 1, last), place(last - 1, last, last)]
    relays.append(wrapping[2])
    far = [place(last, 0, 1), place(0, 1, last), place(1, last, 0), place(0, 0, 0)]
    relayed = lax.ppermute(gathered, "grid", list(zip(far, relays)))
    parts = [lax.ppermute(gathered, "grid", [(device, parent)]) for device in wrapping]
    parts += [lax.ppermute(relayed, "grid", [(device, parent)]) for device in relays]
    parts = [gathered] + parts
    return lay(parts, evolved).reshape(BINS, ROWS, COLS)


def solution(mesh):
    placed = (
        P(None, ("grid", "cell"), None),
        P(("grid", "cell"), None),
        P(("grid", "cell"), None),
        P(("grid", "cell"), None),
        P(("grid", "cell"), None),
        P(("grid", "cell"), None),
        P(),
        P(),
        P(),
    )
    return jax.shard_map(
        on_device,
        mesh=mesh,
        in_specs=placed,
        out_specs=P(None, ("grid", "cell"), None),
        check_vma=False,
    )
```

```python
import functools
import math

import jax
import jax.numpy as jnp
import numpy as np
from jax import lax
from jax.experimental import pallas as pl
from jax.experimental.pallas import tpu as pltpu
from jax.sharding import PartitionSpec as P

NF = 36
ND = 36
SIDE = 4
ROWS = 4
COLS = 128
CELLS = ROWS * COLS
BINS = NF * ND
FLAT = BINS * ROWS
PAD = 8
PIECES = SIDE**3
TOGETHER = 6
PIECE = FLAT // PIECES
TALL = 88
BLOCK = 72
GROUP = 3
CHUNK = 432
WIDTH = 512
UNIT = 512.0
STEPS = 65534.0
OFFSET = 32767
VMEM_BYTES = 24 * 1024 * 1024
SMALL_BYTES = 10 * 1024 * 1024
LARGE_BYTES = 56 * 1024 * 1024
STACK = 8

FRACTIONS = (0.25, 0.5, 0.75, 1.0)


def fraction(frac_index):
    open_share = jnp.zeros(frac_index.shape, jnp.float32)
    for position, share in enumerate(FRACTIONS):
        open_share = open_share + jnp.where(frac_index == position, share, 0.0)
    return open_share


def place(z, y, x):
    return (z % SIDE * SIDE + y % SIDE) * SIDE + x % SIDE


def hub_places():
    last = SIDE - 1
    return [
        place(last, last, last),
        place(last, last, last - 1),
        place(last, last - 1, last),
        place(last - 1, last, last),
    ]


def cube_member(cube, position):
    zyx = [2 * (cube // d % 2) + position // d % 2 for d in (4, 2, 1)]
    return (zyx[0] * SIDE + zyx[1]) * SIDE + zyx[2]


TAKEN = ((7, 0, 7), (6, 4, 2), (5, 1, 4), (3, 2, 1))


def opposite(device, axes):
    zyx = [device // d % SIDE for d in (SIDE * SIDE, SIDE, 1)]
    return place(*[SIDE - 1 - v if axes & d else v for v, d in zip(zyx, (4, 2, 1))])


def own_flags():
    return 1 - lax.axis_index("cell"), jnp.where(lax.axis_index("grid") == PIECES - 1, 0, 1)


def bin_block(ref, index):
    return ref[8 * index : 8 * index + 8, :]


def send_kernel(map_ref, spec_ref, maps_ref, *part_refs):
    lane = lax.broadcasted_iota(jnp.int32, (PIECES, COLS), 1)
    maps = jnp.zeros((PIECES, COLS), jnp.int32)
    for r in range(ROWS):
        for side in range(2):
            maps = jnp.where(lane == 2 * r + side, map_ref[side, r], maps)
    maps_ref[...] = maps
    part = FLAT // SIDE
    for k, ref in enumerate(part_refs):
        ref[...] = spec_ref[(k + 1) * part : (k + 2) * part, :]


def send_first(maps, spec):
    vmem = pl.BlockSpec(memory_space=pltpu.VMEM)
    part = jax.ShapeDtypeStruct((FLAT // SIDE, COLS), jnp.bfloat16)
    return pl.pallas_call(
        send_kernel,
        out_shape=(jax.ShapeDtypeStruct((PIECES, COLS), jnp.int32),) + (part,) * (SIDE - 1),
        in_specs=[pl.BlockSpec(memory_space=pltpu.SMEM), vmem],
        out_specs=(vmem,) * SIDE,
        compiler_params=pltpu.CompilerParams(vmem_limit_bytes=LARGE_BYTES),
    )(maps, spec)


def pick_kernel(maps_ref, spec_ref, a_ref, b_ref, c_ref, out_ref, wide, turned, hot, mine, sem):
    part = FLAT // SIDE
    bins = part // ROWS
    share = jnp.where(own_flags()[1] == 0, 1.0, 0.0)
    copy = pltpu.make_async_copy(spec_ref.at[pl.ds(0, part), :], mine, sem)
    copy.start()
    cell = lax.broadcasted_iota(jnp.int32, (PIECES, CELLS), 1)
    for e in range(2 * ROWS):
        wanted = jnp.broadcast_to(maps_ref[:, e : e + 1], (PIECES, CELLS))
        same = jnp.where(cell == wanted, 1.0, 0.0).astype(jnp.bfloat16)
        hot[e * PIECES : (e + 1) * PIECES, :] = same
    copy.wait()

    def join(i, carry):
        for u in range(9):
            at = pl.multiple_of(i * 144 + u * 16, 16)
            here = pl.ds(at, 16)
            value = mine[here, :].astype(jnp.float32) * share
            for ref in (a_ref, b_ref, c_ref):
                value = value + ref[here, :].astype(jnp.float32)
            wide[here, :] = value
        return carry

    lax.fori_loop(0, part // 144, join, 0)
    wide[part:, :] = jnp.zeros((wide.shape[0] - part, COLS), jnp.float32)
    many = wide.shape[0] // ROWS
    held = [wide[pl.ds(r, many, stride=ROWS), :].astype(jnp.bfloat16) for r in range(ROWS)]
    held = jnp.concatenate(held, axis=1)
    found = lax.dot_general(
        hot[...], held, (((1,), (1,)), ((), ())), preferred_element_type=jnp.float32
    )
    for e in range(2 * ROWS):
        for t in range(many // COLS):
            part = found[e * PIECES : (e + 1) * PIECES, t * COLS : (t + 1) * COLS]
            turned[t, pl.ds(e, PIECES, stride=2 * ROWS), :] = part

    def narrower(i, carry):
        for u in range(8):
            g = i * 8 + u
            at = pl.multiple_of(g * 2 * ROWS, 8)
            for t in range(many // COLS):
                lanes = min(COLS, bins - t * COLS)
                value = turned[t, pl.ds(at, 2 * ROWS), :lanes].astype(jnp.bfloat16)
                out_ref[g, :, t * COLS : t * COLS + lanes] = value
        return carry

    lax.fori_loop(0, PIECES // 8, narrower, 0)


def pick(*operands):
    vmem = pl.BlockSpec(memory_space=pltpu.VMEM)
    part = FLAT // SIDE
    return pl.pallas_call(
        pick_kernel,
        out_shape=jax.ShapeDtypeStruct((PIECES, 2 * ROWS, part // ROWS), jnp.bfloat16),
        in_specs=[vmem, pl.BlockSpec(memory_space=pl.ANY)] + [vmem] * 3,
        out_specs=vmem,
        scratch_shapes=[
            pltpu.VMEM((3 * COLS * ROWS, COLS), jnp.float32),
            pltpu.VMEM((3, PIECES * 2 * ROWS, COLS), jnp.float32),
            pltpu.VMEM((PIECES * 2 * ROWS, CELLS), jnp.bfloat16),
            pltpu.VMEM((part, COLS), jnp.bfloat16),
            pltpu.SemaphoreType.DMA,
        ],
        compiler_params=pltpu.CompilerParams(vmem_limit_bytes=SMALL_BYTES),
    )(*operands)


def prepare_kernel(spec_ref, depth_ref, wet_ref, frac_ref, near_ref, stat_ref, dens):
    first = own_flags()[0] == 1
    wet = wet_ref[...].astype(jnp.float32)
    values = (depth_ref[...], wet * fraction(frac_ref[...]), wet)
    for i, value in enumerate(values):
        stat_ref[2 * i : 2 * i + 1, :] = jnp.where(first, value[3:4], value[0:1])
        stat_ref[2 * i + 1 : 2 * i + 2, :] = jnp.where(first, value[2:3], value[1:2])
    stat_ref[6:8, :] = jnp.zeros((2, COLS), jnp.float32)

    def widen(i, carry):
        for u in range(12):
            at = pl.multiple_of(i * 192 + u * 16, 16)
            dens[pl.ds(at, 16), :] = spec_ref[pl.ds(at, 16), :].astype(jnp.float32)
        return carry

    lax.fori_loop(0, FLAT // 192, widen, 0)
    nearer = 3 * own_flags()[0]
    farther = 1 + own_flags()[0]

    def pull(i, carry):
        for u in range(9):
            at = pl.multiple_of(i * 144 + u * 16, 16)
            for n, row in enumerate((nearer, farther)):
                rows = dens[pl.ds(at * ROWS + row, 16, stride=ROWS), :]
                near_ref[n, pl.ds(at, 16), :] = rows.astype(jnp.bfloat16)
        return carry

    lax.fori_loop(0, BINS // 144, pull, 0)


def prepare(*operands, interpret=False):
    vmem = pl.BlockSpec(memory_space=pltpu.VMEM)
    return pl.pallas_call(
        prepare_kernel,
        out_shape=(
            jax.ShapeDtypeStruct((2, BINS, COLS), jnp.bfloat16),
            jax.ShapeDtypeStruct((8, COLS), jnp.float32),
        ),
        in_specs=[vmem] * 4,
        out_specs=(vmem,) * 2,
        scratch_shapes=[pltpu.VMEM((FLAT, COLS), jnp.float32)],
        compiler_params=pltpu.CompilerParams(vmem_limit_bytes=SMALL_BYTES),
        cost_estimate=pl.CostEstimate(flops=4_000_000, bytes_accessed=5_000_000, transcendentals=0),
        interpret=interpret,
    )(*operands)


def step_kernel(
    plus_ref,
    minus_ref,
    speed_ref,
    coef_ref,
    spec_ref,
    near_ref,
    edge_ref,
    far_ref,
    spot_ref,
    depth_ref,
    wet_ref,
    frac_ref,
    stat_ref,
    cos_ref,
    sin_ref,
    cosb_ref,
    sinb_ref,
    target_ref,
    out_ref,
    pieces_ref,
    dens,
    flat,
    halo,
    evol,
    near,
    hot,
    count,
    tab_x,
    tab_y,
    tab_z,
    tab_an,
    tab_nb,
    tab_n,
    done_out,
    out_sem,
):
    first = own_flags()[0] == 1
    child = own_flags()[1]
    adjacent = 3 * own_flags()[0]
    sign = jnp.where(first, 1.0, -1.0)
    lane = lax.broadcasted_iota(jnp.int32, (16, COLS), 1)
    ends = jnp.where((lane == 0) | (lane == COLS - 1), child, 0) > 0

    values = jnp.concatenate([edge_ref[...], far_ref[...]], axis=0)
    spot = spot_ref[1 - own_flags()[0]]
    for base in range(0, BINS, WIDTH):
        wide_rows = min(WIDTH, BINS - base)
        laid = lax.dot_general(
            values[:, base : base + wide_rows],
            spot,
            (((0,), (0,)), ((), ())),
            preferred_element_type=jnp.float32,
        )
        lanes = lax.broadcasted_iota(jnp.int32, (wide_rows, COLS), 1)
        ends_wide = jnp.where((lanes == 0) | (lanes == COLS - 1), child, 0) > 0
        for r in range(ROWS):
            here = pl.ds(base * ROWS + r, wide_rows, stride=ROWS)
            flat[here, :] = laid[:, r * COLS : (r + 1) * COLS]
        for n in range(2):
            raw = near_ref[n, base : base + wide_rows, :].astype(jnp.float32)
            at = (ROWS + n) * COLS
            raw = jnp.where(ends_wide, laid[:, at : at + COLS], raw)
            near[n, base : base + wide_rows, :] = raw * stat_ref[4 + n : 5 + n, :]

    wet = jnp.concatenate([wet_ref[...]] * 2, axis=0).astype(jnp.float32)
    wet16 = jnp.concatenate([wet, wet], axis=0)

    def begin(i, carry):
        for u in range(12):
            at = pl.multiple_of(i * 192 + u * 16, 16)
            raw = spec_ref[pl.ds(at, 16), :].astype(jnp.float32)
            dens[pl.ds(PAD + at, 16), :] = jnp.where(ends, flat[pl.ds(at, 16), :], raw) * wet16
            halo[pl.ds(at, 16), :] = jnp.zeros((16, COLS), jnp.float32)
        return carry

    lax.fori_loop(0, FLAT // 192, begin, 0)

    sub = lax.broadcasted_iota(jnp.int32, (8, COLS), 0)
    low = sub < ROWS
    depth = jnp.concatenate([depth_ref[...]] * 2, axis=0)
    weight = wet * fraction(jnp.concatenate([frac_ref[...]] * 2, axis=0))

    def between(d0, d1, w0, w1):
        return 0.5 * (d0 + d1) * w0 * w1

    def along(d, w):
        face = between(d, pltpu.roll(d, COLS - 1, 1), w, pltpu.roll(w, COLS - 1, 1))
        return jnp.where(lane[:8] == COLS - 1, 0.0, face)

    def wide(row):
        return jnp.broadcast_to(row, (8, COLS))

    face_x = between(depth, pltpu.roll(depth, 7, 0), weight, pltpu.roll(weight, 7, 0))
    face_x = jnp.where(sub % ROWS == ROWS - 1, 0.0, face_x)
    face_y = along(depth, weight)
    d_own = wide(jnp.where(first, depth[3:4], depth[0:1]))
    w_own = wide(jnp.where(first, weight[3:4], weight[0:1]))
    d_n1, d_n2, w_n1, w_n2 = (wide(stat_ref[i : i + 1, :]) for i in range(4))
    face_an = between(d_own, d_n1, w_own, w_n1)
    face_nb = between(d_n1, d_n2, w_n1, w_n2)
    face_n = along(d_n1, w_n1)

    for q in range(ND // 2):
        tab_x[8 * q : 8 * q + 8, :] = face_x * bin_block(cos_ref, q)
        tab_y[8 * q : 8 * q + 8, :] = face_y * bin_block(sin_ref, q)
        if 2 * q > ND // 2:
            back = 8 * (q - ND // 4)
            tab_z[back : back + 8, :] = pltpu.roll(face_y, 1, 1) * bin_block(sin_ref, q)
    for j in range(BLOCK // 8):
        tab_an[8 * j : 8 * j + 8, :] = face_an * bin_block(cosb_ref, j)
        tab_nb[8 * j : 8 * j + 8, :] = face_nb * bin_block(cosb_ref, j)
        tab_n[8 * j : 8 * j + 8, :] = face_n * bin_block(sinb_ref, j)

    def halo_fluxes(bins, rows):
        many = range(BLOCK // 8)
        n1s = [near[0, pl.ds(bins + 8 * j, 8), :] for j in many]
        owns = [dens[pl.ds(PAD + rows + 32 * j + adjacent, 8, stride=ROWS), :] for j in many]
        fluxes = []
        for j in many:
            along = bin_block(tab_an, j)
            top = jnp.where(first, owns[j], n1s[j])
            bottom = jnp.where(first, n1s[j], owns[j])
            fluxes.append(jnp.maximum(along, 0.0) * top + jnp.minimum(along, 0.0) * bottom)
        for j in many:
            halo[pl.ds(rows + 32 * j + adjacent, 8, stride=ROWS), :] = sign * fluxes[j]
        return n1s, fluxes

    def advance_near(bins, speeds, n1s, fluxes):
        n2s = [near[1, pl.ds(bins + 8 * j, 8), :] for j in range(BLOCK // 8)]
        after_near = []
        for j in range(BLOCK // 8):
            n1, n2 = n1s[j], n2s[j]
            top, bottom = jnp.where(first, n1, n2), jnp.where(first, n2, n1)
            along = bin_block(tab_nb, j)
            beyond = jnp.maximum(along, 0.0) * top + jnp.minimum(along, 0.0) * bottom
            along = bin_block(tab_n, j)
            right = pltpu.roll(n1, COLS - 1, 1)
            fy = jnp.maximum(along, 0.0) * n1 + jnp.minimum(along, 0.0) * right
            change = sign * (beyond - fluxes[j]) + (fy - pltpu.roll(fy, 1, 1))
            speed = speeds[0] if j < 4 else (jnp.where(low, *speeds) if j == 4 else speeds[1])
            after_near.append(n1 - speed * change)
        for j in range(BLOCK // 8):
            near[0, pl.ds(bins + 8 * j, 8), :] = after_near[j]

    def advance(q, speed, rho, across):
        along_x = bin_block(tab_x, q)
        if 2 * q + 1 < ND // 4 or 2 * q > 3 * ND // 4:
            fx = along_x * rho
        else:
            after = pltpu.roll(rho, 7, 0)
            if ND // 4 < 2 * q and 2 * q + 1 < 3 * ND // 4:
                fx = along_x * after
            else:
                fx = jnp.maximum(along_x, 0.0) * rho + jnp.minimum(along_x, 0.0) * after
        along_y = bin_block(tab_y, q)
        if 2 * q + 1 < ND // 2:
            fy = along_y * rho
            out_y = fy - pltpu.roll(fy, 1, 1)
        elif 2 * q > ND // 2:
            out_y = along_y * pltpu.roll(rho, COLS - 1, 1) - bin_block(tab_z, q - ND // 4) * rho
        else:
            right = pltpu.roll(rho, COLS - 1, 1)
            fy = jnp.maximum(along_y, 0.0) * rho + jnp.minimum(along_y, 0.0) * right
            out_y = fy - pltpu.roll(fy, 1, 1)
        change = (fx - pltpu.roll(fx, 1, 0)) + out_y
        return rho - speed * (change + across)

    def advance_all(starts, speeds):
        for q in range(0, ND // 2, GROUP):
            group = [
                (p, rows + 8 * (p + h * ND // 2), speed[h])
                for p in range(q, q + GROUP)
                for rows, speed in zip(starts, speeds)
                for h in range(2)
            ]
            loaded = [(dens[pl.ds(PAD + at, 8), :], halo[pl.ds(at, 8), :]) for _, at, _ in group]
            moved = [advance(p, speed, *pair) for (p, _, speed), pair in zip(group, loaded)]
            for (_, at, _), value in zip(group, moved):
                dens[pl.ds(PAD + at, 8), :] = value

    def blocks(i, carry):
        ks = [i * TOGETHER + u for u in range(TOGETHER)]
        bins = [pl.multiple_of(k * BLOCK, 8) for k in ks]
        rows = [pl.multiple_of(k * (BLOCK * ROWS), 16) for k in ks]
        speeds = [(speed_ref[2 * k], speed_ref[2 * k + 1]) for k in ks]
        halos = [halo_fluxes(*pair) for pair in zip(bins, rows)]
        for start, speed, values in zip(bins, speeds, halos):
            advance_near(start, speed, *values)
        advance_all(rows, speeds)
        for pair in zip(bins, rows):
            halo_fluxes(*pair)
        advance_all(rows, speeds)
        return carry

    lax.fori_loop(0, BINS // BLOCK // TOGETHER, blocks, 0)

    def interact(f, carry):
        rows = pl.multiple_of(f * (ND * ROWS), 16)
        scale = 0.2 * coef_ref[f]

        def partner(ref, b):
            lower = dens[pl.ds(ref[f * ND + b], 8), :]
            upper = dens[pl.ds(ref[f * ND + b + 1] - ROWS, 8), :]
            return jnp.where(low, lower, upper)

        for g in range(0, ND // 4, 3):
            bs = [4 * (g + t) + 2 * h for t in range(3) for h in range(2)]
            mines = [dens[pl.ds(PAD + rows + 4 * b, 8), :] for b in bs]
            pairs = [(partner(plus_ref, b), partner(minus_ref, b)) for b in bs]
            done = []
            for mine, (plus, minus) in zip(mines, pairs):
                source = mine * (mine * (plus + minus) - 2.0 * (plus * minus))
                done.append(jnp.maximum(mine + scale * source, 0.0))
            for b, value in zip(bs, done):
                evol[pl.ds(rows + 4 * b, 8), :] = value
            for t in range(3):
                both = jnp.concatenate(done[2 * t : 2 * t + 2], axis=0).astype(jnp.bfloat16)
                done_out[pl.ds(rows + 16 * (g + t), 16), :] = both
        return carry

    lax.fori_loop(0, NF, interact, 0)
    leaving = pltpu.make_async_copy(done_out, out_ref, out_sem)
    leaving.start()

    row = lax.broadcasted_iota(jnp.int32, (CELLS, COLS), 0)
    for r in range(ROWS):
        own = lane[:1] + r * COLS
        same = row == jnp.where(child == 1, target_ref[r : r + 1, :], own)
        hot[:, r * COLS : (r + 1) * COLS] = jnp.where(same, 1.0, 0.0).astype(jnp.bfloat16)
    inner = (((1,), (1,)), ((), ()))
    number = lax.dot_general(
        jnp.ones((16, CELLS), jnp.bfloat16), hot[...], inner, preferred_element_type=jnp.float32
    )
    share = 1.0 / jnp.maximum(number[0:1], 1.0)
    count[...] = jnp.zeros_like(count)
    for turn in range(ROWS):
        for r in range(ROWS):
            of = (turn + r) % ROWS
            here = number[0:1, of * COLS : (of + 1) * COLS].astype(jnp.int32)
            count[turn, PIECE % 8 + r : PIECE % 8 + r + 1, :] = here

    many = CHUNK

    def sums(c, carry):
        base = c * (many * ROWS)
        parts = [evol[pl.ds(base + r, many, stride=ROWS), :] for r in range(ROWS)]
        value = jnp.concatenate(parts, axis=1)
        head = value.astype(jnp.bfloat16)
        tail = (value - head.astype(jnp.float32)).astype(jnp.bfloat16)
        total = lax.dot_general(head, hot[...], inner, preferred_element_type=jnp.float32)
        total += lax.dot_general(tail, hot[...], inner, preferred_element_type=jnp.float32)
        for r in range(ROWS):
            part = slice(r * COLS, (r + 1) * COLS)
            flat[pl.ds(base + r, many, stride=ROWS), :] = total[:, part] * share[:, part]
        return carry

    lax.fori_loop(0, BINS // many, sums, 0)
    main = PIECE // 8 * 8
    row = main + lax.broadcasted_iota(jnp.int32, (8, COLS), 0)

    def cut(i, carry):
        for u in range(2 * ROWS):
            j, turn = i * 2 * ROWS + u, u % ROWS
            mean = flat[pl.ds(j * PIECE, main), :]
            last = jnp.where(row < PIECE, flat[pl.ds(j * PIECE + main, 8), :], 0.0)
            top = jnp.maximum(
                jnp.max(mean, axis=0, keepdims=True), jnp.max(last, axis=0, keepdims=True)
            )
            size = jnp.minimum((top * UNIT).astype(jnp.int32) + 1, OFFSET)
            steps = (UNIT * STEPS) / size.astype(jnp.float32)
            code = (mean * steps + 0.5).astype(jnp.int32) - OFFSET
            code_last = (last * steps + 0.5).astype(jnp.int32) - OFFSET
            rest = jnp.where(row == PIECE + ROWS, size, count[turn])
            code_last = jnp.where(row < PIECE, code_last, rest)
            code = jnp.concatenate([code, code_last], axis=0)
            pieces_ref[j] = code.astype(jnp.int16)
        return carry

    lax.fori_loop(0, PIECES // ROWS // 2, cut, 0)
    leaving.wait()


def evolve(*operands, interpret=False):
    smem = pl.BlockSpec(memory_space=pltpu.SMEM)
    vmem = pl.BlockSpec(memory_space=pltpu.VMEM)
    return pl.pallas_call(
        step_kernel,
        out_shape=(
            jax.ShapeDtypeStruct((FLAT, COLS), jnp.bfloat16),
            jax.ShapeDtypeStruct((PIECES, TALL, COLS), jnp.int16),
        ),
        in_specs=[smem] * 4 + [vmem] * 14,
        out_specs=(pl.BlockSpec(memory_space=pl.ANY), vmem),
        scratch_shapes=[
            pltpu.VMEM((FLAT + 2 * PAD, COLS), jnp.float32),
            pltpu.VMEM((FLAT + 2 * PAD, COLS), jnp.float32),
            pltpu.VMEM((FLAT, COLS), jnp.float32),
            pltpu.VMEM((FLAT, COLS), jnp.float32),
            pltpu.VMEM((2, BINS, COLS), jnp.float32),
            pltpu.VMEM((CELLS, CELLS), jnp.bfloat16),
            pltpu.VMEM((ROWS, 8, COLS), jnp.int32),
            pltpu.VMEM((ND * ROWS, COLS), jnp.float32),
            pltpu.VMEM((ND * ROWS, COLS), jnp.float32),
            pltpu.VMEM((ND * ROWS // 2, COLS), jnp.float32),
            pltpu.VMEM((BLOCK, COLS), jnp.float32),
            pltpu.VMEM((BLOCK, COLS), jnp.float32),
            pltpu.VMEM((BLOCK, COLS), jnp.float32),
            pltpu.VMEM((FLAT, COLS), jnp.bfloat16),
            pltpu.SemaphoreType.DMA,
        ],
        compiler_params=pltpu.CompilerParams(vmem_limit_bytes=VMEM_BYTES),
        cost_estimate=pl.CostEstimate(
            flops=1_400_000_000, bytes_accessed=10_000_000, transcendentals=0
        ),
        interpret=interpret,
    )(*operands)


def average_kernel(pieces_ref, out_ref):
    blocks = TALL // 8
    sub = lax.broadcasted_iota(jnp.int32, (8, COLS), 0)

    def add(i, carry):
        sums, weights, number = carry
        for u in range(4):
            piece = pieces_ref[4 * i + u].astype(jnp.int32).astype(jnp.float32)
            rest = piece[TALL - 8 :]
            at = PIECE % 8
            turned = [pltpu.roll(rest, shift - at, 0) for shift in (8, ROWS)]
            count = jnp.where(sub < ROWS, *turned)
            weight = count * jnp.broadcast_to(rest[at + ROWS : at + ROWS + 1], (8, COLS))
            sums = tuple(sums[b] + piece[8 * b : 8 * b + 8] * weight for b in range(blocks))
            weights, number = weights + weight, number + count
        return sums, weights, number

    zero = jnp.zeros((8, COLS), jnp.float32)
    carry = ((zero,) * blocks, zero, zero)
    sums, weights, number = lax.fori_loop(0, PIECES // 4, add, carry)
    scale = 1.0 / (UNIT * STEPS * number)
    mean = jnp.concatenate([(part + OFFSET * weights) * scale for part in sums], axis=0)
    mean = mean.astype(jnp.bfloat16)
    out_ref[...] = mean


def average(pieces, interpret=False):
    vmem = pl.BlockSpec(memory_space=pltpu.VMEM)
    return pl.pallas_call(
        average_kernel,
        out_shape=jax.ShapeDtypeStruct((TALL, COLS), jnp.bfloat16),
        in_specs=[vmem],
        out_specs=vmem,
        compiler_params=pltpu.CompilerParams(vmem_limit_bytes=SMALL_BYTES),
        interpret=interpret,
    )(pieces)


def stack_kernel(own_ref, taken_ref, out_ref):
    own, taken = own_ref[...], taken_ref[...]
    for i in range(STACK):
        out_ref[i, 0] = own
        out_ref[i, 1] = taken


def stack(own, taken):
    vmem = pl.BlockSpec(memory_space=pltpu.VMEM)
    return pl.pallas_call(
        stack_kernel,
        out_shape=jax.ShapeDtypeStruct((STACK, 2, TALL, COLS), jnp.bfloat16),
        in_specs=[vmem, vmem],
        out_specs=vmem,
        compiler_params=pltpu.CompilerParams(vmem_limit_bytes=SMALL_BYTES),
    )(own, taken)


def lay_kernel(*refs):
    parts, (_, out_ref, wide, narrow, sems) = refs[: len(TAKEN)], refs[len(TAKEN) :]
    main = PIECE // 8 * 8

    @pl.when(own_flags()[1] == 0)
    def _():
        for (cube, _, axes), ref in zip(TAKEN, parts):
            for i in range(STACK):
                device = cube_member(cube, i)
                for n, source in enumerate((device, opposite(device, axes))):
                    at = source * PIECE
                    piece = ref[i, n].astype(jnp.float32)
                    wide[at : at + main, :] = piece[:main]
                    wide[at + main : at + PIECE, :] = piece[main:PIECE]

        part = FLAT // SIDE
        copies = []
        for k in range(SIDE):

            def narrower(i, carry):
                for u in range(9):
                    at = pl.multiple_of(k * part + i * 144 + u * 16, 16)
                    narrow[pl.ds(at, 16), :] = wide[pl.ds(at, 16), :].astype(jnp.bfloat16)
                return carry

            lax.fori_loop(0, part // 144, narrower, 0)
            here = pl.ds(k * part, part)
            copies.append(pltpu.make_async_copy(narrow.at[here], out_ref.at[here], sems.at[k]))
            copies[k].start()
        for copy in copies:
            copy.wait()


def lay(parts, evolved):
    vmem = pl.BlockSpec(memory_space=pltpu.VMEM)
    anywhere = pl.BlockSpec(memory_space=pl.ANY)
    return pl.pallas_call(
        lay_kernel,
        out_shape=jax.ShapeDtypeStruct((FLAT, COLS), jnp.bfloat16),
        in_specs=[vmem] * len(TAKEN) + [anywhere],
        out_specs=anywhere,
        scratch_shapes=[
            pltpu.VMEM((FLAT + 2 * PAD, COLS), jnp.float32),
            pltpu.VMEM((FLAT, COLS), jnp.bfloat16),
            pltpu.SemaphoreType.DMA((SIDE,)),
        ],
        input_output_aliases={len(TAKEN): 0},
        compiler_params=pltpu.CompilerParams(vmem_limit_bytes=SMALL_BYTES),
    )(*parts, evolved)


def tables():
    group_speed = 0.45 * np.exp(-math.log(1.1) * np.arange(NF))
    angles = 2.0 * math.pi / ND * np.arange(ND)

    def wide(values, times):
        return np.repeat(np.repeat(values, times)[:, None], COLS, axis=1).astype(np.float32)

    cosine, sine = np.cos(angles), np.sin(angles)
    twice = BLOCK // ND
    per_row = (wide(cosine, ROWS), wide(sine, ROWS))
    per_bin = (wide(np.tile(cosine, twice), 1), wide(np.tile(sine, twice), 1))
    return (group_speed.astype(np.float32),) + per_row + per_bin


def spots():
    both = []
    for cell in range(2):
        chosen = np.zeros((4 * ROWS, (ROWS + 2) * COLS), np.float32)
        near = (ROWS - 1, ROWS - 2) if cell else (0, 1)
        for block, source in enumerate(tuple(range(ROWS)) + tuple(ROWS + row for row in near)):
            chosen[2 * source, block * COLS] = 1.0
            chosen[2 * source + 1, (block + 1) * COLS - 1] = 1.0
        both.append(chosen)
    return np.stack(both).astype(jnp.bfloat16)


def swap(x):
    return lax.ppermute(x, "cell", [(0, 1), (1, 0)])


def on_device(
    spectrum,
    depth_factor,
    wet_mask,
    frac_index,
    boundary_map,
    average_map,
    dia_plus,
    dia_minus,
    dia_coef,
):
    parent = lax.axis_size("grid") - 1
    hubs = hub_places()
    spec = spectrum.reshape(FLAT, COLS)
    maps, *parts = send_first(boundary_map.T, spec)

    held = [lax.ppermute(part, "grid", [(parent, hub)]) for part, hub in zip(parts, hubs[1:])]
    maps = lax.all_to_all(maps, "grid", 0, 0)
    near, near_statics = prepare(spec, depth_factor, wet_mask, frac_index)
    near = swap(near)
    near_statics = swap(near_statics)
    picked = lax.all_to_all(pick(maps, spec, *held), "grid", 0, 0)
    picked = jnp.concatenate([picked[hub] for hub in hubs], axis=1)
    far = swap(picked)

    group_speed, cosine, sine, cosine_bin, sine_bin = tables()
    evolved, pieces = evolve(
        dia_plus * ROWS + PAD,
        dia_minus * ROWS + PAD,
        group_speed,
        dia_coef,
        spec,
        near,
        picked,
        far,
        spots(),
        depth_factor,
        wet_mask,
        frac_index,
        near_statics,
        cosine,
        sine,
        cosine_bin,
        sine_bin,
        average_map,
    )
    piece = average(lax.all_to_all(pieces, "grid", 0, 0))
    moves = [
        (opposite(device, axes), device)
        for near_cube, _, axes in TAKEN
        for device in [cube_member(near_cube, i) for i in range(STACK)]
    ]
    both = stack(piece, lax.ppermute(piece, "grid", moves))
    last = SIDE - 1
    cubes = [[cube_member(k, i) for i in range(STACK)] for k in range(2 * SIDE)]
    gathered = lax.all_to_all(both, "grid", 0, 0, axis_index_groups=cubes)
    wrapping = [place(last, last, 0), place(last, 0, last), place(0, last, last)]
    parts = [gathered]
    parts += [lax.ppermute(gathered, "grid", [(device, parent)]) for device in wrapping]
    return lay(parts, evolved).reshape(BINS, ROWS, COLS)


def solution(mesh):
    placed = (
        P(None, ("grid", "cell"), None),
        P(("grid", "cell"), None),
        P(("grid", "cell"), None),
        P(("grid", "cell"), None),
        P(("grid", "cell"), None),
        P(("grid", "cell"), None),
        P(),
        P(),
        P(),
    )
    return jax.shard_map(
        on_device,
        mesh=mesh,
        in_specs=placed,
        out_specs=P(None, ("grid", "cell"), None),
        check_vma=False,
    )
```

```python
import functools
import math

import jax
import jax.numpy as jnp
import numpy as np
from jax import lax
from jax.experimental import pallas as pl
from jax.experimental.pallas import tpu as pltpu
from jax.sharding import PartitionSpec as P

NF = 36
ND = 36
SIDE = 4
ROWS = 4
COLS = 128
CELLS = ROWS * COLS
BINS = NF * ND
FLAT = BINS * ROWS
PAD = 8
PIECES = SIDE**3
TOGETHER = 6
PIECE = FLAT // PIECES
TALL = 88
BLOCK = 72
GROUP = 3
CHUNK = 432
WIDTH = 512
UNIT = 512.0
STEPS = 65534.0
OFFSET = 32767
VMEM_BYTES = 24 * 1024 * 1024
SMALL_BYTES = 10 * 1024 * 1024
LARGE_BYTES = 56 * 1024 * 1024
STACK = 8

FRACTIONS = (0.25, 0.5, 0.75, 1.0)


def fraction(frac_index):
    open_share = jnp.zeros(frac_index.shape, jnp.float32)
    for position, share in enumerate(FRACTIONS):
        open_share = open_share + jnp.where(frac_index == position, share, 0.0)
    return open_share


def place(z, y, x):
    return (z % SIDE * SIDE + y % SIDE) * SIDE + x % SIDE


def hub_places():
    last = SIDE - 1
    return [
        place(last, last, last),
        place(last, last, last - 1),
        place(last, last - 1, last),
        place(last - 1, last, last),
    ]


def cube_member(cube, position):
    zyx = [2 * (cube // d % 2) + position // d % 2 for d in (4, 2, 1)]
    return (zyx[0] * SIDE + zyx[1]) * SIDE + zyx[2]


CUBES = 8
DIRECT = (6, 5, 3)
PASSED = (4, 1, 2, 0)
OWN = 7


def own_flags():
    return 1 - lax.axis_index("cell"), jnp.where(lax.axis_index("grid") == PIECES - 1, 0, 1)


def bin_block(ref, index):
    return ref[8 * index : 8 * index + 8, :]


def send_kernel(map_ref, spec_ref, maps_ref, *part_refs):
    lane = lax.broadcasted_iota(jnp.int32, (PIECES, COLS), 1)
    maps = jnp.zeros((PIECES, COLS), jnp.int32)
    for r in range(ROWS):
        for side in range(2):
            maps = jnp.where(lane == 2 * r + side, map_ref[side, r], maps)
    maps_ref[...] = maps
    part = FLAT // SIDE
    for k, ref in enumerate(part_refs):
        ref[...] = spec_ref[(k + 1) * part : (k + 2) * part, :]


def send_first(maps, spec):
    vmem = pl.BlockSpec(memory_space=pltpu.VMEM)
    part = jax.ShapeDtypeStruct((FLAT // SIDE, COLS), jnp.bfloat16)
    return pl.pallas_call(
        send_kernel,
        out_shape=(jax.ShapeDtypeStruct((PIECES, COLS), jnp.int32),) + (part,) * (SIDE - 1),
        in_specs=[pl.BlockSpec(memory_space=pltpu.SMEM), vmem],
        out_specs=(vmem,) * SIDE,
        compiler_params=pltpu.CompilerParams(vmem_limit_bytes=LARGE_BYTES),
    )(maps, spec)


def pick_kernel(maps_ref, spec_ref, a_ref, b_ref, c_ref, out_ref, wide, turned, hot, mine, sem):
    part = FLAT // SIDE
    bins = part // ROWS
    share = jnp.where(own_flags()[1] == 0, 1.0, 0.0)
    copy = pltpu.make_async_copy(spec_ref.at[pl.ds(0, part), :], mine, sem)
    copy.start()
    cell = lax.broadcasted_iota(jnp.int32, (PIECES, CELLS), 1)
    for e in range(2 * ROWS):
        wanted = jnp.broadcast_to(maps_ref[:, e : e + 1], (PIECES, CELLS))
        same = jnp.where(cell == wanted, 1.0, 0.0).astype(jnp.bfloat16)
        hot[e * PIECES : (e + 1) * PIECES, :] = same
    copy.wait()

    def join(i, carry):
        for u in range(9):
            at = pl.multiple_of(i * 144 + u * 16, 16)
            here = pl.ds(at, 16)
            value = mine[here, :].astype(jnp.float32) * share
            for ref in (a_ref, b_ref, c_ref):
                value = value + ref[here, :].astype(jnp.float32)
            wide[here, :] = value
        return carry

    lax.fori_loop(0, part // 144, join, 0)
    wide[part:, :] = jnp.zeros((wide.shape[0] - part, COLS), jnp.float32)
    many = wide.shape[0] // ROWS
    held = [wide[pl.ds(r, many, stride=ROWS), :].astype(jnp.bfloat16) for r in range(ROWS)]
    held = jnp.concatenate(held, axis=1)
    found = lax.dot_general(
        hot[...], held, (((1,), (1,)), ((), ())), preferred_element_type=jnp.float32
    )
    for e in range(2 * ROWS):
        for t in range(many // COLS):
            part = found[e * PIECES : (e + 1) * PIECES, t * COLS : (t + 1) * COLS]
            turned[t, pl.ds(e, PIECES, stride=2 * ROWS), :] = part

    def narrower(i, carry):
        for u in range(8):
            g = i * 8 + u
            at = pl.multiple_of(g * 2 * ROWS, 8)
            for t in range(many // COLS):
                lanes = min(COLS, bins - t * COLS)
                value = turned[t, pl.ds(at, 2 * ROWS), :lanes].astype(jnp.bfloat16)
                out_ref[g, :, t * COLS : t * COLS + lanes] = value
        return carry

    lax.fori_loop(0, PIECES // 8, narrower, 0)


def pick(*operands):
    vmem = pl.BlockSpec(memory_space=pltpu.VMEM)
    part = FLAT // SIDE
    return pl.pallas_call(
        pick_kernel,
        out_shape=jax.ShapeDtypeStruct((PIECES, 2 * ROWS, part // ROWS), jnp.bfloat16),
        in_specs=[vmem, pl.BlockSpec(memory_space=pl.ANY)] + [vmem] * 3,
        out_specs=vmem,
        scratch_shapes=[
            pltpu.VMEM((3 * COLS * ROWS, COLS), jnp.float32),
            pltpu.VMEM((3, PIECES * 2 * ROWS, COLS), jnp.float32),
            pltpu.VMEM((PIECES * 2 * ROWS, CELLS), jnp.bfloat16),
            pltpu.VMEM((part, COLS), jnp.bfloat16),
            pltpu.SemaphoreType.DMA,
        ],
        compiler_params=pltpu.CompilerParams(vmem_limit_bytes=SMALL_BYTES),
    )(*operands)


def prepare_kernel(spec_ref, depth_ref, wet_ref, frac_ref, near_ref, stat_ref, dens):
    first = own_flags()[0] == 1
    wet = wet_ref[...].astype(jnp.float32)
    values = (depth_ref[...], wet * fraction(frac_ref[...]), wet)
    for i, value in enumerate(values):
        stat_ref[2 * i : 2 * i + 1, :] = jnp.where(first, value[3:4], value[0:1])
        stat_ref[2 * i + 1 : 2 * i + 2, :] = jnp.where(first, value[2:3], value[1:2])
    stat_ref[6:8, :] = jnp.zeros((2, COLS), jnp.float32)

    def widen(i, carry):
        for u in range(12):
            at = pl.multiple_of(i * 192 + u * 16, 16)
            dens[pl.ds(at, 16), :] = spec_ref[pl.ds(at, 16), :].astype(jnp.float32)
        return carry

    lax.fori_loop(0, FLAT // 192, widen, 0)
    nearer = 3 * own_flags()[0]
    farther = 1 + own_flags()[0]

    def pull(i, carry):
        for u in range(9):
            at = pl.multiple_of(i * 144 + u * 16, 16)
            for n, row in enumerate((nearer, farther)):
                rows = dens[pl.ds(at * ROWS + row, 16, stride=ROWS), :]
                near_ref[n, pl.ds(at, 16), :] = rows.astype(jnp.bfloat16)
        return carry

    lax.fori_loop(0, BINS // 144, pull, 0)


def prepare(*operands, interpret=False):
    vmem = pl.BlockSpec(memory_space=pltpu.VMEM)
    return pl.pallas_call(
        prepare_kernel,
        out_shape=(
            jax.ShapeDtypeStruct((2, BINS, COLS), jnp.bfloat16),
            jax.ShapeDtypeStruct((8, COLS), jnp.float32),
        ),
        in_specs=[vmem] * 4,
        out_specs=(vmem,) * 2,
        scratch_shapes=[pltpu.VMEM((FLAT, COLS), jnp.float32)],
        compiler_params=pltpu.CompilerParams(vmem_limit_bytes=SMALL_BYTES),
        cost_estimate=pl.CostEstimate(flops=4_000_000, bytes_accessed=5_000_000, transcendentals=0),
        interpret=interpret,
    )(*operands)


def step_kernel(
    plus_ref,
    minus_ref,
    speed_ref,
    coef_ref,
    spec_ref,
    near_ref,
    edge_ref,
    far_ref,
    spot_ref,
    depth_ref,
    wet_ref,
    frac_ref,
    stat_ref,
    cos_ref,
    sin_ref,
    cosb_ref,
    sinb_ref,
    target_ref,
    out_ref,
    pieces_ref,
    dens,
    flat,
    halo,
    evol,
    near,
    hot,
    count,
    tab_x,
    tab_y,
    tab_z,
    tab_an,
    tab_nb,
    tab_n,
    done_out,
    out_sem,
):
    first = own_flags()[0] == 1
    child = own_flags()[1]
    adjacent = 3 * own_flags()[0]
    sign = jnp.where(first, 1.0, -1.0)
    lane = lax.broadcasted_iota(jnp.int32, (16, COLS), 1)
    ends = jnp.where((lane == 0) | (lane == COLS - 1), child, 0) > 0

    values = jnp.concatenate([edge_ref[...], far_ref[...]], axis=0)
    spot = spot_ref[1 - own_flags()[0]]
    for base in range(0, BINS, WIDTH):
        wide_rows = min(WIDTH, BINS - base)
        laid = lax.dot_general(
            values[:, base : base + wide_rows],
            spot,
            (((0,), (0,)), ((), ())),
            preferred_element_type=jnp.float32,
        )
        lanes = lax.broadcasted_iota(jnp.int32, (wide_rows, COLS), 1)
        ends_wide = jnp.where((lanes == 0) | (lanes == COLS - 1), child, 0) > 0
        for r in range(ROWS):
            here = pl.ds(base * ROWS + r, wide_rows, stride=ROWS)
            flat[here, :] = laid[:, r * COLS : (r + 1) * COLS]
        for n in range(2):
            raw = near_ref[n, base : base + wide_rows, :].astype(jnp.float32)
            at = (ROWS + n) * COLS
            raw = jnp.where(ends_wide, laid[:, at : at + COLS], raw)
            near[n, base : base + wide_rows, :] = raw * stat_ref[4 + n : 5 + n, :]

    wet = jnp.concatenate([wet_ref[...]] * 2, axis=0).astype(jnp.float32)
    wet16 = jnp.concatenate([wet, wet], axis=0)

    def begin(i, carry):
        for u in range(12):
            at = pl.multiple_of(i * 192 + u * 16, 16)
            raw = spec_ref[pl.ds(at, 16), :].astype(jnp.float32)
            dens[pl.ds(PAD + at, 16), :] = jnp.where(ends, flat[pl.ds(at, 16), :], raw) * wet16
            halo[pl.ds(at, 16), :] = jnp.zeros((16, COLS), jnp.float32)
        return carry

    lax.fori_loop(0, FLAT // 192, begin, 0)

    sub = lax.broadcasted_iota(jnp.int32, (8, COLS), 0)
    low = sub < ROWS
    depth = jnp.concatenate([depth_ref[...]] * 2, axis=0)
    weight = wet * fraction(jnp.concatenate([frac_ref[...]] * 2, axis=0))

    def between(d0, d1, w0, w1):
        return 0.5 * (d0 + d1) * w0 * w1

    def along(d, w):
        face = between(d, pltpu.roll(d, COLS - 1, 1), w, pltpu.roll(w, COLS - 1, 1))
        return jnp.where(lane[:8] == COLS - 1, 0.0, face)

    def wide(row):
        return jnp.broadcast_to(row, (8, COLS))

    face_x = between(depth, pltpu.roll(depth, 7, 0), weight, pltpu.roll(weight, 7, 0))
    face_x = jnp.where(sub % ROWS == ROWS - 1, 0.0, face_x)
    face_y = along(depth, weight)
    d_own = wide(jnp.where(first, depth[3:4], depth[0:1]))
    w_own = wide(jnp.where(first, weight[3:4], weight[0:1]))
    d_n1, d_n2, w_n1, w_n2 = (wide(stat_ref[i : i + 1, :]) for i in range(4))
    face_an = between(d_own, d_n1, w_own, w_n1)
    face_nb = between(d_n1, d_n2, w_n1, w_n2)
    face_n = along(d_n1, w_n1)

    for q in range(ND // 2):
        tab_x[8 * q : 8 * q + 8, :] = face_x * bin_block(cos_ref, q)
        tab_y[8 * q : 8 * q + 8, :] = face_y * bin_block(sin_ref, q)
        if 2 * q > ND // 2:
            back = 8 * (q - ND // 4)
            tab_z[back : back + 8, :] = pltpu.roll(face_y, 1, 1) * bin_block(sin_ref, q)
    for j in range(BLOCK // 8):
        tab_an[8 * j : 8 * j + 8, :] = face_an * bin_block(cosb_ref, j)
        tab_nb[8 * j : 8 * j + 8, :] = face_nb * bin_block(cosb_ref, j)
        tab_n[8 * j : 8 * j + 8, :] = face_n * bin_block(sinb_ref, j)

    def halo_fluxes(bins, rows):
        many = range(BLOCK // 8)
        n1s = [near[0, pl.ds(bins + 8 * j, 8), :] for j in many]
        owns = [dens[pl.ds(PAD + rows + 32 * j + adjacent, 8, stride=ROWS), :] for j in many]
        fluxes = []
        for j in many:
            along = bin_block(tab_an, j)
            top = jnp.where(first, owns[j], n1s[j])
            bottom = jnp.where(first, n1s[j], owns[j])
            fluxes.append(jnp.maximum(along, 0.0) * top + jnp.minimum(along, 0.0) * bottom)
        for j in many:
            halo[pl.ds(rows + 32 * j + adjacent, 8, stride=ROWS), :] = sign * fluxes[j]
        return n1s, fluxes

    def advance_near(bins, speeds, n1s, fluxes):
        n2s = [near[1, pl.ds(bins + 8 * j, 8), :] for j in range(BLOCK // 8)]
        after_near = []
        for j in range(BLOCK // 8):
            n1, n2 = n1s[j], n2s[j]
            top, bottom = jnp.where(first, n1, n2), jnp.where(first, n2, n1)
            along = bin_block(tab_nb, j)
            beyond = jnp.maximum(along, 0.0) * top + jnp.minimum(along, 0.0) * bottom
            along = bin_block(tab_n, j)
            right = pltpu.roll(n1, COLS - 1, 1)
            fy = jnp.maximum(along, 0.0) * n1 + jnp.minimum(along, 0.0) * right
            change = sign * (beyond - fluxes[j]) + (fy - pltpu.roll(fy, 1, 1))
            speed = speeds[0] if j < 4 else (jnp.where(low, *speeds) if j == 4 else speeds[1])
            after_near.append(n1 - speed * change)
        for j in range(BLOCK // 8):
            near[0, pl.ds(bins + 8 * j, 8), :] = after_near[j]

    def advance(q, speed, rho, across):
        along_x = bin_block(tab_x, q)
        if 2 * q + 1 < ND // 4 or 2 * q > 3 * ND // 4:
            fx = along_x * rho
        else:
            after = pltpu.roll(rho, 7, 0)
            if ND // 4 < 2 * q and 2 * q + 1 < 3 * ND // 4:
                fx = along_x * after
            else:
                fx = jnp.maximum(along_x, 0.0) * rho + jnp.minimum(along_x, 0.0) * after
        along_y = bin_block(tab_y, q)
        if 2 * q + 1 < ND // 2:
            fy = along_y * rho
            out_y = fy - pltpu.roll(fy, 1, 1)
        elif 2 * q > ND // 2:
            out_y = along_y * pltpu.roll(rho, COLS - 1, 1) - bin_block(tab_z, q - ND // 4) * rho
        else:
            right = pltpu.roll(rho, COLS - 1, 1)
            fy = jnp.maximum(along_y, 0.0) * rho + jnp.minimum(along_y, 0.0) * right
            out_y = fy - pltpu.roll(fy, 1, 1)
        change = (fx - pltpu.roll(fx, 1, 0)) + out_y
        return rho - speed * (change + across)

    def advance_all(starts, speeds):
        for q in range(0, ND // 2, GROUP):
            group = [
                (p, rows + 8 * (p + h * ND // 2), speed[h])
                for p in range(q, q + GROUP)
                for rows, speed in zip(starts, speeds)
                for h in range(2)
            ]
            loaded = [(dens[pl.ds(PAD + at, 8), :], halo[pl.ds(at, 8), :]) for _, at, _ in group]
            moved = [advance(p, speed, *pair) for (p, _, speed), pair in zip(group, loaded)]
            for (_, at, _), value in zip(group, moved):
                dens[pl.ds(PAD + at, 8), :] = value

    def blocks(i, carry):
        ks = [i * TOGETHER + u for u in range(TOGETHER)]
        bins = [pl.multiple_of(k * BLOCK, 8) for k in ks]
        rows = [pl.multiple_of(k * (BLOCK * ROWS), 16) for k in ks]
        speeds = [(speed_ref[2 * k], speed_ref[2 * k + 1]) for k in ks]
        halos = [halo_fluxes(*pair) for pair in zip(bins, rows)]
        for start, speed, values in zip(bins, speeds, halos):
            advance_near(start, speed, *values)
        advance_all(rows, speeds)
        for pair in zip(bins, rows):
            halo_fluxes(*pair)
        advance_all(rows, speeds)
        return carry

    lax.fori_loop(0, BINS // BLOCK // TOGETHER, blocks, 0)

    def interact(f, carry):
        rows = pl.multiple_of(f * (ND * ROWS), 16)
        scale = 0.2 * coef_ref[f]

        def partner(ref, b):
            lower = dens[pl.ds(ref[f * ND + b], 8), :]
            upper = dens[pl.ds(ref[f * ND + b + 1] - ROWS, 8), :]
            return jnp.where(low, lower, upper)

        for g in range(0, ND // 4, 3):
            bs = [4 * (g + t) + 2 * h for t in range(3) for h in range(2)]
            mines = [dens[pl.ds(PAD + rows + 4 * b, 8), :] for b in bs]
            pairs = [(partner(plus_ref, b), partner(minus_ref, b)) for b in bs]
            done = []
            for mine, (plus, minus) in zip(mines, pairs):
                source = mine * (mine * (plus + minus) - 2.0 * (plus * minus))
                done.append(jnp.maximum(mine + scale * source, 0.0))
            for b, value in zip(bs, done):
                evol[pl.ds(rows + 4 * b, 8), :] = value
            for t in range(3):
                both = jnp.concatenate(done[2 * t : 2 * t + 2], axis=0).astype(jnp.bfloat16)
                done_out[pl.ds(rows + 16 * (g + t), 16), :] = both
        return carry

    lax.fori_loop(0, NF, interact, 0)
    leaving = pltpu.make_async_copy(done_out, out_ref, out_sem)
    leaving.start()

    row = lax.broadcasted_iota(jnp.int32, (CELLS, COLS), 0)
    for r in range(ROWS):
        own = lane[:1] + r * COLS
        same = row == jnp.where(child == 1, target_ref[r : r + 1, :], own)
        hot[:, r * COLS : (r + 1) * COLS] = jnp.where(same, 1.0, 0.0).astype(jnp.bfloat16)
    inner = (((1,), (1,)), ((), ()))
    number = lax.dot_general(
        jnp.ones((16, CELLS), jnp.bfloat16), hot[...], inner, preferred_element_type=jnp.float32
    )
    share = 1.0 / jnp.maximum(number[0:1], 1.0)
    count[...] = jnp.zeros_like(count)
    for turn in range(ROWS):
        for r in range(ROWS):
            of = (turn + r) % ROWS
            here = number[0:1, of * COLS : (of + 1) * COLS].astype(jnp.int32)
            count[turn, PIECE % 8 + r : PIECE % 8 + r + 1, :] = here

    many = CHUNK

    def sums(c, carry):
        base = c * (many * ROWS)
        parts = [evol[pl.ds(base + r, many, stride=ROWS), :] for r in range(ROWS)]
        value = jnp.concatenate(parts, axis=1)
        head = value.astype(jnp.bfloat16)
        tail = (value - head.astype(jnp.float32)).astype(jnp.bfloat16)
        total = lax.dot_general(head, hot[...], inner, preferred_element_type=jnp.float32)
        total += lax.dot_general(tail, hot[...], inner, preferred_element_type=jnp.float32)
        for r in range(ROWS):
            part = slice(r * COLS, (r + 1) * COLS)
            flat[pl.ds(base + r, many, stride=ROWS), :] = total[:, part] * share[:, part]
        return carry

    lax.fori_loop(0, BINS // many, sums, 0)
    main = PIECE // 8 * 8
    row = main + lax.broadcasted_iota(jnp.int32, (8, COLS), 0)

    def cut(i, carry):
        for u in range(2 * ROWS):
            j, turn = i * 2 * ROWS + u, u % ROWS
            mean = flat[pl.ds(j * PIECE, main), :]
            last = jnp.where(row < PIECE, flat[pl.ds(j * PIECE + main, 8), :], 0.0)
            top = jnp.maximum(
                jnp.max(mean, axis=0, keepdims=True), jnp.max(last, axis=0, keepdims=True)
            )
            size = jnp.minimum((top * UNIT).astype(jnp.int32) + 1, OFFSET)
            steps = (UNIT * STEPS) / size.astype(jnp.float32)
            code = (mean * steps + 0.5).astype(jnp.int32) - OFFSET
            code_last = (last * steps + 0.5).astype(jnp.int32) - OFFSET
            rest = jnp.where(row == PIECE + ROWS, size, count[turn])
            code_last = jnp.where(row < PIECE, code_last, rest)
            code = jnp.concatenate([code, code_last], axis=0)
            pieces_ref[j] = code.astype(jnp.int16)
        return carry

    lax.fori_loop(0, PIECES // ROWS // 2, cut, 0)
    leaving.wait()


def evolve(*operands, interpret=False):
    smem = pl.BlockSpec(memory_space=pltpu.SMEM)
    vmem = pl.BlockSpec(memory_space=pltpu.VMEM)
    return pl.pallas_call(
        step_kernel,
        out_shape=(
            jax.ShapeDtypeStruct((FLAT, COLS), jnp.bfloat16),
            jax.ShapeDtypeStruct((PIECES, TALL, COLS), jnp.int16),
        ),
        in_specs=[smem] * 4 + [vmem] * 14,
        out_specs=(pl.BlockSpec(memory_space=pl.ANY), vmem),
        scratch_shapes=[
            pltpu.VMEM((FLAT + 2 * PAD, COLS), jnp.float32),
            pltpu.VMEM((FLAT + 2 * PAD, COLS), jnp.float32),
            pltpu.VMEM((FLAT, COLS), jnp.float32),
            pltpu.VMEM((FLAT, COLS), jnp.float32),
            pltpu.VMEM((2, BINS, COLS), jnp.float32),
            pltpu.VMEM((CELLS, CELLS), jnp.bfloat16),
            pltpu.VMEM((ROWS, 8, COLS), jnp.int32),
            pltpu.VMEM((ND * ROWS, COLS), jnp.float32),
            pltpu.VMEM((ND * ROWS, COLS), jnp.float32),
            pltpu.VMEM((ND * ROWS // 2, COLS), jnp.float32),
            pltpu.VMEM((BLOCK, COLS), jnp.float32),
            pltpu.VMEM((BLOCK, COLS), jnp.float32),
            pltpu.VMEM((BLOCK, COLS), jnp.float32),
            pltpu.VMEM((FLAT, COLS), jnp.bfloat16),
            pltpu.SemaphoreType.DMA,
        ],
        compiler_params=pltpu.CompilerParams(vmem_limit_bytes=VMEM_BYTES),
        cost_estimate=pl.CostEstimate(
            flops=1_400_000_000, bytes_accessed=10_000_000, transcendentals=0
        ),
        interpret=interpret,
    )(*operands)


def average_kernel(pieces_ref, out_ref):
    blocks = TALL // 8
    sub = lax.broadcasted_iota(jnp.int32, (8, COLS), 0)

    def add(i, carry):
        sums, weights, number = carry
        for u in range(4):
            piece = pieces_ref[4 * i + u].astype(jnp.int32).astype(jnp.float32)
            rest = piece[TALL - 8 :]
            at = PIECE % 8
            turned = [pltpu.roll(rest, shift - at, 0) for shift in (8, ROWS)]
            count = jnp.where(sub < ROWS, *turned)
            weight = count * jnp.broadcast_to(rest[at + ROWS : at + ROWS + 1], (8, COLS))
            sums = tuple(sums[b] + piece[8 * b : 8 * b + 8] * weight for b in range(blocks))
            weights, number = weights + weight, number + count
        return sums, weights, number

    zero = jnp.zeros((8, COLS), jnp.float32)
    carry = ((zero,) * blocks, zero, zero)
    sums, weights, number = lax.fori_loop(0, PIECES // 4, add, carry)
    scale = 1.0 / (UNIT * STEPS * number)
    mean = jnp.concatenate([(part + OFFSET * weights) * scale for part in sums], axis=0)
    mean = mean.astype(jnp.bfloat16)

    def write(i, carry):
        out_ref[i] = mean
        return carry

    lax.fori_loop(0, STACK, write, 0)


def average(pieces, interpret=False):
    vmem = pl.BlockSpec(memory_space=pltpu.VMEM)
    return pl.pallas_call(
        average_kernel,
        out_shape=jax.ShapeDtypeStruct((STACK, TALL, COLS), jnp.bfloat16),
        in_specs=[vmem],
        out_specs=vmem,
        compiler_params=pltpu.CompilerParams(vmem_limit_bytes=SMALL_BYTES),
        interpret=interpret,
    )(pieces)


def lay_kernel(*refs):
    parts, (_, out_ref, wide, narrow, sems) = refs[:CUBES], refs[CUBES:]
    main = PIECE // 8 * 8

    @pl.when(own_flags()[1] == 0)
    def _():
        for cube, ref in zip((OWN,) + DIRECT + PASSED, parts):
            for i in range(STACK):
                at = cube_member(cube, i) * PIECE
                piece = ref[i].astype(jnp.float32)
                wide[at : at + main, :] = piece[:main]
                wide[at + main : at + PIECE, :] = piece[main:PIECE]

        part = FLAT // SIDE
        copies = []
        for k in range(SIDE):

            def narrower(i, carry):
                for u in range(9):
                    at = pl.multiple_of(k * part + i * 144 + u * 16, 16)
                    narrow[pl.ds(at, 16), :] = wide[pl.ds(at, 16), :].astype(jnp.bfloat16)
                return carry

            lax.fori_loop(0, part // 144, narrower, 0)
            here = pl.ds(k * part, part)
            copies.append(pltpu.make_async_copy(narrow.at[here], out_ref.at[here], sems.at[k]))
            copies[k].start()
        for copy in copies:
            copy.wait()


def lay(parts, evolved):
    vmem = pl.BlockSpec(memory_space=pltpu.VMEM)
    anywhere = pl.BlockSpec(memory_space=pl.ANY)
    return pl.pallas_call(
        lay_kernel,
        out_shape=jax.ShapeDtypeStruct((FLAT, COLS), jnp.bfloat16),
        in_specs=[vmem] * CUBES + [anywhere],
        out_specs=anywhere,
        scratch_shapes=[
            pltpu.VMEM((FLAT + 2 * PAD, COLS), jnp.float32),
            pltpu.VMEM((FLAT, COLS), jnp.bfloat16),
            pltpu.SemaphoreType.DMA((SIDE,)),
        ],
        input_output_aliases={CUBES: 0},
        compiler_params=pltpu.CompilerParams(vmem_limit_bytes=SMALL_BYTES),
    )(*parts, evolved)


def tables():
    group_speed = 0.45 * np.exp(-math.log(1.1) * np.arange(NF))
    angles = 2.0 * math.pi / ND * np.arange(ND)

    def wide(values, times):
        return np.repeat(np.repeat(values, times)[:, None], COLS, axis=1).astype(np.float32)

    cosine, sine = np.cos(angles), np.sin(angles)
    twice = BLOCK // ND
    per_row = (wide(cosine, ROWS), wide(sine, ROWS))
    per_bin = (wide(np.tile(cosine, twice), 1), wide(np.tile(sine, twice), 1))
    return (group_speed.astype(np.float32),) + per_row + per_bin


def spots():
    both = []
    for cell in range(2):
        chosen = np.zeros((4 * ROWS, (ROWS + 2) * COLS), np.float32)
        near = (ROWS - 1, ROWS - 2) if cell else (0, 1)
        for block, source in enumerate(tuple(range(ROWS)) + tuple(ROWS + row for row in near)):
            chosen[2 * source, block * COLS] = 1.0
            chosen[2 * source + 1, (block + 1) * COLS - 1] = 1.0
        both.append(chosen)
    return np.stack(both).astype(jnp.bfloat16)


def swap(x):
    return lax.ppermute(x, "cell", [(0, 1), (1, 0)])


def on_device(
    spectrum,
    depth_factor,
    wet_mask,
    frac_index,
    boundary_map,
    average_map,
    dia_plus,
    dia_minus,
    dia_coef,
):
    parent = lax.axis_size("grid") - 1
    hubs = hub_places()
    spec = spectrum.reshape(FLAT, COLS)
    maps, *parts = send_first(boundary_map.T, spec)

    held = [lax.ppermute(part, "grid", [(parent, hub)]) for part, hub in zip(parts, hubs[1:])]
    maps = lax.all_to_all(maps, "grid", 0, 0)
    near, near_statics = prepare(spec, depth_factor, wet_mask, frac_index)
    near = swap(near)
    near_statics = swap(near_statics)
    picked = lax.all_to_all(pick(maps, spec, *held), "grid", 0, 0)
    picked = jnp.concatenate([picked[hub] for hub in hubs], axis=1)
    far = swap(picked)

    group_speed, cosine, sine, cosine_bin, sine_bin = tables()
    evolved, pieces = evolve(
        dia_plus * ROWS + PAD,
        dia_minus * ROWS + PAD,
        group_speed,
        dia_coef,
        spec,
        near,
        picked,
        far,
        spots(),
        depth_factor,
        wet_mask,
        frac_index,
        near_statics,
        cosine,
        sine,
        cosine_bin,
        sine_bin,
        average_map,
    )
    copies = average(lax.all_to_all(pieces, "grid", 0, 0))
    last = SIDE - 1
    cubes = [[cube_member(k, i) for i in range(STACK)] for k in range(CUBES)]
    gathered = lax.all_to_all(copies, "grid", 0, 0, axis_index_groups=cubes)
    wrapping = [place(last, last, 0), place(last, 0, last), place(0, last, last)]
    relays = [place(last, last, last - 1), place(last, last - 1, last), place(last - 1, last, last)]
    relays.append(wrapping[2])
    far = [place(last, 0, 1), place(0, 1, last), place(1, last, 0), place(0, 0, 0)]
    relayed = lax.ppermute(gathered, "grid", list(zip(far, relays)))
    parts = [lax.ppermute(gathered, "grid", [(device, parent)]) for device in wrapping]
    parts += [lax.ppermute(relayed, "grid", [(device, parent)]) for device in relays]
    parts = [gathered] + parts
    return lay(parts, evolved).reshape(BINS, ROWS, COLS)


def solution(mesh):
    placed = (
        P(None, ("grid", "cell"), None),
        P(("grid", "cell"), None),
        P(("grid", "cell"), None),
        P(("grid", "cell"), None),
        P(("grid", "cell"), None),
        P(("grid", "cell"), None),
        P(),
        P(),
        P(),
    )
    return jax.shard_map(
        on_device,
        mesh=mesh,
        in_specs=placed,
        out_specs=P(None, ("grid", "cell"), None),
        check_vma=False,
    )
```

```python
import functools
import math

import jax
import jax.numpy as jnp
import numpy as np
from jax import lax
from jax.experimental import pallas as pl
from jax.experimental.pallas import tpu as pltpu
from jax.sharding import PartitionSpec as P

NF = 36
ND = 36
SIDE = 4
ROWS = 4
COLS = 128
CELLS = ROWS * COLS
BINS = NF * ND
FLAT = BINS * ROWS
PAD = 8
PIECES = SIDE**3
TOGETHER = 6
PIECE = FLAT // PIECES
TALL = 88
BLOCK = 72
GROUP = 3
CHUNK = 432
WIDTH = 512
UNIT = 512.0
STEPS = 65534.0
OFFSET = 32767
VMEM_BYTES = 24 * 1024 * 1024
SMALL_BYTES = 10 * 1024 * 1024
LARGE_BYTES = 56 * 1024 * 1024
STACK = 8
HELD = 384

FRACTIONS = (0.25, 0.5, 0.75, 1.0)


def fraction(frac_index):
    open_share = jnp.zeros(frac_index.shape, jnp.float32)
    for position, share in enumerate(FRACTIONS):
        open_share = open_share + jnp.where(frac_index == position, share, 0.0)
    return open_share


def place(z, y, x):
    return (z % SIDE * SIDE + y % SIDE) * SIDE + x % SIDE


def hub_places():
    last = SIDE - 1
    return [
        place(last, last, last),
        place(last, last, last - 1),
        place(last, last - 1, last),
        place(last - 1, last, last),
    ]


def cube_member(cube, position):
    zyx = [2 * (cube // d % 2) + position // d % 2 for d in (4, 2, 1)]
    return (zyx[0] * SIDE + zyx[1]) * SIDE + zyx[2]


CUBES = 8
DIRECT = (6, 5, 3)
PASSED = (4, 1, 2, 0)
OWN = 7


def own_flags():
    return 1 - lax.axis_index("cell"), jnp.where(lax.axis_index("grid") == PIECES - 1, 0, 1)


def bin_block(ref, index):
    return ref[8 * index : 8 * index + 8, :]


def send_kernel(map_ref, spec_ref, maps_ref, *part_refs):
    lane = lax.broadcasted_iota(jnp.int32, (PIECES, COLS), 1)
    maps = jnp.zeros((PIECES, COLS), jnp.int32)
    for r in range(ROWS):
        for side in range(2):
            maps = jnp.where(lane == 2 * r + side, map_ref[side, r], maps)
    maps_ref[...] = maps
    part = FLAT // SIDE
    for k, ref in enumerate(part_refs):
        ref[...] = spec_ref[(k + 1) * part : (k + 2) * part, :]


def send_first(maps, spec):
    vmem = pl.BlockSpec(memory_space=pltpu.VMEM)
    part = jax.ShapeDtypeStruct((FLAT // SIDE, COLS), jnp.bfloat16)
    return pl.pallas_call(
        send_kernel,
        out_shape=(jax.ShapeDtypeStruct((PIECES, COLS), jnp.int32),) + (part,) * (SIDE - 1),
        in_specs=[pl.BlockSpec(memory_space=pltpu.SMEM), vmem],
        out_specs=(vmem,) * SIDE,
        compiler_params=pltpu.CompilerParams(vmem_limit_bytes=LARGE_BYTES),
    )(maps, spec)


def join_kernel(spec_ref, a_ref, b_ref, c_ref, out_ref, wide, mine, sem):
    part = FLAT // SIDE
    share = jnp.where(own_flags()[1] == 0, 1.0, 0.0)
    copy = pltpu.make_async_copy(spec_ref.at[pl.ds(0, part), :], mine, sem)
    copy.start()
    copy.wait()

    def join(i, carry):
        for u in range(9):
            at = pl.multiple_of(i * 144 + u * 16, 16)
            here = pl.ds(at, 16)
            value = mine[here, :].astype(jnp.float32) * share
            for ref in (a_ref, b_ref, c_ref):
                value = value + ref[here, :].astype(jnp.float32)
            wide[here, :] = value
        return carry

    lax.fori_loop(0, part // 144, join, 0)
    wide[part:, :] = jnp.zeros((wide.shape[0] - part, COLS), jnp.float32)
    many = wide.shape[0] // ROWS
    for r in range(ROWS):
        row = wide[pl.ds(r, many, stride=ROWS), :].astype(jnp.bfloat16)
        out_ref[:, r * COLS : (r + 1) * COLS] = row


def join_held(*operands):
    vmem = pl.BlockSpec(memory_space=pltpu.VMEM)
    part = FLAT // SIDE
    return pl.pallas_call(
        join_kernel,
        out_shape=jax.ShapeDtypeStruct((HELD, CELLS), jnp.bfloat16),
        in_specs=[pl.BlockSpec(memory_space=pl.ANY)] + [vmem] * 3,
        out_specs=vmem,
        scratch_shapes=[
            pltpu.VMEM((HELD * ROWS, COLS), jnp.float32),
            pltpu.VMEM((part, COLS), jnp.bfloat16),
            pltpu.SemaphoreType.DMA,
        ],
        compiler_params=pltpu.CompilerParams(vmem_limit_bytes=SMALL_BYTES),
        cost_estimate=pl.CostEstimate(flops=2_000_000, bytes_accessed=2_000_000, transcendentals=0),
    )(*operands)


def pick_kernel(maps_ref, held_ref, out_ref, turned, hot):
    bins = BINS // SIDE
    cell = lax.broadcasted_iota(jnp.int32, (PIECES, CELLS), 1)
    for e in range(2 * ROWS):
        wanted = jnp.broadcast_to(maps_ref[:, e : e + 1], (PIECES, CELLS))
        same = jnp.where(cell == wanted, 1.0, 0.0).astype(jnp.bfloat16)
        hot[e * PIECES : (e + 1) * PIECES, :] = same
    found = lax.dot_general(
        hot[...], held_ref[...], (((1,), (1,)), ((), ())), preferred_element_type=jnp.float32
    )
    for e in range(2 * ROWS):
        for t in range(HELD // COLS):
            part = found[e * PIECES : (e + 1) * PIECES, t * COLS : (t + 1) * COLS]
            turned[t, pl.ds(e, PIECES, stride=2 * ROWS), :] = part

    def narrower(i, carry):
        for u in range(8):
            g = i * 8 + u
            at = pl.multiple_of(g * 2 * ROWS, 8)
            for t in range(HELD // COLS):
                lanes = min(COLS, bins - t * COLS)
                value = turned[t, pl.ds(at, 2 * ROWS), :lanes].astype(jnp.bfloat16)
                out_ref[g, :, t * COLS : t * COLS + lanes] = value
        return carry

    lax.fori_loop(0, PIECES // 8, narrower, 0)


def pick(maps, held):
    vmem = pl.BlockSpec(memory_space=pltpu.VMEM)
    return pl.pallas_call(
        pick_kernel,
        out_shape=jax.ShapeDtypeStruct((PIECES, 2 * ROWS, BINS // SIDE), jnp.bfloat16),
        in_specs=[vmem] * 2,
        out_specs=vmem,
        scratch_shapes=[
            pltpu.VMEM((HELD // COLS, PIECES * 2 * ROWS, COLS), jnp.float32),
            pltpu.VMEM((PIECES * 2 * ROWS, CELLS), jnp.bfloat16),
        ],
        compiler_params=pltpu.CompilerParams(vmem_limit_bytes=SMALL_BYTES),
    )(maps, held)


def prepare_kernel(spec_ref, depth_ref, wet_ref, frac_ref, near_ref, stat_ref, dens):
    first = own_flags()[0] == 1
    wet = wet_ref[...].astype(jnp.float32)
    values = (depth_ref[...], wet * fraction(frac_ref[...]), wet)
    for i, value in enumerate(values):
        stat_ref[2 * i : 2 * i + 1, :] = jnp.where(first, value[3:4], value[0:1])
        stat_ref[2 * i + 1 : 2 * i + 2, :] = jnp.where(first, value[2:3], value[1:2])
    stat_ref[6:8, :] = jnp.zeros((2, COLS), jnp.float32)

    def widen(i, carry):
        for u in range(12):
            at = pl.multiple_of(i * 192 + u * 16, 16)
            dens[pl.ds(at, 16), :] = spec_ref[pl.ds(at, 16), :].astype(jnp.float32)
        return carry

    lax.fori_loop(0, FLAT // 192, widen, 0)
    nearer = 3 * own_flags()[0]
    farther = 1 + own_flags()[0]

    def pull(i, carry):
        for u in range(9):
            at = pl.multiple_of(i * 144 + u * 16, 16)
            for n, row in enumerate((nearer, farther)):
                rows = dens[pl.ds(at * ROWS + row, 16, stride=ROWS), :]
                near_ref[n, pl.ds(at, 16), :] = rows.astype(jnp.bfloat16)
        return carry

    lax.fori_loop(0, BINS // 144, pull, 0)


def prepare(*operands, interpret=False):
    vmem = pl.BlockSpec(memory_space=pltpu.VMEM)
    return pl.pallas_call(
        prepare_kernel,
        out_shape=(
            jax.ShapeDtypeStruct((2, BINS, COLS), jnp.bfloat16),
            jax.ShapeDtypeStruct((8, COLS), jnp.float32),
        ),
        in_specs=[vmem] * 4,
        out_specs=(vmem,) * 2,
        scratch_shapes=[pltpu.VMEM((FLAT, COLS), jnp.float32)],
        compiler_params=pltpu.CompilerParams(vmem_limit_bytes=SMALL_BYTES),
        cost_estimate=pl.CostEstimate(flops=4_000_000, bytes_accessed=5_000_000, transcendentals=0),
        interpret=interpret,
    )(*operands)


def step_kernel(
    plus_ref,
    minus_ref,
    speed_ref,
    coef_ref,
    spec_ref,
    near_ref,
    edge_ref,
    far_ref,
    spot_ref,
    depth_ref,
    wet_ref,
    frac_ref,
    stat_ref,
    cos_ref,
    sin_ref,
    cosb_ref,
    sinb_ref,
    target_ref,
    out_ref,
    pieces_ref,
    dens,
    flat,
    halo,
    evol,
    near,
    hot,
    count,
    tab_x,
    tab_y,
    tab_z,
    tab_an,
    tab_nb,
    tab_n,
    done_out,
    out_sem,
):
    first = own_flags()[0] == 1
    child = own_flags()[1]
    adjacent = 3 * own_flags()[0]
    sign = jnp.where(first, 1.0, -1.0)
    lane = lax.broadcasted_iota(jnp.int32, (16, COLS), 1)
    ends = jnp.where((lane == 0) | (lane == COLS - 1), child, 0) > 0

    values = jnp.concatenate([edge_ref[...], far_ref[...]], axis=0)
    spot = spot_ref[1 - own_flags()[0]]
    for base in range(0, BINS, WIDTH):
        wide_rows = min(WIDTH, BINS - base)
        laid = lax.dot_general(
            values[:, base : base + wide_rows],
            spot,
            (((0,), (0,)), ((), ())),
            preferred_element_type=jnp.float32,
        )
        lanes = lax.broadcasted_iota(jnp.int32, (wide_rows, COLS), 1)
        ends_wide = jnp.where((lanes == 0) | (lanes == COLS - 1), child, 0) > 0
        for r in range(ROWS):
            here = pl.ds(base * ROWS + r, wide_rows, stride=ROWS)
            flat[here, :] = laid[:, r * COLS : (r + 1) * COLS]
        for n in range(2):
            raw = near_ref[n, base : base + wide_rows, :].astype(jnp.float32)
            at = (ROWS + n) * COLS
            raw = jnp.where(ends_wide, laid[:, at : at + COLS], raw)
            near[n, base : base + wide_rows, :] = raw * stat_ref[4 + n : 5 + n, :]

    wet = jnp.concatenate([wet_ref[...]] * 2, axis=0).astype(jnp.float32)
    wet16 = jnp.concatenate([wet, wet], axis=0)

    def begin(i, carry):
        for u in range(12):
            at = pl.multiple_of(i * 192 + u * 16, 16)
            raw = spec_ref[pl.ds(at, 16), :].astype(jnp.float32)
            dens[pl.ds(PAD + at, 16), :] = jnp.where(ends, flat[pl.ds(at, 16), :], raw) * wet16
            halo[pl.ds(at, 16), :] = jnp.zeros((16, COLS), jnp.float32)
        return carry

    lax.fori_loop(0, FLAT // 192, begin, 0)

    sub = lax.broadcasted_iota(jnp.int32, (8, COLS), 0)
    low = sub < ROWS
    depth = jnp.concatenate([depth_ref[...]] * 2, axis=0)
    weight = wet * fraction(jnp.concatenate([frac_ref[...]] * 2, axis=0))

    def between(d0, d1, w0, w1):
        return 0.5 * (d0 + d1) * w0 * w1

    def along(d, w):
        face = between(d, pltpu.roll(d, COLS - 1, 1), w, pltpu.roll(w, COLS - 1, 1))
        return jnp.where(lane[:8] == COLS - 1, 0.0, face)

    def wide(row):
        return jnp.broadcast_to(row, (8, COLS))

    face_x = between(depth, pltpu.roll(depth, 7, 0), weight, pltpu.roll(weight, 7, 0))
    face_x = jnp.where(sub % ROWS == ROWS - 1, 0.0, face_x)
    face_y = along(depth, weight)
    d_own = wide(jnp.where(first, depth[3:4], depth[0:1]))
    w_own = wide(jnp.where(first, weight[3:4], weight[0:1]))
    d_n1, d_n2, w_n1, w_n2 = (wide(stat_ref[i : i + 1, :]) for i in range(4))
    face_an = between(d_own, d_n1, w_own, w_n1)
    face_nb = between(d_n1, d_n2, w_n1, w_n2)
    face_n = along(d_n1, w_n1)

    for q in range(ND // 2):
        tab_x[8 * q : 8 * q + 8, :] = face_x * bin_block(cos_ref, q)
        tab_y[8 * q : 8 * q + 8, :] = face_y * bin_block(sin_ref, q)
        if 2 * q > ND // 2:
            back = 8 * (q - ND // 4)
            tab_z[back : back + 8, :] = pltpu.roll(face_y, 1, 1) * bin_block(sin_ref, q)
    for j in range(BLOCK // 8):
        tab_an[8 * j : 8 * j + 8, :] = face_an * bin_block(cosb_ref, j)
        tab_nb[8 * j : 8 * j + 8, :] = face_nb * bin_block(cosb_ref, j)
        tab_n[8 * j : 8 * j + 8, :] = face_n * bin_block(sinb_ref, j)

    def halo_fluxes(bins, rows):
        many = range(BLOCK // 8)
        n1s = [near[0, pl.ds(bins + 8 * j, 8), :] for j in many]
        owns = [dens[pl.ds(PAD + rows + 32 * j + adjacent, 8, stride=ROWS), :] for j in many]
        fluxes = []
        for j in many:
            along = bin_block(tab_an, j)
            top = jnp.where(first, owns[j], n1s[j])
            bottom = jnp.where(first, n1s[j], owns[j])
            fluxes.append(jnp.maximum(along, 0.0) * top + jnp.minimum(along, 0.0) * bottom)
        for j in many:
            halo[pl.ds(rows + 32 * j + adjacent, 8, stride=ROWS), :] = sign * fluxes[j]
        return n1s, fluxes

    def advance_near(bins, speeds, n1s, fluxes):
        n2s = [near[1, pl.ds(bins + 8 * j, 8), :] for j in range(BLOCK // 8)]
        after_near = []
        for j in range(BLOCK // 8):
            n1, n2 = n1s[j], n2s[j]
            top, bottom = jnp.where(first, n1, n2), jnp.where(first, n2, n1)
            along = bin_block(tab_nb, j)
            beyond = jnp.maximum(along, 0.0) * top + jnp.minimum(along, 0.0) * bottom
            along = bin_block(tab_n, j)
            right = pltpu.roll(n1, COLS - 1, 1)
            fy = jnp.maximum(along, 0.0) * n1 + jnp.minimum(along, 0.0) * right
            change = sign * (beyond - fluxes[j]) + (fy - pltpu.roll(fy, 1, 1))
            speed = speeds[0] if j < 4 else (jnp.where(low, *speeds) if j == 4 else speeds[1])
            after_near.append(n1 - speed * change)
        for j in range(BLOCK // 8):
            near[0, pl.ds(bins + 8 * j, 8), :] = after_near[j]

    def advance(q, speed, rho, across):
        along_x = bin_block(tab_x, q)
        if 2 * q + 1 < ND // 4 or 2 * q > 3 * ND // 4:
            fx = along_x * rho
        else:
            after = pltpu.roll(rho, 7, 0)
            if ND // 4 < 2 * q and 2 * q + 1 < 3 * ND // 4:
                fx = along_x * after
            else:
                fx = jnp.maximum(along_x, 0.0) * rho + jnp.minimum(along_x, 0.0) * after
        along_y = bin_block(tab_y, q)
        if 2 * q + 1 < ND // 2:
            fy = along_y * rho
            out_y = fy - pltpu.roll(fy, 1, 1)
        elif 2 * q > ND // 2:
            out_y = along_y * pltpu.roll(rho, COLS - 1, 1) - bin_block(tab_z, q - ND // 4) * rho
        else:
            right = pltpu.roll(rho, COLS - 1, 1)
            fy = jnp.maximum(along_y, 0.0) * rho + jnp.minimum(along_y, 0.0) * right
            out_y = fy - pltpu.roll(fy, 1, 1)
        change = (fx - pltpu.roll(fx, 1, 0)) + out_y
        return rho - speed * (change + across)

    def advance_all(starts, speeds):
        for q in range(0, ND // 2, GROUP):
            group = [
                (p, rows + 8 * (p + h * ND // 2), speed[h])
                for p in range(q, q + GROUP)
                for rows, speed in zip(starts, speeds)
                for h in range(2)
            ]
            loaded = [(dens[pl.ds(PAD + at, 8), :], halo[pl.ds(at, 8), :]) for _, at, _ in group]
            moved = [advance(p, speed, *pair) for (p, _, speed), pair in zip(group, loaded)]
            for (_, at, _), value in zip(group, moved):
                dens[pl.ds(PAD + at, 8), :] = value

    def blocks(i, carry):
        ks = [i * TOGETHER + u for u in range(TOGETHER)]
        bins = [pl.multiple_of(k * BLOCK, 8) for k in ks]
        rows = [pl.multiple_of(k * (BLOCK * ROWS), 16) for k in ks]
        speeds = [(speed_ref[2 * k], speed_ref[2 * k + 1]) for k in ks]
        halos = [halo_fluxes(*pair) for pair in zip(bins, rows)]
        for start, speed, values in zip(bins, speeds, halos):
            advance_near(start, speed, *values)
        advance_all(rows, speeds)
        for pair in zip(bins, rows):
            halo_fluxes(*pair)
        advance_all(rows, speeds)
        return carry

    lax.fori_loop(0, BINS // BLOCK // TOGETHER, blocks, 0)

    def interact(f, carry):
        rows = pl.multiple_of(f * (ND * ROWS), 16)
        scale = 0.2 * coef_ref[f]

        def partner(ref, b):
            lower = dens[pl.ds(ref[f * ND + b], 8), :]
            upper = dens[pl.ds(ref[f * ND + b + 1] - ROWS, 8), :]
            return jnp.where(low, lower, upper)

        for g in range(0, ND // 4, 3):
            bs = [4 * (g + t) + 2 * h for t in range(3) for h in range(2)]
            mines = [dens[pl.ds(PAD + rows + 4 * b, 8), :] for b in bs]
            pairs = [(partner(plus_ref, b), partner(minus_ref, b)) for b in bs]
            done = []
            for mine, (plus, minus) in zip(mines, pairs):
                source = mine * (mine * (plus + minus) - 2.0 * (plus * minus))
                done.append(jnp.maximum(mine + scale * source, 0.0))
            for b, value in zip(bs, done):
                evol[pl.ds(rows + 4 * b, 8), :] = value
            for t in range(3):
                both = jnp.concatenate(done[2 * t : 2 * t + 2], axis=0).astype(jnp.bfloat16)
                done_out[pl.ds(rows + 16 * (g + t), 16), :] = both
        return carry

    lax.fori_loop(0, NF, interact, 0)
    leaving = pltpu.make_async_copy(done_out, out_ref, out_sem)
    leaving.start()

    row = lax.broadcasted_iota(jnp.int32, (CELLS, COLS), 0)
    for r in range(ROWS):
        own = lane[:1] + r * COLS
        same = row == jnp.where(child == 1, target_ref[r : r + 1, :], own)
        hot[:, r * COLS : (r + 1) * COLS] = jnp.where(same, 1.0, 0.0).astype(jnp.bfloat16)
    inner = (((1,), (1,)), ((), ()))
    number = lax.dot_general(
        jnp.ones((16, CELLS), jnp.bfloat16), hot[...], inner, preferred_element_type=jnp.float32
    )
    share = 1.0 / jnp.maximum(number[0:1], 1.0)
    count[...] = jnp.zeros_like(count)
    for turn in range(ROWS):
        for r in range(ROWS):
            of = (turn + r) % ROWS
            here = number[0:1, of * COLS : (of + 1) * COLS].astype(jnp.int32)
            count[turn, PIECE % 8 + r : PIECE % 8 + r + 1, :] = here

    many = CHUNK

    def sums(c, carry):
        base = c * (many * ROWS)
        parts = [evol[pl.ds(base + r, many, stride=ROWS), :] for r in range(ROWS)]
        value = jnp.concatenate(parts, axis=1)
        head = value.astype(jnp.bfloat16)
        tail = (value - head.astype(jnp.float32)).astype(jnp.bfloat16)
        total = lax.dot_general(head, hot[...], inner, preferred_element_type=jnp.float32)
        total += lax.dot_general(tail, hot[...], inner, preferred_element_type=jnp.float32)
        for r in range(ROWS):
            part = slice(r * COLS, (r + 1) * COLS)
            flat[pl.ds(base + r, many, stride=ROWS), :] = total[:, part] * share[:, part]
        return carry

    lax.fori_loop(0, BINS // many, sums, 0)
    main = PIECE // 8 * 8
    row = main + lax.broadcasted_iota(jnp.int32, (8, COLS), 0)

    def cut(i, carry):
        for u in range(2 * ROWS):
            j, turn = i * 2 * ROWS + u, u % ROWS
            mean = flat[pl.ds(j * PIECE, main), :]
            last = jnp.where(row < PIECE, flat[pl.ds(j * PIECE + main, 8), :], 0.0)
            top = jnp.maximum(
                jnp.max(mean, axis=0, keepdims=True), jnp.max(last, axis=0, keepdims=True)
            )
            size = jnp.minimum((top * UNIT).astype(jnp.int32) + 1, OFFSET)
            steps = (UNIT * STEPS) / size.astype(jnp.float32)
            code = (mean * steps + 0.5).astype(jnp.int32) - OFFSET
            code_last = (last * steps + 0.5).astype(jnp.int32) - OFFSET
            rest = jnp.where(row == PIECE + ROWS, size, count[turn])
            code_last = jnp.where(row < PIECE, code_last, rest)
            code = jnp.concatenate([code, code_last], axis=0)
            pieces_ref[j] = code.astype(jnp.int16)
        return carry

    lax.fori_loop(0, PIECES // ROWS // 2, cut, 0)
    leaving.wait()


def evolve(*operands, interpret=False):
    smem = pl.BlockSpec(memory_space=pltpu.SMEM)
    vmem = pl.BlockSpec(memory_space=pltpu.VMEM)
    return pl.pallas_call(
        step_kernel,
        out_shape=(
            jax.ShapeDtypeStruct((FLAT, COLS), jnp.bfloat16),
            jax.ShapeDtypeStruct((PIECES, TALL, COLS), jnp.int16),
        ),
        in_specs=[smem] * 4 + [vmem] * 14,
        out_specs=(pl.BlockSpec(memory_space=pl.ANY), vmem),
        scratch_shapes=[
            pltpu.VMEM((FLAT + 2 * PAD, COLS), jnp.float32),
            pltpu.VMEM((FLAT + 2 * PAD, COLS), jnp.float32),
            pltpu.VMEM((FLAT, COLS), jnp.float32),
            pltpu.VMEM((FLAT, COLS), jnp.float32),
            pltpu.VMEM((2, BINS, COLS), jnp.float32),
            pltpu.VMEM((CELLS, CELLS), jnp.bfloat16),
            pltpu.VMEM((ROWS, 8, COLS), jnp.int32),
            pltpu.VMEM((ND * ROWS, COLS), jnp.float32),
            pltpu.VMEM((ND * ROWS, COLS), jnp.float32),
            pltpu.VMEM((ND * ROWS // 2, COLS), jnp.float32),
            pltpu.VMEM((BLOCK, COLS), jnp.float32),
            pltpu.VMEM((BLOCK, COLS), jnp.float32),
            pltpu.VMEM((BLOCK, COLS), jnp.float32),
            pltpu.VMEM((FLAT, COLS), jnp.bfloat16),
            pltpu.SemaphoreType.DMA,
        ],
        compiler_params=pltpu.CompilerParams(vmem_limit_bytes=VMEM_BYTES),
        cost_estimate=pl.CostEstimate(
            flops=1_400_000_000, bytes_accessed=10_000_000, transcendentals=0
        ),
        interpret=interpret,
    )(*operands)


def average_kernel(pieces_ref, out_ref):
    blocks = TALL // 8
    sub = lax.broadcasted_iota(jnp.int32, (8, COLS), 0)

    def add(i, carry):
        sums, weights, number = carry
        for u in range(4):
            piece = pieces_ref[4 * i + u].astype(jnp.int32).astype(jnp.float32)
            rest = piece[TALL - 8 :]
            at = PIECE % 8
            turned = [pltpu.roll(rest, shift - at, 0) for shift in (8, ROWS)]
            count = jnp.where(sub < ROWS, *turned)
            weight = count * jnp.broadcast_to(rest[at + ROWS : at + ROWS + 1], (8, COLS))
            sums = tuple(sums[b] + piece[8 * b : 8 * b + 8] * weight for b in range(blocks))
            weights, number = weights + weight, number + count
        return sums, weights, number

    zero = jnp.zeros((8, COLS), jnp.float32)
    carry = ((zero,) * blocks, zero, zero)
    sums, weights, number = lax.fori_loop(0, PIECES // 4, add, carry)
    scale = 1.0 / (UNIT * STEPS * number)
    mean = jnp.concatenate([(part + OFFSET * weights) * scale for part in sums], axis=0)
    mean = mean.astype(jnp.bfloat16)

    def write(i, carry):
        out_ref[i] = mean
        return carry

    lax.fori_loop(0, STACK, write, 0)


def average(pieces, interpret=False):
    vmem = pl.BlockSpec(memory_space=pltpu.VMEM)
    return pl.pallas_call(
        average_kernel,
        out_shape=jax.ShapeDtypeStruct((STACK, TALL, COLS), jnp.bfloat16),
        in_specs=[vmem],
        out_specs=vmem,
        compiler_params=pltpu.CompilerParams(vmem_limit_bytes=SMALL_BYTES),
        interpret=interpret,
    )(pieces)


def lay_kernel(*refs):
    parts, (_, out_ref, wide, narrow, sems) = refs[:CUBES], refs[CUBES:]
    main = PIECE // 8 * 8

    @pl.when(own_flags()[1] == 0)
    def _():
        for cube, ref in zip((OWN,) + DIRECT + PASSED, parts):
            for i in range(STACK):
                at = cube_member(cube, i) * PIECE
                piece = ref[i].astype(jnp.float32)
                wide[at : at + main, :] = piece[:main]
                wide[at + main : at + PIECE, :] = piece[main:PIECE]

        part = FLAT // SIDE
        copies = []
        for k in range(SIDE):

            def narrower(i, carry):
                for u in range(9):
                    at = pl.multiple_of(k * part + i * 144 + u * 16, 16)
                    narrow[pl.ds(at, 16), :] = wide[pl.ds(at, 16), :].astype(jnp.bfloat16)
                return carry

            lax.fori_loop(0, part // 144, narrower, 0)
            here = pl.ds(k * part, part)
            copies.append(pltpu.make_async_copy(narrow.at[here], out_ref.at[here], sems.at[k]))
            copies[k].start()
        for copy in copies:
            copy.wait()


def lay(parts, evolved):
    vmem = pl.BlockSpec(memory_space=pltpu.VMEM)
    anywhere = pl.BlockSpec(memory_space=pl.ANY)
    return pl.pallas_call(
        lay_kernel,
        out_shape=jax.ShapeDtypeStruct((FLAT, COLS), jnp.bfloat16),
        in_specs=[vmem] * CUBES + [anywhere],
        out_specs=anywhere,
        scratch_shapes=[
            pltpu.VMEM((FLAT + 2 * PAD, COLS), jnp.float32),
            pltpu.VMEM((FLAT, COLS), jnp.bfloat16),
            pltpu.SemaphoreType.DMA((SIDE,)),
        ],
        input_output_aliases={CUBES: 0},
        compiler_params=pltpu.CompilerParams(vmem_limit_bytes=SMALL_BYTES),
    )(*parts, evolved)


def tables():
    group_speed = 0.45 * np.exp(-math.log(1.1) * np.arange(NF))
    angles = 2.0 * math.pi / ND * np.arange(ND)

    def wide(values, times):
        return np.repeat(np.repeat(values, times)[:, None], COLS, axis=1).astype(np.float32)

    cosine, sine = np.cos(angles), np.sin(angles)
    twice = BLOCK // ND
    per_row = (wide(cosine, ROWS), wide(sine, ROWS))
    per_bin = (wide(np.tile(cosine, twice), 1), wide(np.tile(sine, twice), 1))
    return (group_speed.astype(np.float32),) + per_row + per_bin


def spots():
    both = []
    for cell in range(2):
        chosen = np.zeros((4 * ROWS, (ROWS + 2) * COLS), np.float32)
        near = (ROWS - 1, ROWS - 2) if cell else (0, 1)
        for block, source in enumerate(tuple(range(ROWS)) + tuple(ROWS + row for row in near)):
            chosen[2 * source, block * COLS] = 1.0
            chosen[2 * source + 1, (block + 1) * COLS - 1] = 1.0
        both.append(chosen)
    return np.stack(both).astype(jnp.bfloat16)


def swap(x):
    return lax.ppermute(x, "cell", [(0, 1), (1, 0)])


def on_device(
    spectrum,
    depth_factor,
    wet_mask,
    frac_index,
    boundary_map,
    average_map,
    dia_plus,
    dia_minus,
    dia_coef,
):
    parent = lax.axis_size("grid") - 1
    hubs = hub_places()
    spec = spectrum.reshape(FLAT, COLS)
    maps, *parts = send_first(boundary_map.T, spec)

    held = [lax.ppermute(part, "grid", [(parent, hub)]) for part, hub in zip(parts, hubs[1:])]
    maps = lax.all_to_all(maps, "grid", 0, 0)
    near, near_statics = prepare(spec, depth_factor, wet_mask, frac_index)
    near = swap(near)
    near_statics = swap(near_statics)
    picked = lax.all_to_all(pick(maps, join_held(spec, *held)), "grid", 0, 0)
    picked = jnp.concatenate([picked[hub] for hub in hubs], axis=1)
    far = swap(picked)

    group_speed, cosine, sine, cosine_bin, sine_bin = tables()
    evolved, pieces = evolve(
        dia_plus * ROWS + PAD,
        dia_minus * ROWS + PAD,
        group_speed,
        dia_coef,
        spec,
        near,
        picked,
        far,
        spots(),
        depth_factor,
        wet_mask,
        frac_index,
        near_statics,
        cosine,
        sine,
        cosine_bin,
        sine_bin,
        average_map,
    )
    copies = average(lax.all_to_all(pieces, "grid", 0, 0))
    last = SIDE - 1
    cubes = [[cube_member(k, i) for i in range(STACK)] for k in range(CUBES)]
    gathered = lax.all_to_all(copies, "grid", 0, 0, axis_index_groups=cubes)
    wrapping = [place(last, last, 0), place(last, 0, last), place(0, last, last)]
    relays = [place(last, last, last - 1), place(last, last - 1, last), place(last - 1, last, last)]
    relays.append(wrapping[2])
    far = [place(last, 0, 1), place(0, 1, last), place(1, last, 0), place(0, 0, 0)]
    relayed = lax.ppermute(gathered, "grid", list(zip(far, relays)))
    parts = [lax.ppermute(gathered, "grid", [(device, parent)]) for device in wrapping]
    parts += [lax.ppermute(relayed, "grid", [(device, parent)]) for device in relays]
    parts = [gathered] + parts
    return lay(parts, evolved).reshape(BINS, ROWS, COLS)


def solution(mesh):
    placed = (
        P(None, ("grid", "cell"), None),
        P(("grid", "cell"), None),
        P(("grid", "cell"), None),
        P(("grid", "cell"), None),
        P(("grid", "cell"), None),
        P(("grid", "cell"), None),
        P(),
        P(),
        P(),
    )
    return jax.shard_map(
        on_device,
        mesh=mesh,
        in_specs=placed,
        out_specs=P(None, ("grid", "cell"), None),
        check_vma=False,
    )
```

```python
import functools
import math

import jax
import jax.numpy as jnp
import numpy as np
from jax import lax
from jax.experimental import pallas as pl
from jax.experimental.pallas import tpu as pltpu
from jax.sharding import PartitionSpec as P

NF = 36
ND = 36
SIDE = 4
ROWS = 4
COLS = 128
CELLS = ROWS * COLS
BINS = NF * ND
FLAT = BINS * ROWS
PAD = 8
PIECES = SIDE**3
TOGETHER = 9
PIECE = FLAT // PIECES
TALL = 88
BLOCK = 72
GROUP = 3
CHUNK = 432
WIDTH = 512
UNIT = 512.0
STEPS = 65534.0
OFFSET = 32767
VMEM_BYTES = 24 * 1024 * 1024
SMALL_BYTES = 10 * 1024 * 1024
LARGE_BYTES = 56 * 1024 * 1024
STACK = 8
HELD = 384

FRACTIONS = (0.25, 0.5, 0.75, 1.0)


def fraction(frac_index):
    open_share = jnp.zeros(frac_index.shape, jnp.float32)
    for position, share in enumerate(FRACTIONS):
        open_share = open_share + jnp.where(frac_index == position, share, 0.0)
    return open_share


def place(z, y, x):
    return (z % SIDE * SIDE + y % SIDE) * SIDE + x % SIDE


def hub_places():
    last = SIDE - 1
    return [
        place(last, last, last),
        place(last, last, last - 1),
        place(last, last - 1, last),
        place(last - 1, last, last),
    ]


def cube_member(cube, position):
    zyx = [2 * (cube // d % 2) + position // d % 2 for d in (4, 2, 1)]
    return (zyx[0] * SIDE + zyx[1]) * SIDE + zyx[2]


CUBES = 8
DIRECT = (6, 5, 3)
PASSED = (4, 1, 2, 0)
OWN = 7


def own_flags():
    return 1 - lax.axis_index("cell"), jnp.where(lax.axis_index("grid") == PIECES - 1, 0, 1)


def bin_block(ref, index):
    return ref[8 * index : 8 * index + 8, :]


def send_kernel(map_ref, spec_ref, maps_ref, *part_refs):
    lane = lax.broadcasted_iota(jnp.int32, (PIECES, COLS), 1)
    maps = jnp.zeros((PIECES, COLS), jnp.int32)
    for r in range(ROWS):
        for side in range(2):
            maps = jnp.where(lane == 2 * r + side, map_ref[side, r], maps)
    maps_ref[...] = maps
    part = FLAT // SIDE
    for k, ref in enumerate(part_refs):
        ref[...] = spec_ref[(k + 1) * part : (k + 2) * part, :]


def send_first(maps, spec):
    vmem = pl.BlockSpec(memory_space=pltpu.VMEM)
    part = jax.ShapeDtypeStruct((FLAT // SIDE, COLS), jnp.bfloat16)
    return pl.pallas_call(
        send_kernel,
        out_shape=(jax.ShapeDtypeStruct((PIECES, COLS), jnp.int32),) + (part,) * (SIDE - 1),
        in_specs=[pl.BlockSpec(memory_space=pltpu.SMEM), vmem],
        out_specs=(vmem,) * SIDE,
        compiler_params=pltpu.CompilerParams(vmem_limit_bytes=LARGE_BYTES),
    )(maps, spec)


def join_kernel(spec_ref, a_ref, b_ref, c_ref, out_ref, wide, mine, sem):
    part = FLAT // SIDE
    share = jnp.where(own_flags()[1] == 0, 1.0, 0.0)
    copy = pltpu.make_async_copy(spec_ref.at[pl.ds(0, part), :], mine, sem)
    copy.start()
    copy.wait()

    def join(i, carry):
        for u in range(9):
            at = pl.multiple_of(i * 144 + u * 16, 16)
            here = pl.ds(at, 16)
            value = mine[here, :].astype(jnp.float32) * share
            for ref in (a_ref, b_ref, c_ref):
                value = value + ref[here, :].astype(jnp.float32)
            wide[here, :] = value
        return carry

    lax.fori_loop(0, part // 144, join, 0)
    wide[part:, :] = jnp.zeros((wide.shape[0] - part, COLS), jnp.float32)
    many = wide.shape[0] // ROWS
    for r in range(ROWS):
        row = wide[pl.ds(r, many, stride=ROWS), :].astype(jnp.bfloat16)
        out_ref[:, r * COLS : (r + 1) * COLS] = row


def join_held(*operands):
    vmem = pl.BlockSpec(memory_space=pltpu.VMEM)
    part = FLAT // SIDE
    return pl.pallas_call(
        join_kernel,
        out_shape=jax.ShapeDtypeStruct((HELD, CELLS), jnp.bfloat16),
        in_specs=[pl.BlockSpec(memory_space=pl.ANY)] + [vmem] * 3,
        out_specs=vmem,
        scratch_shapes=[
            pltpu.VMEM((HELD * ROWS, COLS), jnp.float32),
            pltpu.VMEM((part, COLS), jnp.bfloat16),
            pltpu.SemaphoreType.DMA,
        ],
        compiler_params=pltpu.CompilerParams(vmem_limit_bytes=SMALL_BYTES),
        cost_estimate=pl.CostEstimate(flops=2_000_000, bytes_accessed=2_000_000, transcendentals=0),
    )(*operands)


def pick_kernel(maps_ref, held_ref, out_ref, turned, hot):
    bins = BINS // SIDE
    cell = lax.broadcasted_iota(jnp.int32, (PIECES, CELLS), 1)
    for e in range(2 * ROWS):
        wanted = jnp.broadcast_to(maps_ref[:, e : e + 1], (PIECES, CELLS))
        same = jnp.where(cell == wanted, 1.0, 0.0).astype(jnp.bfloat16)
        hot[e * PIECES : (e + 1) * PIECES, :] = same
    found = lax.dot_general(
        hot[...], held_ref[...], (((1,), (1,)), ((), ())), preferred_element_type=jnp.float32
    )
    for e in range(2 * ROWS):
        for t in range(HELD // COLS):
            part = found[e * PIECES : (e + 1) * PIECES, t * COLS : (t + 1) * COLS]
            turned[t, pl.ds(e, PIECES, stride=2 * ROWS), :] = part

    def narrower(i, carry):
        for u in range(8):
            g = i * 8 + u
            at = pl.multiple_of(g * 2 * ROWS, 8)
            for t in range(HELD // COLS):
                lanes = min(COLS, bins - t * COLS)
                value = turned[t, pl.ds(at, 2 * ROWS), :lanes].astype(jnp.bfloat16)
                out_ref[g, :, t * COLS : t * COLS + lanes] = value
        return carry

    lax.fori_loop(0, PIECES // 8, narrower, 0)


def pick(maps, held):
    vmem = pl.BlockSpec(memory_space=pltpu.VMEM)
    return pl.pallas_call(
        pick_kernel,
        out_shape=jax.ShapeDtypeStruct((PIECES, 2 * ROWS, BINS // SIDE), jnp.bfloat16),
        in_specs=[vmem] * 2,
        out_specs=vmem,
        scratch_shapes=[
            pltpu.VMEM((HELD // COLS, PIECES * 2 * ROWS, COLS), jnp.float32),
            pltpu.VMEM((PIECES * 2 * ROWS, CELLS), jnp.bfloat16),
        ],
        compiler_params=pltpu.CompilerParams(vmem_limit_bytes=SMALL_BYTES),
    )(maps, held)


def prepare_kernel(spec_ref, depth_ref, wet_ref, frac_ref, near_ref, stat_ref, dens):
    first = own_flags()[0] == 1
    wet = wet_ref[...].astype(jnp.float32)
    values = (depth_ref[...], wet * fraction(frac_ref[...]), wet)
    for i, value in enumerate(values):
        stat_ref[2 * i : 2 * i + 1, :] = jnp.where(first, value[3:4], value[0:1])
        stat_ref[2 * i + 1 : 2 * i + 2, :] = jnp.where(first, value[2:3], value[1:2])
    stat_ref[6:8, :] = jnp.zeros((2, COLS), jnp.float32)

    def widen(i, carry):
        for u in range(12):
            at = pl.multiple_of(i * 192 + u * 16, 16)
            dens[pl.ds(at, 16), :] = spec_ref[pl.ds(at, 16), :].astype(jnp.float32)
        return carry

    lax.fori_loop(0, FLAT // 192, widen, 0)
    nearer = 3 * own_flags()[0]
    farther = 1 + own_flags()[0]

    def pull(i, carry):
        for u in range(9):
            at = pl.multiple_of(i * 144 + u * 16, 16)
            for n, row in enumerate((nearer, farther)):
                rows = dens[pl.ds(at * ROWS + row, 16, stride=ROWS), :]
                near_ref[n, pl.ds(at, 16), :] = rows.astype(jnp.bfloat16)
        return carry

    lax.fori_loop(0, BINS // 144, pull, 0)


def prepare(*operands, interpret=False):
    vmem = pl.BlockSpec(memory_space=pltpu.VMEM)
    return pl.pallas_call(
        prepare_kernel,
        out_shape=(
            jax.ShapeDtypeStruct((2, BINS, COLS), jnp.bfloat16),
            jax.ShapeDtypeStruct((8, COLS), jnp.float32),
        ),
        in_specs=[vmem] * 4,
        out_specs=(vmem,) * 2,
        scratch_shapes=[pltpu.VMEM((FLAT, COLS), jnp.float32)],
        compiler_params=pltpu.CompilerParams(vmem_limit_bytes=SMALL_BYTES),
        cost_estimate=pl.CostEstimate(flops=4_000_000, bytes_accessed=5_000_000, transcendentals=0),
        interpret=interpret,
    )(*operands)


def step_kernel(
    plus_ref,
    minus_ref,
    speed_ref,
    coef_ref,
    spec_ref,
    near_ref,
    edge_ref,
    far_ref,
    spot_ref,
    depth_ref,
    wet_ref,
    frac_ref,
    stat_ref,
    cos_ref,
    sin_ref,
    cosb_ref,
    sinb_ref,
    target_ref,
    out_ref,
    pieces_ref,
    dens,
    flat,
    halo,
    evol,
    near,
    hot,
    count,
    tab_x,
    tab_y,
    tab_z,
    tab_an,
    tab_nb,
    tab_n,
    done_out,
    out_sem,
):
    first = own_flags()[0] == 1
    child = own_flags()[1]
    adjacent = 3 * own_flags()[0]
    sign = jnp.where(first, 1.0, -1.0)
    lane = lax.broadcasted_iota(jnp.int32, (16, COLS), 1)
    ends = jnp.where((lane == 0) | (lane == COLS - 1), child, 0) > 0

    values = jnp.concatenate([edge_ref[...], far_ref[...]], axis=0)
    spot = spot_ref[1 - own_flags()[0]]
    for base in range(0, BINS, WIDTH):
        wide_rows = min(WIDTH, BINS - base)
        laid = lax.dot_general(
            values[:, base : base + wide_rows],
            spot,
            (((0,), (0,)), ((), ())),
            preferred_element_type=jnp.float32,
        )
        lanes = lax.broadcasted_iota(jnp.int32, (wide_rows, COLS), 1)
        ends_wide = jnp.where((lanes == 0) | (lanes == COLS - 1), child, 0) > 0
        for r in range(ROWS):
            here = pl.ds(base * ROWS + r, wide_rows, stride=ROWS)
            flat[here, :] = laid[:, r * COLS : (r + 1) * COLS]
        for n in range(2):
            raw = near_ref[n, base : base + wide_rows, :].astype(jnp.float32)
            at = (ROWS + n) * COLS
            raw = jnp.where(ends_wide, laid[:, at : at + COLS], raw)
            near[n, base : base + wide_rows, :] = raw * stat_ref[4 + n : 5 + n, :]

    wet = jnp.concatenate([wet_ref[...]] * 2, axis=0).astype(jnp.float32)
    wet16 = jnp.concatenate([wet, wet], axis=0)

    def begin(i, carry):
        for u in range(12):
            at = pl.multiple_of(i * 192 + u * 16, 16)
            raw = spec_ref[pl.ds(at, 16), :].astype(jnp.float32)
            dens[pl.ds(PAD + at, 16), :] = jnp.where(ends, flat[pl.ds(at, 16), :], raw) * wet16
            halo[pl.ds(at, 16), :] = jnp.zeros((16, COLS), jnp.float32)
        return carry

    lax.fori_loop(0, FLAT // 192, begin, 0)

    sub = lax.broadcasted_iota(jnp.int32, (8, COLS), 0)
    low = sub < ROWS
    depth = jnp.concatenate([depth_ref[...]] * 2, axis=0)
    weight = wet * fraction(jnp.concatenate([frac_ref[...]] * 2, axis=0))

    def between(d0, d1, w0, w1):
        return 0.5 * (d0 + d1) * w0 * w1

    def along(d, w):
        face = between(d, pltpu.roll(d, COLS - 1, 1), w, pltpu.roll(w, COLS - 1, 1))
        return jnp.where(lane[:8] == COLS - 1, 0.0, face)

    def wide(row):
        return jnp.broadcast_to(row, (8, COLS))

    face_x = between(depth, pltpu.roll(depth, 7, 0), weight, pltpu.roll(weight, 7, 0))
    face_x = jnp.where(sub % ROWS == ROWS - 1, 0.0, face_x)
    face_y = along(depth, weight)
    d_own = wide(jnp.where(first, depth[3:4], depth[0:1]))
    w_own = wide(jnp.where(first, weight[3:4], weight[0:1]))
    d_n1, d_n2, w_n1, w_n2 = (wide(stat_ref[i : i + 1, :]) for i in range(4))
    face_an = between(d_own, d_n1, w_own, w_n1)
    face_nb = between(d_n1, d_n2, w_n1, w_n2)
    face_n = along(d_n1, w_n1)

    for q in range(ND // 2):
        tab_x[8 * q : 8 * q + 8, :] = face_x * bin_block(cos_ref, q)
        tab_y[8 * q : 8 * q + 8, :] = face_y * bin_block(sin_ref, q)
        if 2 * q > ND // 2:
            back = 8 * (q - ND // 4)
            tab_z[back : back + 8, :] = pltpu.roll(face_y, 1, 1) * bin_block(sin_ref, q)
    for j in range(BLOCK // 8):
        tab_an[8 * j : 8 * j + 8, :] = face_an * bin_block(cosb_ref, j)
        tab_nb[8 * j : 8 * j + 8, :] = face_nb * bin_block(cosb_ref, j)
        tab_n[8 * j : 8 * j + 8, :] = face_n * bin_block(sinb_ref, j)

    def halo_fluxes(bins, rows):
        many = range(BLOCK // 8)
        n1s = [near[0, pl.ds(bins + 8 * j, 8), :] for j in many]
        owns = [dens[pl.ds(PAD + rows + 32 * j + adjacent, 8, stride=ROWS), :] for j in many]
        fluxes = []
        for j in many:
            along = bin_block(tab_an, j)
            top = jnp.where(first, owns[j], n1s[j])
            bottom = jnp.where(first, n1s[j], owns[j])
            fluxes.append(jnp.maximum(along, 0.0) * top + jnp.minimum(along, 0.0) * bottom)
        for j in many:
            halo[pl.ds(rows + 32 * j + adjacent, 8, stride=ROWS), :] = sign * fluxes[j]
        return n1s, fluxes

    def advance_near(bins, speeds, n1s, fluxes):
        n2s = [near[1, pl.ds(bins + 8 * j, 8), :] for j in range(BLOCK // 8)]
        after_near = []
        for j in range(BLOCK // 8):
            n1, n2 = n1s[j], n2s[j]
            top, bottom = jnp.where(first, n1, n2), jnp.where(first, n2, n1)
            along = bin_block(tab_nb, j)
            beyond = jnp.maximum(along, 0.0) * top + jnp.minimum(along, 0.0) * bottom
            along = bin_block(tab_n, j)
            right = pltpu.roll(n1, COLS - 1, 1)
            fy = jnp.maximum(along, 0.0) * n1 + jnp.minimum(along, 0.0) * right
            change = sign * (beyond - fluxes[j]) + (fy - pltpu.roll(fy, 1, 1))
            speed = speeds[0] if j < 4 else (jnp.where(low, *speeds) if j == 4 else speeds[1])
            after_near.append(n1 - speed * change)
        for j in range(BLOCK // 8):
            near[0, pl.ds(bins + 8 * j, 8), :] = after_near[j]

    def advance(q, speed, rho, across):
        along_x = bin_block(tab_x, q)
        if 2 * q + 1 < ND // 4 or 2 * q > 3 * ND // 4:
            fx = along_x * rho
        else:
            after = pltpu.roll(rho, 7, 0)
            if ND // 4 < 2 * q and 2 * q + 1 < 3 * ND // 4:
                fx = along_x * after
            else:
                fx = jnp.maximum(along_x, 0.0) * rho + jnp.minimum(along_x, 0.0) * after
        along_y = bin_block(tab_y, q)
        if 2 * q + 1 < ND // 2:
            fy = along_y * rho
            out_y = fy - pltpu.roll(fy, 1, 1)
        elif 2 * q > ND // 2:
            out_y = along_y * pltpu.roll(rho, COLS - 1, 1) - bin_block(tab_z, q - ND // 4) * rho
        else:
            right = pltpu.roll(rho, COLS - 1, 1)
            fy = jnp.maximum(along_y, 0.0) * rho + jnp.minimum(along_y, 0.0) * right
            out_y = fy - pltpu.roll(fy, 1, 1)
        change = (fx - pltpu.roll(fx, 1, 0)) + out_y
        return rho - speed * (change + across)

    def advance_all(starts, speeds):
        for q in range(0, ND // 2, GROUP):
            group = [
                (p, rows + 8 * (p + h * ND // 2), speed[h])
                for p in range(q, q + GROUP)
                for rows, speed in zip(starts, speeds)
                for h in range(2)
            ]
            loaded = [(dens[pl.ds(PAD + at, 8), :], halo[pl.ds(at, 8), :]) for _, at, _ in group]
            moved = [advance(p, speed, *pair) for (p, _, speed), pair in zip(group, loaded)]
            for (_, at, _), value in zip(group, moved):
                dens[pl.ds(PAD + at, 8), :] = value

    def blocks(i, carry):
        ks = [i * TOGETHER + u for u in range(TOGETHER)]
        bins = [pl.multiple_of(k * BLOCK, 8) for k in ks]
        rows = [pl.multiple_of(k * (BLOCK * ROWS), 16) for k in ks]
        speeds = [(speed_ref[2 * k], speed_ref[2 * k + 1]) for k in ks]
        halos = [halo_fluxes(*pair) for pair in zip(bins, rows)]
        for start, speed, values in zip(bins, speeds, halos):
            advance_near(start, speed, *values)
        advance_all(rows, speeds)
        for pair in zip(bins, rows):
            halo_fluxes(*pair)
        advance_all(rows, speeds)
        return carry

    lax.fori_loop(0, BINS // BLOCK // TOGETHER, blocks, 0)

    def interact(f, carry):
        rows = pl.multiple_of(f * (ND * ROWS), 16)
        scale = 0.2 * coef_ref[f]

        def partner(ref, b):
            lower = dens[pl.ds(ref[f * ND + b], 8), :]
            upper = dens[pl.ds(ref[f * ND + b + 1] - ROWS, 8), :]
            return jnp.where(low, lower, upper)

        for g in range(0, ND // 4, 3):
            bs = [4 * (g + t) + 2 * h for t in range(3) for h in range(2)]
            mines = [dens[pl.ds(PAD + rows + 4 * b, 8), :] for b in bs]
            pairs = [(partner(plus_ref, b), partner(minus_ref, b)) for b in bs]
            done = []
            for mine, (plus, minus) in zip(mines, pairs):
                source = mine * (mine * (plus + minus) - 2.0 * (plus * minus))
                done.append(jnp.maximum(mine + scale * source, 0.0))
            for b, value in zip(bs, done):
                evol[pl.ds(rows + 4 * b, 8), :] = value
            for t in range(3):
                both = jnp.concatenate(done[2 * t : 2 * t + 2], axis=0).astype(jnp.bfloat16)
                done_out[pl.ds(rows + 16 * (g + t), 16), :] = both
        return carry

    lax.fori_loop(0, NF, interact, 0)
    leaving = pltpu.make_async_copy(done_out, out_ref, out_sem)
    leaving.start()

    row = lax.broadcasted_iota(jnp.int32, (CELLS, COLS), 0)
    for r in range(ROWS):
        own = lane[:1] + r * COLS
        same = row == jnp.where(child == 1, target_ref[r : r + 1, :], own)
        hot[:, r * COLS : (r + 1) * COLS] = jnp.where(same, 1.0, 0.0).astype(jnp.bfloat16)
    inner = (((1,), (1,)), ((), ()))
    number = lax.dot_general(
        jnp.ones((16, CELLS), jnp.bfloat16), hot[...], inner, preferred_element_type=jnp.float32
    )
    share = 1.0 / jnp.maximum(number[0:1], 1.0)
    count[...] = jnp.zeros_like(count)
    for turn in range(ROWS):
        for r in range(ROWS):
            of = (turn + r) % ROWS
            here = number[0:1, of * COLS : (of + 1) * COLS].astype(jnp.int32)
            count[turn, PIECE % 8 + r : PIECE % 8 + r + 1, :] = here

    many = CHUNK

    def sums(c, carry):
        base = c * (many * ROWS)
        parts = [evol[pl.ds(base + r, many, stride=ROWS), :] for r in range(ROWS)]
        value = jnp.concatenate(parts, axis=1)
        head = value.astype(jnp.bfloat16)
        tail = (value - head.astype(jnp.float32)).astype(jnp.bfloat16)
        total = lax.dot_general(head, hot[...], inner, preferred_element_type=jnp.float32)
        total += lax.dot_general(tail, hot[...], inner, preferred_element_type=jnp.float32)
        for r in range(ROWS):
            part = slice(r * COLS, (r + 1) * COLS)
            flat[pl.ds(base + r, many, stride=ROWS), :] = total[:, part] * share[:, part]
        return carry

    lax.fori_loop(0, BINS // many, sums, 0)
    main = PIECE // 8 * 8
    row = main + lax.broadcasted_iota(jnp.int32, (8, COLS), 0)

    def cut(i, carry):
        for u in range(2 * ROWS):
            j, turn = i * 2 * ROWS + u, u % ROWS
            mean = flat[pl.ds(j * PIECE, main), :]
            last = jnp.where(row < PIECE, flat[pl.ds(j * PIECE + main, 8), :], 0.0)
            top = jnp.maximum(
                jnp.max(mean, axis=0, keepdims=True), jnp.max(last, axis=0, keepdims=True)
            )
            size = jnp.minimum((top * UNIT).astype(jnp.int32) + 1, OFFSET)
            steps = (UNIT * STEPS) / size.astype(jnp.float32)
            code = (mean * steps + 0.5).astype(jnp.int32) - OFFSET
            code_last = (last * steps + 0.5).astype(jnp.int32) - OFFSET
            rest = jnp.where(row == PIECE + ROWS, size, count[turn])
            code_last = jnp.where(row < PIECE, code_last, rest)
            code = jnp.concatenate([code, code_last], axis=0)
            pieces_ref[j] = code.astype(jnp.int16)
        return carry

    lax.fori_loop(0, PIECES // ROWS // 2, cut, 0)
    leaving.wait()


def evolve(*operands, interpret=False):
    smem = pl.BlockSpec(memory_space=pltpu.SMEM)
    vmem = pl.BlockSpec(memory_space=pltpu.VMEM)
    return pl.pallas_call(
        step_kernel,
        out_shape=(
            jax.ShapeDtypeStruct((FLAT, COLS), jnp.bfloat16),
            jax.ShapeDtypeStruct((PIECES, TALL, COLS), jnp.int16),
        ),
        in_specs=[smem] * 4 + [vmem] * 14,
        out_specs=(pl.BlockSpec(memory_space=pl.ANY), vmem),
        scratch_shapes=[
            pltpu.VMEM((FLAT + 2 * PAD, COLS), jnp.float32),
            pltpu.VMEM((FLAT + 2 * PAD, COLS), jnp.float32),
            pltpu.VMEM((FLAT, COLS), jnp.float32),
            pltpu.VMEM((FLAT, COLS), jnp.float32),
            pltpu.VMEM((2, BINS, COLS), jnp.float32),
            pltpu.VMEM((CELLS, CELLS), jnp.bfloat16),
            pltpu.VMEM((ROWS, 8, COLS), jnp.int32),
            pltpu.VMEM((ND * ROWS, COLS), jnp.float32),
            pltpu.VMEM((ND * ROWS, COLS), jnp.float32),
            pltpu.VMEM((ND * ROWS // 2, COLS), jnp.float32),
            pltpu.VMEM((BLOCK, COLS), jnp.float32),
            pltpu.VMEM((BLOCK, COLS), jnp.float32),
            pltpu.VMEM((BLOCK, COLS), jnp.float32),
            pltpu.VMEM((FLAT, COLS), jnp.bfloat16),
            pltpu.SemaphoreType.DMA,
        ],
        compiler_params=pltpu.CompilerParams(vmem_limit_bytes=VMEM_BYTES),
        cost_estimate=pl.CostEstimate(
            flops=1_400_000_000, bytes_accessed=10_000_000, transcendentals=0
        ),
        interpret=interpret,
    )(*operands)


def average_kernel(pieces_ref, out_ref):
    blocks = TALL // 8
    sub = lax.broadcasted_iota(jnp.int32, (8, COLS), 0)

    def add(i, carry):
        sums, weights, number = carry
        for u in range(8):
            piece = pieces_ref[8 * i + u].astype(jnp.int32).astype(jnp.float32)
            rest = piece[TALL - 8 :]
            at = PIECE % 8
            turned = [pltpu.roll(rest, shift - at, 0) for shift in (8, ROWS)]
            count = jnp.where(sub < ROWS, *turned)
            weight = count * jnp.broadcast_to(rest[at + ROWS : at + ROWS + 1], (8, COLS))
            sums = tuple(sums[b] + piece[8 * b : 8 * b + 8] * weight for b in range(blocks))
            weights, number = weights + weight, number + count
        return sums, weights, number

    zero = jnp.zeros((8, COLS), jnp.float32)
    carry = ((zero,) * blocks, zero, zero)
    sums, weights, number = lax.fori_loop(0, PIECES // 8, add, carry)
    scale = 1.0 / (UNIT * STEPS * number)
    mean = jnp.concatenate([(part + OFFSET * weights) * scale for part in sums], axis=0)
    mean = mean.astype(jnp.bfloat16)

    def write(i, carry):
        out_ref[i] = mean
        return carry

    lax.fori_loop(0, STACK, write, 0)


def average(pieces, interpret=False):
    vmem = pl.BlockSpec(memory_space=pltpu.VMEM)
    return pl.pallas_call(
        average_kernel,
        out_shape=jax.ShapeDtypeStruct((STACK, TALL, COLS), jnp.bfloat16),
        in_specs=[vmem],
        out_specs=vmem,
        compiler_params=pltpu.CompilerParams(vmem_limit_bytes=SMALL_BYTES),
        interpret=interpret,
    )(pieces)


def lay_kernel(*refs):
    parts, (_, out_ref, wide, narrow, sems) = refs[:CUBES], refs[CUBES:]
    main = PIECE // 8 * 8

    @pl.when(own_flags()[1] == 0)
    def _():
        for cube, ref in zip((OWN,) + DIRECT + PASSED, parts):
            for i in range(STACK):
                at = cube_member(cube, i) * PIECE
                piece = ref[i].astype(jnp.float32)
                wide[at : at + main, :] = piece[:main]
                wide[at + main : at + PIECE, :] = piece[main:PIECE]

        part = FLAT // SIDE
        copies = []
        for k in range(SIDE):

            def narrower(i, carry):
                for u in range(9):
                    at = pl.multiple_of(k * part + i * 144 + u * 16, 16)
                    narrow[pl.ds(at, 16), :] = wide[pl.ds(at, 16), :].astype(jnp.bfloat16)
                return carry

            lax.fori_loop(0, part // 144, narrower, 0)
            here = pl.ds(k * part, part)
            copies.append(pltpu.make_async_copy(narrow.at[here], out_ref.at[here], sems.at[k]))
            copies[k].start()
        for copy in copies:
            copy.wait()


def lay(parts, evolved):
    vmem = pl.BlockSpec(memory_space=pltpu.VMEM)
    anywhere = pl.BlockSpec(memory_space=pl.ANY)
    return pl.pallas_call(
        lay_kernel,
        out_shape=jax.ShapeDtypeStruct((FLAT, COLS), jnp.bfloat16),
        in_specs=[vmem] * CUBES + [anywhere],
        out_specs=anywhere,
        scratch_shapes=[
            pltpu.VMEM((FLAT + 2 * PAD, COLS), jnp.float32),
            pltpu.VMEM((FLAT, COLS), jnp.bfloat16),
            pltpu.SemaphoreType.DMA((SIDE,)),
        ],
        input_output_aliases={CUBES: 0},
        compiler_params=pltpu.CompilerParams(vmem_limit_bytes=SMALL_BYTES),
    )(*parts, evolved)


def tables():
    group_speed = 0.45 * np.exp(-math.log(1.1) * np.arange(NF))
    angles = 2.0 * math.pi / ND * np.arange(ND)

    def wide(values, times):
        return np.repeat(np.repeat(values, times)[:, None], COLS, axis=1).astype(np.float32)

    cosine, sine = np.cos(angles), np.sin(angles)
    twice = BLOCK // ND
    per_row = (wide(cosine, ROWS), wide(sine, ROWS))
    per_bin = (wide(np.tile(cosine, twice), 1), wide(np.tile(sine, twice), 1))
    return (group_speed.astype(np.float32),) + per_row + per_bin


def spots():
    both = []
    for cell in range(2):
        chosen = np.zeros((4 * ROWS, (ROWS + 2) * COLS), np.float32)
        near = (ROWS - 1, ROWS - 2) if cell else (0, 1)
        for block, source in enumerate(tuple(range(ROWS)) + tuple(ROWS + row for row in near)):
            chosen[2 * source, block * COLS] = 1.0
            chosen[2 * source + 1, (block + 1) * COLS - 1] = 1.0
        both.append(chosen)
    return np.stack(both).astype(jnp.bfloat16)


def swap(x):
    return lax.ppermute(x, "cell", [(0, 1), (1, 0)])


def on_device(
    spectrum,
    depth_factor,
    wet_mask,
    frac_index,
    boundary_map,
    average_map,
    dia_plus,
    dia_minus,
    dia_coef,
):
    parent = lax.axis_size("grid") - 1
    hubs = hub_places()
    spec = spectrum.reshape(FLAT, COLS)
    maps, *parts = send_first(boundary_map.T, spec)

    held = [lax.ppermute(part, "grid", [(parent, hub)]) for part, hub in zip(parts, hubs[1:])]
    maps = lax.all_to_all(maps, "grid", 0, 0)
    near, near_statics = prepare(spec, depth_factor, wet_mask, frac_index)
    near = swap(near)
    near_statics = swap(near_statics)
    picked = lax.all_to_all(pick(maps, join_held(spec, *held)), "grid", 0, 0)
    picked = jnp.concatenate([picked[hub] for hub in hubs], axis=1)
    far = swap(picked)

    group_speed, cosine, sine, cosine_bin, sine_bin = tables()
    evolved, pieces = evolve(
        dia_plus * ROWS + PAD,
        dia_minus * ROWS + PAD,
        group_speed,
        dia_coef,
        spec,
        near,
        picked,
        far,
        spots(),
        depth_factor,
        wet_mask,
        frac_index,
        near_statics,
        cosine,
        sine,
        cosine_bin,
        sine_bin,
        average_map,
    )
    copies = average(lax.all_to_all(pieces, "grid", 0, 0))
    last = SIDE - 1
    cubes = [[cube_member(k, i) for i in range(STACK)] for k in range(CUBES)]
    gathered = lax.all_to_all(copies, "grid", 0, 0, axis_index_groups=cubes)
    wrapping = [place(last, last, 0), place(last, 0, last), place(0, last, last)]
    relays = [place(last, last, last - 1), place(last, last - 1, last), place(last - 1, last, last)]
    relays.append(wrapping[2])
    far = [place(last, 0, 1), place(0, 1, last), place(1, last, 0), place(0, 0, 0)]
    relayed = lax.ppermute(gathered, "grid", list(zip(far, relays)))
    parts = [lax.ppermute(gathered, "grid", [(device, parent)]) for device in wrapping]
    parts += [lax.ppermute(relayed, "grid", [(device, parent)]) for device in relays]
    parts = [gathered] + parts
    return lay(parts, evolved).reshape(BINS, ROWS, COLS)


def solution(mesh):
    placed = (
        P(None, ("grid", "cell"), None),
        P(("grid", "cell"), None),
        P(("grid", "cell"), None),
        P(("grid", "cell"), None),
        P(("grid", "cell"), None),
        P(("grid", "cell"), None),
        P(),
        P(),
        P(),
    )
    return jax.shard_map(
        on_device,
        mesh=mesh,
        in_specs=placed,
        out_specs=P(None, ("grid", "cell"), None),
        check_vma=False,
    )
```
